32 devices in a mesh: gx: 8 (over z, y), gy: 4 (over x, core).
Axes of the slice: x: 2, y: 2, z: 4, core: 2. Of those that a mesh axis runs over, the one named last changes fastest.
Arguments:
- delta: float32 [4, 128, 64, 128], P(None, 'gx', 'gy'), may hold values from -6 to 6
- alpha: float32 [8, 16, 4, 128], P('gx', 'gy'), may hold values from -6 to 6
- eddy: float32 [128, 64, 128], P('gx', 'gy'), may hold values from 0.02 to 0.2
- courant: float32 [2, 128, 64, 128], P(None, 'gx', 'gy'), may hold values from -0.4 to 0.4
- tile_map: int32 [128, 64], P('gx', 'gy'), may hold values from 0 to 15
- obs_rows: float32 [256, 3, 128], P(('gx', 'gy')), may hold values from -6 to 6
- gate_beam: int32 [8, 4, 256], P('gx', 'gy'), may hold values from 0 to 63
- gate_index: int32 [8, 4, 256], P('gx', 'gy'), may hold values from 0 to 127
- gate_column: int32 [8, 4, 256], P('gx', 'gy'), may hold values from 0 to 255
- gate_live: int32 [8, 4, 256], P('gx', 'gy'), may hold values 0 or 1
- obs_weight: float32 [8, 4, 256, 4, 128], P('gx', 'gy'), may hold values from -0.25 to 0.25
- obs_precision: float32 [8, 4, 256], P('gx', 'gy'), may hold values from 4 to 64
Outputs:
- grad_delta: float32 [4, 128, 64, 128], P(None, 'gx', 'gy')
- grad_alpha: float32 [8, 16, 4, 128], P('gx', 'gy')
The draws below stay inside these ranges and needn't reach their ends.
Inputs may be any that keep to these rules, and one draw needn't show every extreme that they name: `gate_beam`: a slot's beam is numbered within its own north-south row of tiles as the east-west index of the beam's owner times 8 plus its place among that owner's beams. `gate_column`: column index within the tile is east-west offset times 16 plus north-south offset.
All inputs are finite; a program needn't handle non-finite values. No bound on the sum of `gate_live` on one device may be relied on, other than what follows from the above.
Results may differ from the reference program's by a relative error of at most 0.00011.
Values sent between devices are 32-bit elements; how exact they have to be, the bound alone decides.
No kernel may reach another device: no remote copies, remote signals or barrier semaphores. Data moves between devices by JAX's collectives and lax.ppermute only.
A program may use at most 64 MiB of HBM per device.

```python
import math
import jax
import jax.numpy as jnp
from jax import lax

CX = 16
CY = 16
NZ = 128
STEPS = 3
BD = 8
NG = 128
GT = 256
NX = 128
NY = 64
NCT = 16
BEAMS = 256
N_GX = 8
N_GY = 4


def touch_ends(drawn, key, smallest, largest):
    place = [jax.random.randint(jax.random.fold_in(key, axis), (), 0, length) for axis, length in enumerate(drawn.shape)]
    longest = drawn.shape.index(max(drawn.shape))
    next_to = place[:longest] + [(place[longest] + 1) % drawn.shape[longest]] + place[longest + 1:]
    return drawn.at[tuple(place)].set(smallest).at[tuple(next_to)].set(largest)


def steps_of(key, shape, pieces, least, top_value):
    gain = 1.0
    for dim, blocks in pieces:
        draws = jax.random.uniform(jax.random.fold_in(jax.random.fold_in(key, 6), dim), (blocks,), jnp.float32, least / len(pieces), top_value / len(pieces))
        gain = gain * jnp.repeat(jnp.exp(draws), shape[dim] // blocks).reshape((-1,) + (1,) * (len(shape) - 1 - dim))
    return gain


def normal_values(rng, dims, scale, most, shards=(), held_as=jnp.bfloat16):
    array = jax.random.normal(rng, dims, jnp.float32) * scale
    if len(shards) > 0:
        array = steps_of(rng, dims, shards, -0.22, 0.18) * array
    return jnp.clip(array, min=-most, max=most).astype(held_as)


def setup_inputs(seed: int = 0) -> dict:
    streams_of = jax.random.split(jax.random.key(seed), 13)
    delta = normal_values(streams_of[0], (4, NX, NY, NZ), 1.0, 6.0, ((1, 8), (2, 4)), jnp.float32)
    alpha = normal_values(streams_of[1], (N_GX, NCT, 4, NZ), 1.0, 6.0, ((0, 8), (1, 4)), jnp.float32)
    eddy = jnp.clip(jnp.exp(math.log(0.2) - 2.3025851 * jax.random.uniform(streams_of[2], (NX, NY, NZ), jnp.float32) ** steps_of(streams_of[2], (NX, NY, NZ), ((0, 8), (1, 4)), -0.2, 0.2)), 0.02, 0.2)
    courant = jnp.clip(jax.random.uniform(streams_of[3], (2, NX, NY, NZ), jnp.float32, -0.4, 0.4) * steps_of(streams_of[3], (2, NX, NY, NZ), ((1, 8), (2, 4)), -0.4, 0.0), -0.4, 0.4)
    tile_map = touch_ends(jax.random.randint(streams_of[4], (NX, NY), 0, NCT), jax.random.fold_in(streams_of[4], 1), 0, NCT - 1).astype(jnp.int32)
    obs_rows = normal_values(streams_of[5], (BEAMS, STEPS, NG), 1.0, 6.0, ((0, 32),), jnp.float32)
    gate_beam = touch_ends(jax.random.randint(streams_of[6], (N_GX, N_GY, GT), 0, N_GX * BD), jax.random.fold_in(streams_of[6], 1), 0, (N_GX * BD) - 1).astype(jnp.int32)
    gate_index = touch_ends(jax.random.randint(streams_of[7], (N_GX, N_GY, GT), 0, NG), jax.random.fold_in(streams_of[7], 1), 0, NG - 1).astype(jnp.int32)
    gate_column = touch_ends(jax.random.randint(streams_of[8], (N_GX, N_GY, GT), 0, CX * CY), jax.random.fold_in(streams_of[8], 1), 0, (CX * CY) - 1).astype(jnp.int32)
    gate_live = touch_ends((jax.random.randint(streams_of[9], (N_GX, N_GY, GT), 0, 4) < 3).astype(jnp.int32), jax.random.fold_in(streams_of[9], 1), 0, 1)
    obs_weight = normal_values(streams_of[10], (N_GX, N_GY, GT, 4, NZ), (4 * NZ) ** -0.5, 0.25, ((0, 8), (1, 4)), jnp.float32)
    obs_precision = jnp.clip(jnp.exp(math.log(64.0) - 2.7725887 * jax.random.uniform(streams_of[11], (N_GX, N_GY, GT), jnp.float32) ** steps_of(streams_of[11], (N_GX, N_GY, GT), ((0, 8), (1, 4)), -0.2, 0.2)), 4.0, 64.0)
    return {"delta": delta, "alpha": alpha, "eddy": eddy, "courant": courant, "tile_map": tile_map, "obs_rows": obs_rows, "gate_beam": gate_beam, "gate_index": gate_index, "gate_column": gate_column, "gate_live": gate_live, "obs_weight": obs_weight, "obs_precision": obs_precision}


profile_weight = 0.125
highest = lax.Precision.HIGHEST

def advance(state, eddy, courant):
    padded = jnp.pad(state, ((0, 0), (1, 1), (1, 1), (0, 0)))
    east_side = padded[:, 2:, 1:-1]
    west_side = padded[:, :-2, 1:-1]
    north_side = padded[:, 1:-1, 2:]
    south_side = padded[:, 1:-1, :-2]
    return state + eddy * (east_side + west_side + north_side + south_side - 4.0 * state) - 0.5 * courant[0] * (east_side - west_side) - 0.5 * courant[1] * (north_side - south_side)

def to_tiles(grid):
    return grid.reshape(4, N_GX, CX, N_GY, CY, NZ).transpose(1, 3, 0, 2, 4, 5).reshape(N_GX, N_GY, 4, CX * CY, NZ)

def from_tiles(tiles):
    return tiles.reshape(N_GX, N_GY, 4, CX, CY, NZ).transpose(2, 0, 3, 1, 4, 5).reshape(4, NX, NY, NZ)

def tile_seen(tile, columns, weights):
    picked = jnp.take(tile, columns, axis=1)
    return jnp.einsum('cgz,gcz->g', picked, weights, precision=highest)

def tile_push(misfit, columns, weights):
    pushed = jax.ops.segment_sum(misfit[:, None, None] * weights, columns, num_segments=CX * CY)
    return jnp.transpose(pushed, (1, 0, 2))

def reference(delta, alpha, eddy, courant, tile_map, obs_rows, gate_beam, gate_index, gate_column, gate_live, obs_weight, obs_precision):
    column_x = (jnp.arange(NX, dtype=jnp.int32) // CX)[:, None]
    profiles = alpha[column_x, tile_map]
    state = delta + profile_weight * jnp.transpose(profiles, (2, 0, 1, 3))
    row_y = jnp.arange(N_GY, dtype=jnp.int32)[None, :, None]
    owner_beam = (gate_beam // BD * N_GY + row_y) * BD + gate_beam % BD
    scaled = gate_live.astype(jnp.float32) * obs_precision
    seen_fn = jax.vmap(jax.vmap(tile_seen))
    push_fn = jax.vmap(jax.vmap(tile_push))
    forcings = []
    for step in range(STEPS):
        state = advance(state, eddy, courant)
        seen = seen_fn(to_tiles(state), gate_column, obs_weight)
        observed = obs_rows[owner_beam, step, gate_index]
        misfit = scaled * (seen - observed)
        forcings.append(from_tiles(push_fn(misfit, gate_column, obs_weight)))
    adjoint = forcings[STEPS - 1]
    for step in range(STEPS - 1, -1, -1):
        _, backward = jax.vjp(lambda value: advance(value, eddy, courant), adjoint)
        adjoint = backward(adjoint)[0]
        if step > 0:
            adjoint = adjoint + forcings[step - 1]
    segment = (column_x * NCT + tile_map).reshape(-1)
    flat_adjoint = jnp.transpose(adjoint, (1, 2, 0, 3)).reshape(NX * NY, 4, NZ)
    sums = jax.ops.segment_sum(flat_adjoint, segment, num_segments=N_GX * NCT).reshape(N_GX, NCT, 4, NZ)
    return (delta + adjoint, alpha + profile_weight * sums)
```

```python
import jax
import jax.numpy as jnp
from jax import lax
from jax.sharding import PartitionSpec as P

STEPS = 3
RIM = 3

profile_weight = 0.125
highest = lax.Precision.HIGHEST


def as_rows(block):
    return block.reshape(-1, block.shape[-1])


def lane_rows(block, count, levels):
    return jnp.pad(block, ((0, count - block.shape[0]), (0, levels - block.shape[1])))


def take_rows(buffer, start, shape):
    count = 1
    for length in shape[:-1]:
        count *= length
    return buffer[start : start + count].reshape(shape), start + count


def line_shift(block, axis, forward):
    count = lax.axis_size(axis)
    pairs = [(i, i + 1) for i in range(count - 1)]
    if not forward:
        pairs = [(target, source) for source, target in pairs]
    return lax.ppermute(block, axis, pairs)


def ring_shift(block, axis, step):
    count = lax.axis_size(axis)
    return lax.ppermute(block, axis, [(i, (i + step) % count) for i in range(count)])


def on_device(
    delta,
    alpha,
    eddy,
    courant,
    tile_map,
    obs_rows,
    gate_beam,
    gate_index,
    gate_column,
    gate_live,
    obs_weight,
    obs_precision,
):
    nc, rows, columns, levels = delta.shape
    owned = alpha.shape[1]
    ny = lax.axis_size("gy")
    me = lax.axis_index("gy")
    inner = RIM - 1
    wide = rows + 2 * RIM
    high = columns + 2 * RIM
    coefs = jnp.concatenate([eddy[None], courant], axis=0)
    tiles = tile_map.astype(jnp.float32)

    def x_pack(edge, coef_edge, tile_edge):
        return jnp.concatenate(
            [as_rows(edge), as_rows(coef_edge), as_rows(alpha), lane_rows(tile_edge, 8, levels)]
        )

    from_west = line_shift(x_pack(delta[:, -RIM:], coefs[:, -inner:], tiles[-RIM:]), "gx", True)
    from_east = line_shift(x_pack(delta[:, :RIM], coefs[:, :inner], tiles[:RIM]), "gx", False)

    def x_unpack(buffer):
        edge, at = take_rows(buffer, 0, (nc, RIM, columns, levels))
        coef_edge, at = take_rows(buffer, at, (3, inner, columns, levels))
        profile, at = take_rows(buffer, at, (owned, nc, levels))
        return edge, coef_edge, profile, buffer[at : at + RIM, :columns]

    west = x_unpack(from_west)
    east = x_unpack(from_east)
    delta_x = jnp.concatenate([west[0], delta, east[0]], axis=1)
    coefs_x = jnp.concatenate([west[1], coefs, east[1]], axis=1)
    profiles = jnp.stack([west[2], alpha[0], east[2]])
    tiles_x = jnp.concatenate([west[3], tiles, east[3]], axis=0)

    def y_pack(edge, coef_edge):
        return jnp.concatenate(
            [as_rows(edge), as_rows(coef_edge), as_rows(profiles), lane_rows(tiles_x, 24, levels)]
        )

    from_south = ring_shift(y_pack(delta_x[:, :, -RIM:], coefs_x[:, :, -inner:]), "gy", 1)
    from_north = ring_shift(y_pack(delta_x[:, :, :RIM], coefs_x[:, :, :inner]), "gy", -1)
    others = [ring_shift(as_rows(profiles), "gy", shift) for shift in range(2, ny - 1)]

    def y_unpack(buffer, valid, place):
        edge, at = take_rows(buffer, 0, (nc, wide, RIM, levels))
        coef_edge, at = take_rows(buffer, at, (3, rows + 2 * inner, inner, levels))
        profile, at = take_rows(buffer, at, (3, owned, nc, levels))
        return (
            jnp.where(valid, edge, 0.0),
            jnp.where(valid, coef_edge, 0.0),
            profile,
            jnp.where(valid, buffer[at : at + wide, place : place + RIM], -1.0),
        )

    has_south = me > 0
    has_north = me < ny - 1
    south = y_unpack(from_south, has_south, columns - RIM)
    north = y_unpack(from_north, has_north, 0)
    delta_all = jnp.concatenate([south[0], delta_x, north[0]], axis=2)
    coefs_all = jnp.concatenate([south[1], coefs_x, north[1]], axis=2)
    tiles_all = jnp.concatenate([south[3], tiles_x, north[3]], axis=1)
    by_shift = (
        [profiles, south[2]]
        + [other.reshape(3, owned, nc, levels) for other in others]
        + [north[2]]
    )
    known = jnp.stack(by_shift, axis=1)
    shift_id = (me - lax.iota(jnp.int32, ny)) % ny
    tile_id = (shift_id[:, None] * owned + lax.iota(jnp.int32, owned)[None]).astype(jnp.float32)
    strip = jnp.concatenate(
        [jnp.full((RIM,), 0), jnp.full((rows,), 1), jnp.full((RIM,), 2)]
    ).astype(jnp.int32)
    selector = (
        (tiles_all[:, :, None, None, None] == tile_id[None, None, None])
        & (strip[:, None, None, None, None] == lax.iota(jnp.int32, 3)[None, None, :, None, None])
    ).astype(jnp.float32)
    selector = selector.reshape(wide * high, 3 * ny * owned)
    state = delta_all + profile_weight * jnp.transpose(
        jnp.dot(
            selector, known.reshape(3 * ny * owned, nc * levels), precision=highest
        ).reshape(wide, high, nc, levels),
        (2, 0, 1, 3),
    )

    gathered = lax.all_gather(obs_rows, "gx", axis=0, tiled=True)
    weights = obs_weight[0, 0]
    scaled = gate_live[0, 0].astype(jnp.float32) * obs_precision[0, 0]
    slots = gate_column[0, 0]
    slot_pick = (slots[:, None] == lax.iota(jnp.int32, rows * columns)[None]).astype(jnp.float32)
    beam_pick = (gate_beam[0, 0][:, None] == lax.iota(jnp.int32, gathered.shape[0])[None]).astype(
        jnp.float32
    )
    gate_pick = (gate_index[0, 0][:, None] == lax.iota(jnp.int32, obs_rows.shape[2])[None]).astype(
        jnp.float32
    )
    rows_seen = jnp.einsum("gb,bkn->kgn", beam_pick, gathered, precision=highest)
    observed = jnp.sum(rows_seen * gate_pick[None], axis=2)

    centre = 1.0 - 4.0 * coefs_all[0]
    to_east = coefs_all[0] - 0.5 * coefs_all[1]
    to_west = coefs_all[0] + 0.5 * coefs_all[1]
    to_north = coefs_all[0] - 0.5 * coefs_all[2]
    to_south = coefs_all[0] + 0.5 * coefs_all[2]

    def cut(field, margin):
        first = inner - margin
        return field[first : first + rows + 2 * margin, first : first + columns + 2 * margin]

    forcings = []
    for step in range(STEPS):
        margin = STEPS - 1 - step
        state = (
            cut(centre, margin) * state[:, 1:-1, 1:-1]
            + cut(to_east, margin) * state[:, 2:, 1:-1]
            + cut(to_west, margin) * state[:, :-2, 1:-1]
            + cut(to_north, margin) * state[:, 1:-1, 2:]
            + cut(to_south, margin) * state[:, 1:-1, :-2]
        )
        own = state[:, margin : margin + rows, margin : margin + columns]
        picked = jnp.einsum(
            "gp,cpz->gcz", slot_pick, own.reshape(nc, rows * columns, levels), precision=highest
        )
        seen = jnp.sum(picked * weights, axis=(1, 2))
        misfit = scaled * (seen - observed[step])
        forcing = jnp.einsum(
            "gp,gcz->cpz", slot_pick, misfit[:, None, None] * weights, precision=highest
        )
        forcings.append(forcing.reshape(nc, rows, columns, levels))
    adjoint = forcings[STEPS - 1]
    for margin in range(STEPS):
        if margin > 0:
            adjoint = adjoint + jnp.pad(
                forcings[STEPS - 1 - margin],
                ((0, 0), (margin, margin), (margin, margin), (0, 0)),
            )

        def spread(field, low_x, low_y):
            return jnp.pad(
                cut(field, margin)[None] * adjoint,
                ((0, 0), (low_x, 2 - low_x), (low_y, 2 - low_y), (0, 0)),
            )

        adjoint = (
            spread(centre, 1, 1)
            + spread(to_east, 2, 1)
            + spread(to_west, 0, 1)
            + spread(to_north, 1, 2)
            + spread(to_south, 1, 0)
        )

    sums = lax.dot_general(
        selector,
        jnp.transpose(adjoint, (1, 2, 0, 3)).reshape(wide * high, nc * levels),
        (((0,), (0,)), ((), ())),
        precision=highest,
    ).reshape(3, ny, owned, nc, levels)

    def back_pack(edge, shift):
        return jnp.concatenate([as_rows(edge), as_rows(sums[:, shift])])

    got_north = ring_shift(back_pack(adjoint[:, :, :RIM], 1), "gy", -1)
    got_south = ring_shift(back_pack(adjoint[:, :, -RIM:], ny - 1), "gy", 1)
    got_others = [ring_shift(as_rows(sums[:, shift]), "gy", -shift) for shift in range(2, ny - 1)]
    edge_shape = (nc, wide, RIM, levels)
    sum_shape = (3, owned, nc, levels)
    edge_north, at = take_rows(got_north, 0, edge_shape)
    sum_north, _ = take_rows(got_north, at, sum_shape)
    edge_south, at = take_rows(got_south, 0, edge_shape)
    sum_south, _ = take_rows(got_south, at, sum_shape)
    total = sums[:, 0] + sum_north + sum_south
    for other in got_others:
        total = total + other.reshape(sum_shape)
    adjoint = adjoint[:, :, RIM:-RIM]
    adjoint = adjoint.at[:, :, :RIM].add(jnp.where(has_south, edge_south, 0.0))
    adjoint = adjoint.at[:, :, -RIM:].add(jnp.where(has_north, edge_north, 0.0))

    def home_pack(edge, strip_sum):
        return jnp.concatenate([as_rows(edge), as_rows(strip_sum)])

    got_east = line_shift(home_pack(adjoint[:, :RIM], total[0]), "gx", False)
    got_west = line_shift(home_pack(adjoint[:, -RIM:], total[2]), "gx", True)
    edge_shape = (nc, RIM, columns, levels)
    sum_shape = (owned, nc, levels)
    edge_east, at = take_rows(got_east, 0, edge_shape)
    sum_east, _ = take_rows(got_east, at, sum_shape)
    edge_west, at = take_rows(got_west, 0, edge_shape)
    sum_west, _ = take_rows(got_west, at, sum_shape)
    adjoint = adjoint[:, RIM:-RIM]
    adjoint = adjoint.at[:, :RIM].add(edge_west)
    adjoint = adjoint.at[:, -RIM:].add(edge_east)
    grad_alpha = alpha + profile_weight * (total[1] + sum_east + sum_west)[None]
    return (delta + adjoint, grad_alpha)


def solution(mesh):
    return jax.shard_map(
        on_device,
        mesh=mesh,
        in_specs=(
            P(None, "gx", "gy", None),
            P("gx", "gy", None, None),
            P("gx", "gy", None),
            P(None, "gx", "gy", None),
            P("gx", "gy"),
            P(("gx", "gy"), None, None),
            P("gx", "gy", None),
            P("gx", "gy", None),
            P("gx", "gy", None),
            P("gx", "gy", None),
            P("gx", "gy", None, None, None),
            P("gx", "gy", None),
        ),
        out_specs=(P(None, "gx", "gy", None), P("gx", "gy", None, None)),
        check_vma=False,
    )
```

```python
import jax
import jax.numpy as jnp
from jax import lax
from jax.experimental import pallas as pl
from jax.experimental.pallas import tpu as pltpu
from jax.sharding import PartitionSpec as P

STEPS = 3
RIM = 3
INNER = RIM - 1
NC = 4
CX = 16
CY = 16
BLOCKS = CX + 8
PITCH = CY + 8
FIRST = 4
FIELD = BLOCKS * PITCH
NORTH = CY
SOUTH = PITCH - RIM

X_COEF = NC * RIM * CY
X_ALPHA = X_COEF + 3 * INNER * CY
Y_COEF = NC * RIM * BLOCKS
Y_ALPHA = Y_COEF + 3 * INNER * BLOCKS

profile_weight = 0.125
f32 = jnp.float32
bf16 = jnp.bfloat16

VMEM = pl.BlockSpec(memory_space=pltpu.VMEM)
ANY = pl.BlockSpec(memory_space=pl.ANY)


def call(body, outs, ins, scratch=(), in_specs=None, aliases=None, flops=1000000, limit=40 * 2**20):
    single = not isinstance(outs, list)
    shapes = [jax.ShapeDtypeStruct(shape, f32) for shape in ([outs] if single else outs)]
    size = sum(4 * value.size for value in ins)
    got = pl.pallas_call(
        body,
        out_shape=shapes,
        in_specs=in_specs or [VMEM] * len(ins),
        out_specs=[VMEM] * len(shapes),
        scratch_shapes=list(scratch),
        input_output_aliases=aliases or {},
        compiler_params=pltpu.CompilerParams(vmem_limit_bytes=limit),
        cost_estimate=pl.CostEstimate(flops=flops, bytes_accessed=size, transcendentals=0),
    )(*ins)
    return got[0] if single else got


def parity(axis):
    return lax.rem(lax.axis_index(axis), 2) == 0


def pair_a(block, axis):
    count = lax.axis_size(axis)
    return lax.ppermute(block, axis, [(i, i ^ 1) for i in range(count)])


def pair_b(block, axis, wrap):
    count = lax.axis_size(axis)
    pairs = []
    for low in range(1, count, 2):
        other = (low + 1) % count
        if other or wrap:
            pairs += [(low, other), (other, low)]
    return lax.ppermute(block, axis, pairs)


def partner(axis, xor):
    return [(i, i ^ xor) for i in range(lax.axis_size(axis))]


def split(value):
    top = value.astype(bf16)
    return top, (value - top.astype(f32)).astype(bf16)


def pack_x(delta, eddy, courant, alpha, tiles, out_a, out_b):
    even = parity("gx")

    def put(at, count, east_side, west_side):
        out_a[at : at + count] = jnp.where(even, east_side, west_side)
        out_b[at : at + count] = jnp.where(even, west_side, east_side)

    wide = RIM * CY
    for c in range(NC):
        put(c * wide, wide, delta[c, CX * CY - wide :], delta[c, :wide])
    slim = INNER * CY
    for f in range(3):
        field = eddy if f == 0 else courant.at[f - 1]
        put(X_COEF + f * slim, slim, field[CX * CY - slim :], field[:slim])
    own = alpha[...]
    put(X_ALPHA, own.shape[0], own, own)
    at = X_ALPHA + own.shape[0]
    for out in (out_a, out_b):
        out[at : at + CX] = jnp.full((CX, 128), -1.0, f32)
        out[at : at + CX, 0:CY] = tiles[...].astype(f32)


def pack_y(delta, eddy, courant, alpha, tiles, got_a, got_b, out_a, out_b, shared):
    even = parity("gy")
    even_x = parity("gx")
    owned = alpha.shape[0]
    out_a[...] = jnp.zeros(out_a.shape, f32)
    out_b[...] = jnp.zeros(out_b.shape, f32)

    def sides(rows):
        first, second = got_a[rows], got_b[rows]
        return jnp.where(even_x, second, first), jnp.where(even_x, first, second)

    def put(at, count, north_side, south_side):
        out_a[at : at + count] = jnp.where(even, north_side, south_side)
        out_b[at : at + count] = jnp.where(even, south_side, north_side)

    def edge(at, own, base, layers, north_y, south_y):
        north_w, north_e = sides(pl.ds(base + north_y, layers, stride=CY))
        south_w, south_e = sides(pl.ds(base + south_y, layers, stride=CY))
        put(at + FIRST - layers, layers, north_w, south_w)
        put(
            at + FIRST,
            CX,
            own[pl.ds(north_y, CX, stride=CY)],
            own[pl.ds(south_y, CX, stride=CY)],
        )
        put(at + FIRST + CX, layers, north_e, south_e)

    for c in range(NC):
        for d in range(RIM):
            edge((c * RIM + d) * BLOCKS, delta.at[c], c * RIM * CY, RIM, CY - RIM + d, d)
    for f in range(3):
        for d in range(INNER):
            edge(
                Y_COEF + (f * INNER + d) * BLOCKS,
                eddy if f == 0 else courant.at[f - 1],
                X_COEF + f * INNER * CY,
                INNER,
                CY - INNER + d,
                d,
            )
    west, east = sides(pl.ds(X_ALPHA, owned))
    shared[0:owned] = west
    shared[owned : 2 * owned] = alpha[...]
    shared[2 * owned : 3 * owned] = east
    west, east = sides(pl.ds(X_ALPHA + owned, CX))
    at = 3 * owned
    shared[at : at + BLOCKS] = jnp.full((BLOCKS, 128), -1.0, f32)
    shared[at + FIRST - RIM : at + FIRST] = west[CX - RIM :]
    shared[at + FIRST : at + FIRST + CX, 0:CY] = tiles[...].astype(f32)
    shared[at + FIRST + CX : at + FIRST + CX + RIM] = east[:RIM]
    whole = shared[...]
    for out in (out_a, out_b):
        out[Y_ALPHA:] = whole


def main(
    ny,
    parts,
    delta,
    eddy,
    courant,
    gate_beam,
    gate_index,
    gate_column,
    gate_live,
    precision,
    weights,
    x_a,
    x_b,
    shared,
    y_a,
    y_b,
    *rest,
):
    others = rest[: ny - 3]
    beams = rest[ny - 3 : ny - 3 + parts]
    out_a, out_b, out_sums, out_adjoint = rest[ny - 3 + parts : ny + 1 + parts]
    (state_0, state_1, coef, forcing, known, picks, meta, tiles, table, sums) = rest[
        ny + 1 + parts :
    ]
    per_slot = shared.shape[0] - BLOCKS
    group = per_slot // NC
    owned = group // 3
    total = ny * group
    me = lax.axis_index("gy")
    me_x = lax.axis_index("gx")
    even = parity("gy")
    even_x = parity("gx")
    has_south = me > 0
    has_north = me < ny - 1

    def x_sides(rows):
        first, second = x_a[rows], x_b[rows]
        return jnp.where(even_x, second, first), jnp.where(even_x, first, second)

    def y_sides(rows):
        first, second = y_a[rows], y_b[rows]
        north, south = jnp.where(even, first, second), jnp.where(even, second, first)
        return jnp.where(has_north, north, 0.0), jnp.where(has_south, south, 0.0)

    coef[...] = jnp.zeros(coef.shape, f32)
    state_0[...] = jnp.zeros(state_0.shape, f32)
    state_1[...] = jnp.zeros(state_1.shape, f32)

    def place(ref, base, own, x_base, layers, y_base, south_row):
        for x in range(CX):
            at = base + (FIRST + x) * PITCH
            ref[at : at + CY] = own[x * CY : (x + 1) * CY]
        for h in range(layers):
            west, east = x_sides(pl.ds(x_base + h * CY, CY))
            at = base + (FIRST - layers + h) * PITCH
            ref[at : at + CY] = west
            at = base + (FIRST + CX + h) * PITCH
            ref[at : at + CY] = east
        for d in range(layers):
            north, south = y_sides(pl.ds(y_base + d * BLOCKS, BLOCKS))
            ref[pl.ds(base + NORTH + d, BLOCKS, stride=PITCH)] = north
            ref[pl.ds(base + south_row + d, BLOCKS, stride=PITCH)] = south

    for c in range(NC):
        place(
            state_0,
            c * FIELD,
            delta.at[c],
            c * RIM * CY,
            RIM,
            c * RIM * BLOCKS,
            SOUTH,
        )
    for f in range(3):
        place(
            coef,
            f * FIELD,
            eddy if f == 0 else courant.at[f - 1],
            X_COEF + f * INNER * CY,
            INNER,
            Y_COEF + f * INNER * BLOCKS,
            SOUTH + 1,
        )

    def combine(b, carry):
        at = pl.multiple_of(b * PITCH, 8)
        viscous = coef[pl.ds(at, PITCH)]
        along_x = 0.5 * coef[pl.ds(FIELD + at, PITCH)]
        along_y = 0.5 * coef[pl.ds(2 * FIELD + at, PITCH)]
        coef[pl.ds(at, PITCH)] = 1.0 - 4.0 * viscous
        coef[pl.ds(FIELD + at, PITCH)] = viscous - along_x
        coef[pl.ds(2 * FIELD + at, PITCH)] = viscous + along_x
        coef[pl.ds(3 * FIELD + at, PITCH)] = viscous - along_y
        coef[pl.ds(4 * FIELD + at, PITCH)] = viscous + along_y
        return carry

    lax.fori_loop(0, BLOCKS, combine, 0)

    known[0:per_slot] = shared[0:per_slot]
    known[per_slot : 2 * per_slot] = y_a[Y_ALPHA : Y_ALPHA + per_slot]
    known[2 * per_slot : 3 * per_slot] = y_b[Y_ALPHA : Y_ALPHA + per_slot]
    for s, other in enumerate(others):
        known[(3 + s) * per_slot : (4 + s) * per_slot] = other[0:per_slot]
    lane = lax.broadcasted_iota(jnp.int32, (1, total), 1)
    partner_a = jnp.where(even, me + 1, me - 1)
    partner_b = lax.rem(jnp.where(even, me - 1, me + 1) + ny, ny)
    owner = [me, partner_a, partner_b] + [lax.rem(me - s + ny, ny) for s in range(2, ny - 1)]
    tile_ids = []
    for strip in range(3):
        ids = jnp.full((1, total), -2, jnp.int32)
        for s in range(ny):
            base = s * group + strip * owned
            ids = jnp.where(
                (lane >= base) & (lane < base + owned), owner[s] * owned + lane - base, ids
            )
        tile_ids.append(ids.astype(f32))
    spot = lax.broadcasted_iota(jnp.int32, (BLOCKS, 128), 1)
    from_north, from_south = y_sides(pl.ds(Y_ALPHA + per_slot, BLOCKS))
    near = jnp.where(
        (spot >= NORTH) & (spot < NORTH + RIM) & has_north,
        pltpu.roll(from_north, NORTH, 1),
        jnp.where(
            (spot >= SOUTH) & (spot < PITCH) & has_south,
            pltpu.roll(from_south, PITCH - CY, 1),
            -1.0,
        ),
    )
    tiles[...] = jnp.full(tiles.shape, -1.0, f32)
    tiles[0:BLOCKS] = jnp.where(spot < CY, shared[per_slot:], near)
    turned = jnp.transpose(tiles[...])[0:PITCH]
    for b in range(BLOCKS):
        strip = 0 if b < FIRST else 1 if b < FIRST + CX else 2
        picks[b * PITCH : (b + 1) * PITCH] = (turned[:, b : b + 1] == tile_ids[strip]).astype(f32)

    def by_variable(ref, count):
        return jnp.concatenate([ref[pl.ds(c, count, stride=NC)] for c in range(NC)], axis=1)

    def two_part_dot(left, value):
        top, low = split(value)
        return jnp.dot(left, top, preferred_element_type=f32) + jnp.dot(
            left, low, preferred_element_type=f32
        )

    profiles = two_part_dot(picks[...].astype(bf16), by_variable(known, total))
    for c in range(NC):
        state_0[c * FIELD : (c + 1) * FIELD] += (
            profile_weight * profiles[:, c * 128 : (c + 1) * 128]
        )

    slots = gate_column.shape[1]
    per_beam = table.shape[0] // STEPS
    beam = gate_beam[...]
    block = beams[0].shape[0] // STEPS
    relative = jnp.bitwise_xor(beam >> 3, me_x) * 8 + (beam & 7)
    meta[...] = jnp.zeros(meta.shape, f32)
    meta[0:1] = gate_column[...].astype(f32)
    meta[1:2] = relative.astype(f32)
    meta[2:3] = gate_index[...].astype(f32)
    meta[3:4] = gate_live[...].astype(f32) * precision[...]
    columns = jnp.transpose(meta[...])
    scaled = columns[:, 3:4]
    slot_lane = lax.broadcasted_iota(jnp.int32, (slots, CX * CY), 1).astype(f32)
    slot_pick = (slot_lane == columns[:, 0:1]).astype(f32).astype(bf16)
    column_row = lax.broadcasted_iota(jnp.int32, (CX * CY, slots), 0)
    slot_push = (column_row == gate_column[...]).astype(f32).astype(bf16)
    beam_lane = lax.broadcasted_iota(jnp.int32, (slots, per_beam), 1).astype(f32)
    beam_pick = (beam_lane == columns[:, 1:2]).astype(f32).astype(bf16)
    gate_lane = lax.broadcasted_iota(jnp.int32, (slots, 128), 1).astype(f32)
    gate_here = gate_lane == columns[:, 2:3]
    for p, part in enumerate(beams):
        table[p * block * STEPS : (p + 1) * block * STEPS] = part[...]

    def forward(source, target, low, high):
        def body(b, carry):
            at = pl.multiple_of(b * PITCH, 8)
            k = [coef[pl.ds(f * FIELD + at, PITCH)] for f in range(5)]
            for c in range(NC):
                base = c * FIELD + at
                here = source[pl.ds(base, PITCH)]
                target[pl.ds(base, PITCH)] = (
                    k[0] * here
                    + k[1] * source[pl.ds(base + PITCH, PITCH)]
                    + k[2] * source[pl.ds(base - PITCH, PITCH)]
                    + k[3] * pltpu.roll(here, PITCH - 1, 0)
                    + k[4] * pltpu.roll(here, 1, 0)
                )
            return carry

        lax.fori_loop(low, high, body, 0)

    buffers = [state_0, state_1]
    for step in range(STEPS):
        source, target = buffers[step % 2], buffers[(step + 1) % 2]
        forward(source, target, 2 + step, BLOCKS - 2 - step)
        own = jnp.concatenate(
            [
                jnp.concatenate(
                    [
                        target[c * FIELD + b * PITCH : c * FIELD + b * PITCH + CY]
                        for b in range(FIRST, FIRST + CX)
                    ],
                    axis=0,
                )
                for c in range(NC)
            ],
            axis=1,
        )
        picked = two_part_dot(slot_pick, own)
        rows = two_part_dot(beam_pick, table[pl.ds(step, per_beam, stride=STEPS)])
        tally = -jnp.where(gate_here, rows, 0.0)
        for c in range(NC):
            tally = tally + picked[:, c * 128 : (c + 1) * 128] * weights[pl.ds(c, slots, stride=NC)]
        misfit = scaled * jnp.sum(tally, axis=1, keepdims=True)
        pushed = jnp.concatenate(
            [misfit * weights[pl.ds(c, slots, stride=NC)] for c in range(NC)], axis=1
        )
        forcing[step * CX * CY : (step + 1) * CX * CY] = two_part_dot(slot_push, pushed)

    state_0[...] = jnp.zeros(state_0.shape, f32)
    state_1[...] = jnp.zeros(state_1.shape, f32)

    def add_forcing(ref, step):
        for c in range(NC):
            for x in range(CX):
                at = c * FIELD + (FIRST + x) * PITCH
                first = step * CX * CY + x * CY
                ref[at : at + CY] += forcing[first : first + CY, c * 128 : (c + 1) * 128]

    def backward(source, target, low, high):
        def body(b, carry):
            at = pl.multiple_of(b * PITCH, 8)
            k = [
                coef[pl.ds(at, PITCH)],
                coef[pl.ds(FIELD + at - PITCH, PITCH)],
                coef[pl.ds(2 * FIELD + at + PITCH, PITCH)],
                coef[pl.ds(3 * FIELD + at, PITCH)],
                coef[pl.ds(4 * FIELD + at, PITCH)],
            ]
            for c in range(NC):
                base = c * FIELD + at
                here = source[pl.ds(base, PITCH)]
                target[pl.ds(base, PITCH)] = (
                    k[0] * here
                    + k[1] * source[pl.ds(base - PITCH, PITCH)]
                    + k[2] * source[pl.ds(base + PITCH, PITCH)]
                    + pltpu.roll(k[3] * here, 1, 0)
                    + pltpu.roll(k[4] * here, PITCH - 1, 0)
                )
            return carry

        lax.fori_loop(low, high, body, 0)

    for step in range(STEPS):
        source, target = buffers[step % 2], buffers[(step + 1) % 2]
        add_forcing(source, STEPS - 1 - step)
        backward(source, target, FIRST - 1 - step, FIRST + CX + 1 + step)
    final = buffers[STEPS % 2]

    adjoint = jnp.concatenate([final[c * FIELD : (c + 1) * FIELD] for c in range(NC)], axis=1)
    top, low = split(adjoint)
    turned = jnp.transpose(picks[...]).astype(bf16)
    tile_sums = jnp.dot(turned, top, preferred_element_type=f32) + jnp.dot(
        turned, low, preferred_element_type=f32
    )
    for c in range(NC):
        sums[pl.ds(c, total, stride=NC)] = tile_sums[:, c * 128 : (c + 1) * 128]
    edge_rows = NC * RIM * BLOCKS
    for c in range(NC):
        for d in range(RIM):
            north = final[pl.ds(c * FIELD + NORTH + d, BLOCKS, stride=PITCH)]
            south = final[pl.ds(c * FIELD + SOUTH + d, BLOCKS, stride=PITCH)]
            at = (c * RIM + d) * BLOCKS
            out_a[at : at + BLOCKS] = jnp.where(even, north, south)
            out_b[at : at + BLOCKS] = jnp.where(even, south, north)
    out_a[edge_rows:] = sums[per_slot : 2 * per_slot]
    out_b[edge_rows:] = sums[2 * per_slot : 3 * per_slot]
    out_sums[0:per_slot] = sums[0:per_slot]
    out_sums[per_slot:] = sums[3 * per_slot :]
    for c in range(NC):
        for b in range(BLOCKS):
            at = (c * BLOCKS + b) * CY
            first = c * FIELD + b * PITCH
            out_adjoint[at : at + CY] = final[first : first + CY]


def add_y(ny, delta, alpha, sums, adjoint, got_a, got_b, *rest):
    others = rest[: ny - 3]
    out_a, out_b, out_delta, out_alpha, field = rest[ny - 3 :]
    owned = alpha.shape[0]
    even = parity("gy")
    even_x = parity("gx")
    me = lax.axis_index("gy")
    field[...] = adjoint[...]
    for c in range(NC):
        for d in range(RIM):
            rows = pl.ds((c * RIM + d) * BLOCKS, BLOCKS)
            first, second = got_a[rows], got_b[rows]
            north = jnp.where(me < ny - 1, jnp.where(even, first, second), 0.0)
            south = jnp.where(me > 0, jnp.where(even, second, first), 0.0)
            low = pl.ds(c * BLOCKS * CY + d, BLOCKS, stride=CY)
            high = pl.ds(c * BLOCKS * CY + CY - RIM + d, BLOCKS, stride=CY)
            field[low] = field[low] + south
            field[high] = field[high] + north
    tail = NC * RIM * BLOCKS
    total = sums[0 : 3 * owned] + got_a[tail:] + got_b[tail:]
    for other in others:
        total = total + other[...]
    wide = RIM * CY
    for c in range(NC):
        base = c * BLOCKS * CY
        west = field[base + CY : base + CY + wide]
        at = base + (FIRST + CX) * CY
        east = field[at : at + wide]
        out_a[c * wide : (c + 1) * wide] = jnp.where(even_x, east, west)
        out_b[c * wide : (c + 1) * wide] = jnp.where(even_x, west, east)
        at = base + FIRST * CY
        out_delta[c] = delta[c] + field[at : at + CX * CY]
    west, east = total[0:owned], total[2 * owned :]
    out_a[NC * wide :] = jnp.where(even_x, east, west)
    out_b[NC * wide :] = jnp.where(even_x, west, east)
    out_alpha[...] = alpha[...] + profile_weight * total[owned : 2 * owned]


def add_x(near_delta, near_alpha, got_a, got_b, out_delta, out_alpha):
    even_x = parity("gx")
    wide = RIM * CY
    out_delta[...] = near_delta[...]
    for c in range(NC):
        rows = pl.ds(c * wide, wide)
        first, second = got_a[rows], got_b[rows]
        out_delta[c, 0:wide] += jnp.where(even_x, second, first)
        out_delta[c, CX * CY - wide :] += jnp.where(even_x, first, second)
    out_alpha[...] = near_alpha[...] + profile_weight * (
        got_a[NC * wide :] + got_b[NC * wide :]
    )


def on_device(
    delta,
    alpha,
    eddy,
    courant,
    tile_map,
    obs_rows,
    gate_beam,
    gate_index,
    gate_column,
    gate_live,
    obs_weight,
    obs_precision,
):
    nx = lax.axis_size("gx")
    ny = lax.axis_size("gy")
    owned = alpha.shape[1]
    slots = gate_column.shape[2]
    fine = delta.reshape(NC, CX * CY, 128)
    eddy = eddy.reshape(CX * CY, 128)
    courant = courant.reshape(2, CX * CY, 128)
    control = alpha.reshape(owned * NC, 128)
    weights = obs_weight.reshape(slots * NC, 128)
    gates = [
        value.reshape(1, slots)
        for value in (gate_beam, gate_index, gate_column, gate_live, obs_precision)
    ]
    beam_rows = obs_rows.reshape(-1, 128)

    x_rows = X_ALPHA + owned * NC + CX
    pieces = call(pack_x, [(x_rows, 128)] * 2, [fine, eddy, courant, control, tile_map])
    x_a = pair_a(pieces[0], "gx")
    x_b = pair_b(pieces[1], "gx", False)
    beam_pair = jnp.concatenate([beam_rows, pair_a(beam_rows, "gx")])

    shared_rows = 3 * owned * NC + BLOCKS
    y_rows = Y_ALPHA + shared_rows
    piece_a, piece_b, shared = call(
        pack_y,
        [(y_rows, 128), (y_rows, 128), (shared_rows, 128)],
        [fine, eddy, courant, control, tile_map, x_a, x_b],
    )
    y_a = pair_a(piece_a, "gy")
    y_b = pair_b(piece_b, "gy", True)
    others = [
        lax.ppermute(shared, "gy", [(i, (i + s) % ny) for i in range(ny)])
        for s in range(2, ny - 1)
    ]
    beams = [beam_pair] + [
        lax.ppermute(beam_pair, "gx", partner("gx", xor)) for xor in range(2, nx, 2)
    ]

    per_slot = 3 * owned * NC
    total = ny * 3 * owned
    edge_rows = NC * RIM * BLOCKS
    back_a, back_b, sums, adjoint = call(
        lambda *refs: main(ny, len(beams), *refs),
        [
            (edge_rows + per_slot, 128),
            (edge_rows + per_slot, 128),
            ((ny - 2) * per_slot, 128),
            (NC * BLOCKS * CY, 128),
        ],
        [fine, eddy, courant, *gates, weights, x_a, x_b, shared, y_a, y_b, *others, *beams],
        [
            pltpu.VMEM((NC * FIELD, 128), f32),
            pltpu.VMEM((NC * FIELD, 128), f32),
            pltpu.VMEM((5 * FIELD, 128), f32),
            pltpu.VMEM((STEPS * CX * CY, NC * 128), f32),
            pltpu.VMEM((ny * per_slot, 128), f32),
            pltpu.VMEM((FIELD, total), f32),
            pltpu.VMEM((8, slots), f32),
            pltpu.VMEM((128, 128), f32),
            pltpu.VMEM((nx * beam_rows.shape[0], 128), f32),
            pltpu.VMEM((ny * per_slot, 128), f32),
        ],
        flops=30000000,
    )
    got_a = pair_a(back_a, "gy")
    got_b = pair_b(back_b, "gy", True)
    got_others = [
        lax.ppermute(
            sums[(s - 1) * per_slot : s * per_slot], "gy", [(i, (i - s) % ny) for i in range(ny)]
        )
        for s in range(2, ny - 1)
    ]
    home_rows = NC * RIM * CY + owned * NC
    home_a, home_b, near_delta, near_alpha = call(
        lambda *refs: add_y(ny, *refs),
        [(home_rows, 128), (home_rows, 128), fine.shape, control.shape],
        [fine, control, sums, adjoint, got_a, got_b, *got_others],
        [pltpu.VMEM((NC * BLOCKS * CY, 128), f32)],
    )
    grad_delta, grad_alpha = call(
        add_x,
        [fine.shape, control.shape],
        [near_delta, near_alpha, pair_a(home_a, "gx"), pair_b(home_b, "gx", False)],
    )
    return grad_delta.reshape(delta.shape), grad_alpha.reshape(alpha.shape)


def solution(mesh):
    return jax.shard_map(
        on_device,
        mesh=mesh,
        in_specs=(
            P(None, "gx", "gy", None),
            P("gx", "gy", None, None),
            P("gx", "gy", None),
            P(None, "gx", "gy", None),
            P("gx", "gy"),
            P(("gx", "gy"), None, None),
            P("gx", "gy", None),
            P("gx", "gy", None),
            P("gx", "gy", None),
            P("gx", "gy", None),
            P("gx", "gy", None, None, None),
            P("gx", "gy", None),
        ),
        out_specs=(P(None, "gx", "gy", None), P("gx", "gy", None, None)),
        check_vma=False,
    )
```

```python
import jax
import jax.numpy as jnp
from jax import lax
from jax.experimental import pallas as pl
from jax.experimental.pallas import tpu as pltpu
from jax.sharding import PartitionSpec as P

STEPS = 3
RIM = 3
INNER = RIM - 1
NC = 4
CX = 16
CY = 16
BLOCKS = CX + 8
PITCH = CY + 8
FIRST = 4
FIELD = BLOCKS * PITCH

BULK_COEF = NC * RIM * CY
BULK = BULK_COEF + 3 * INNER * CY

profile_weight = 0.125
f32 = jnp.float32
bf16 = jnp.bfloat16

VMEM = pl.BlockSpec(memory_space=pltpu.VMEM)
ANY = pl.BlockSpec(memory_space=pl.ANY)


def call(body, outs, ins, scratch=(), in_specs=None, flops=1000000, limit=40 * 2**20):
    shapes = [jax.ShapeDtypeStruct(shape, f32) for shape in outs]
    size = sum(4 * value.size for value in ins)
    return pl.pallas_call(
        body,
        out_shape=shapes,
        in_specs=in_specs or [VMEM] * len(ins),
        out_specs=[VMEM] * len(shapes),
        scratch_shapes=list(scratch),
        compiler_params=pltpu.CompilerParams(vmem_limit_bytes=limit),
        cost_estimate=pl.CostEstimate(flops=flops, bytes_accessed=size, transcendentals=0),
    )(*ins)


def parity(axis):
    return lax.rem(lax.axis_index(axis), 2) == 0


def swap(block, axis, xor):
    return lax.ppermute(block, axis, [(i, i ^ xor) for i in range(lax.axis_size(axis))])


def pair_b(block, axis):
    pairs = []
    for low in range(1, lax.axis_size(axis) - 1, 2):
        pairs += [(low, low + 1), (low + 1, low)]
    return lax.ppermute(block, axis, pairs)


def split(value):
    top = value.astype(bf16)
    return top, (value - top.astype(f32)).astype(bf16)


def layers(reach):
    found, at = [], 0
    for away in range(1, reach + 1):
        count = CX + 2 * (reach - away)
        found.append((away, at, FIRST - (reach - away), count))
        at += count
    return found, at


WIDE, WIDE_ROWS = layers(RIM)
SLIM, SLIM_ROWS = layers(INNER)
Y_COEF = NC * WIDE_ROWS
Y_HALO = Y_COEF + 3 * SLIM_ROWS

CORNER = sum(RIM - away for away in range(1, RIM + 1))
COEF_CORNER = sum(INNER - away for away in range(1, INNER + 1))


def small_places(profile_rows):
    tile = profile_rows
    corner = tile + 8
    coef_corner = corner + 2 * NC * CORNER
    beams = coef_corner + 8
    return tile, corner, coef_corner, beams


def pack_x(
    delta,
    eddy,
    courant,
    alpha,
    tile_map,
    beam_rows,
    bulk_a,
    bulk_b,
    small_a,
    small_b,
    east,
    west,
    own,
    tiles,
    beams,
    sems,
):
    even = parity("gx")
    wide, slim = RIM * CY, INNER * CY
    copies = []

    def copy(source, target):
        move = pltpu.make_async_copy(source, target, sems.at[len(copies)])
        move.start()
        copies.append(move)

    last = CX * CY
    for c in range(NC):
        rows = pl.ds(c * wide, wide)
        copy(delta.at[c, pl.ds(last - wide, wide)], east.at[rows])
        copy(delta.at[c, pl.ds(0, wide)], west.at[rows])
    for f in range(3):
        field = eddy if f == 0 else courant.at[f - 1]
        rows = pl.ds(BULK_COEF + f * slim, slim)
        copy(field.at[pl.ds(last - slim, slim)], east.at[rows])
        copy(field.at[pl.ds(0, slim)], west.at[rows])
    copy(alpha, own)
    copy(tile_map, tiles)
    copy(beam_rows, beams)
    for move in copies:
        move.wait()

    bulk_a[...] = jnp.where(even, east[...], west[...])
    bulk_b[...] = jnp.where(even, west[...], east[...])
    count = own.shape[0]
    tile, corner, coef_corner, beam = small_places(count)

    def put(at, size, east_side, west_side):
        small_a[at : at + size] = jnp.where(even, east_side, west_side)
        small_b[at : at + size] = jnp.where(even, west_side, east_side)

    small_a[0:count] = own[...]
    small_b[0:count] = own[...]
    numbers = tiles[...].astype(f32)
    put(tile, 8, jnp.zeros((8, 128), f32), jnp.zeros((8, 128), f32))
    for out in (small_a, small_b):
        out[coef_corner : coef_corner + 8] = jnp.zeros((8, 128), f32)
    small_a[tile : tile + RIM, 0:CY] = jnp.where(even, numbers[CX - RIM :], numbers[:RIM])
    small_b[tile : tile + RIM, 0:CY] = jnp.where(even, numbers[:RIM], numbers[CX - RIM :])

    def corners(at, base, reach, side):
        for away in range(1, reach):
            y = CY - away if side == 0 else away - 1
            width = reach - away
            for i in range(width):
                put(
                    at,
                    1,
                    east[pl.ds(base + (reach - width + i) * CY + y, 1)],
                    west[pl.ds(base + i * CY + y, 1)],
                )
                at += 1

    for side in range(2):
        for c in range(NC):
            corners(corner + (side * NC + c) * CORNER, c * wide, RIM, side)
        for f in range(3):
            corners(
                coef_corner + (side * 3 + f) * COEF_CORNER, BULK_COEF + f * slim, INNER, side
            )
    small_a[beam:] = beams[...]


def pack_y(
    delta,
    eddy,
    courant,
    alpha,
    tiles,
    beam_rows,
    got_a,
    got_b,
    out_a,
    out_b,
    profiles,
    near_tiles,
    beam_pair,
):
    even = parity("gy")
    even_x = parity("gx")
    count = alpha.shape[0]
    tile, corner, coef_corner, beam = small_places(count)

    def sides(at, size):
        first, second = got_a[at : at + size], got_b[at : at + size]
        return jnp.where(even_x, second, first), jnp.where(even_x, first, second)

    def put(at, size, north_side, south_side):
        out_a[at : at + size] = jnp.where(even, north_side, south_side)
        out_b[at : at + size] = jnp.where(even, south_side, north_side)

    def edge(at, found, own, north_corner, south_corner):
        for away, start, _, size in found:
            here = at + start
            width = (size - CX) // 2
            if width:
                north_w, north_e = sides(north_corner, width)
                south_w, south_e = sides(south_corner, width)
                put(here, width, north_w, south_w)
                put(here + width + CX, width, north_e, south_e)
                north_corner += width
                south_corner += width
            put(
                here + width,
                CX,
                own[pl.ds(CY - away, CX, stride=CY)],
                own[pl.ds(away - 1, CX, stride=CY)],
            )

    for c in range(NC):
        edge(
            c * WIDE_ROWS,
            WIDE,
            delta.at[c],
            corner + c * CORNER,
            corner + (NC + c) * CORNER,
        )
    for f in range(3):
        edge(
            Y_COEF + f * SLIM_ROWS,
            SLIM,
            eddy if f == 0 else courant.at[f - 1],
            coef_corner + f * COEF_CORNER,
            coef_corner + (3 + f) * COEF_CORNER,
        )
    west, east = sides(0, count)
    profiles[0:count] = west
    profiles[count : 2 * count] = alpha[...]
    profiles[2 * count :] = east
    west, east = sides(tile, RIM)
    near_tiles[...] = jnp.full(near_tiles.shape, -1.0, f32)
    near_tiles[FIRST - RIM : FIRST] = west
    near_tiles[FIRST : FIRST + CX, 0:CY] = tiles[...].astype(f32)
    near_tiles[FIRST + CX : FIRST + CX + RIM] = east
    out_a[Y_HALO : Y_HALO + BLOCKS] = near_tiles[...]
    out_b[Y_HALO : Y_HALO + BLOCKS] = near_tiles[...]
    out_a[Y_HALO + BLOCKS :] = profiles[...]
    beam_pair[0 : beam_rows.shape[0]] = beam_rows[...]
    beam_pair[beam_rows.shape[0] :] = got_a[beam:]


def main(
    ny,
    parts,
    delta,
    eddy,
    courant,
    gate_beam,
    gate_index,
    gate_column,
    gate_live,
    precision,
    weights,
    x_a,
    x_b,
    profiles,
    near_tiles,
    y_a,
    y_b,
    *rest,
):
    others = rest[: ny - 2]
    beams = rest[ny - 2 : ny - 2 + parts]
    outs = rest[ny - 2 + parts : 2 * ny + 2 + parts]
    out_a, out_b, bulk_a, bulk_b, out_near, out_sums = outs[:6]
    out_others = outs[6:]
    (state_0, state_1, coef, forcing, known, picks, meta, tiles, table, sums) = rest[
        2 * ny + 2 + parts :
    ]
    per_slot = profiles.shape[0]
    group = per_slot // NC
    owned = group // 3
    total = ny * group
    me = lax.axis_index("gy")
    me_x = lax.axis_index("gx")
    even = parity("gy")
    even_x = parity("gx")
    has_south = me > 0
    has_north = me < ny - 1

    def x_sides(rows):
        first, second = x_a[rows], x_b[rows]
        return jnp.where(even_x, second, first), jnp.where(even_x, first, second)

    def y_sides(rows):
        first, second = y_a[rows], y_b[rows]
        return jnp.where(even, first, second), jnp.where(even, second, first)

    coef[...] = jnp.zeros(coef.shape, f32)
    state_0[...] = jnp.zeros(state_0.shape, f32)
    state_1[...] = jnp.zeros(state_1.shape, f32)

    def place(ref, base, own, x_base, reach, y_base, found):
        for x in range(CX):
            at = base + (FIRST + x) * PITCH
            ref[at : at + CY] = own[x * CY : (x + 1) * CY]
        for h in range(reach):
            west, east = x_sides(pl.ds(x_base + h * CY, CY))
            at = base + (FIRST - reach + h) * PITCH
            ref[at : at + CY] = west
            at = base + (FIRST + CX + h) * PITCH
            ref[at : at + CY] = east
        for away, start, block, size in found:
            north, south = y_sides(pl.ds(y_base + start, size))
            at = base + block * PITCH
            ref[pl.ds(at + CY - 1 + away, size, stride=PITCH)] = north
            ref[pl.ds(at + PITCH - away, size, stride=PITCH)] = south

    for c in range(NC):
        place(state_0, c * FIELD, delta.at[c], c * RIM * CY, RIM, c * WIDE_ROWS, WIDE)
    for f in range(3):
        place(
            coef,
            f * FIELD,
            eddy if f == 0 else courant.at[f - 1],
            BULK_COEF + f * INNER * CY,
            INNER,
            Y_COEF + f * SLIM_ROWS,
            SLIM,
        )

    def combine(b, carry):
        at = pl.multiple_of(b * PITCH, 8)
        viscous = coef[pl.ds(at, PITCH)]
        along_x = 0.5 * coef[pl.ds(FIELD + at, PITCH)]
        along_y = 0.5 * coef[pl.ds(2 * FIELD + at, PITCH)]
        coef[pl.ds(at, PITCH)] = 1.0 - 4.0 * viscous
        coef[pl.ds(FIELD + at, PITCH)] = viscous - along_x
        coef[pl.ds(2 * FIELD + at, PITCH)] = viscous + along_x
        coef[pl.ds(3 * FIELD + at, PITCH)] = viscous - along_y
        coef[pl.ds(4 * FIELD + at, PITCH)] = viscous + along_y
        return carry

    lax.fori_loop(0, BLOCKS, combine, 0)

    known[0:per_slot] = profiles[...]
    known[per_slot : 2 * per_slot] = y_a[Y_HALO + BLOCKS :]
    for s, other in enumerate(others):
        known[(2 + s) * per_slot : (3 + s) * per_slot] = other[...]
    lane = lax.broadcasted_iota(jnp.int32, (1, total), 1)
    tile_ids = []
    for strip in range(3):
        ids = jnp.full((1, total), -2, jnp.int32)
        for s in range(ny):
            base = s * group + strip * owned
            ids = jnp.where(
                (lane >= base) & (lane < base + owned),
                jnp.bitwise_xor(me, s) * owned + lane - base,
                ids,
            )
        tile_ids.append(ids.astype(f32))
    spot = lax.broadcasted_iota(jnp.int32, (BLOCKS, 128), 1)
    from_north, from_south = y_sides(pl.ds(Y_HALO, BLOCKS))
    near = jnp.where(
        (spot >= CY) & (spot < CY + RIM) & has_north,
        pltpu.roll(from_north, CY, 1),
        jnp.where(
            (spot >= PITCH - RIM) & (spot < PITCH) & has_south,
            pltpu.roll(from_south, PITCH - CY, 1),
            -1.0,
        ),
    )
    tiles[...] = jnp.full(tiles.shape, -1.0, f32)
    tiles[0:BLOCKS] = jnp.where(spot < CY, near_tiles[...], near)
    turned = jnp.transpose(tiles[...])[0:PITCH]
    for b in range(BLOCKS):
        strip = 0 if b < FIRST else 1 if b < FIRST + CX else 2
        picks[b * PITCH : (b + 1) * PITCH] = (turned[:, b : b + 1] == tile_ids[strip]).astype(f32)

    def by_variable(ref, count):
        return jnp.concatenate([ref[pl.ds(c, count, stride=NC)] for c in range(NC)], axis=1)

    def two_part_dot(left, value):
        top, low = split(value)
        return jnp.dot(left, top, preferred_element_type=f32) + jnp.dot(
            left, low, preferred_element_type=f32
        )

    fine = two_part_dot(picks[...].astype(bf16), by_variable(known, total))
    for c in range(NC):
        state_0[c * FIELD : (c + 1) * FIELD] += profile_weight * fine[:, c * 128 : (c + 1) * 128]

    slots = gate_column.shape[1]
    per_beam = table.shape[0] // STEPS
    beam = gate_beam[...]
    pair = beams[0].shape[0]
    relative = jnp.bitwise_xor(beam >> 3, me_x) * 8 + (beam & 7)
    meta[...] = jnp.zeros(meta.shape, f32)
    meta[0:1] = gate_column[...].astype(f32)
    meta[1:2] = relative.astype(f32)
    meta[2:3] = gate_index[...].astype(f32)
    meta[3:4] = gate_live[...].astype(f32) * precision[...]
    columns = jnp.transpose(meta[...])
    scaled = columns[:, 3:4]
    slot_lane = lax.broadcasted_iota(jnp.int32, (slots, CX * CY), 1).astype(f32)
    slot_pick = (slot_lane == columns[:, 0:1]).astype(f32).astype(bf16)
    column_row = lax.broadcasted_iota(jnp.int32, (CX * CY, slots), 0)
    slot_push = (column_row == gate_column[...]).astype(f32).astype(bf16)
    beam_lane = lax.broadcasted_iota(jnp.int32, (slots, per_beam), 1).astype(f32)
    beam_pick = (beam_lane == columns[:, 1:2]).astype(f32).astype(bf16)
    gate_lane = lax.broadcasted_iota(jnp.int32, (slots, 128), 1).astype(f32)
    gate_here = gate_lane == columns[:, 2:3]
    for p, part in enumerate(beams):
        table[p * pair : (p + 1) * pair] = part[...]

    def forward(source, target, low, high):
        def body(b, carry):
            at = pl.multiple_of(b * PITCH, 8)
            k = [coef[pl.ds(f * FIELD + at, PITCH)] for f in range(5)]
            for c in range(NC):
                base = c * FIELD + at
                here = source[pl.ds(base, PITCH)]
                target[pl.ds(base, PITCH)] = (
                    k[0] * here
                    + k[1] * source[pl.ds(base + PITCH, PITCH)]
                    + k[2] * source[pl.ds(base - PITCH, PITCH)]
                    + k[3] * pltpu.roll(here, PITCH - 1, 0)
                    + k[4] * pltpu.roll(here, 1, 0)
                )
            return carry

        lax.fori_loop(low, high, body, 0)

    buffers = [state_0, state_1]
    for step in range(STEPS):
        source, target = buffers[step % 2], buffers[(step + 1) % 2]
        forward(source, target, 2 + step, BLOCKS - 2 - step)
        own = jnp.concatenate(
            [
                jnp.concatenate(
                    [
                        target[c * FIELD + b * PITCH : c * FIELD + b * PITCH + CY]
                        for b in range(FIRST, FIRST + CX)
                    ],
                    axis=0,
                )
                for c in range(NC)
            ],
            axis=1,
        )
        picked = two_part_dot(slot_pick, own)
        rows = two_part_dot(beam_pick, table[pl.ds(step, per_beam, stride=STEPS)])
        tally = -jnp.where(gate_here, rows, 0.0)
        for c in range(NC):
            tally = tally + picked[:, c * 128 : (c + 1) * 128] * weights[pl.ds(c, slots, stride=NC)]
        misfit = scaled * jnp.sum(tally, axis=1, keepdims=True)
        pushed = jnp.concatenate(
            [misfit * weights[pl.ds(c, slots, stride=NC)] for c in range(NC)], axis=1
        )
        forcing[step * CX * CY : (step + 1) * CX * CY] = two_part_dot(slot_push, pushed)

    state_0[...] = jnp.zeros(state_0.shape, f32)
    state_1[...] = jnp.zeros(state_1.shape, f32)

    def add_forcing(ref, step):
        for c in range(NC):
            for x in range(CX):
                at = c * FIELD + (FIRST + x) * PITCH
                first = step * CX * CY + x * CY
                ref[at : at + CY] += forcing[first : first + CY, c * 128 : (c + 1) * 128]

    def backward(source, target, low, high):
        def body(b, carry):
            at = pl.multiple_of(b * PITCH, 8)
            k = [
                coef[pl.ds(at, PITCH)],
                coef[pl.ds(FIELD + at - PITCH, PITCH)],
                coef[pl.ds(2 * FIELD + at + PITCH, PITCH)],
                coef[pl.ds(3 * FIELD + at, PITCH)],
                coef[pl.ds(4 * FIELD + at, PITCH)],
            ]
            for c in range(NC):
                base = c * FIELD + at
                here = source[pl.ds(base, PITCH)]
                target[pl.ds(base, PITCH)] = (
                    k[0] * here
                    + k[1] * source[pl.ds(base - PITCH, PITCH)]
                    + k[2] * source[pl.ds(base + PITCH, PITCH)]
                    + pltpu.roll(k[3] * here, 1, 0)
                    + pltpu.roll(k[4] * here, PITCH - 1, 0)
                )
            return carry

        lax.fori_loop(low, high, body, 0)

    for step in range(STEPS):
        source, target = buffers[step % 2], buffers[(step + 1) % 2]
        add_forcing(source, STEPS - 1 - step)
        backward(source, target, FIRST - 1 - step, FIRST + CX + 1 + step)
    final = buffers[STEPS % 2]

    for c in range(NC):
        for h in range(RIM):
            at = c * FIELD + (FIRST - RIM + h) * PITCH
            west = final[at : at + CY]
            at = c * FIELD + (FIRST + CX + h) * PITCH
            east = final[at : at + CY]
            at = (c * RIM + h) * CY
            bulk_a[at : at + CY] = jnp.where(even_x, east, west)
            bulk_b[at : at + CY] = jnp.where(even_x, west, east)
        for away, start, block, size in WIDE:
            at = c * FIELD + block * PITCH
            north = final[pl.ds(at + CY - 1 + away, size, stride=PITCH)]
            south = final[pl.ds(at + PITCH - away, size, stride=PITCH)]
            at = c * WIDE_ROWS + start
            out_a[at : at + size] = jnp.where(even, north, south)
            out_b[at : at + size] = jnp.where(even, south, north)
        for x in range(CX):
            at = c * FIELD + (FIRST + x) * PITCH
            rows = slice(x * CY, (x + 1) * CY)
            out_near[c, rows] = delta[c, rows] + final[at : at + CY]

    adjoint = jnp.concatenate([final[c * FIELD : (c + 1) * FIELD] for c in range(NC)], axis=1)
    tile_sums = two_part_dot(jnp.transpose(picks[...]).astype(bf16), adjoint)
    for c in range(NC):
        sums[pl.ds(c, total, stride=NC)] = tile_sums[:, c * 128 : (c + 1) * 128]
    out_sums[...] = sums[0:per_slot]
    out_a[NC * WIDE_ROWS :] = sums[per_slot : 2 * per_slot]
    for s, other in enumerate(out_others):
        other[...] = sums[(2 + s) * per_slot : (3 + s) * per_slot]


def pack_home(sums, got_a, got_b, *rest):
    others = rest[:-3]
    out_a, out_b, out_sum = rest[-3:]
    owned = sums.shape[0] // 3
    even = parity("gy")
    even_x = parity("gx")
    total = sums[...] + got_a[NC * WIDE_ROWS :]
    for other in others:
        total = total + other[...]

    def put(at, size, west, east):
        out_a[at : at + size] = jnp.where(even_x, east, west)
        out_b[at : at + size] = jnp.where(even_x, west, east)

    put(0, owned, total[0:owned], total[2 * owned :])
    out_sum[...] = total[owned : 2 * owned]
    at = owned
    for c in range(NC):
        for away, start, _, size in WIDE:
            width = (size - CX) // 2
            first = c * WIDE_ROWS + start
            for side in range(2):
                if width:
                    pieces = []
                    for rows in (
                        slice(first, first + width),
                        slice(first + size - width, first + size),
                    ):
                        north = jnp.where(even, got_a[rows], got_b[rows])
                        south = jnp.where(even, got_b[rows], got_a[rows])
                        pieces.append((north, south)[side])
                    put(at, width, *pieces)
                    at += width


def finish(alpha, near, own_sum, y_a, y_b, bulk_a, bulk_b, small_a, small_b, out_delta, out_alpha):
    even = parity("gy")
    even_x = parity("gx")
    owned = own_sum.shape[0]
    wide = RIM * CY
    out_delta[...] = near[...]
    at = owned
    for c in range(NC):
        rows = pl.ds(c * wide, wide)
        first, second = bulk_a[rows], bulk_b[rows]
        out_delta[c, 0:wide] += jnp.where(even_x, second, first)
        out_delta[c, CX * CY - wide :] += jnp.where(even_x, first, second)
        for away, start, _, size in WIDE:
            width = (size - CX) // 2
            rows = pl.ds(c * WIDE_ROWS + start + width, CX)
            first, second = y_a[rows], y_b[rows]
            high = pl.ds(CY - away, CX, stride=CY)
            low = pl.ds(away - 1, CX, stride=CY)
            out_delta[c, high] = out_delta[c, high] + jnp.where(even, first, second)
            out_delta[c, low] = out_delta[c, low] + jnp.where(even, second, first)
            for y in (CY - away, away - 1):
                for i in range(width):
                    first, second = small_a[at + i : at + i + 1], small_b[at + i : at + i + 1]
                    out_delta[c, pl.ds((CX - width + i) * CY + y, 1)] += jnp.where(
                        even_x, first, second
                    )
                    out_delta[c, pl.ds(i * CY + y, 1)] += jnp.where(even_x, second, first)
                at += width
    out_alpha[...] = alpha[...] + profile_weight * (
        own_sum[...] + small_a[0:owned] + small_b[0:owned]
    )


def on_device(
    delta,
    alpha,
    eddy,
    courant,
    tile_map,
    obs_rows,
    gate_beam,
    gate_index,
    gate_column,
    gate_live,
    obs_weight,
    obs_precision,
):
    nx = lax.axis_size("gx")
    ny = lax.axis_size("gy")
    owned = alpha.shape[1]
    slots = gate_column.shape[2]
    fine = delta.reshape(NC, CX * CY, 128)
    eddy = eddy.reshape(CX * CY, 128)
    courant = courant.reshape(2, CX * CY, 128)
    control = alpha.reshape(owned * NC, 128)
    weights = obs_weight.reshape(slots * NC, 128)
    gates = [
        value.reshape(1, slots)
        for value in (gate_beam, gate_index, gate_column, gate_live, obs_precision)
    ]
    beam_rows = obs_rows.reshape(-1, 128)
    profile_rows = owned * NC
    per_slot = 3 * profile_rows
    total = ny * 3 * owned
    beam_at = small_places(profile_rows)[-1]

    bulk_a, bulk_b, small_a, small_b = call(
        pack_x,
        [(BULK, 128), (BULK, 128), (beam_at + beam_rows.shape[0], 128), (beam_at, 128)],
        [fine, eddy, courant, control, tile_map, beam_rows],
        [
            pltpu.VMEM((BULK, 128), f32),
            pltpu.VMEM((BULK, 128), f32),
            pltpu.VMEM(control.shape, f32),
            pltpu.VMEM(tile_map.shape, jnp.int32),
            pltpu.VMEM(beam_rows.shape, f32),
            pltpu.SemaphoreType.DMA((2 * NC + 9,)),
        ],
        in_specs=[ANY] * 6,
    )
    small_a = swap(small_a, "gx", 1)
    small_b = pair_b(small_b, "gx")
    bulk_a = swap(bulk_a, "gx", 1)
    bulk_b = pair_b(bulk_b, "gx")

    y_a, y_b, profiles, near_tiles, beam_pair = call(
        pack_y,
        [
            (Y_HALO + BLOCKS + per_slot, 128),
            (Y_HALO + BLOCKS, 128),
            (per_slot, 128),
            (BLOCKS, 128),
            (2 * beam_rows.shape[0], 128),
        ],
        [fine, eddy, courant, control, tile_map, beam_rows, small_a, small_b],
    )
    y_a = swap(y_a, "gy", 1)
    y_b = pair_b(y_b, "gy")
    others = [swap(profiles, "gy", xor) for xor in range(2, ny)]
    beams = [beam_pair] + [swap(beam_pair, "gx", xor) for xor in range(2, nx, 2)]

    edge_rows = NC * WIDE_ROWS
    back_a, back_b, bulk_a, bulk_b, near, sums, *back = call(
        lambda *refs: main(ny, len(beams), *refs),
        [
            (edge_rows + per_slot, 128),
            (edge_rows, 128),
            (BULK_COEF, 128),
            (BULK_COEF, 128),
            fine.shape,
            (per_slot, 128),
        ]
        + [(per_slot, 128)] * (ny - 2),
        [
            fine,
            eddy,
            courant,
            *gates,
            weights,
            bulk_a,
            bulk_b,
            profiles,
            near_tiles,
            y_a,
            y_b,
            *others,
            *beams,
        ],
        [
            pltpu.VMEM((NC * FIELD, 128), f32),
            pltpu.VMEM((NC * FIELD, 128), f32),
            pltpu.VMEM((5 * FIELD, 128), f32),
            pltpu.VMEM((STEPS * CX * CY, NC * 128), f32),
            pltpu.VMEM((ny * per_slot, 128), f32),
            pltpu.VMEM((FIELD, total), f32),
            pltpu.VMEM((8, slots), f32),
            pltpu.VMEM((128, 128), f32),
            pltpu.VMEM((nx * beam_rows.shape[0], 128), f32),
            pltpu.VMEM((ny * per_slot, 128), f32),
        ],
        flops=30000000,
    )
    y_a = swap(back_a, "gy", 1)
    y_b = pair_b(back_b, "gy")
    others = [swap(value, "gy", xor) for xor, value in zip(range(2, ny), back)]
    bulk_a = swap(bulk_a, "gx", 1)
    bulk_b = pair_b(bulk_b, "gx")
    home_rows = profile_rows + 2 * NC * CORNER
    small_a, small_b, own_sum = call(
        pack_home,
        [(home_rows, 128), (home_rows, 128), control.shape],
        [sums, y_a, y_b, *others],
    )
    small_a = swap(small_a, "gx", 1)
    small_b = pair_b(small_b, "gx")
    grad_delta, grad_alpha = call(
        finish,
        [fine.shape, control.shape],
        [control, near, own_sum, y_a, y_b, bulk_a, bulk_b, small_a, small_b],
    )
    return grad_delta.reshape(delta.shape), grad_alpha.reshape(alpha.shape)


def solution(mesh):
    return jax.shard_map(
        on_device,
        mesh=mesh,
        in_specs=(
            P(None, "gx", "gy", None),
            P("gx", "gy", None, None),
            P("gx", "gy", None),
            P(None, "gx", "gy", None),
            P("gx", "gy"),
            P(("gx", "gy"), None, None),
            P("gx", "gy", None),
            P("gx", "gy", None),
            P("gx", "gy", None),
            P("gx", "gy", None),
            P("gx", "gy", None, None, None),
            P("gx", "gy", None),
        ),
        out_specs=(P(None, "gx", "gy", None), P("gx", "gy", None, None)),
        check_vma=False,
    )
```

```python
import jax
import jax.numpy as jnp
from jax import lax
from jax.experimental import pallas as pl
from jax.experimental.pallas import tpu as pltpu
from jax.sharding import PartitionSpec as P

STEPS = 3
RIM = 3
INNER = RIM - 1
NC = 4
CX = 16
CY = 16
BLOCKS = CX + 8
PITCH = CY + 8
FIRST = 4
FIELD = BLOCKS * PITCH
CORE = CX * PITCH

profile_weight = 0.125
f32 = jnp.float32
bf16 = jnp.bfloat16

VMEM = pl.BlockSpec(memory_space=pltpu.VMEM)
HBM = pl.BlockSpec(memory_space=pltpu.HBM)


def call(body, outs, ins, scratch=(), in_specs=None, flops=1000000, limit=40 * 2**20):
    shapes = [
        out if isinstance(out, jax.ShapeDtypeStruct) else jax.ShapeDtypeStruct(out, f32)
        for out in outs
    ]
    size = sum(4 * value.size for value in ins)
    return pl.pallas_call(
        body,
        out_shape=shapes,
        in_specs=in_specs or [VMEM] * len(ins),
        out_specs=[VMEM] * len(shapes),
        scratch_shapes=list(scratch),
        compiler_params=pltpu.CompilerParams(vmem_limit_bytes=limit),
        cost_estimate=pl.CostEstimate(flops=flops, bytes_accessed=size, transcendentals=0),
    )(*ins)


def swap(block, axis, xor):
    return lax.ppermute(block, axis, [(i, i ^ xor) for i in range(lax.axis_size(axis))])


def pair_b(block, axis):
    count = lax.axis_size(axis)
    pairs = [(0, 0), (count - 1, count - 1)]
    for low in range(1, count - 1, 2):
        pairs += [(low, low + 1), (low + 1, low)]
    return lax.ppermute(block, axis, pairs)


def place_on(axis):
    me = lax.axis_index(axis)
    return lax.rem(me, 2) == 0, me > 0, me < lax.axis_size(axis) - 1


def split(value):
    top = value.astype(bf16)
    return top, (value - top.astype(f32)).astype(bf16)


def two_part_dot(left, value):
    top, low = split(value)
    return jnp.dot(left, top, preferred_element_type=f32) + jnp.dot(
        left, low, preferred_element_type=f32
    )


def layers(reach):
    found, at = [], 0
    for away in range(1, reach + 1):
        found.append((away, at, reach - away))
        at += CY + 2 * (reach - away)
    return found, at


WIDE, WIDE_ROWS = layers(RIM)
SLIM, SLIM_ROWS = layers(INNER)
X_COEF = NC * WIDE_ROWS
X_HALO = X_COEF + 3 * SLIM_ROWS

Y_COEF = NC * RIM * CX
Y_TILE = Y_COEF + 3 * INNER * CX
Y_HALO = Y_TILE + CX


def pack_y(
    delta, eddy, courant, alpha, tile_map, beam_rows, out_a, out_b, out_beams, *scratch
):
    fine, coefs, tiles, beams, profiles, sems = scratch
    even, _, _ = place_on("gy")
    moves = [
        pltpu.make_async_copy(source, target, sems.at[i])
        for i, (source, target) in enumerate(
            [
                (delta, fine),
                (eddy, coefs.at[0]),
                (courant.at[0], coefs.at[1]),
                (courant.at[1], coefs.at[2]),
                (tile_map, tiles),
                (beam_rows, beams),
                (alpha, profiles),
            ]
        )
    ]
    for move in moves:
        move.start()
    for move in moves:
        move.wait()

    def put(at, field, away):
        north = field[pl.ds(CY - away, CX, stride=CY)]
        south = field[pl.ds(away - 1, CX, stride=CY)]
        out_a[at : at + CX] = jnp.where(even, north, south)
        out_b[at : at + CX] = jnp.where(even, south, north)

    for c in range(NC):
        for away in range(1, RIM + 1):
            put((c * RIM + away - 1) * CX, fine.at[c], away)
    for f in range(3):
        for away in range(1, INNER + 1):
            put(Y_COEF + (f * INNER + away - 1) * CX, coefs.at[f], away)
    for out in (out_a, out_b):
        out[Y_TILE : Y_TILE + CX] = jnp.full((CX, 128), -1.0, f32)
        out[Y_TILE : Y_TILE + CX, 0:CY] = tiles[...].astype(f32)
    out_a[Y_HALO:] = profiles[...]
    per = beams.shape[1]
    for i in range(beams.shape[0]):
        out_beams[i * per : (i + 1) * per] = beams[i]


def y_sides(got_a, got_b, rows, fill=0.0):
    even, low, high = place_on("gy")
    first, second = got_a[rows], got_b[rows]
    north, south = jnp.where(even, first, second), jnp.where(even, second, first)
    return jnp.where(high, north, fill), jnp.where(low, south, fill)


def x_sides(got_a, got_b, rows):
    even, low, high = place_on("gx")
    first, second = got_a[rows], got_b[rows]
    west, east = jnp.where(even, second, first), jnp.where(even, first, second)
    return jnp.where(low, west, 0.0), jnp.where(high, east, 0.0)


def gather_known(ny, alpha, got_a, others, known):
    owned = alpha.shape[0]
    known[0:owned] = alpha[...]
    known[owned : 2 * owned] = got_a[Y_HALO:]
    for s, other in enumerate(others):
        known[(2 + s) * owned : (3 + s) * owned] = other[...]


def tile_numbers(ny, tile_map, got_a, got_b, tiles):
    spot = lax.broadcasted_iota(jnp.int32, (CX, 128), 1)
    north, south = y_sides(got_a, got_b, pl.ds(Y_TILE, CX), -1.0)
    near = jnp.where(
        (spot >= CY) & (spot < CY + RIM),
        pltpu.roll(north, CY, 1),
        jnp.where((spot >= PITCH - RIM) & (spot < PITCH), pltpu.roll(south, PITCH - CY, 1), -1.0),
    )
    tiles[...] = jnp.full(tiles.shape, -1.0, f32)
    tiles[0:CX] = near
    tiles[0:CX, 0:CY] = tile_map[...].astype(f32)
    return jnp.transpose(tiles[...])[0:PITCH]


def tile_ids(ny, owned):
    me = lax.axis_index("gy")
    lane = lax.broadcasted_iota(jnp.int32, (1, ny * owned), 1)
    ids = lane
    for s in range(ny):
        here = (lane >= s * owned) & (lane < (s + 1) * owned)
        ids = jnp.where(here, jnp.bitwise_xor(me, s) * owned + lane - s * owned, ids)
    return ids.astype(f32)


def by_variable(ref, count):
    return jnp.concatenate([ref[pl.ds(c, count, stride=NC)] for c in range(NC)], axis=1)


def pack_x(ny, delta, eddy, courant, alpha, tile_map, y_a, y_b, beams, *rest):
    others = rest[: ny - 2]
    out_a, out_b, field, picks, known, tiles = rest[ny - 2 :]
    even, _, _ = place_on("gx")
    owned = alpha.shape[0] // NC
    gather_known(ny, alpha, y_a, others, known)
    turned = tile_numbers(ny, tile_map, y_a, y_b, tiles)
    ids = tile_ids(ny, owned)
    columns = [x for x in range(RIM)] + [CX - RIM + x for x in range(RIM)]
    for i, x in enumerate(columns):
        picks[i * PITCH : (i + 1) * PITCH] = (turned[:, x : x + 1] == ids).astype(f32)
    fine = two_part_dot(picks[...].astype(bf16), by_variable(known, ny * owned))

    def fill(own, y_base, reach, c):
        for i, x in enumerate(columns):
            at = i * PITCH
            field[at + CY : at + PITCH] = jnp.zeros((PITCH - CY, 128), f32)
            field[at : at + CY] = own[x * CY : (x + 1) * CY]
        for away in range(1, reach + 1):
            for first, base in ((0, 0), (CX - RIM, RIM * PITCH)):
                rows = pl.ds(y_base + (away - 1) * CX + first, RIM)
                north, south = y_sides(y_a, y_b, rows)
                field[pl.ds(base + CY - 1 + away, RIM, stride=PITCH)] = north
                field[pl.ds(base + PITCH - away, RIM, stride=PITCH)] = south
        if c is not None:
            field[...] += profile_weight * fine[:, c * 128 : (c + 1) * 128]

    def put(at, found):
        for away, start, extra in found:
            east, west = (2 * RIM - away) * PITCH, (away - 1) * PITCH
            here = at + start
            for source, target, size in (
                (PITCH - extra, 0, extra),
                (0, extra, CY + extra),
            ):
                if size:
                    first = field[east + source : east + source + size]
                    second = field[west + source : west + source + size]
                    rows = slice(here + target, here + target + size)
                    out_a[rows] = jnp.where(even, first, second)
                    out_b[rows] = jnp.where(even, second, first)

    for c in range(NC):
        fill(delta.at[c], c * RIM * CX, RIM, c)
        put(c * WIDE_ROWS, WIDE)
    for f in range(3):
        own = eddy if f == 0 else courant.at[f - 1]
        fill(own, Y_COEF + f * INNER * CX, INNER, None)
        put(X_COEF + f * SLIM_ROWS, SLIM)
    out_a[X_HALO:] = beams[...]


def prepare(
    ny,
    nx,
    delta,
    eddy,
    courant,
    alpha,
    tile_map,
    gate_beam,
    gate_index,
    gate_column,
    gate_live,
    precision,
    weights,
    y_a,
    y_b,
    *rest,
):
    others = rest[: ny - 2]
    core, coef, picks, wide, slot_pick, slot_push, beam_pick, columns = rest[ny - 2 : ny + 6]
    known, tiles, meta = rest[ny + 6 :]
    owned = alpha.shape[0] // NC

    def fill(ref, base, own, y_base, reach):
        for x in range(CX):
            at = base + x * PITCH
            ref[at : at + CY] = own[x * CY : (x + 1) * CY]
            ref[at + CY : at + PITCH] = jnp.zeros((PITCH - CY, 128), f32)
        for away in range(1, reach + 1):
            north, south = y_sides(y_a, y_b, pl.ds(y_base + (away - 1) * CX, CX))
            ref[pl.ds(base + CY - 1 + away, CX, stride=PITCH)] = north
            ref[pl.ds(base + PITCH - away, CX, stride=PITCH)] = south

    for c in range(NC):
        fill(core, c * CORE, delta.at[c], c * RIM * CX, RIM)
    for f in range(3):
        own = eddy if f == 0 else courant.at[f - 1]
        fill(coef, f * CORE, own, Y_COEF + f * INNER * CX, INNER)

    def combine(b, carry):
        at = pl.multiple_of(b * PITCH, 8)
        combined = combine_coefs(*[coef[pl.ds(f * CORE + at, PITCH)] for f in range(3)])
        for f, value in enumerate(combined):
            coef[pl.ds(f * CORE + at, PITCH)] = value
        return carry

    lax.fori_loop(0, CX, combine, 0)

    gather_known(ny, alpha, y_a, others, known)
    turned = tile_numbers(ny, tile_map, y_a, y_b, tiles)
    ids = tile_ids(ny, owned)
    for x in range(CX):
        picks[x * PITCH : (x + 1) * PITCH] = (turned[:, x : x + 1] == ids).astype(f32)
    fine = two_part_dot(picks[...].astype(bf16), by_variable(known, ny * owned))
    for c in range(NC):
        core[c * CORE : (c + 1) * CORE] += profile_weight * fine[:, c * 128 : (c + 1) * 128]

    slots = gate_column.shape[1]
    for c in range(NC):
        wide[:, c * 128 : (c + 1) * 128] = weights[pl.ds(c, slots, stride=NC)]
    beam = gate_beam[...]
    per_beam = beam_pick.shape[1]
    held = per_beam // nx
    relative = jnp.bitwise_xor(beam // held, lax.axis_index("gx"))
    relative = ((relative & 1) * (nx // 2) + (relative >> 1)) * held + lax.rem(beam, held)
    meta[...] = jnp.zeros(meta.shape, f32)
    meta[0:1] = gate_column[...].astype(f32)
    meta[1:2] = relative.astype(f32)
    meta[2:3] = gate_index[...].astype(f32)
    meta[3:4] = gate_live[...].astype(f32) * precision[...]
    turned = jnp.transpose(meta[...])
    columns[...] = turned
    slot_lane = lax.broadcasted_iota(jnp.int32, (slots, CX * CY), 1).astype(f32)
    slot_pick[...] = (slot_lane == turned[:, 0:1]).astype(f32).astype(bf16)
    column_row = lax.broadcasted_iota(jnp.int32, (CX * CY, slots), 0)
    slot_push[...] = (column_row == gate_column[...]).astype(f32).astype(bf16)
    beam_lane = lax.broadcasted_iota(jnp.int32, (slots, per_beam), 1).astype(f32)
    beam_pick[...] = (beam_lane == turned[:, 1:2]).astype(f32).astype(bf16)


def combine_coefs(viscous, along_x, along_y):
    half_x, half_y = 0.5 * along_x, 0.5 * along_y
    return (
        1.0 - 4.0 * viscous,
        viscous - half_x,
        viscous + half_x,
        viscous - half_y,
        viscous + half_y,
    )


def main(core, coef_core, wide, slot_pick, slot_push, beam_pick, columns, beams, x_a, x_b, *rest):
    out_a, out_b, out_core, state_0, state_1, coef, raw, forcing, table = rest
    even, _, _ = place_on("gx")
    slots = columns.shape[0]
    per_beam = beam_pick.shape[1]
    half = beams.shape[0]
    table[0:half] = beams[...]
    table[half:] = x_a[X_HALO:]

    def clear(ref, base, blocks):
        for b in blocks:
            at = base + b * PITCH
            ref[at : at + PITCH] = jnp.zeros((PITCH, 128), f32)

    def fill(ref, base, x_base, found):
        for away, start, extra in found:
            for source, target, size in (
                (0, PITCH - extra, extra),
                (extra, 0, CY + extra),
            ):
                if size:
                    at = x_base + start + source
                    west, east = x_sides(x_a, x_b, pl.ds(at, size))
                    at = base + (FIRST - away) * PITCH + target
                    ref[at : at + size] = west
                    at = base + (FIRST + CX - 1 + away) * PITCH + target
                    ref[at : at + size] = east

    rim = [FIRST - 3, FIRST - 2, FIRST - 1, FIRST + CX, FIRST + CX + 1, FIRST + CX + 2]
    for c in range(NC):
        at = c * FIELD + FIRST * PITCH
        state_0[at : at + CORE] = core[c * CORE : (c + 1) * CORE]
        clear(state_0, c * FIELD, rim)
        fill(state_0, c * FIELD, c * WIDE_ROWS, WIDE)
    for f in range(3):
        clear(raw, f * FIELD, rim[1:5])
        fill(raw, f * FIELD, X_COEF + f * SLIM_ROWS, SLIM)
    for f in range(5):
        at = f * FIELD + FIRST * PITCH
        coef[at : at + CORE] = coef_core[f * CORE : (f + 1) * CORE]
        clear(coef, f * FIELD, [0, 1, BLOCKS - 2, BLOCKS - 1])
    for b in rim[1:5]:
        rows = [slice(f * FIELD + b * PITCH, f * FIELD + (b + 1) * PITCH) for f in range(5)]
        for f, value in enumerate(combine_coefs(*[raw[rows[f]] for f in range(3)])):
            coef[rows[f]] = value

    gate_lane = lax.broadcasted_iota(jnp.int32, (slots, 128), 1).astype(f32)
    gate_here = gate_lane == columns[:, 2:3]
    scaled = columns[:, 3:4]

    def forward(source, target, low, high):
        def body(b, carry):
            at = pl.multiple_of(b * PITCH, 8)
            k = [coef[pl.ds(f * FIELD + at, PITCH)] for f in range(5)]
            for c in range(NC):
                base = c * FIELD + at
                here = source[pl.ds(base, PITCH)]
                target[pl.ds(base, PITCH)] = (
                    k[0] * here
                    + k[1] * source[pl.ds(base + PITCH, PITCH)]
                    + k[2] * source[pl.ds(base - PITCH, PITCH)]
                    + k[3] * pltpu.roll(here, PITCH - 1, 0)
                    + k[4] * pltpu.roll(here, 1, 0)
                )
            return carry

        lax.fori_loop(low, high, body, 0)

    buffers = [state_0, state_1]
    for step in range(STEPS):
        source, target = buffers[step % 2], buffers[(step + 1) % 2]
        forward(source, target, 2 + step, BLOCKS - 2 - step)
        own = jnp.concatenate(
            [
                jnp.concatenate(
                    [
                        target[c * FIELD + b * PITCH : c * FIELD + b * PITCH + CY]
                        for b in range(FIRST, FIRST + CX)
                    ],
                    axis=0,
                )
                for c in range(NC)
            ],
            axis=1,
        )
        picked = two_part_dot(slot_pick[...], own) * wide[...]
        rows = two_part_dot(beam_pick[...], table[pl.ds(step, per_beam, stride=STEPS)])
        tally = -jnp.where(gate_here, rows, 0.0)
        for c in range(NC):
            tally = tally + picked[:, c * 128 : (c + 1) * 128]
        misfit = scaled * jnp.sum(tally, axis=1, keepdims=True)
        forcing[step * CX * CY : (step + 1) * CX * CY] = two_part_dot(
            slot_push[...], misfit * wide[...]
        )

    for c in range(NC):
        clear(state_0, c * FIELD, [0, 1, 2, 3, BLOCKS - 4, BLOCKS - 3, BLOCKS - 2, BLOCKS - 1])
        clear(state_1, c * FIELD, [1, 2, BLOCKS - 3, BLOCKS - 2])

    def add_forcing(ref, step):
        for c in range(NC):
            for x in range(CX):
                at = c * FIELD + (FIRST + x) * PITCH
                first = step * CX * CY + x * CY
                value = forcing[first : first + CY, c * 128 : (c + 1) * 128]
                if step == STEPS - 1:
                    ref[at : at + CY] = value
                    ref[at + CY : at + PITCH] = jnp.zeros((PITCH - CY, 128), f32)
                else:
                    ref[at : at + CY] += value

    def backward(source, target, low, high):
        def body(b, carry):
            at = pl.multiple_of(b * PITCH, 8)
            k = [
                coef[pl.ds(at, PITCH)],
                coef[pl.ds(FIELD + at - PITCH, PITCH)],
                coef[pl.ds(2 * FIELD + at + PITCH, PITCH)],
                coef[pl.ds(3 * FIELD + at, PITCH)],
                coef[pl.ds(4 * FIELD + at, PITCH)],
            ]
            for c in range(NC):
                base = c * FIELD + at
                here = source[pl.ds(base, PITCH)]
                target[pl.ds(base, PITCH)] = (
                    k[0] * here
                    + k[1] * source[pl.ds(base - PITCH, PITCH)]
                    + k[2] * source[pl.ds(base + PITCH, PITCH)]
                    + pltpu.roll(k[3] * here, 1, 0)
                    + pltpu.roll(k[4] * here, PITCH - 1, 0)
                )
            return carry

        lax.fori_loop(low, high, body, 0)

    for step in range(STEPS):
        source, target = buffers[step % 2], buffers[(step + 1) % 2]
        add_forcing(source, STEPS - 1 - step)
        backward(source, target, FIRST - 1 - step, FIRST + CX + 1 + step)
    final = buffers[STEPS % 2]

    for c in range(NC):
        at = c * FIELD + FIRST * PITCH
        out_core[c * CORE : (c + 1) * CORE] = final[at : at + CORE]
        for away, start, extra in WIDE:
            for source, target, size in (
                (PITCH - extra, 0, extra),
                (0, extra, CY + extra),
            ):
                if size:
                    at = c * FIELD + (FIRST - away) * PITCH + source
                    west = final[at : at + size]
                    at = c * FIELD + (FIRST + CX - 1 + away) * PITCH + source
                    east = final[at : at + size]
                    at = c * WIDE_ROWS + start + target
                    out_a[at : at + size] = jnp.where(even, east, west)
                    out_b[at : at + size] = jnp.where(even, west, east)


def add_x(ny, delta, picks, core, x_a, x_b, *rest):
    out_a, out_b, out_near, out_sums = rest[:4]
    out_others = rest[4:-2]
    field, sums = rest[-2:]
    even, _, _ = place_on("gy")
    total = picks.shape[1]
    rows = total * NC // ny
    field[...] = core[...]
    for c in range(NC):
        for away, start, extra in WIDE:
            for source, target, size in (
                (0, PITCH - extra, extra),
                (extra, 0, CY + extra),
            ):
                if size:
                    at = c * WIDE_ROWS + start + source
                    west, east = x_sides(x_a, x_b, pl.ds(at, size))
                    at = c * CORE + (away - 1) * PITCH + target
                    field[at : at + size] += west
                    at = c * CORE + (CX - away) * PITCH + target
                    field[at : at + size] += east
    for c in range(NC):
        for away in range(1, RIM + 1):
            north = field[pl.ds(c * CORE + CY - 1 + away, CX, stride=PITCH)]
            south = field[pl.ds(c * CORE + PITCH - away, CX, stride=PITCH)]
            at = (c * RIM + away - 1) * CX
            out_a[at : at + CX] = jnp.where(even, north, south)
            out_b[at : at + CX] = jnp.where(even, south, north)
        for x in range(CX):
            at = c * CORE + x * PITCH
            here = slice(x * CY, (x + 1) * CY)
            out_near[c, here] = delta[c, here] + field[at : at + CY]
    adjoint = jnp.concatenate([field[c * CORE : (c + 1) * CORE] for c in range(NC)], axis=1)
    tile_sums = two_part_dot(jnp.transpose(picks[...]).astype(bf16), adjoint)
    for c in range(NC):
        sums[pl.ds(c, total, stride=NC)] = tile_sums[:, c * 128 : (c + 1) * 128]
    out_sums[...] = sums[0:rows]
    out_a[Y_COEF:] = sums[rows : 2 * rows]
    for s, other in enumerate(out_others):
        other[...] = sums[(2 + s) * rows : (3 + s) * rows]


def add_y(alpha, near, sums, y_a, y_b, *rest):
    others = rest[:-2]
    out_delta, out_alpha = rest[-2:]
    out_delta[...] = near[...]
    for c in range(NC):
        for away in range(1, RIM + 1):
            north, south = y_sides(y_a, y_b, pl.ds((c * RIM + away - 1) * CX, CX))
            high = pl.ds(CY - away, CX, stride=CY)
            low = pl.ds(away - 1, CX, stride=CY)
            out_delta[c, high] = out_delta[c, high] + north
            out_delta[c, low] = out_delta[c, low] + south
    total = sums[...] + y_a[Y_COEF:]
    for other in others:
        total = total + other[...]
    out_alpha[...] = alpha[...] + profile_weight * total


def on_device(
    delta,
    alpha,
    eddy,
    courant,
    tile_map,
    obs_rows,
    gate_beam,
    gate_index,
    gate_column,
    gate_live,
    obs_weight,
    obs_precision,
):
    nx = lax.axis_size("gx")
    ny = lax.axis_size("gy")
    owned = alpha.shape[1]
    slots = gate_column.shape[2]
    fine = delta.reshape(NC, CX * CY, 128)
    eddy = eddy.reshape(CX * CY, 128)
    courant = courant.reshape(2, CX * CY, 128)
    control = alpha.reshape(owned * NC, 128)
    weights = obs_weight.reshape(slots * NC, 128)
    gates = [
        value.reshape(1, slots)
        for value in (gate_beam, gate_index, gate_column, gate_live, obs_precision)
    ]
    own_beams = obs_rows.shape[0]
    beam_count = nx * own_beams
    rows = owned * NC
    total = ny * owned

    y_a, y_b, beams = call(
        pack_y,
        [(Y_HALO + rows, 128), (Y_HALO, 128), (own_beams * STEPS, 128)],
        [fine, eddy, courant, control, tile_map, obs_rows],
        [
            pltpu.VMEM(fine.shape, f32),
            pltpu.VMEM((3, CX * CY, 128), f32),
            pltpu.VMEM(tile_map.shape, jnp.int32),
            pltpu.VMEM(obs_rows.shape, f32),
            pltpu.VMEM(control.shape, f32),
            pltpu.SemaphoreType.DMA((7,)),
        ],
        in_specs=[HBM] * 6,
    )
    y_a = swap(y_a, "gy", 1)
    y_b = pair_b(y_b, "gy")
    others = [swap(control, "gy", xor) for xor in range(2, ny)]
    xor = 2
    while xor < nx:
        beams = jnp.concatenate([beams, swap(beams, "gx", xor)])
        xor *= 2

    x_a, x_b = call(
        lambda *refs: pack_x(ny, *refs),
        [(X_HALO + beams.shape[0], 128), (X_HALO, 128)],
        [fine, eddy, courant, control, tile_map, y_a, y_b, beams, *others],
        [
            pltpu.VMEM((2 * RIM * PITCH, 128), f32),
            pltpu.VMEM((2 * RIM * PITCH, total), f32),
            pltpu.VMEM((total * NC, 128), f32),
            pltpu.VMEM((128, 128), f32),
        ],
    )
    x_a = swap(x_a, "gx", 1)
    x_b = pair_b(x_b, "gx")

    core, coef, picks, wide, slot_pick, slot_push, beam_pick, columns = call(
        lambda *refs: prepare(ny, nx, *refs),
        [
            (NC * CORE, 128),
            (5 * CORE, 128),
            (CORE, total),
            (slots, NC * 128),
            jax.ShapeDtypeStruct((slots, CX * CY), bf16),
            jax.ShapeDtypeStruct((CX * CY, slots), bf16),
            jax.ShapeDtypeStruct((slots, beam_count), bf16),
            (slots, 8),
        ],
        [fine, eddy, courant, control, tile_map, *gates, weights, y_a, y_b, *others],
        [
            pltpu.VMEM((total * NC, 128), f32),
            pltpu.VMEM((128, 128), f32),
            pltpu.VMEM((8, slots), f32),
        ],
        flops=3000000,
    )

    back_a, back_b, core = call(
        main,
        [(X_COEF, 128), (X_COEF, 128), (NC * CORE, 128)],
        [core, coef, wide, slot_pick, slot_push, beam_pick, columns, beams, x_a, x_b],
        [
            pltpu.VMEM((NC * FIELD, 128), f32),
            pltpu.VMEM((NC * FIELD, 128), f32),
            pltpu.VMEM((5 * FIELD, 128), f32),
            pltpu.VMEM((3 * FIELD, 128), f32),
            pltpu.VMEM((STEPS * CX * CY, NC * 128), f32),
            pltpu.VMEM((beam_count * STEPS, 128), f32),
        ],
        flops=30000000,
    )
    x_a = swap(back_a, "gx", 1)
    x_b = pair_b(back_b, "gx")
    back_a, back_b, near, sums, *back = call(
        lambda *refs: add_x(ny, *refs),
        [(Y_COEF + rows, 128), (Y_COEF, 128), fine.shape, (rows, 128)] + [(rows, 128)] * (ny - 2),
        [fine, picks, core, x_a, x_b],
        [pltpu.VMEM((NC * CORE, 128), f32), pltpu.VMEM((total * NC, 128), f32)],
    )
    y_a = swap(back_a, "gy", 1)
    y_b = pair_b(back_b, "gy")
    others = [swap(value, "gy", xor) for xor, value in zip(range(2, ny), back)]
    grad_delta, grad_alpha = call(
        add_y,
        [fine.shape, control.shape],
        [control, near, sums, y_a, y_b, *others],
    )
    return grad_delta.reshape(delta.shape), grad_alpha.reshape(alpha.shape)


def solution(mesh):
    return jax.shard_map(
        on_device,
        mesh=mesh,
        in_specs=(
            P(None, "gx", "gy", None),
            P("gx", "gy", None, None),
            P("gx", "gy", None),
            P(None, "gx", "gy", None),
            P("gx", "gy"),
            P(("gx", "gy"), None, None),
            P("gx", "gy", None),
            P("gx", "gy", None),
            P("gx", "gy", None),
            P("gx", "gy", None),
            P("gx", "gy", None, None, None),
            P("gx", "gy", None),
        ),
        out_specs=(P(None, "gx", "gy", None), P("gx", "gy", None, None)),
        check_vma=False,
    )
```

```python
import jax
import jax.numpy as jnp
from jax import lax
from jax.experimental import pallas as pl
from jax.experimental.pallas import tpu as pltpu
from jax.sharding import PartitionSpec as P

STEPS = 3
RIM = 3
INNER = RIM - 1
NC = 4
CX = 16
CY = 16
BLOCKS = CX + 8
PITCH = CY + 8
FIRST = 4
FIELD = BLOCKS * PITCH
CORE = CX * PITCH
OWN_BEAMS = 8
BEAM_BITS = 3

profile_weight = 0.125
f32 = jnp.float32
bf16 = jnp.bfloat16

VMEM = pl.BlockSpec(memory_space=pltpu.VMEM)
HBM = pl.BlockSpec(memory_space=pltpu.HBM)


def call(body, outs, ins, scratch=(), in_specs=None, flops=1000000, limit=40 * 2**20):
    shapes = [
        out if isinstance(out, jax.ShapeDtypeStruct) else jax.ShapeDtypeStruct(out, f32)
        for out in outs
    ]
    size = sum(4 * value.size for value in ins)
    return pl.pallas_call(
        body,
        out_shape=shapes,
        in_specs=in_specs or [VMEM] * len(ins),
        out_specs=[VMEM] * len(shapes),
        scratch_shapes=list(scratch),
        compiler_params=pltpu.CompilerParams(vmem_limit_bytes=limit),
        cost_estimate=pl.CostEstimate(flops=flops, bytes_accessed=size, transcendentals=0),
    )(*ins)


def swap(block, axis, xor):
    return lax.ppermute(block, axis, [(i, i ^ xor) for i in range(lax.axis_size(axis))])


def pair_b(block, axis, other):
    count, across = lax.axis_size(axis), lax.axis_size(other)

    def place(i, j):
        return i * across + j if axis == "gx" else j * count + i

    pairs = []
    for j in range(across):
        for i in range(count):
            if i in (0, count - 1):
                pairs.append((place(i, j), place(i, j ^ 1)))
            else:
                pairs.append((place(i, j), place(i + 1 if i % 2 else i - 1, j)))
    return lax.ppermute(block, ("gx", "gy"), pairs)


def ring_b(block, axis):
    count = lax.axis_size(axis)
    pairs = [(i, (i + 1 if i % 2 else i - 1) % count) for i in range(count)]
    return lax.ppermute(block, axis, pairs)


def place_on(axis):
    me = lax.axis_index(axis)
    return lax.rem(me, 2) == 0, me > 0, me < lax.axis_size(axis) - 1


def split(value):
    top = value.astype(bf16)
    return top, (value - top.astype(f32)).astype(bf16)


def two_part_dot(left, value):
    top, low = split(value)
    return jnp.dot(left, top, preferred_element_type=f32) + jnp.dot(
        left, low, preferred_element_type=f32
    )


def layers(reach):
    found, at = [], 0
    for away in range(1, reach + 1):
        found.append((away, at, reach - away))
        at += CY + 2 * (reach - away)
    return found, at


WIDE, WIDE_ROWS = layers(RIM)
SLIM, SLIM_ROWS = layers(INNER)
X_COEF = NC * WIDE_ROWS
X_HALO = X_COEF + 3 * SLIM_ROWS

Y_COEF = NC * RIM * CX
Y_TILE = Y_COEF + 3 * INNER * CX
Y_HALO = Y_TILE + CX


def pack_y(
    delta,
    eddy,
    courant,
    alpha,
    tile_map,
    gate_beam,
    gate_index,
    gate_column,
    gate_live,
    precision,
    beam_rows,
    out_a,
    out_b,
    fine,
    coefs,
    profiles,
    near_tiles,
    meta,
    beams,
    tiles,
    gates,
    values,
    sems,
):
    even, _, _ = place_on("gy")
    moves = [
        pltpu.make_async_copy(source, target, sems.at[i])
        for i, (source, target) in enumerate(
            [
                (delta, fine),
                (eddy, coefs.at[0]),
                (courant.at[0], coefs.at[1]),
                (courant.at[1], coefs.at[2]),
                (tile_map, tiles),
                (alpha, profiles),
                (gate_beam, gates.at[0]),
                (gate_index, gates.at[1]),
                (gate_column, gates.at[2]),
                (gate_live, gates.at[3]),
                (precision, values),
                (beam_rows, beams),
            ]
        )
    ]
    for move in moves:
        move.start()
    for move in moves:
        move.wait()

    def put(at, field, away):
        north = field[pl.ds(CY - away, CX, stride=CY)]
        south = field[pl.ds(away - 1, CX, stride=CY)]
        out_a[at : at + CX] = jnp.where(even, north, south)
        out_b[at : at + CX] = jnp.where(even, south, north)

    for c in range(NC):
        for away in range(1, RIM + 1):
            put((c * RIM + away - 1) * CX, fine.at[c], away)
    for f in range(3):
        for away in range(1, INNER + 1):
            put(Y_COEF + (f * INNER + away - 1) * CX, coefs.at[f], away)
    near_tiles[...] = jnp.full((CX, 128), -1.0, f32)
    near_tiles[:, 0:CY] = tiles[...].astype(f32)
    for out in (out_a, out_b):
        out[Y_TILE : Y_TILE + CX] = near_tiles[...]
    out_a[Y_HALO:] = profiles[...]
    held = BEAM_BITS
    beam = gates[0]
    owner = jnp.bitwise_xor(beam >> held, lax.axis_index("gx"))
    block = (owner & -4) | ((owner & 1) << 1) | ((owner >> 1) & 1)
    meta[...] = jnp.zeros(meta.shape, f32)
    meta[0:1] = gates[2].astype(f32)
    meta[1:2] = ((block << held) | (beam & ((1 << held) - 1))).astype(f32)
    meta[2:3] = gates[1].astype(f32)
    meta[3:4] = gates[3].astype(f32) * values[...]


def y_sides(got_a, got_b, rows, fill=0.0):
    even, low, high = place_on("gy")
    first, second = got_a[rows], got_b[rows]
    north, south = jnp.where(even, first, second), jnp.where(even, second, first)
    return jnp.where(high, north, fill), jnp.where(low, south, fill)


def x_sides(got_a, got_b, rows):
    even, low, high = place_on("gx")
    first, second = got_a[rows], got_b[rows]
    west, east = jnp.where(even, second, first), jnp.where(even, first, second)
    return jnp.where(low, west, 0.0), jnp.where(high, east, 0.0)


def gather_known(alpha, got_a, others, known):
    owned = alpha.shape[0]
    known[0:owned] = alpha[...]
    known[owned : 2 * owned] = got_a[Y_HALO:]
    for s, other in enumerate(others):
        known[(2 + s) * owned : (3 + s) * owned] = other[...]


def tile_numbers(near_tiles, got_a, got_b, tiles):
    spot = lax.broadcasted_iota(jnp.int32, (CX, 128), 1)
    north, south = y_sides(got_a, got_b, pl.ds(Y_TILE, CX), -1.0)
    near = jnp.where(
        (spot >= CY) & (spot < CY + RIM),
        pltpu.roll(north, CY, 1),
        jnp.where((spot >= PITCH - RIM) & (spot < PITCH), pltpu.roll(south, PITCH - CY, 1), -1.0),
    )
    tiles[...] = jnp.full(tiles.shape, -1.0, f32)
    tiles[0:CX] = jnp.where(spot < CY, near_tiles[...], near)
    return jnp.transpose(tiles[...])[0:PITCH]


def tile_ids(ny, owned):
    me = lax.axis_index("gy")
    lane = lax.broadcasted_iota(jnp.int32, (1, ny * owned), 1)
    ids = lane
    for s in range(ny):
        here = (lane >= s * owned) & (lane < (s + 1) * owned)
        ids = jnp.where(here, jnp.bitwise_xor(me, s) * owned + lane - s * owned, ids)
    return ids.astype(f32)


def by_variable(ref, count):
    return jnp.concatenate([ref[pl.ds(c, count, stride=NC)] for c in range(NC)], axis=1)


def pack_x(ny, delta, coefs, alpha, near_tiles, y_a, y_b, own_beams, got_beams, *rest):
    others = rest[: ny - 2]
    out_a, out_b, beams, field, picks, known, tiles = rest[ny - 2 :]
    even, _, _ = place_on("gx")
    owned = alpha.shape[0] // NC
    gather_known(alpha, y_a, others, known)
    turned = tile_numbers(near_tiles, y_a, y_b, tiles)
    ids = tile_ids(ny, owned)
    columns = [x for x in range(RIM)] + [CX - RIM + x for x in range(RIM)]
    for i, x in enumerate(columns):
        picks[i * PITCH : (i + 1) * PITCH] = (turned[:, x : x + 1] == ids).astype(f32)
    fine = two_part_dot(picks[...].astype(bf16), by_variable(known, ny * owned))

    def fill(own, y_base, reach, c):
        for i, x in enumerate(columns):
            at = i * PITCH
            field[at + CY : at + PITCH] = jnp.zeros((PITCH - CY, 128), f32)
            field[at : at + CY] = own[x * CY : (x + 1) * CY]
        for away in range(1, reach + 1):
            for first, base in ((0, 0), (CX - RIM, RIM * PITCH)):
                rows = pl.ds(y_base + (away - 1) * CX + first, RIM)
                north, south = y_sides(y_a, y_b, rows)
                field[pl.ds(base + CY - 1 + away, RIM, stride=PITCH)] = north
                field[pl.ds(base + PITCH - away, RIM, stride=PITCH)] = south
        if c is not None:
            field[...] += profile_weight * fine[:, c * 128 : (c + 1) * 128]

    def put(at, found):
        for away, start, extra in found:
            east, west = (2 * RIM - away) * PITCH, (away - 1) * PITCH
            here = at + start
            for source, target, size in (
                (PITCH - extra, 0, extra),
                (0, extra, CY + extra),
            ):
                if size:
                    first = field[east + source : east + source + size]
                    second = field[west + source : west + source + size]
                    rows = slice(here + target, here + target + size)
                    out_a[rows] = jnp.where(even, first, second)
                    out_b[rows] = jnp.where(even, second, first)

    for c in range(NC):
        fill(delta.at[c], c * RIM * CX, RIM, c)
        put(c * WIDE_ROWS, WIDE)
    for f in range(3):
        fill(coefs.at[f], Y_COEF + f * INNER * CX, INNER, None)
        put(X_COEF + f * SLIM_ROWS, SLIM)
    half = own_beams.shape[0]
    beams[0:half] = own_beams[...]
    beams[half:] = got_beams[...]
    out_a[X_HALO:] = beams[...]


def prepare(ny, delta, coefs, alpha, near_tiles, meta, weights, y_a, y_b, *rest):
    others = rest[: ny - 2]
    core, coef, picks, wide, slot_pick, slot_push, beam_pick, columns = rest[ny - 2 : ny + 6]
    known, tiles = rest[ny + 6 :]
    owned = alpha.shape[0] // NC

    def fill(ref, base, own, y_base, reach):
        for x in range(CX):
            at = base + x * PITCH
            ref[at : at + CY] = own[x * CY : (x + 1) * CY]
            ref[at + CY : at + PITCH] = jnp.zeros((PITCH - CY, 128), f32)
        for away in range(1, reach + 1):
            north, south = y_sides(y_a, y_b, pl.ds(y_base + (away - 1) * CX, CX))
            ref[pl.ds(base + CY - 1 + away, CX, stride=PITCH)] = north
            ref[pl.ds(base + PITCH - away, CX, stride=PITCH)] = south

    for c in range(NC):
        fill(core, c * CORE, delta.at[c], c * RIM * CX, RIM)
    for f in range(3):
        fill(coef, f * CORE, coefs.at[f], Y_COEF + f * INNER * CX, INNER)

    def combine(b, carry):
        at = pl.multiple_of(b * PITCH, 8)
        combined = combine_coefs(*[coef[pl.ds(f * CORE + at, PITCH)] for f in range(3)])
        for f, value in enumerate(combined):
            coef[pl.ds(f * CORE + at, PITCH)] = value
        return carry

    lax.fori_loop(0, CX, combine, 0)

    gather_known(alpha, y_a, others, known)
    turned = tile_numbers(near_tiles, y_a, y_b, tiles)
    ids = tile_ids(ny, owned)
    for x in range(CX):
        picks[x * PITCH : (x + 1) * PITCH] = (turned[:, x : x + 1] == ids).astype(f32)
    fine = two_part_dot(picks[...].astype(bf16), by_variable(known, ny * owned))
    for c in range(NC):
        core[c * CORE : (c + 1) * CORE] += profile_weight * fine[:, c * 128 : (c + 1) * 128]

    slots = meta.shape[1]
    for c in range(NC):
        wide[:, c * 128 : (c + 1) * 128] = weights[pl.ds(c, slots, stride=NC)]
    per_beam = beam_pick.shape[1]
    turned = jnp.transpose(meta[...])
    columns[...] = turned
    slot_lane = lax.broadcasted_iota(jnp.int32, (slots, CX * CY), 1).astype(f32)
    slot_pick[...] = (slot_lane == turned[:, 0:1]).astype(f32).astype(bf16)
    column_row = lax.broadcasted_iota(jnp.int32, (CX * CY, slots), 0).astype(f32)
    slot_push[...] = (column_row == meta[0:1]).astype(f32).astype(bf16)
    beam_lane = lax.broadcasted_iota(jnp.int32, (slots, per_beam), 1).astype(f32)
    beam_pick[...] = (beam_lane == turned[:, 1:2]).astype(f32).astype(bf16)


def combine_coefs(viscous, along_x, along_y):
    half_x, half_y = 0.5 * along_x, 0.5 * along_y
    return (
        1.0 - 4.0 * viscous,
        viscous - half_x,
        viscous + half_x,
        viscous - half_y,
        viscous + half_y,
    )


def clear(ref, base, blocks):
    for b in blocks:
        at = base + b * PITCH
        ref[at : at + PITCH] = jnp.zeros((PITCH, 128), f32)


def forecast(core, coef_core, x_a, x_b, tops, lows, coef, state_0, state_1, raw):
    def fill(ref, base, x_base, found):
        for away, start, extra in found:
            for source, target, size in (
                (0, PITCH - extra, extra),
                (extra, 0, CY + extra),
            ):
                if size:
                    at = x_base + start + source
                    west, east = x_sides(x_a, x_b, pl.ds(at, size))
                    at = base + (FIRST - away) * PITCH + target
                    ref[at : at + size] = west
                    at = base + (FIRST + CX - 1 + away) * PITCH + target
                    ref[at : at + size] = east

    rim = [FIRST - 3, FIRST - 2, FIRST - 1, FIRST + CX, FIRST + CX + 1, FIRST + CX + 2]
    for c in range(NC):
        at = c * FIELD + FIRST * PITCH
        state_0[at : at + CORE] = core[c * CORE : (c + 1) * CORE]
        clear(state_0, c * FIELD, rim)
        fill(state_0, c * FIELD, c * WIDE_ROWS, WIDE)
    for f in range(3):
        clear(raw, f * FIELD, rim[1:5])
        fill(raw, f * FIELD, X_COEF + f * SLIM_ROWS, SLIM)
    for f in range(5):
        at = f * FIELD + FIRST * PITCH
        coef[at : at + CORE] = coef_core[f * CORE : (f + 1) * CORE]
        clear(coef, f * FIELD, [0, 1, BLOCKS - 2, BLOCKS - 1])
    for b in rim[1:5]:
        rows = [slice(f * FIELD + b * PITCH, f * FIELD + (b + 1) * PITCH) for f in range(5)]
        for f, value in enumerate(combine_coefs(*[raw[rows[f]] for f in range(3)])):
            coef[rows[f]] = value

    def forward(source, target, low, high):
        def body(b, carry):
            at = pl.multiple_of(b * PITCH, 8)
            k = [coef[pl.ds(f * FIELD + at, PITCH)] for f in range(5)]
            for c in range(NC):
                base = c * FIELD + at
                here = source[pl.ds(base, PITCH)]
                target[pl.ds(base, PITCH)] = (
                    k[0] * here
                    + k[1] * source[pl.ds(base + PITCH, PITCH)]
                    + k[2] * source[pl.ds(base - PITCH, PITCH)]
                    + k[3] * pltpu.roll(here, PITCH - 1, 0)
                    + k[4] * pltpu.roll(here, 1, 0)
                )
            return carry

        lax.fori_loop(low, high, body, 0)

    buffers = [state_0, state_1]
    for step in range(STEPS):
        source, target = buffers[step % 2], buffers[(step + 1) % 2]
        forward(source, target, 2 + step, BLOCKS - 2 - step)
        own = jnp.concatenate(
            [
                jnp.concatenate(
                    [
                        target[c * FIELD + b * PITCH : c * FIELD + b * PITCH + CY]
                        for b in range(FIRST, FIRST + CX)
                    ],
                    axis=0,
                )
                for c in range(NC)
            ],
            axis=1,
        )
        rows = slice(step * CX * CY, (step + 1) * CX * CY)
        tops[rows], lows[rows] = split(own)


def main(
    coef,
    tops,
    lows,
    wide,
    slot_pick,
    slot_push,
    beam_pick,
    columns,
    *rest,
):
    beams = rest[:-6]
    out_a, out_b, out_core, state_0, state_1, forcing = rest[-6:]
    even, _, _ = place_on("gx")
    slots = columns.shape[0]
    gate_lane = lax.broadcasted_iota(jnp.int32, (slots, 128), 1).astype(f32)
    gate_here = gate_lane == columns[:, 2:3]
    scaled = columns[:, 3:4]
    for step in range(STEPS):
        rows = slice(step * CX * CY, (step + 1) * CX * CY)
        picked = jnp.dot(slot_pick[...], tops[rows], preferred_element_type=f32)
        picked = picked + jnp.dot(slot_pick[...], lows[rows], preferred_element_type=f32)
        picked = picked * wide[...]
        table = []
        for part in beams:
            for at in range(0, part.shape[0], STEPS * OWN_BEAMS):
                first = at + step * OWN_BEAMS
                table.append(part[first : first + OWN_BEAMS])
        table = two_part_dot(beam_pick[...], jnp.concatenate(table, axis=0))
        tally = -jnp.where(gate_here, table, 0.0)
        for c in range(NC):
            tally = tally + picked[:, c * 128 : (c + 1) * 128]
        misfit = scaled * jnp.sum(tally, axis=1, keepdims=True)
        forcing[rows] = two_part_dot(slot_push[...], misfit * wide[...])

    buffers = [state_0, state_1]

    for c in range(NC):
        clear(state_0, c * FIELD, [0, 1, 2, 3, BLOCKS - 4, BLOCKS - 3, BLOCKS - 2, BLOCKS - 1])
        clear(state_1, c * FIELD, [1, 2, BLOCKS - 3, BLOCKS - 2])

    def add_forcing(ref, step):
        for c in range(NC):
            for x in range(CX):
                at = c * FIELD + (FIRST + x) * PITCH
                first = step * CX * CY + x * CY
                value = forcing[first : first + CY, c * 128 : (c + 1) * 128]
                if step == STEPS - 1:
                    ref[at : at + CY] = value
                    ref[at + CY : at + PITCH] = jnp.zeros((PITCH - CY, 128), f32)
                else:
                    ref[at : at + CY] += value

    def backward(source, target, low, high):
        def body(b, carry):
            at = pl.multiple_of(b * PITCH, 8)
            k = [
                coef[pl.ds(at, PITCH)],
                coef[pl.ds(FIELD + at - PITCH, PITCH)],
                coef[pl.ds(2 * FIELD + at + PITCH, PITCH)],
                coef[pl.ds(3 * FIELD + at, PITCH)],
                coef[pl.ds(4 * FIELD + at, PITCH)],
            ]
            for c in range(NC):
                base = c * FIELD + at
                here = source[pl.ds(base, PITCH)]
                target[pl.ds(base, PITCH)] = (
                    k[0] * here
                    + k[1] * source[pl.ds(base - PITCH, PITCH)]
                    + k[2] * source[pl.ds(base + PITCH, PITCH)]
                    + pltpu.roll(k[3] * here, 1, 0)
                    + pltpu.roll(k[4] * here, PITCH - 1, 0)
                )
            return carry

        lax.fori_loop(low, high, body, 0)

    for step in range(STEPS):
        source, target = buffers[step % 2], buffers[(step + 1) % 2]
        add_forcing(source, STEPS - 1 - step)
        backward(source, target, FIRST - 1 - step, FIRST + CX + 1 + step)
    final = buffers[STEPS % 2]

    for c in range(NC):
        at = c * FIELD + FIRST * PITCH
        out_core[c * CORE : (c + 1) * CORE] = final[at : at + CORE]
        for away, start, extra in WIDE:
            for source, target, size in (
                (PITCH - extra, 0, extra),
                (0, extra, CY + extra),
            ):
                if size:
                    at = c * FIELD + (FIRST - away) * PITCH + source
                    west = final[at : at + size]
                    at = c * FIELD + (FIRST + CX - 1 + away) * PITCH + source
                    east = final[at : at + size]
                    at = c * WIDE_ROWS + start + target
                    out_a[at : at + size] = jnp.where(even, east, west)
                    out_b[at : at + size] = jnp.where(even, west, east)


def add_x(ny, delta, picks, core, x_a, x_b, *rest):
    out_a, out_b, out_near, out_sums = rest[:4]
    out_others = rest[4:-2]
    merged = ny == 4
    field, sums = rest[-2:]
    even, _, _ = place_on("gy")
    total = picks.shape[1]
    rows = total * NC // ny
    field[...] = core[...]
    for c in range(NC):
        for away, start, extra in WIDE:
            for source, target, size in (
                (0, PITCH - extra, extra),
                (extra, 0, CY + extra),
            ):
                if size:
                    at = c * WIDE_ROWS + start + source
                    west, east = x_sides(x_a, x_b, pl.ds(at, size))
                    at = c * CORE + (away - 1) * PITCH + target
                    field[at : at + size] += west
                    at = c * CORE + (CX - away) * PITCH + target
                    field[at : at + size] += east
    for c in range(NC):
        for away in range(1, RIM + 1):
            north = field[pl.ds(c * CORE + CY - 1 + away, CX, stride=PITCH)]
            south = field[pl.ds(c * CORE + PITCH - away, CX, stride=PITCH)]
            at = (c * RIM + away - 1) * CX
            out_a[at : at + CX] = jnp.where(even, north, south)
            out_b[at : at + CX] = jnp.where(even, south, north)
        for x in range(CX):
            at = c * CORE + x * PITCH
            here = slice(x * CY, (x + 1) * CY)
            out_near[c, here] = delta[c, here] + field[at : at + CY]
    adjoint = jnp.concatenate([field[c * CORE : (c + 1) * CORE] for c in range(NC)], axis=1)
    tile_sums = two_part_dot(jnp.transpose(picks[...]).astype(bf16), adjoint)
    for c in range(NC):
        sums[pl.ds(c, total, stride=NC)] = tile_sums[:, c * 128 : (c + 1) * 128]
    out_sums[...] = sums[0:rows]
    out_a[Y_COEF:] = sums[rows : 2 * rows]
    if merged:
        out_b[Y_COEF:] = sums[3 * rows : 4 * rows]
    for s, other in enumerate(out_others):
        other[...] = sums[(2 + s) * rows : (3 + s) * rows]


def add_y(alpha, near, sums, y_a, y_b, *rest):
    others = rest[:-2]
    out_delta, out_alpha = rest[-2:]
    out_delta[...] = near[...]
    for c in range(NC):
        for away in range(1, RIM + 1):
            north, south = y_sides(y_a, y_b, pl.ds((c * RIM + away - 1) * CX, CX))
            high = pl.ds(CY - away, CX, stride=CY)
            low = pl.ds(away - 1, CX, stride=CY)
            out_delta[c, high] = out_delta[c, high] + north
            out_delta[c, low] = out_delta[c, low] + south
    total = sums[...] + y_a[Y_COEF:]
    if y_b.shape[0] > Y_COEF:
        total = total + y_b[Y_COEF:]
    for other in others:
        total = total + other[...]
    out_alpha[...] = alpha[...] + profile_weight * total


def on_device(
    delta,
    alpha,
    eddy,
    courant,
    tile_map,
    obs_rows,
    gate_beam,
    gate_index,
    gate_column,
    gate_live,
    obs_weight,
    obs_precision,
):
    nx = lax.axis_size("gx")
    ny = lax.axis_size("gy")
    owned = alpha.shape[1]
    slots = gate_column.shape[2]
    fine = delta.reshape(NC, CX * CY, 128)
    eddy = eddy.reshape(CX * CY, 128)
    courant = courant.reshape(2, CX * CY, 128)
    control = alpha.reshape(owned * NC, 128)
    weights = obs_weight.reshape(slots * NC, 128)
    gates = [
        value.reshape(1, slots)
        for value in (gate_beam, gate_index, gate_column, gate_live, obs_precision)
    ]
    own_beams = jnp.transpose(obs_rows, (1, 0, 2)).reshape(STEPS * OWN_BEAMS, 128)
    beam_count = nx * OWN_BEAMS
    rows = owned * NC
    total = ny * owned

    y_a, y_b, fine, coefs, control_near, near_tiles, meta, near_beams = call(
        pack_y,
        [
            (Y_HALO + rows, 128),
            (Y_HALO, 128),
            fine.shape,
            (3, CX * CY, 128),
            control.shape,
            (CX, 128),
            (8, slots),
            own_beams.shape,
        ],
        [
            pltpu.with_memory_space_constraint(value, pltpu.HBM)
            for value in (fine, eddy, courant, control, tile_map, *gates, own_beams)
        ],
        [
            pltpu.VMEM(tile_map.shape, jnp.int32),
            pltpu.VMEM((4, 1, slots), jnp.int32),
            pltpu.VMEM((1, slots), f32),
            pltpu.SemaphoreType.DMA((12,)),
        ],
        in_specs=[HBM] * 11,
    )
    y_a = swap(y_a, "gy", 1)
    y_b = pair_b(y_b, "gy", "gx")
    others = [swap(control, "gy", xor) for xor in range(2, ny)]
    got_beams = swap(own_beams, "gx", 2)

    x_a, x_b, beams = call(
        lambda *refs: pack_x(ny, *refs),
        [(X_HALO + 2 * own_beams.shape[0], 128), (X_HALO, 128), (2 * own_beams.shape[0], 128)],
        [fine, coefs, control_near, near_tiles, y_a, y_b, near_beams, got_beams, *others],
        [
            pltpu.VMEM((2 * RIM * PITCH, 128), f32),
            pltpu.VMEM((2 * RIM * PITCH, total), f32),
            pltpu.VMEM((total * NC, 128), f32),
            pltpu.VMEM((128, 128), f32),
        ],
    )
    x_a = swap(x_a, "gx", 1)
    x_b = pair_b(x_b, "gx", "gy")

    core, coef, picks, wide, slot_pick, slot_push, beam_pick, columns = call(
        lambda *refs: prepare(ny, *refs),
        [
            (NC * CORE, 128),
            (5 * CORE, 128),
            (CORE, total),
            (slots, NC * 128),
            jax.ShapeDtypeStruct((slots, CX * CY), bf16),
            jax.ShapeDtypeStruct((CX * CY, slots), bf16),
            jax.ShapeDtypeStruct((slots, beam_count), bf16),
            (slots, 8),
        ],
        [fine, coefs, control_near, near_tiles, meta, weights, y_a, y_b, *others],
        [
            pltpu.VMEM((total * NC, 128), f32),
            pltpu.VMEM((128, 128), f32),
        ],
        flops=3000000,
    )

    beams = [beams, x_a[X_HALO:]]
    xor = 4
    while xor < nx:
        beams = beams + [swap(jnp.concatenate(beams), "gx", xor)]
        xor *= 2

    tops, lows, coef = call(
        forecast,
        [
            jax.ShapeDtypeStruct((STEPS * CX * CY, NC * 128), bf16),
            jax.ShapeDtypeStruct((STEPS * CX * CY, NC * 128), bf16),
            (5 * FIELD, 128),
        ],
        [core, coef, x_a, x_b],
        [
            pltpu.VMEM((NC * FIELD, 128), f32),
            pltpu.VMEM((NC * FIELD, 128), f32),
            pltpu.VMEM((3 * FIELD, 128), f32),
        ],
        flops=10000000,
    )
    back_a, back_b, core = call(
        main,
        [(X_COEF, 128), (X_COEF, 128), (NC * CORE, 128)],
        [coef, tops, lows, wide, slot_pick, slot_push, beam_pick, columns, *beams],
        [
            pltpu.VMEM((NC * FIELD, 128), f32),
            pltpu.VMEM((NC * FIELD, 128), f32),
            pltpu.VMEM((STEPS * CX * CY, NC * 128), f32),
        ],
        flops=20000000,
    )
    x_a = swap(back_a, "gx", 1)
    x_b = pair_b(back_b, "gx", "gy")
    loose = [xor for xor in range(2, ny) if ny != 4 or xor != 3]
    back_a, back_b, near, sums, *back = call(
        lambda *refs: add_x(ny, *refs),
        [
            (Y_COEF + rows, 128),
            (Y_COEF + (rows if ny == 4 else 0), 128),
            fine.shape,
            (rows, 128),
        ]
        + [(rows, 128)] * len(loose),
        [fine, picks, core, x_a, x_b],
        [pltpu.VMEM((NC * CORE, 128), f32), pltpu.VMEM((total * NC, 128), f32)],
    )
    y_a = swap(back_a, "gy", 1)
    y_b = ring_b(back_b, "gy")
    others = [swap(value, "gy", xor) for xor, value in zip(loose, back)]
    grad_delta, grad_alpha = call(
        add_y,
        [fine.shape, control.shape],
        [control_near, near, sums, y_a, y_b, *others],
    )
    return grad_delta.reshape(delta.shape), grad_alpha.reshape(alpha.shape)


def solution(mesh):
    return jax.shard_map(
        on_device,
        mesh=mesh,
        in_specs=(
            P(None, "gx", "gy", None),
            P("gx", "gy", None, None),
            P("gx", "gy", None),
            P(None, "gx", "gy", None),
            P("gx", "gy"),
            P(("gx", "gy"), None, None),
            P("gx", "gy", None),
            P("gx", "gy", None),
            P("gx", "gy", None),
            P("gx", "gy", None),
            P("gx", "gy", None, None, None),
            P("gx", "gy", None),
        ),
        out_specs=(P(None, "gx", "gy", None), P("gx", "gy", None, None)),
        check_vma=False,
    )
```

```python
import jax
import jax.numpy as jnp
from jax import lax
from jax.experimental import pallas as pl
from jax.experimental.pallas import tpu as pltpu
from jax.sharding import PartitionSpec as P

STEPS = 3
RIM = 3
INNER = RIM - 1
NC = 4
CX = 16
CY = 16
BLOCKS = CX + 8
PITCH = CY + 8
FIRST = 4
FIELD = BLOCKS * PITCH
OWN_BEAMS = 8
BEAM_BITS = 3
BEAM_ROWS = STEPS * OWN_BEAMS

BULK_COEF = NC * RIM * CY
BULK = BULK_COEF + 3 * INNER * CY

profile_weight = 0.125
f32 = jnp.float32
bf16 = jnp.bfloat16

VMEM = pl.BlockSpec(memory_space=pltpu.VMEM)
HBM = pl.BlockSpec(memory_space=pltpu.HBM)


def call(body, outs, ins, scratch=(), in_specs=None, flops=1000000, limit=40 * 2**20):
    shapes = [
        out if isinstance(out, jax.ShapeDtypeStruct) else jax.ShapeDtypeStruct(out, f32)
        for out in outs
    ]
    size = sum(4 * value.size for value in ins)
    return pl.pallas_call(
        body,
        out_shape=shapes,
        in_specs=in_specs or [VMEM] * len(ins),
        out_specs=[VMEM] * len(shapes),
        scratch_shapes=list(scratch),
        compiler_params=pltpu.CompilerParams(vmem_limit_bytes=limit),
        cost_estimate=pl.CostEstimate(flops=flops, bytes_accessed=size, transcendentals=0),
    )(*ins)


def swap(block, axis, xor):
    return lax.ppermute(block, axis, [(i, i ^ xor) for i in range(lax.axis_size(axis))])


def pair_b(block, axis, other):
    count, across = lax.axis_size(axis), lax.axis_size(other)

    def place(i, j):
        return i * across + j if axis == "gx" else j * count + i

    pairs = []
    for j in range(across):
        for i in range(count):
            if i in (0, count - 1):
                pairs.append((place(i, j), place(i, j ^ 1)))
            else:
                pairs.append((place(i, j), place(i + 1 if i % 2 else i - 1, j)))
    return lax.ppermute(block, ("gx", "gy"), pairs)


def ring_b(block, axis):
    count = lax.axis_size(axis)
    pairs = [(i, (i + 1 if i % 2 else i - 1) % count) for i in range(count)]
    return lax.ppermute(block, axis, pairs)


def place_on(axis):
    me = lax.axis_index(axis)
    return lax.rem(me, 2) == 0, me > 0, me < lax.axis_size(axis) - 1


def split(value):
    top = value.astype(bf16)
    return top, (value - top.astype(f32)).astype(bf16)


def two_part_dot(left, value):
    top, low = split(value)
    return jnp.dot(left, top, preferred_element_type=f32) + jnp.dot(
        left, low, preferred_element_type=f32
    )


def layers(reach):
    found, at = [], 0
    for away in range(1, reach + 1):
        found.append((away, at, reach - away))
        at += CX + 2 * (reach - away)
    return found, at


WIDE, WIDE_ROWS = layers(RIM)
SLIM, SLIM_ROWS = layers(INNER)
Y_COEF = NC * WIDE_ROWS
Y_TILE = Y_COEF + 3 * SLIM_ROWS
Y_HALO = Y_TILE + BLOCKS

CORNER = sum(extra for _, _, extra in WIDE)
COEF_CORNER = sum(extra for _, _, extra in SLIM)


def small_places(profile_rows):
    corner = profile_rows + RIM
    coef_corner = corner + 2 * NC * CORNER
    return profile_rows, corner, coef_corner, coef_corner + 2 * 3 * COEF_CORNER


def y_sides(got_a, got_b, rows, fill=0.0):
    even, low, high = place_on("gy")
    first, second = got_a[rows], got_b[rows]
    north, south = jnp.where(even, first, second), jnp.where(even, second, first)
    return jnp.where(high, north, fill), jnp.where(low, south, fill)


def x_sides(got_a, got_b, rows, fill=0.0):
    even, low, high = place_on("gx")
    first, second = got_a[rows], got_b[rows]
    west, east = jnp.where(even, second, first), jnp.where(even, first, second)
    return jnp.where(low, west, fill), jnp.where(high, east, fill)


def put_pair(out_a, out_b, even, at, above, below):
    rows = slice(at, at + above.shape[0])
    out_a[rows] = jnp.where(even, above, below)
    out_b[rows] = jnp.where(even, below, above)


def pack_x(
    delta,
    eddy,
    courant,
    alpha,
    tile_map,
    gate_beam,
    gate_index,
    gate_column,
    gate_live,
    precision,
    beam_rows,
    small_a,
    small_b,
    bulk_a,
    bulk_b,
    fine,
    coefs,
    profiles,
    near_tiles,
    meta,
    beams,
    tiles,
    gates,
    values,
    sems,
):
    even, _, _ = place_on("gx")
    moves = [
        pltpu.make_async_copy(source, target, sems.at[i])
        for i, (source, target) in enumerate(
            [
                (delta, fine),
                (eddy, coefs.at[0]),
                (courant.at[0], coefs.at[1]),
                (courant.at[1], coefs.at[2]),
                (tile_map, tiles),
                (alpha, profiles),
                (gate_beam, gates.at[0]),
                (gate_index, gates.at[1]),
                (gate_column, gates.at[2]),
                (gate_live, gates.at[3]),
                (precision, values),
                (beam_rows, beams),
            ]
        )
    ]
    for move in moves:
        move.start()
    for move in moves:
        move.wait()

    tile, corner, coef_corner, beam = small_places(profiles.shape[0])
    near_tiles[...] = jnp.full((CX, 128), -1.0, f32)
    near_tiles[:, 0:CY] = tiles[...].astype(f32)
    small_a[0:tile] = profiles[...]
    small_b[0:tile] = profiles[...]
    numbers = near_tiles[...]
    put_pair(small_a, small_b, even, tile, numbers[CX - RIM :], numbers[:RIM])

    def corners(at, field, reach, side):
        for away in range(1, reach):
            y = CY - away if side == 0 else away - 1
            width = reach - away
            for i in range(width):
                east = field[pl.ds((CX - width + i) * CY + y, 1)]
                west = field[pl.ds(i * CY + y, 1)]
                put_pair(small_a, small_b, even, at, east, west)
                at += 1

    for side in range(2):
        for c in range(NC):
            corners(corner + (side * NC + c) * CORNER, fine.at[c], RIM, side)
        for f in range(3):
            corners(coef_corner + (side * 3 + f) * COEF_CORNER, coefs.at[f], INNER, side)
    small_a[beam:] = beams[...]

    wide, slim = RIM * CY, INNER * CY
    for c in range(NC):
        put_pair(bulk_a, bulk_b, even, c * wide, fine[c, CX * CY - wide :], fine[c, :wide])
    for f in range(3):
        east, west = coefs[f, CX * CY - slim :], coefs[f, :slim]
        put_pair(bulk_a, bulk_b, even, BULK_COEF + f * slim, east, west)

    beam = gates[0]
    block = jnp.bitwise_xor(beam >> BEAM_BITS, lax.axis_index("gx"))
    meta[...] = jnp.zeros(meta.shape, f32)
    meta[0:1] = gates[2].astype(f32)
    meta[1:2] = ((block << BEAM_BITS) | (beam & (OWN_BEAMS - 1))).astype(f32)
    meta[2:3] = gates[1].astype(f32)
    meta[3:4] = gates[3].astype(f32) * values[...]


def pack_y(
    fine,
    coefs,
    control,
    tiles,
    beams,
    got_a,
    got_b,
    out_a,
    out_b,
    profiles,
    near_tiles,
    beam_pair,
):
    even, _, _ = place_on("gy")
    count = control.shape[0]
    tile, corner, coef_corner, beam = small_places(count)

    def sides(at, size, fill=0.0):
        return x_sides(got_a, got_b, slice(at, at + size), fill)

    def edge(at, found, own, north_corner, south_corner):
        for away, start, width in found:
            here = at + start
            if width:
                north_w, north_e = sides(north_corner, width)
                south_w, south_e = sides(south_corner, width)
                put_pair(out_a, out_b, even, here, north_w, south_w)
                put_pair(out_a, out_b, even, here + width + CX, north_e, south_e)
                north_corner += width
                south_corner += width
            north = own[pl.ds(CY - away, CX, stride=CY)]
            south = own[pl.ds(away - 1, CX, stride=CY)]
            put_pair(out_a, out_b, even, here + width, north, south)

    west, east = sides(0, count)
    profiles[0:count] = west
    profiles[count : 2 * count] = control[...]
    profiles[2 * count :] = east
    for c in range(NC):
        north, south = corner + c * CORNER, corner + (NC + c) * CORNER
        edge(c * WIDE_ROWS, WIDE, fine.at[c], north, south)
    for f in range(3):
        north, south = coef_corner + f * COEF_CORNER, coef_corner + (3 + f) * COEF_CORNER
        edge(Y_COEF + f * SLIM_ROWS, SLIM, coefs.at[f], north, south)
    west, east = sides(tile, RIM, -1.0)
    near_tiles[...] = jnp.full(near_tiles.shape, -1.0, f32)
    near_tiles[FIRST - RIM : FIRST] = west
    near_tiles[FIRST : FIRST + CX] = tiles[...]
    near_tiles[FIRST + CX : FIRST + CX + RIM] = east
    out_a[Y_TILE:Y_HALO] = near_tiles[...]
    out_b[Y_TILE:Y_HALO] = near_tiles[...]
    out_a[Y_HALO:] = profiles[...]
    beam_pair[0:BEAM_ROWS] = beams[...]
    beam_pair[BEAM_ROWS:] = got_a[beam:]


def slot_xor(ny, slot):
    half = ny // 2
    return 2 * slot if slot < half else 2 * (slot - half) + 1


def tile_ids(ny, owned):
    me = lax.axis_index("gy")
    group = 3 * owned
    lane = lax.broadcasted_iota(jnp.int32, (1, ny * group), 1)
    found = []
    for strip in range(3):
        ids = jnp.full((1, ny * group), -2, jnp.int32)
        for s in range(ny):
            base = s * group + strip * owned
            here = (lane >= base) & (lane < base + owned)
            ids = jnp.where(
                here, jnp.bitwise_xor(me, slot_xor(ny, s)) * owned + lane - base, ids
            )
        found.append(ids.astype(f32))
    return found


def by_variable(ref, count):
    return jnp.concatenate([ref[pl.ds(c, count, stride=NC)] for c in range(NC)], axis=1)


def combine_coefs(viscous, along_x, along_y):
    half_x, half_y = 0.5 * along_x, 0.5 * along_y
    return (
        1.0 - 4.0 * viscous,
        viscous - half_x,
        viscous + half_x,
        viscous - half_y,
        viscous + half_y,
    )


def prepare(
    ny, parts, fine, coefs, near_tiles, meta, weights, y_a, y_b, profiles, *rest
):
    others = rest[:parts]
    field, coef, picks, wide, slot_pick, slot_push, beam_pick, columns, known, tiles = rest[parts:]
    per_slot = profiles.shape[0]
    total = picks.shape[1]
    owned = total // (3 * ny)
    inner = [FIRST - 2, FIRST - 1, FIRST + CX, FIRST + CX + 1]

    def fill(ref, base, own, y_base, reach, found):
        for b in range(FIRST - reach, FIRST + CX + reach):
            at = base + b * PITCH
            if FIRST <= b < FIRST + CX:
                ref[at : at + CY] = own[(b - FIRST) * CY : (b - FIRST + 1) * CY]
                ref[at + CY : at + PITCH] = jnp.zeros((PITCH - CY, 128), f32)
            else:
                ref[at : at + PITCH] = jnp.zeros((PITCH, 128), f32)
        for away, start, width in found:
            size = CX + 2 * width
            north, south = y_sides(y_a, y_b, pl.ds(y_base + start, size))
            at = base + (FIRST - width) * PITCH
            ref[pl.ds(at + CY - 1 + away, size, stride=PITCH)] = north
            ref[pl.ds(at + PITCH - away, size, stride=PITCH)] = south

    for f in range(3):
        fill(coef, f * FIELD, coefs.at[f], Y_COEF + f * SLIM_ROWS, INNER, SLIM)

    def combine(b, carry):
        at = pl.multiple_of(b * PITCH, 8)
        combined = combine_coefs(*[coef[pl.ds(f * FIELD + at, PITCH)] for f in range(3)])
        for f, value in enumerate(combined):
            coef[pl.ds(f * FIELD + at, PITCH)] = value
        return carry

    lax.fori_loop(FIRST, FIRST + CX, combine, 0)
    for f in range(5):
        for b in [0, 1, BLOCKS - 2, BLOCKS - 1] + (inner if f > 2 else []):
            at = f * FIELD + b * PITCH
            coef[at : at + PITCH] = jnp.zeros((PITCH, 128), f32)

    known[0:per_slot] = profiles[...]
    half = ny // 2 * per_slot
    at = per_slot
    for other in others:
        if at == half:
            known[at : at + per_slot] = y_a[Y_HALO:]
            at += per_slot
        known[at : at + other.shape[0]] = other[...]
        at += other.shape[0]

    spot = lax.broadcasted_iota(jnp.int32, (BLOCKS, 128), 1)
    north, south = y_sides(y_a, y_b, pl.ds(Y_TILE, BLOCKS), -1.0)
    near = jnp.where(
        (spot >= CY) & (spot < CY + RIM),
        pltpu.roll(north, CY, 1),
        jnp.where((spot >= PITCH - RIM) & (spot < PITCH), pltpu.roll(south, PITCH - CY, 1), -1.0),
    )
    tiles[...] = jnp.full(tiles.shape, -1.0, f32)
    tiles[0:BLOCKS] = jnp.where(spot < CY, near_tiles[...], near)
    turned = jnp.transpose(tiles[...])[0:PITCH]
    ids = tile_ids(ny, owned)
    for b in range(BLOCKS):
        strip = 0 if b < FIRST else 1 if b < FIRST + CX else 2
        picks[b * PITCH : (b + 1) * PITCH] = (turned[:, b : b + 1] == ids[strip]).astype(f32)
    control = two_part_dot(picks[...].astype(bf16), by_variable(known, total))
    for c in range(NC):
        fill(field, c * FIELD, fine.at[c], c * WIDE_ROWS, RIM, WIDE)
        rows = slice(c * FIELD + PITCH, (c + 1) * FIELD - PITCH)
        field[rows] += profile_weight * control[PITCH:-PITCH, c * 128 : (c + 1) * 128]

    slots = meta.shape[1]
    for c in range(NC):
        wide[:, c * 128 : (c + 1) * 128] = weights[pl.ds(c, slots, stride=NC)]
    per_beam = beam_pick.shape[1]
    turned = jnp.transpose(meta[...])
    columns[...] = turned
    slot_lane = lax.broadcasted_iota(jnp.int32, (slots, CX * CY), 1).astype(f32)
    slot_pick[...] = (slot_lane == turned[:, 0:1]).astype(f32).astype(bf16)
    column_row = lax.broadcasted_iota(jnp.int32, (CX * CY, slots), 0).astype(f32)
    slot_push[...] = (column_row == meta[0:1]).astype(f32).astype(bf16)
    beam_lane = lax.broadcasted_iota(jnp.int32, (slots, per_beam), 1).astype(f32)
    beam_pick[...] = (beam_lane == turned[:, 1:2]).astype(f32).astype(bf16)


def clear(ref, base, blocks):
    for b in blocks:
        at = base + b * PITCH
        ref[at : at + PITCH] = jnp.zeros((PITCH, 128), f32)


def forecast(field, near_coef, bulk_a, bulk_b, tops, lows, coef, state_0, state_1):
    for c in range(NC):
        rows = slice(c * FIELD + PITCH, (c + 1) * FIELD - PITCH)
        state_0[rows] = field[rows]
        for h in range(RIM):
            west, east = x_sides(bulk_a, bulk_b, pl.ds((c * RIM + h) * CY, CY))
            at = c * FIELD + (FIRST - RIM + h) * PITCH
            state_0[at : at + CY] += west
            at = c * FIELD + (FIRST + CX + h) * PITCH
            state_0[at : at + CY] += east
    coef[...] = near_coef[...]
    for h in range(INNER):
        sides = []
        for f in range(3):
            sides.append(x_sides(bulk_a, bulk_b, pl.ds(BULK_COEF + (f * INNER + h) * CY, CY)))
        for side, b in enumerate((FIRST - INNER + h, FIRST + CX + h)):
            raw = []
            for f in range(3):
                at = f * FIELD + b * PITCH
                coef[at : at + CY] += sides[f][side]
                raw.append(coef[at : at + PITCH])
            for f, value in enumerate(combine_coefs(*raw)):
                at = f * FIELD + b * PITCH
                coef[at : at + PITCH] = value

    def forward(source, target, low, high):
        def body(b, carry):
            at = pl.multiple_of(b * PITCH, 8)
            k = [coef[pl.ds(f * FIELD + at, PITCH)] for f in range(5)]
            for c in range(NC):
                base = c * FIELD + at
                here = source[pl.ds(base, PITCH)]
                target[pl.ds(base, PITCH)] = (
                    k[0] * here
                    + k[1] * source[pl.ds(base + PITCH, PITCH)]
                    + k[2] * source[pl.ds(base - PITCH, PITCH)]
                    + k[3] * pltpu.roll(here, PITCH - 1, 0)
                    + k[4] * pltpu.roll(here, 1, 0)
                )
            return carry

        lax.fori_loop(low, high, body, 0)

    buffers = [state_0, state_1]
    for step in range(STEPS):
        source, target = buffers[step % 2], buffers[(step + 1) % 2]
        forward(source, target, 2 + step, BLOCKS - 2 - step)
        own = jnp.concatenate(
            [
                jnp.concatenate(
                    [
                        target[c * FIELD + b * PITCH : c * FIELD + b * PITCH + CY]
                        for b in range(FIRST, FIRST + CX)
                    ],
                    axis=0,
                )
                for c in range(NC)
            ],
            axis=1,
        )
        rows = slice(step * CX * CY, (step + 1) * CX * CY)
        tops[rows], lows[rows] = split(own)


def main(
    ny,
    parts,
    coef,
    tops,
    lows,
    wide,
    slot_pick,
    slot_push,
    beam_pick,
    columns,
    *rest,
):
    picks, fine, *beams = rest[: 2 + parts]
    out_a, out_b, bulk_a, bulk_b, out_near, out_sums, *out_others = rest[2 + parts : -4]
    state_0, state_1, forcing, sums = rest[-4:]
    even, _, _ = place_on("gy")
    even_x, _, _ = place_on("gx")
    total = picks.shape[1]
    per_slot = total * NC // ny
    slots = columns.shape[0]
    gate_lane = lax.broadcasted_iota(jnp.int32, (slots, 128), 1).astype(f32)
    gate_here = gate_lane == columns[:, 2:3]
    scaled = columns[:, 3:4]
    for step in range(STEPS):
        rows = slice(step * CX * CY, (step + 1) * CX * CY)
        picked = jnp.dot(slot_pick[...], tops[rows], preferred_element_type=f32)
        picked = picked + jnp.dot(slot_pick[...], lows[rows], preferred_element_type=f32)
        picked = picked * wide[...]
        table = []
        for part in beams:
            for at in range(0, part.shape[0], STEPS * OWN_BEAMS):
                first = at + step * OWN_BEAMS
                table.append(part[first : first + OWN_BEAMS])
        table = two_part_dot(beam_pick[...], jnp.concatenate(table, axis=0))
        tally = -jnp.where(gate_here, table, 0.0)
        for c in range(NC):
            tally = tally + picked[:, c * 128 : (c + 1) * 128]
        misfit = scaled * jnp.sum(tally, axis=1, keepdims=True)
        forcing[rows] = two_part_dot(slot_push[...], misfit * wide[...])

    buffers = [state_0, state_1]

    for c in range(NC):
        clear(state_0, c * FIELD, [0, 1, 2, 3, BLOCKS - 4, BLOCKS - 3, BLOCKS - 2, BLOCKS - 1])
        clear(state_1, c * FIELD, [1, 2, BLOCKS - 3, BLOCKS - 2])

    def add_forcing(ref, step):
        for c in range(NC):
            for x in range(CX):
                at = c * FIELD + (FIRST + x) * PITCH
                first = step * CX * CY + x * CY
                value = forcing[first : first + CY, c * 128 : (c + 1) * 128]
                if step == STEPS - 1:
                    ref[at : at + CY] = value
                    ref[at + CY : at + PITCH] = jnp.zeros((PITCH - CY, 128), f32)
                else:
                    ref[at : at + CY] += value

    def backward(source, target, low, high):
        def body(b, carry):
            at = pl.multiple_of(b * PITCH, 8)
            k = [
                coef[pl.ds(at, PITCH)],
                coef[pl.ds(FIELD + at - PITCH, PITCH)],
                coef[pl.ds(2 * FIELD + at + PITCH, PITCH)],
                coef[pl.ds(3 * FIELD + at, PITCH)],
                coef[pl.ds(4 * FIELD + at, PITCH)],
            ]
            for c in range(NC):
                base = c * FIELD + at
                here = source[pl.ds(base, PITCH)]
                target[pl.ds(base, PITCH)] = (
                    k[0] * here
                    + k[1] * source[pl.ds(base - PITCH, PITCH)]
                    + k[2] * source[pl.ds(base + PITCH, PITCH)]
                    + pltpu.roll(k[3] * here, 1, 0)
                    + pltpu.roll(k[4] * here, PITCH - 1, 0)
                )
            return carry

        lax.fori_loop(low, high, body, 0)

    for step in range(STEPS):
        source, target = buffers[step % 2], buffers[(step + 1) % 2]
        add_forcing(source, STEPS - 1 - step)
        backward(source, target, FIRST - 1 - step, FIRST + CX + 1 + step)
    final = buffers[STEPS % 2]

    for c in range(NC):
        for h in range(RIM):
            at = c * FIELD + (FIRST - RIM + h) * PITCH
            west = final[at : at + CY]
            at = c * FIELD + (FIRST + CX + h) * PITCH
            put_pair(bulk_a, bulk_b, even_x, (c * RIM + h) * CY, final[at : at + CY], west)
        for away, start, width in WIDE:
            at = c * FIELD + (FIRST - width) * PITCH
            size = CX + 2 * width
            north = final[pl.ds(at + CY - 1 + away, size, stride=PITCH)]
            south = final[pl.ds(at + PITCH - away, size, stride=PITCH)]
            put_pair(out_a, out_b, even, c * WIDE_ROWS + start, north, south)
        for x in range(CX):
            at = c * FIELD + (FIRST + x) * PITCH
            rows = slice(x * CY, (x + 1) * CY)
            out_near[c, rows] = fine[c, rows] + final[at : at + CY]

    for c in range(NC):
        clear(final, c * FIELD, [0, BLOCKS - 1])
    adjoint = jnp.concatenate([final[c * FIELD : (c + 1) * FIELD] for c in range(NC)], axis=1)
    tile_sums = two_part_dot(jnp.transpose(picks[...]).astype(bf16), adjoint)
    for c in range(NC):
        sums[pl.ds(c, total, stride=NC)] = tile_sums[:, c * 128 : (c + 1) * 128]
    out_sums[...] = sums[0:per_slot]
    outs = dict(zip(loose_slots(ny), out_others))
    for s in range(1, ny):
        rows = slice(s * per_slot, (s + 1) * per_slot)
        if s in outs:
            outs[s][...] = sums[rows]
        elif slot_xor(ny, s) == 1:
            out_a[Y_COEF:] = sums[rows]
        else:
            out_b[Y_COEF:] = sums[rows]


def loose_slots(ny):
    ridden = (0, 1, 3) if ny == 4 else (0, 1)
    return [s for s in range(ny) if slot_xor(ny, s) not in ridden]


def pack_home(sums, got_a, got_b, *rest):
    others = rest[:-3]
    out_a, out_b, out_sum = rest[-3:]
    owned = sums.shape[0] // 3
    even, _, _ = place_on("gx")
    total = sums[...] + got_a[Y_COEF:]
    if got_b.shape[0] > Y_COEF:
        total = total + got_b[Y_COEF:]
    for other in others:
        total = total + other[...]
    put_pair(out_a, out_b, even, 0, total[2 * owned :], total[0:owned])
    out_sum[...] = total[owned : 2 * owned]
    at = owned
    for c in range(NC):
        for away, start, width in WIDE:
            if width:
                first = c * WIDE_ROWS + start
                west = y_sides(got_a, got_b, pl.ds(first, width))
                east = y_sides(got_a, got_b, pl.ds(first + width + CX, width))
                for side in range(2):
                    put_pair(out_a, out_b, even, at, east[side], west[side])
                    at += width


def finish(alpha, near, own_sum, y_a, y_b, bulk_a, bulk_b, small_a, small_b, out_delta, out_alpha):
    owned = own_sum.shape[0]
    wide = RIM * CY
    out_delta[...] = near[...]
    at = owned
    for c in range(NC):
        west, east = x_sides(bulk_a, bulk_b, pl.ds(c * wide, wide))
        out_delta[c, 0:wide] += west
        out_delta[c, CX * CY - wide :] += east
        for away, start, width in WIDE:
            north, south = y_sides(y_a, y_b, pl.ds(c * WIDE_ROWS + start + width, CX))
            high = pl.ds(CY - away, CX, stride=CY)
            low = pl.ds(away - 1, CX, stride=CY)
            out_delta[c, high] = out_delta[c, high] + north
            out_delta[c, low] = out_delta[c, low] + south
            for y in (CY - away, away - 1):
                for i in range(width):
                    west, east = x_sides(small_a, small_b, slice(at + i, at + i + 1))
                    out_delta[c, pl.ds(i * CY + y, 1)] += west
                    out_delta[c, pl.ds((CX - width + i) * CY + y, 1)] += east
                at += width
    west, east = x_sides(small_a, small_b, slice(0, owned))
    out_alpha[...] = alpha[...] + profile_weight * (own_sum[...] + west + east)


def on_device(
    delta,
    alpha,
    eddy,
    courant,
    tile_map,
    obs_rows,
    gate_beam,
    gate_index,
    gate_column,
    gate_live,
    obs_weight,
    obs_precision,
):
    nx = lax.axis_size("gx")
    ny = lax.axis_size("gy")
    owned = alpha.shape[1]
    slots = gate_column.shape[2]
    gates = [
        value.reshape(1, slots)
        for value in (gate_beam, gate_index, gate_column, gate_live, obs_precision)
    ]
    control = alpha.reshape(owned * NC, 128)
    weights = obs_weight.reshape(slots * NC, 128)
    rows = owned * NC
    per_slot = 3 * rows
    total = 3 * ny * owned
    beam_at = small_places(rows)[-1]
    tile = (NC, CX * CY, 128)

    small_a, small_b, bulk_a, bulk_b, fine, coefs, control, tiles, meta, beams = call(
        pack_x,
        [
            (beam_at + BEAM_ROWS, 128),
            (beam_at, 128),
            (BULK, 128),
            (BULK, 128),
            tile,
            (3, CX * CY, 128),
            (rows, 128),
            (CX, 128),
            (8, slots),
            (BEAM_ROWS, 128),
        ],
        [
            pltpu.with_memory_space_constraint(value, pltpu.HBM)
            for value in (
                delta.reshape(tile),
                eddy.reshape(CX * CY, 128),
                courant.reshape(2, CX * CY, 128),
                control,
                tile_map,
                *gates,
                jnp.transpose(obs_rows, (1, 0, 2)).reshape(BEAM_ROWS, 128),
            )
        ],
        [
            pltpu.VMEM(tile_map.shape, jnp.int32),
            pltpu.VMEM((4, 1, slots), jnp.int32),
            pltpu.VMEM((1, slots), f32),
            pltpu.SemaphoreType.DMA((12,)),
        ],
        in_specs=[HBM] * 11,
    )
    small_a = swap(small_a, "gx", 1)
    small_b = pair_b(small_b, "gx", "gy")
    bulk_a = swap(bulk_a, "gx", 1)
    bulk_b = pair_b(bulk_b, "gx", "gy")

    y_a, y_b, profiles, near_tiles, beams = call(
        pack_y,
        [
            (Y_HALO + per_slot, 128),
            (Y_HALO, 128),
            (per_slot, 128),
            (BLOCKS, 128),
            (2 * BEAM_ROWS, 128),
        ],
        [fine, coefs, control, tiles, beams, small_a, small_b],
    )
    others, xor = [], 2
    while xor < ny:
        held = jnp.concatenate([profiles] + others) if others else profiles
        others.append(swap(held, "gy", xor))
        xor *= 2
    y_a = swap(y_a, "gy", 1)
    y_b = pair_b(y_b, "gy", "gx")
    others.append(swap(jnp.concatenate(others) if len(others) > 1 else others[0], "gy", 1))
    beams = [beams]
    xor = 2
    while xor < nx:
        held = jnp.concatenate(beams) if len(beams) > 1 else beams[0]
        beams.append(swap(held, "gx", xor))
        xor *= 2

    field, coef, picks, wide, slot_pick, slot_push, beam_pick, columns = call(
        lambda *refs: prepare(ny, len(others), *refs),
        [
            (NC * FIELD, 128),
            (5 * FIELD, 128),
            (FIELD, total),
            (slots, NC * 128),
            jax.ShapeDtypeStruct((slots, CX * CY), bf16),
            jax.ShapeDtypeStruct((CX * CY, slots), bf16),
            jax.ShapeDtypeStruct((slots, nx * OWN_BEAMS), bf16),
            (slots, 8),
        ],
        [fine, coefs, near_tiles, meta, weights, y_a, y_b, profiles, *others],
        [pltpu.VMEM((total * NC, 128), f32), pltpu.VMEM((128, 128), f32)],
        flops=3000000,
    )
    tops, lows, coef = call(
        forecast,
        [
            jax.ShapeDtypeStruct((STEPS * CX * CY, NC * 128), bf16),
            jax.ShapeDtypeStruct((STEPS * CX * CY, NC * 128), bf16),
            (5 * FIELD, 128),
        ],
        [field, coef, bulk_a, bulk_b],
        [pltpu.VMEM((NC * FIELD, 128), f32), pltpu.VMEM((NC * FIELD, 128), f32)],
        flops=10000000,
    )
    loose = loose_slots(ny)
    back_a, back_b, bulk_a, bulk_b, near, sums, *back = call(
        lambda *refs: main(ny, len(beams), *refs),
        [
            (Y_COEF + per_slot, 128),
            (Y_COEF + (per_slot if ny == 4 else 0), 128),
            (BULK_COEF, 128),
            (BULK_COEF, 128),
            tile,
            (per_slot, 128),
        ]
        + [(per_slot, 128)] * len(loose),
        [
            coef,
            tops,
            lows,
            wide,
            slot_pick,
            slot_push,
            beam_pick,
            columns,
            picks,
            fine,
            *beams,
        ],
        [
            pltpu.VMEM((NC * FIELD, 128), f32),
            pltpu.VMEM((NC * FIELD, 128), f32),
            pltpu.VMEM((STEPS * CX * CY, NC * 128), f32),
            pltpu.VMEM((total * NC, 128), f32),
        ],
        flops=20000000,
    )
    y_a = swap(back_a, "gy", 1)
    y_b = ring_b(back_b, "gy")
    others = [swap(value, "gy", slot_xor(ny, s)) for s, value in zip(loose, back)]
    bulk_a = swap(bulk_a, "gx", 1)
    bulk_b = pair_b(bulk_b, "gx", "gy")
    home_rows = rows + 2 * NC * CORNER
    small_a, small_b, own_sum = call(
        pack_home,
        [(home_rows, 128), (home_rows, 128), (rows, 128)],
        [sums, y_a, y_b, *others],
    )
    small_a = swap(small_a, "gx", 1)
    small_b = pair_b(small_b, "gx", "gy")
    grad_delta, grad_alpha = call(
        finish,
        [tile, (rows, 128)],
        [control, near, own_sum, y_a, y_b, bulk_a, bulk_b, small_a, small_b],
    )
    return grad_delta.reshape(delta.shape), grad_alpha.reshape(alpha.shape)


def solution(mesh):
    return jax.shard_map(
        on_device,
        mesh=mesh,
        in_specs=(
            P(None, "gx", "gy", None),
            P("gx", "gy", None, None),
            P("gx", "gy", None),
            P(None, "gx", "gy", None),
            P("gx", "gy"),
            P(("gx", "gy"), None, None),
            P("gx", "gy", None),
            P("gx", "gy", None),
            P("gx", "gy", None),
            P("gx", "gy", None),
            P("gx", "gy", None, None, None),
            P("gx", "gy", None),
        ),
        out_specs=(P(None, "gx", "gy", None), P("gx", "gy", None, None)),
        check_vma=False,
    )
```

```python
import jax
import jax.numpy as jnp
from jax import lax
from jax.experimental import pallas as pl
from jax.experimental.pallas import tpu as pltpu
from jax.sharding import PartitionSpec as P

STEPS = 3
RIM = 3
INNER = RIM - 1
NC = 4
CX = 16
CY = 16
BLOCKS = CX + 8
PITCH = CY + 8
FIRST = 4
FIELD = BLOCKS * PITCH
OWN_BEAMS = 8
BEAM_BITS = 3
BEAM_ROWS = STEPS * OWN_BEAMS

BULK_COEF = NC * RIM * CY
BULK = BULK_COEF + 3 * INNER * CY

profile_weight = 0.125
f32 = jnp.float32
bf16 = jnp.bfloat16

VMEM = pl.BlockSpec(memory_space=pltpu.VMEM)
HBM = pl.BlockSpec(memory_space=pltpu.HBM)


def call(body, outs, ins, scratch=(), in_specs=None, flops=1000000, limit=40 * 2**20):
    shapes = [
        out if isinstance(out, jax.ShapeDtypeStruct) else jax.ShapeDtypeStruct(out, f32)
        for out in outs
    ]
    size = sum(4 * value.size for value in ins)
    return pl.pallas_call(
        body,
        out_shape=shapes,
        in_specs=in_specs or [VMEM] * len(ins),
        out_specs=[VMEM] * len(shapes),
        scratch_shapes=list(scratch),
        compiler_params=pltpu.CompilerParams(vmem_limit_bytes=limit),
        cost_estimate=pl.CostEstimate(flops=flops, bytes_accessed=size, transcendentals=0),
    )(*ins)


def swap(block, axis, xor):
    return lax.ppermute(block, axis, [(i, i ^ xor) for i in range(lax.axis_size(axis))])


def pair_b(block, axis, other):
    count, across = lax.axis_size(axis), lax.axis_size(other)

    def place(i, j):
        return i * across + j if axis == "gx" else j * count + i

    pairs = []
    for j in range(across):
        for i in range(count):
            if i in (0, count - 1):
                pairs.append((place(i, j), place(i, j ^ 1)))
            else:
                pairs.append((place(i, j), place(i + 1 if i % 2 else i - 1, j)))
    return lax.ppermute(block, ("gx", "gy"), pairs)


def ring_b(block, axis):
    count = lax.axis_size(axis)
    pairs = [(i, (i + 1 if i % 2 else i - 1) % count) for i in range(count)]
    return lax.ppermute(block, axis, pairs)


def place_on(axis):
    me = lax.axis_index(axis)
    return lax.rem(me, 2) == 0, me > 0, me < lax.axis_size(axis) - 1


def split(value):
    top = value.astype(bf16)
    return top, (value - top.astype(f32)).astype(bf16)


def two_part_dot(left, value):
    top, low = split(value)
    return jnp.dot(left, top, preferred_element_type=f32) + jnp.dot(
        left, low, preferred_element_type=f32
    )


def layers(reach):
    found, at = [], 0
    for away in range(1, reach + 1):
        found.append((away, at, reach - away))
        at += CX + 2 * (reach - away)
    return found, at


WIDE, WIDE_ROWS = layers(RIM)
BACK = NC * WIDE_ROWS
CORNER = sum(extra for _, _, extra in WIDE)

Y_COEF = NC * RIM * CX
Y_TILE = Y_COEF + 3 * INNER * CX
Y_HALO = Y_TILE + CX


def corners(reach):
    return [
        (dx, side, dy)
        for dx in range(1, reach)
        for side in range(2)
        for dy in range(1, reach - dx + 1)
    ]


def small_places(profile_rows):
    corner = profile_rows + RIM
    coef_corner = corner + NC * len(corners(RIM))
    return profile_rows, corner, coef_corner, coef_corner + 3 * len(corners(INNER))


def y_sides(got_a, got_b, rows, fill=0.0):
    even, low, high = place_on("gy")
    first, second = got_a[rows], got_b[rows]
    north, south = jnp.where(even, first, second), jnp.where(even, second, first)
    return jnp.where(high, north, fill), jnp.where(low, south, fill)


def x_sides(got_a, got_b, rows, fill=0.0):
    even, low, high = place_on("gx")
    first, second = got_a[rows], got_b[rows]
    west, east = jnp.where(even, second, first), jnp.where(even, first, second)
    return jnp.where(low, west, fill), jnp.where(high, east, fill)


def put_pair(out_a, out_b, even, at, above, below):
    rows = slice(at, at + above.shape[0])
    out_a[rows] = jnp.where(even, above, below)
    out_b[rows] = jnp.where(even, below, above)


def pack_first(
    delta,
    eddy,
    courant,
    alpha,
    tile_map,
    gate_beam,
    gate_index,
    gate_column,
    gate_live,
    precision,
    beam_rows,
    y_a,
    y_b,
    bulk_a,
    bulk_b,
    fine,
    coefs,
    profiles,
    near_tiles,
    meta,
    beams,
    tiles,
    gates,
    values,
    sems,
):
    even_x, _, _ = place_on("gx")
    even, _, _ = place_on("gy")
    moves = [
        pltpu.make_async_copy(source, target, sems.at[i])
        for i, (source, target) in enumerate(
            [
                (delta, fine),
                (eddy, coefs.at[0]),
                (courant.at[0], coefs.at[1]),
                (courant.at[1], coefs.at[2]),
                (tile_map, tiles),
                (alpha, profiles),
                (gate_beam, gates.at[0]),
                (gate_index, gates.at[1]),
                (gate_column, gates.at[2]),
                (gate_live, gates.at[3]),
                (precision, values),
                (beam_rows, beams),
            ]
        )
    ]
    for move in moves:
        move.start()
    for move in moves:
        move.wait()

    near_tiles[...] = jnp.full((CX, 128), -1.0, f32)
    near_tiles[:, 0:CY] = tiles[...].astype(f32)

    def edges(at, field, reach):
        for away in range(1, reach + 1):
            north = field[pl.ds(CY - away, CX, stride=CY)]
            south = field[pl.ds(away - 1, CX, stride=CY)]
            put_pair(y_a, y_b, even, at + (away - 1) * CX, north, south)

    for c in range(NC):
        edges(c * RIM * CX, fine.at[c], RIM)
    for f in range(3):
        edges(Y_COEF + f * INNER * CX, coefs.at[f], INNER)
    y_a[Y_TILE:Y_HALO] = near_tiles[...]
    y_b[Y_TILE:Y_HALO] = near_tiles[...]
    y_a[Y_HALO:] = profiles[...]

    wide, slim = RIM * CY, INNER * CY
    for c in range(NC):
        put_pair(bulk_a, bulk_b, even_x, c * wide, fine[c, CX * CY - wide :], fine[c, :wide])
    for f in range(3):
        east, west = coefs[f, CX * CY - slim :], coefs[f, :slim]
        put_pair(bulk_a, bulk_b, even_x, BULK_COEF + f * slim, east, west)

    beam = gates[0]
    owner = jnp.bitwise_xor(beam >> BEAM_BITS, lax.axis_index("gx"))
    half = lax.axis_size("gx") // 2
    block = (owner >> 1) + (owner & 1) * half
    meta[...] = jnp.zeros(meta.shape, f32)
    meta[0:1] = gates[2].astype(f32)
    meta[1:2] = ((block << BEAM_BITS) | (beam & (OWN_BEAMS - 1))).astype(f32)
    meta[2:3] = gates[1].astype(f32)
    meta[3:4] = gates[3].astype(f32) * values[...]


def tile_numbers(near_tiles, y_a, y_b):
    spot = lax.broadcasted_iota(jnp.int32, (CX, 128), 1)
    north, south = y_sides(y_a, y_b, pl.ds(Y_TILE, CX), -1.0)
    near = jnp.where(
        (spot >= CY) & (spot < CY + RIM),
        pltpu.roll(north, CY, 1),
        jnp.where((spot >= PITCH - RIM) & (spot < PITCH), pltpu.roll(south, PITCH - CY, 1), -1.0),
    )
    return jnp.where(spot < CY, near_tiles[...], near)


def strip_profiles(ny, control, y_a, others):
    return [control[...]] + [o[...] for o in others[:-1]] + [y_a[Y_HALO:], others[-1][...]]


def pack_small(ny, control, near_tiles, y_a, y_b, beams, *rest):
    others = rest[:-3]
    out_a, out_b, numbers = rest[-3:]
    even, _, _ = place_on("gx")
    rows = ny * control.shape[0]
    tile, corner, coef_corner, beam = small_places(rows)
    at = 0
    for piece in strip_profiles(ny, control, y_a, others):
        out_a[at : at + piece.shape[0]] = piece
        out_b[at : at + piece.shape[0]] = piece
        at += piece.shape[0]
    numbers[...] = tile_numbers(near_tiles, y_a, y_b)
    put_pair(out_a, out_b, even, tile, numbers[CX - RIM :], numbers[:RIM])

    def put_corners(at, base, reach):
        for dx, side, dy in corners(reach):
            first = base + (dy - 1) * CX
            east = y_sides(y_a, y_b, pl.ds(first + CX - dx, 1))[side]
            west = y_sides(y_a, y_b, pl.ds(first + dx - 1, 1))[side]
            put_pair(out_a, out_b, even, at, east, west)
            at += 1
        return at

    at = corner
    for c in range(NC):
        at = put_corners(at, c * RIM * CX, RIM)
    for f in range(3):
        at = put_corners(at, Y_COEF + f * INNER * CX, INNER)
    out_a[beam:] = beams[...]


def slot_xor(ny, slot):
    half = ny // 2
    return 2 * slot if slot < half else 2 * (slot - half) + 1


def tile_ids(ny, owned):
    me = lax.axis_index("gy")
    group = 3 * owned
    lane = lax.broadcasted_iota(jnp.int32, (1, ny * group), 1)
    found = []
    for strip in range(3):
        ids = jnp.full((1, ny * group), -2, jnp.int32)
        for s in range(ny):
            base = s * group + strip * owned
            here = (lane >= base) & (lane < base + owned)
            ids = jnp.where(
                here, jnp.bitwise_xor(me, slot_xor(ny, s)) * owned + lane - base, ids
            )
        found.append(ids.astype(f32))
    return found


def by_variable(ref, count):
    return jnp.concatenate([ref[pl.ds(c, count, stride=NC)] for c in range(NC)], axis=1)


def combine_coefs(viscous, along_x, along_y):
    half_x, half_y = 0.5 * along_x, 0.5 * along_y
    return (
        1.0 - 4.0 * viscous,
        viscous - half_x,
        viscous + half_x,
        viscous - half_y,
        viscous + half_y,
    )


def clear(ref, base, blocks):
    for b in blocks:
        at = base + b * PITCH
        ref[at : at + PITCH] = jnp.zeros((PITCH, 128), f32)


def add_profiles(known, picks, pieces_by_strip, place):
    known[...] = jnp.zeros(known.shape, f32)
    for strip, pieces, rows in pieces_by_strip:
        slot = 0
        for piece in pieces:
            for first in range(0, piece.shape[0], rows):
                at = (slot * 3 + strip) * rows
                known[at : at + rows] = piece[first : first + rows]
                slot += 1
    control = two_part_dot(picks[...].astype(bf16), by_variable(known, picks.shape[1]))
    for c in range(NC):
        place(c, profile_weight * control[:, c * 128 : (c + 1) * 128])


def prepare(
    ny,
    parts,
    fine,
    coefs,
    near_tiles,
    meta,
    weights,
    y_a,
    y_b,
    bulk_a,
    bulk_b,
    control,
    *rest,
):
    others = rest[:parts]
    field, coef, picks, wide, slot_pick, slot_push, beam_pick, columns, known, tiles = rest[parts:]
    total = picks.shape[1]
    rows = control.shape[0]
    owned = rows // NC

    def fill(ref, base, own, y_base, reach, bulk_base):
        for x in range(CX):
            at = base + (FIRST + x) * PITCH
            ref[at : at + CY] = own[x * CY : (x + 1) * CY]
            ref[at + CY : at + PITCH] = jnp.zeros((PITCH - CY, 128), f32)
        for away in range(1, reach + 1):
            north, south = y_sides(y_a, y_b, pl.ds(y_base + (away - 1) * CX, CX))
            at = base + FIRST * PITCH
            ref[pl.ds(at + CY - 1 + away, CX, stride=PITCH)] = north
            ref[pl.ds(at + PITCH - away, CX, stride=PITCH)] = south
        clear(ref, base, [*range(FIRST), *range(FIRST + CX, BLOCKS)])
        for h in range(reach):
            west, east = x_sides(bulk_a, bulk_b, pl.ds(bulk_base + h * CY, CY))
            at = base + (FIRST - reach + h) * PITCH
            ref[at : at + CY] = west
            at = base + (FIRST + CX + h) * PITCH
            ref[at : at + CY] = east

    for f in range(3):
        bulk_base = BULK_COEF + f * INNER * CY
        fill(coef, f * FIELD, coefs.at[f], Y_COEF + f * INNER * CX, INNER, bulk_base)
    for f in range(3, 5):
        clear(coef, f * FIELD, [*range(FIRST), *range(FIRST + CX, BLOCKS)])

    def combine(b, carry):
        at = pl.multiple_of(b * PITCH, 8)
        combined = combine_coefs(*[coef[pl.ds(f * FIELD + at, PITCH)] for f in range(3)])
        for f, value in enumerate(combined):
            coef[pl.ds(f * FIELD + at, PITCH)] = value
        return carry

    lax.fori_loop(FIRST, FIRST + CX, combine, 0)

    tiles[...] = jnp.full(tiles.shape, -1.0, f32)
    tiles[0:CX] = tile_numbers(near_tiles, y_a, y_b)
    turned = jnp.transpose(tiles[...])[0:PITCH]
    ids = tile_ids(ny, owned)
    for x in range(CX):
        picks[x * PITCH : (x + 1) * PITCH] = (turned[:, x : x + 1] == ids[1]).astype(f32)
    for c in range(NC):
        fill(field, c * FIELD, fine.at[c], c * RIM * CX, RIM, c * RIM * CY)

    def place(c, value):
        at = c * FIELD + FIRST * PITCH
        field[at : at + CX * PITCH] += value

    add_profiles(known, picks, [(1, strip_profiles(ny, control, y_a, others), rows)], place)

    slots = meta.shape[1]
    for c in range(NC):
        wide[:, c * 128 : (c + 1) * 128] = weights[pl.ds(c, slots, stride=NC)]
    per_beam = beam_pick.shape[1]
    turned = jnp.transpose(meta[...])
    columns[...] = turned
    slot_lane = lax.broadcasted_iota(jnp.int32, (slots, CX * CY), 1).astype(f32)
    slot_pick[...] = (slot_lane == turned[:, 0:1]).astype(f32).astype(bf16)
    column_row = lax.broadcasted_iota(jnp.int32, (CX * CY, slots), 0).astype(f32)
    slot_push[...] = (column_row == meta[0:1]).astype(f32).astype(bf16)
    beam_lane = lax.broadcasted_iota(jnp.int32, (slots, per_beam), 1).astype(f32)
    beam_pick[...] = (beam_lane == turned[:, 1:2]).astype(f32).astype(bf16)


def forecast(
    ny,
    rows,
    field,
    near_coef,
    small_a,
    small_b,
    tops,
    lows,
    coef,
    picks,
    state_0,
    state_1,
    known,
    tiles,
):
    strip_rows = ny * rows
    tile, corner, coef_corner, _ = small_places(strip_rows)

    def put_corners(ref, base, reach, small_base):
        for i, (dx, side, dy) in enumerate(corners(reach)):
            west, east = x_sides(small_a, small_b, pl.ds(small_base + i, 1))
            row = CY - 1 + dy if side == 0 else PITCH - dy
            at = base + (FIRST - dx) * PITCH + row
            ref[at : at + 1] = west
            at = base + (FIRST + CX - 1 + dx) * PITCH + row
            ref[at : at + 1] = east

    for c in range(NC):
        part = slice(c * FIELD + PITCH, (c + 1) * FIELD - PITCH)
        state_0[part] = field[part]
        base = c * len(corners(RIM))
        put_corners(state_0, c * FIELD, RIM, corner + base)
    coef[...] = near_coef[...]
    for f in range(3):
        base = f * len(corners(INNER))
        put_corners(coef, f * FIELD, INNER, coef_corner + base)
    for b in (FIRST - 2, FIRST - 1, FIRST + CX, FIRST + CX + 1):
        at = [slice(f * FIELD + b * PITCH, f * FIELD + (b + 1) * PITCH) for f in range(5)]
        for f, value in enumerate(combine_coefs(*[coef[at[f]] for f in range(3)])):
            coef[at[f]] = value

    west, east = x_sides(small_a, small_b, slice(tile, tile + RIM), -1.0)
    tiles[...] = jnp.full(tiles.shape, -1.0, f32)
    tiles[0:RIM] = west
    tiles[RIM : 2 * RIM] = east
    turned = jnp.transpose(tiles[...])[0:PITCH]
    ids = tile_ids(ny, rows // NC)
    for i in range(2 * RIM):
        here = turned[:, i : i + 1] == ids[0 if i < RIM else 2]
        picks[i * PITCH : (i + 1) * PITCH] = here.astype(f32)

    def place(c, value):
        at = c * FIELD + (FIRST - RIM) * PITCH
        state_0[at : at + RIM * PITCH] += value[: RIM * PITCH]
        at = c * FIELD + (FIRST + CX) * PITCH
        state_0[at : at + RIM * PITCH] += value[RIM * PITCH :]

    west, east = x_sides(small_a, small_b, slice(0, strip_rows))
    add_profiles(known, picks, [(0, [west], rows), (2, [east], rows)], place)

    def forward(source, target, low, high):
        def body(b, carry):
            at = pl.multiple_of(b * PITCH, 8)
            k = [coef[pl.ds(f * FIELD + at, PITCH)] for f in range(5)]
            for c in range(NC):
                base = c * FIELD + at
                here = source[pl.ds(base, PITCH)]
                target[pl.ds(base, PITCH)] = (
                    k[0] * here
                    + k[1] * source[pl.ds(base + PITCH, PITCH)]
                    + k[2] * source[pl.ds(base - PITCH, PITCH)]
                    + k[3] * pltpu.roll(here, PITCH - 1, 0)
                    + k[4] * pltpu.roll(here, 1, 0)
                )
            return carry

        lax.fori_loop(low, high, body, 0)

    buffers = [state_0, state_1]
    for step in range(STEPS):
        source, target = buffers[step % 2], buffers[(step + 1) % 2]
        forward(source, target, 2 + step, BLOCKS - 2 - step)
        own = jnp.concatenate(
            [
                jnp.concatenate(
                    [
                        target[c * FIELD + b * PITCH : c * FIELD + b * PITCH + CY]
                        for b in range(FIRST, FIRST + CX)
                    ],
                    axis=0,
                )
                for c in range(NC)
            ],
            axis=1,
        )
        rows = slice(step * CX * CY, (step + 1) * CX * CY)
        tops[rows], lows[rows] = split(own)


def main(
    ny,
    parts,
    coef,
    tops,
    lows,
    wide,
    slot_pick,
    slot_push,
    beam_pick,
    columns,
    *rest,
):
    picks, rim_picks, *beams = rest[: 2 + parts]
    out_a, out_b, final, out_sums, *out_others = rest[2 + parts : -3]
    state_0, forcing, sums = rest[-3:]
    state_1 = final
    even, _, _ = place_on("gy")
    total = picks.shape[1]
    per_slot = total * NC // ny
    slots = columns.shape[0]
    gate_lane = lax.broadcasted_iota(jnp.int32, (slots, 128), 1).astype(f32)
    gate_here = gate_lane == columns[:, 2:3]
    scaled = columns[:, 3:4]
    for step in range(STEPS):
        rows = slice(step * CX * CY, (step + 1) * CX * CY)
        picked = jnp.dot(slot_pick[...], tops[rows], preferred_element_type=f32)
        picked = picked + jnp.dot(slot_pick[...], lows[rows], preferred_element_type=f32)
        picked = picked * wide[...]
        table = []
        for part in beams:
            for at in range(0, part.shape[0], STEPS * OWN_BEAMS):
                first = at + step * OWN_BEAMS
                table.append(part[first : first + OWN_BEAMS])
        table = two_part_dot(beam_pick[...], jnp.concatenate(table, axis=0))
        tally = -jnp.where(gate_here, table, 0.0)
        for c in range(NC):
            tally = tally + picked[:, c * 128 : (c + 1) * 128]
        misfit = scaled * jnp.sum(tally, axis=1, keepdims=True)
        forcing[rows] = two_part_dot(slot_push[...], misfit * wide[...])

    buffers = [state_0, state_1]

    for c in range(NC):
        clear(state_0, c * FIELD, [0, 1, 2, 3, BLOCKS - 4, BLOCKS - 3, BLOCKS - 2, BLOCKS - 1])
        clear(state_1, c * FIELD, [1, 2, BLOCKS - 3, BLOCKS - 2])

    def add_forcing(ref, step):
        for c in range(NC):
            for x in range(CX):
                at = c * FIELD + (FIRST + x) * PITCH
                first = step * CX * CY + x * CY
                value = forcing[first : first + CY, c * 128 : (c + 1) * 128]
                if step == STEPS - 1:
                    ref[at : at + CY] = value
                    ref[at + CY : at + PITCH] = jnp.zeros((PITCH - CY, 128), f32)
                else:
                    ref[at : at + CY] += value

    def backward(source, target, low, high):
        def body(b, carry):
            at = pl.multiple_of(b * PITCH, 8)
            k = [
                coef[pl.ds(at, PITCH)],
                coef[pl.ds(FIELD + at - PITCH, PITCH)],
                coef[pl.ds(2 * FIELD + at + PITCH, PITCH)],
                coef[pl.ds(3 * FIELD + at, PITCH)],
                coef[pl.ds(4 * FIELD + at, PITCH)],
            ]
            for c in range(NC):
                base = c * FIELD + at
                here = source[pl.ds(base, PITCH)]
                target[pl.ds(base, PITCH)] = (
                    k[0] * here
                    + k[1] * source[pl.ds(base - PITCH, PITCH)]
                    + k[2] * source[pl.ds(base + PITCH, PITCH)]
                    + pltpu.roll(k[3] * here, 1, 0)
                    + pltpu.roll(k[4] * here, PITCH - 1, 0)
                )
            return carry

        lax.fori_loop(low, high, body, 0)

    for step in range(STEPS):
        source, target = buffers[step % 2], buffers[(step + 1) % 2]
        add_forcing(source, STEPS - 1 - step)
        backward(source, target, FIRST - 1 - step, FIRST + CX + 1 + step)
    for c in range(NC):
        for away, start, width in WIDE:
            at = c * FIELD + (FIRST - width) * PITCH
            size = CX + 2 * width
            north = final[pl.ds(at + CY - 1 + away, size, stride=PITCH)]
            south = final[pl.ds(at + PITCH - away, size, stride=PITCH)]
            put_pair(out_a, out_b, even, c * WIDE_ROWS + start, north, south)

    def blocks(low, high):
        return jnp.concatenate(
            [final[c * FIELD + low * PITCH : c * FIELD + high * PITCH] for c in range(NC)], axis=1
        )

    def across(one_hot):
        return jnp.transpose(one_hot[...]).astype(bf16)

    rim = jnp.concatenate(
        [blocks(FIRST - RIM, FIRST), blocks(FIRST + CX, FIRST + CX + RIM)], axis=0
    )
    tile_sums = two_part_dot(across(picks), blocks(FIRST, FIRST + CX))
    tile_sums = tile_sums + two_part_dot(across(rim_picks), rim)
    for c in range(NC):
        sums[pl.ds(c, total, stride=NC)] = tile_sums[:, c * 128 : (c + 1) * 128]
    out_sums[...] = sums[0:per_slot]
    outs = dict(zip(loose_slots(ny), out_others))
    for s in range(1, ny):
        rows = slice(s * per_slot, (s + 1) * per_slot)
        if s in outs:
            outs[s][...] = sums[rows]
        elif slot_xor(ny, s) == 1:
            out_a[BACK:] = sums[rows]
        else:
            out_b[BACK:] = sums[rows]


def loose_slots(ny):
    ridden = (0, 1, 3) if ny == 4 else (0, 1)
    return [s for s in range(ny) if slot_xor(ny, s) not in ridden]


def pack_bulk(fine, final, bulk_a, bulk_b, near):
    even, _, _ = place_on("gx")
    for c in range(NC):
        for h in range(RIM):
            at = c * FIELD + (FIRST - RIM + h) * PITCH
            west = final[at : at + CY]
            at = c * FIELD + (FIRST + CX + h) * PITCH
            put_pair(bulk_a, bulk_b, even, (c * RIM + h) * CY, final[at : at + CY], west)
        for x in range(CX):
            at = c * FIELD + (FIRST + x) * PITCH
            rows = slice(x * CY, (x + 1) * CY)
            near[c, rows] = fine[c, rows] + final[at : at + CY]


def pack_home(sums, got_a, got_b, *rest):
    others = rest[:-3]
    out_a, out_b, out_sum = rest[-3:]
    owned = sums.shape[0] // 3
    even, _, _ = place_on("gx")
    total = sums[...] + got_a[BACK:]
    if got_b.shape[0] > BACK:
        total = total + got_b[BACK:]
    for other in others:
        total = total + other[...]
    put_pair(out_a, out_b, even, 0, total[2 * owned :], total[0:owned])
    out_sum[...] = total[owned : 2 * owned]
    at = owned
    for c in range(NC):
        for away, start, width in WIDE:
            if width:
                first = c * WIDE_ROWS + start
                west = y_sides(got_a, got_b, pl.ds(first, width))
                east = y_sides(got_a, got_b, pl.ds(first + width + CX, width))
                for side in range(2):
                    put_pair(out_a, out_b, even, at, east[side], west[side])
                    at += width


def finish(alpha, near, own_sum, y_a, y_b, bulk_a, bulk_b, small_a, small_b, out_delta, out_alpha):
    owned = own_sum.shape[0]
    wide = RIM * CY
    out_delta[...] = near[...]
    at = owned
    for c in range(NC):
        west, east = x_sides(bulk_a, bulk_b, pl.ds(c * wide, wide))
        out_delta[c, 0:wide] += west
        out_delta[c, CX * CY - wide :] += east
        for away, start, width in WIDE:
            north, south = y_sides(y_a, y_b, pl.ds(c * WIDE_ROWS + start + width, CX))
            high = pl.ds(CY - away, CX, stride=CY)
            low = pl.ds(away - 1, CX, stride=CY)
            out_delta[c, high] = out_delta[c, high] + north
            out_delta[c, low] = out_delta[c, low] + south
            for y in (CY - away, away - 1):
                for i in range(width):
                    west, east = x_sides(small_a, small_b, slice(at + i, at + i + 1))
                    out_delta[c, pl.ds(i * CY + y, 1)] += west
                    out_delta[c, pl.ds((CX - width + i) * CY + y, 1)] += east
                at += width
    west, east = x_sides(small_a, small_b, slice(0, owned))
    out_alpha[...] = alpha[...] + profile_weight * (own_sum[...] + west + east)


def on_device(
    delta,
    alpha,
    eddy,
    courant,
    tile_map,
    obs_rows,
    gate_beam,
    gate_index,
    gate_column,
    gate_live,
    obs_weight,
    obs_precision,
):
    nx = lax.axis_size("gx")
    ny = lax.axis_size("gy")
    owned = alpha.shape[1]
    slots = gate_column.shape[2]
    gates = [
        value.reshape(1, slots)
        for value in (gate_beam, gate_index, gate_column, gate_live, obs_precision)
    ]
    control = alpha.reshape(owned * NC, 128)
    weights = obs_weight.reshape(slots * NC, 128)
    rows = owned * NC
    per_slot = 3 * rows
    total = 3 * ny * owned
    beam_at = small_places(ny * rows)[-1]
    tile = (NC, CX * CY, 128)
    own_beams = jnp.transpose(obs_rows, (1, 0, 2)).reshape(BEAM_ROWS, 128)

    y_a, y_b, bulk_a, bulk_b, fine, coefs, near_control, near_tiles, meta, near_beams = call(
        pack_first,
        [
            (Y_HALO + rows, 128),
            (Y_HALO, 128),
            (BULK, 128),
            (BULK, 128),
            tile,
            (3, CX * CY, 128),
            (rows, 128),
            (CX, 128),
            (8, slots),
            (BEAM_ROWS, 128),
        ],
        [
            pltpu.with_memory_space_constraint(value, pltpu.HBM)
            for value in (
                delta.reshape(tile),
                eddy.reshape(CX * CY, 128),
                courant.reshape(2, CX * CY, 128),
                control,
                tile_map,
                *gates,
                own_beams,
            )
        ],
        [
            pltpu.VMEM(tile_map.shape, jnp.int32),
            pltpu.VMEM((4, 1, slots), jnp.int32),
            pltpu.VMEM((1, slots), f32),
            pltpu.SemaphoreType.DMA((12,)),
        ],
        in_specs=[HBM] * 11,
    )
    y_a = swap(y_a, "gy", 1)
    y_b = pair_b(y_b, "gy", "gx")
    bulk_a = swap(bulk_a, "gx", 1)
    bulk_b = pair_b(bulk_b, "gx", "gy")
    got_beams, xor = own_beams, 2
    while xor < nx:
        got_beams = jnp.concatenate([got_beams, swap(got_beams, "gx", xor)])
        xor *= 2
    others, xor = [], 2
    while xor < ny:
        held = jnp.concatenate([control] + others) if others else control
        others.append(swap(held, "gy", xor))
        xor *= 2
    others.append(swap(jnp.concatenate(others) if len(others) > 1 else others[0], "gy", 1))

    small_a, small_b = call(
        lambda *refs: pack_small(ny, *refs),
        [(beam_at + got_beams.shape[0], 128), (beam_at, 128)],
        [near_control, near_tiles, y_a, y_b, got_beams, *others],
        [pltpu.VMEM((CX, 128), f32)],
    )
    small_a = swap(small_a, "gx", 1)
    small_b = pair_b(small_b, "gx", "gy")

    field, coef, picks, wide, slot_pick, slot_push, beam_pick, columns = call(
        lambda *refs: prepare(ny, len(others), *refs),
        [
            (NC * FIELD, 128),
            (5 * FIELD, 128),
            (CX * PITCH, total),
            (slots, NC * 128),
            jax.ShapeDtypeStruct((slots, CX * CY), bf16),
            jax.ShapeDtypeStruct((CX * CY, slots), bf16),
            jax.ShapeDtypeStruct((slots, nx * OWN_BEAMS), bf16),
            (slots, 8),
        ],
        [fine, coefs, near_tiles, meta, weights, y_a, y_b, bulk_a, bulk_b, near_control, *others],
        [pltpu.VMEM((total * NC, 128), f32), pltpu.VMEM((128, 128), f32)],
        flops=3000000,
    )
    beams = [got_beams, small_a[beam_at:]]
    tops, lows, coef, rim_picks = call(
        lambda *refs: forecast(ny, rows, *refs),
        [
            jax.ShapeDtypeStruct((STEPS * CX * CY, NC * 128), bf16),
            jax.ShapeDtypeStruct((STEPS * CX * CY, NC * 128), bf16),
            (5 * FIELD, 128),
            (2 * RIM * PITCH, total),
        ],
        [field, coef, small_a, small_b],
        [
            pltpu.VMEM((NC * FIELD, 128), f32),
            pltpu.VMEM((NC * FIELD, 128), f32),
            pltpu.VMEM((total * NC, 128), f32),
            pltpu.VMEM((128, 128), f32),
        ],
        flops=10000000,
    )
    loose = loose_slots(ny)
    back_a, back_b, final, sums, *back = call(
        lambda *refs: main(ny, len(beams), *refs),
        [
            (BACK + per_slot, 128),
            (BACK + (per_slot if ny == 4 else 0), 128),
            (NC * FIELD, 128),
            (per_slot, 128),
        ]
        + [(per_slot, 128)] * len(loose),
        [
            coef,
            tops,
            lows,
            wide,
            slot_pick,
            slot_push,
            beam_pick,
            columns,
            picks,
            rim_picks,
            *beams,
        ],
        [
            pltpu.VMEM((NC * FIELD, 128), f32),
            pltpu.VMEM((STEPS * CX * CY, NC * 128), f32),
            pltpu.VMEM((total * NC, 128), f32),
        ],
        flops=20000000,
    )
    y_a = swap(back_a, "gy", 1)
    y_b = ring_b(back_b, "gy")
    others = [swap(value, "gy", slot_xor(ny, s)) for s, value in zip(loose, back)]
    bulk_a, bulk_b, near = call(
        pack_bulk, [(BULK_COEF, 128), (BULK_COEF, 128), tile], [fine, final]
    )
    bulk_a = swap(bulk_a, "gx", 1)
    bulk_b = pair_b(bulk_b, "gx", "gy")
    home_rows = rows + 2 * NC * CORNER
    small_a, small_b, own_sum = call(
        pack_home,
        [(home_rows, 128), (home_rows, 128), (rows, 128)],
        [sums, y_a, y_b, *others],
    )
    small_a = swap(small_a, "gx", 1)
    small_b = pair_b(small_b, "gx", "gy")
    grad_delta, grad_alpha = call(
        finish,
        [tile, (rows, 128)],
        [near_control, near, own_sum, y_a, y_b, bulk_a, bulk_b, small_a, small_b],
    )
    return grad_delta.reshape(delta.shape), grad_alpha.reshape(alpha.shape)


def solution(mesh):
    return jax.shard_map(
        on_device,
        mesh=mesh,
        in_specs=(
            P(None, "gx", "gy", None),
            P("gx", "gy", None, None),
            P("gx", "gy", None),
            P(None, "gx", "gy", None),
            P("gx", "gy"),
            P(("gx", "gy"), None, None),
            P("gx", "gy", None),
            P("gx", "gy", None),
            P("gx", "gy", None),
            P("gx", "gy", None),
            P("gx", "gy", None, None, None),
            P("gx", "gy", None),
        ),
        out_specs=(P(None, "gx", "gy", None), P("gx", "gy", None, None)),
        check_vma=False,
    )
```

```python
import jax
import jax.numpy as jnp
from jax import lax
from jax.experimental import pallas as pl
from jax.experimental.pallas import tpu as pltpu
from jax.sharding import PartitionSpec as P

STEPS = 3
RIM = 3
INNER = RIM - 1
NC = 4
CX = 16
CY = 16
BLOCKS = CX + 8
PITCH = CY + 8
FIRST = 4
FIELD = BLOCKS * PITCH
CORE = CX * PITCH
OWN_BEAMS = 8

profile_weight = 0.125
f32 = jnp.float32
bf16 = jnp.bfloat16

VMEM = pl.BlockSpec(memory_space=pltpu.VMEM)
HBM = pl.BlockSpec(memory_space=pltpu.HBM)


def call(body, outs, ins, scratch=(), in_specs=None, flops=1000000, limit=40 * 2**20):
    shapes = [
        out if isinstance(out, jax.ShapeDtypeStruct) else jax.ShapeDtypeStruct(out, f32)
        for out in outs
    ]
    size = sum(4 * value.size for value in ins)
    return pl.pallas_call(
        body,
        out_shape=shapes,
        in_specs=in_specs or [VMEM] * len(ins),
        out_specs=[VMEM] * len(shapes),
        scratch_shapes=list(scratch),
        compiler_params=pltpu.CompilerParams(vmem_limit_bytes=limit),
        cost_estimate=pl.CostEstimate(flops=flops, bytes_accessed=size, transcendentals=0),
    )(*ins)


def swap(block, axis, xor):
    return lax.ppermute(block, axis, [(i, i ^ xor) for i in range(lax.axis_size(axis))])


def pair_b(block, axis, other):
    count, across = lax.axis_size(axis), lax.axis_size(other)

    def place(i, j):
        return i * across + j if axis == "gx" else j * count + i

    pairs = []
    for j in range(across):
        for i in range(count):
            if i in (0, count - 1):
                pairs.append((place(i, j), place(i, j ^ 1)))
            else:
                pairs.append((place(i, j), place(i + 1 if i % 2 else i - 1, j)))
    return lax.ppermute(block, ("gx", "gy"), pairs)


def ring_b(block, axis):
    count = lax.axis_size(axis)
    pairs = [(i, (i + 1 if i % 2 else i - 1) % count) for i in range(count)]
    return lax.ppermute(block, axis, pairs)


def place_on(axis):
    me = lax.axis_index(axis)
    return lax.rem(me, 2) == 0, me > 0, me < lax.axis_size(axis) - 1


def split(value):
    top = value.astype(bf16)
    return top, (value - top.astype(f32)).astype(bf16)


def two_part_dot(left, value):
    top, low = split(value)
    return jnp.dot(left, top, preferred_element_type=f32) + jnp.dot(
        left, low, preferred_element_type=f32
    )


def layers(reach):
    found, at = [], 0
    for away in range(1, reach + 1):
        found.append((away, at, reach - away))
        at += CY + 2 * (reach - away)
    return found, at


WIDE, WIDE_ROWS = layers(RIM)
SLIM, SLIM_ROWS = layers(INNER)
X_COEF = NC * WIDE_ROWS
X_HALO = X_COEF + 3 * SLIM_ROWS

Y_COEF = NC * RIM * CX
Y_TILE = Y_COEF + 3 * INNER * CX
Y_HALO = Y_TILE + CX


def pack_y(
    delta,
    eddy,
    courant,
    alpha,
    tile_map,
    gate_beam,
    gate_index,
    gate_column,
    gate_live,
    precision,
    beam_rows,
    out_a,
    out_b,
    fine,
    coefs,
    profiles,
    near_tiles,
    meta,
    beams,
    tiles,
    gates,
    values,
    sems,
):
    even, _, _ = place_on("gy")
    moves = [
        pltpu.make_async_copy(source, target, sems.at[i])
        for i, (source, target) in enumerate(
            [
                (delta, fine),
                (eddy, coefs.at[0]),
                (courant.at[0], coefs.at[1]),
                (courant.at[1], coefs.at[2]),
                (tile_map, tiles),
                (alpha, profiles),
                (gate_beam, gates.at[0]),
                (gate_index, gates.at[1]),
                (gate_column, gates.at[2]),
                (gate_live, gates.at[3]),
                (precision, values),
                (beam_rows, beams),
            ]
        )
    ]
    for move in moves:
        move.start()
    for move in moves:
        move.wait()

    def put(at, field, away):
        north = field[pl.ds(CY - away, CX, stride=CY)]
        south = field[pl.ds(away - 1, CX, stride=CY)]
        out_a[at : at + CX] = jnp.where(even, north, south)
        out_b[at : at + CX] = jnp.where(even, south, north)

    for c in range(NC):
        for away in range(1, RIM + 1):
            put((c * RIM + away - 1) * CX, fine.at[c], away)
    for f in range(3):
        for away in range(1, INNER + 1):
            put(Y_COEF + (f * INNER + away - 1) * CX, coefs.at[f], away)
    near_tiles[...] = jnp.full((CX, 128), -1.0, f32)
    near_tiles[:, 0:CY] = tiles[...].astype(f32)
    for out in (out_a, out_b):
        out[Y_TILE : Y_TILE + CX] = near_tiles[...]
    out_a[Y_HALO:] = profiles[...]
    meta[...] = jnp.zeros(meta.shape, f32)
    meta[0:1] = gates[2].astype(f32)
    meta[1:2] = gates[0].astype(f32)
    meta[2:3] = gates[1].astype(f32)
    meta[3:4] = gates[3].astype(f32) * values[...]


def y_sides(got_a, got_b, rows, fill=0.0):
    even, low, high = place_on("gy")
    first, second = got_a[rows], got_b[rows]
    north, south = jnp.where(even, first, second), jnp.where(even, second, first)
    return jnp.where(high, north, fill), jnp.where(low, south, fill)


def x_sides(got_a, got_b, rows):
    even, low, high = place_on("gx")
    first, second = got_a[rows], got_b[rows]
    west, east = jnp.where(even, second, first), jnp.where(even, first, second)
    return jnp.where(low, west, 0.0), jnp.where(high, east, 0.0)


def gather_known(alpha, got_a, others, known):
    owned = alpha.shape[0]
    known[0:owned] = alpha[...]
    known[owned : 2 * owned] = got_a[Y_HALO:]
    for s, other in enumerate(others):
        known[(2 + s) * owned : (3 + s) * owned] = other[...]


def tile_numbers(near_tiles, got_a, got_b, tiles):
    spot = lax.broadcasted_iota(jnp.int32, (CX, 128), 1)
    north, south = y_sides(got_a, got_b, pl.ds(Y_TILE, CX), -1.0)
    near = jnp.where(
        (spot >= CY) & (spot < CY + RIM),
        pltpu.roll(north, CY, 1),
        jnp.where((spot >= PITCH - RIM) & (spot < PITCH), pltpu.roll(south, PITCH - CY, 1), -1.0),
    )
    tiles[...] = jnp.full(tiles.shape, -1.0, f32)
    tiles[0:CX] = jnp.where(spot < CY, near_tiles[...], near)
    return jnp.transpose(tiles[...])[0:PITCH]


def tile_ids(ny, owned):
    me = lax.axis_index("gy")
    lane = lax.broadcasted_iota(jnp.int32, (1, ny * owned), 1)
    ids = lane
    for s in range(ny):
        here = (lane >= s * owned) & (lane < (s + 1) * owned)
        ids = jnp.where(here, jnp.bitwise_xor(me, s) * owned + lane - s * owned, ids)
    return ids.astype(f32)


def by_variable(ref, count):
    return jnp.concatenate([ref[pl.ds(c, count, stride=NC)] for c in range(NC)], axis=1)


def pack_x(ny, delta, coefs, alpha, near_tiles, y_a, y_b, own_beams, *rest):
    others = rest[: ny - 2]
    out_a, out_b, beams, field, picks, known, tiles = rest[ny - 2 :]
    even, _, _ = place_on("gx")
    owned = alpha.shape[0] // NC
    gather_known(alpha, y_a, others, known)
    turned = tile_numbers(near_tiles, y_a, y_b, tiles)
    ids = tile_ids(ny, owned)
    columns = [x for x in range(RIM)] + [CX - RIM + x for x in range(RIM)]
    for i, x in enumerate(columns):
        picks[i * PITCH : (i + 1) * PITCH] = (turned[:, x : x + 1] == ids).astype(f32)
    fine = two_part_dot(picks[...].astype(bf16), by_variable(known, ny * owned))

    def fill(own, y_base, reach, c):
        for i, x in enumerate(columns):
            at = i * PITCH
            field[at + CY : at + PITCH] = jnp.zeros((PITCH - CY, 128), f32)
            field[at : at + CY] = own[x * CY : (x + 1) * CY]
        for away in range(1, reach + 1):
            for first, base in ((0, 0), (CX - RIM, RIM * PITCH)):
                rows = pl.ds(y_base + (away - 1) * CX + first, RIM)
                north, south = y_sides(y_a, y_b, rows)
                field[pl.ds(base + CY - 1 + away, RIM, stride=PITCH)] = north
                field[pl.ds(base + PITCH - away, RIM, stride=PITCH)] = south
        if c is not None:
            field[...] += profile_weight * fine[:, c * 128 : (c + 1) * 128]

    def put(at, found):
        for away, start, extra in found:
            east, west = (2 * RIM - away) * PITCH, (away - 1) * PITCH
            here = at + start
            for source, target, size in (
                (PITCH - extra, 0, extra),
                (0, extra, CY + extra),
            ):
                if size:
                    first = field[east + source : east + source + size]
                    second = field[west + source : west + source + size]
                    rows = slice(here + target, here + target + size)
                    out_a[rows] = jnp.where(even, first, second)
                    out_b[rows] = jnp.where(even, second, first)

    for c in range(NC):
        fill(delta.at[c], c * RIM * CX, RIM, c)
        put(c * WIDE_ROWS, WIDE)
    for f in range(3):
        fill(coefs.at[f], Y_COEF + f * INNER * CX, INNER, None)
        put(X_COEF + f * SLIM_ROWS, SLIM)
    rows = own_beams.shape[0]
    for at in range(0, beams.shape[0], rows):
        beams[at : at + rows] = own_beams[...]


def prepare(ny, delta, coefs, alpha, near_tiles, meta, weights, y_a, y_b, *rest):
    others = rest[: ny - 2]
    core, coef, picks, wide, slot_pick, slot_push, beam_pick, columns = rest[ny - 2 : ny + 6]
    known, tiles = rest[ny + 6 :]
    owned = alpha.shape[0] // NC

    def fill(ref, base, own, y_base, reach):
        for x in range(CX):
            at = base + x * PITCH
            ref[at : at + CY] = own[x * CY : (x + 1) * CY]
            ref[at + CY : at + PITCH] = jnp.zeros((PITCH - CY, 128), f32)
        for away in range(1, reach + 1):
            north, south = y_sides(y_a, y_b, pl.ds(y_base + (away - 1) * CX, CX))
            ref[pl.ds(base + CY - 1 + away, CX, stride=PITCH)] = north
            ref[pl.ds(base + PITCH - away, CX, stride=PITCH)] = south

    for c in range(NC):
        fill(core, c * CORE, delta.at[c], c * RIM * CX, RIM)
    for f in range(3):
        fill(coef, f * CORE, coefs.at[f], Y_COEF + f * INNER * CX, INNER)

    def combine(b, carry):
        at = pl.multiple_of(b * PITCH, 8)
        combined = combine_coefs(*[coef[pl.ds(f * CORE + at, PITCH)] for f in range(3)])
        for f, value in enumerate(combined):
            coef[pl.ds(f * CORE + at, PITCH)] = value
        return carry

    lax.fori_loop(0, CX, combine, 0)

    gather_known(alpha, y_a, others, known)
    turned = tile_numbers(near_tiles, y_a, y_b, tiles)
    ids = tile_ids(ny, owned)
    for x in range(CX):
        picks[x * PITCH : (x + 1) * PITCH] = (turned[:, x : x + 1] == ids).astype(f32)
    fine = two_part_dot(picks[...].astype(bf16), by_variable(known, ny * owned))
    for c in range(NC):
        core[c * CORE : (c + 1) * CORE] += profile_weight * fine[:, c * 128 : (c + 1) * 128]

    slots = meta.shape[1]
    for c in range(NC):
        wide[:, c * 128 : (c + 1) * 128] = weights[pl.ds(c, slots, stride=NC)]
    per_beam = beam_pick.shape[1]
    turned = jnp.transpose(meta[...])
    columns[...] = turned
    slot_lane = lax.broadcasted_iota(jnp.int32, (slots, CX * CY), 1).astype(f32)
    slot_pick[...] = (slot_lane == turned[:, 0:1]).astype(f32).astype(bf16)
    column_row = lax.broadcasted_iota(jnp.int32, (CX * CY, slots), 0).astype(f32)
    slot_push[...] = (column_row == meta[0:1]).astype(f32).astype(bf16)
    beam_lane = lax.broadcasted_iota(jnp.int32, (slots, per_beam), 1).astype(f32)
    beam_pick[...] = (beam_lane == turned[:, 1:2]).astype(f32).astype(bf16)


def combine_coefs(viscous, along_x, along_y):
    half_x, half_y = 0.5 * along_x, 0.5 * along_y
    return (
        1.0 - 4.0 * viscous,
        viscous - half_x,
        viscous + half_x,
        viscous - half_y,
        viscous + half_y,
    )


def clear(ref, base, blocks):
    for b in blocks:
        at = base + b * PITCH
        ref[at : at + PITCH] = jnp.zeros((PITCH, 128), f32)


def forecast(core, coef_core, x_a, x_b, tops, lows, coef, state_0, state_1, raw):
    def fill(ref, base, x_base, found):
        for away, start, extra in found:
            for source, target, size in (
                (0, PITCH - extra, extra),
                (extra, 0, CY + extra),
            ):
                if size:
                    at = x_base + start + source
                    west, east = x_sides(x_a, x_b, pl.ds(at, size))
                    at = base + (FIRST - away) * PITCH + target
                    ref[at : at + size] = west
                    at = base + (FIRST + CX - 1 + away) * PITCH + target
                    ref[at : at + size] = east

    rim = [FIRST - 3, FIRST - 2, FIRST - 1, FIRST + CX, FIRST + CX + 1, FIRST + CX + 2]
    for c in range(NC):
        at = c * FIELD + FIRST * PITCH
        state_0[at : at + CORE] = core[c * CORE : (c + 1) * CORE]
        clear(state_0, c * FIELD, rim)
        fill(state_0, c * FIELD, c * WIDE_ROWS, WIDE)
    for f in range(3):
        clear(raw, f * FIELD, rim[1:5])
        fill(raw, f * FIELD, X_COEF + f * SLIM_ROWS, SLIM)
    for f in range(5):
        at = f * FIELD + FIRST * PITCH
        coef[at : at + CORE] = coef_core[f * CORE : (f + 1) * CORE]
        clear(coef, f * FIELD, [0, 1, BLOCKS - 2, BLOCKS - 1])
    for b in rim[1:5]:
        rows = [slice(f * FIELD + b * PITCH, f * FIELD + (b + 1) * PITCH) for f in range(5)]
        for f, value in enumerate(combine_coefs(*[raw[rows[f]] for f in range(3)])):
            coef[rows[f]] = value

    def forward(source, target, low, high):
        def body(b, carry):
            at = pl.multiple_of(b * PITCH, 8)
            k = [coef[pl.ds(f * FIELD + at, PITCH)] for f in range(5)]
            for c in range(NC):
                base = c * FIELD + at
                here = source[pl.ds(base, PITCH)]
                target[pl.ds(base, PITCH)] = (
                    k[0] * here
                    + k[1] * source[pl.ds(base + PITCH, PITCH)]
                    + k[2] * source[pl.ds(base - PITCH, PITCH)]
                    + k[3] * pltpu.roll(here, PITCH - 1, 0)
                    + k[4] * pltpu.roll(here, 1, 0)
                )
            return carry

        lax.fori_loop(low, high, body, 0)

    buffers = [state_0, state_1]
    for step in range(STEPS):
        source, target = buffers[step % 2], buffers[(step + 1) % 2]
        forward(source, target, 2 + step, BLOCKS - 2 - step)
        own = jnp.concatenate(
            [
                jnp.concatenate(
                    [
                        target[c * FIELD + b * PITCH : c * FIELD + b * PITCH + CY]
                        for b in range(FIRST, FIRST + CX)
                    ],
                    axis=0,
                )
                for c in range(NC)
            ],
            axis=1,
        )
        rows = slice(step * CX * CY, (step + 1) * CX * CY)
        tops[rows], lows[rows] = split(own)


def main(
    coef,
    tops,
    lows,
    wide,
    slot_pick,
    slot_push,
    beam_pick,
    columns,
    *rest,
):
    beams = rest[:-6]
    out_a, out_b, out_core, state_0, state_1, forcing = rest[-6:]
    even, _, _ = place_on("gx")
    slots = columns.shape[0]
    gate_lane = lax.broadcasted_iota(jnp.int32, (slots, 128), 1).astype(f32)
    gate_here = gate_lane == columns[:, 2:3]
    scaled = columns[:, 3:4]
    for step in range(STEPS):
        rows = slice(step * CX * CY, (step + 1) * CX * CY)
        picked = jnp.dot(slot_pick[...], tops[rows], preferred_element_type=f32)
        picked = picked + jnp.dot(slot_pick[...], lows[rows], preferred_element_type=f32)
        picked = picked * wide[...]
        table = []
        for part in beams:
            for at in range(0, part.shape[0], STEPS * OWN_BEAMS):
                first = at + step * OWN_BEAMS
                table.append(part[first : first + OWN_BEAMS])
        table = two_part_dot(beam_pick[...], jnp.concatenate(table, axis=0))
        tally = -jnp.where(gate_here, table, 0.0)
        for c in range(NC):
            tally = tally + picked[:, c * 128 : (c + 1) * 128]
        misfit = scaled * jnp.sum(tally, axis=1, keepdims=True)
        forcing[rows] = two_part_dot(slot_push[...], misfit * wide[...])

    buffers = [state_0, state_1]

    for c in range(NC):
        clear(state_0, c * FIELD, [0, 1, 2, 3, BLOCKS - 4, BLOCKS - 3, BLOCKS - 2, BLOCKS - 1])
        clear(state_1, c * FIELD, [1, 2, BLOCKS - 3, BLOCKS - 2])

    def add_forcing(ref, step):
        for c in range(NC):
            for x in range(CX):
                at = c * FIELD + (FIRST + x) * PITCH
                first = step * CX * CY + x * CY
                value = forcing[first : first + CY, c * 128 : (c + 1) * 128]
                if step == STEPS - 1:
                    ref[at : at + CY] = value
                    ref[at + CY : at + PITCH] = jnp.zeros((PITCH - CY, 128), f32)
                else:
                    ref[at : at + CY] += value

    def backward(source, target, low, high):
        def body(b, carry):
            at = pl.multiple_of(b * PITCH, 8)
            k = [
                coef[pl.ds(at, PITCH)],
                coef[pl.ds(FIELD + at - PITCH, PITCH)],
                coef[pl.ds(2 * FIELD + at + PITCH, PITCH)],
                coef[pl.ds(3 * FIELD + at, PITCH)],
                coef[pl.ds(4 * FIELD + at, PITCH)],
            ]
            for c in range(NC):
                base = c * FIELD + at
                here = source[pl.ds(base, PITCH)]
                target[pl.ds(base, PITCH)] = (
                    k[0] * here
                    + k[1] * source[pl.ds(base - PITCH, PITCH)]
                    + k[2] * source[pl.ds(base + PITCH, PITCH)]
                    + pltpu.roll(k[3] * here, 1, 0)
                    + pltpu.roll(k[4] * here, PITCH - 1, 0)
                )
            return carry

        lax.fori_loop(low, high, body, 0)

    for step in range(STEPS):
        source, target = buffers[step % 2], buffers[(step + 1) % 2]
        add_forcing(source, STEPS - 1 - step)
        backward(source, target, FIRST - 1 - step, FIRST + CX + 1 + step)
    final = buffers[STEPS % 2]

    for c in range(NC):
        at = c * FIELD + FIRST * PITCH
        out_core[c * CORE : (c + 1) * CORE] = final[at : at + CORE]
        for away, start, extra in WIDE:
            for source, target, size in (
                (PITCH - extra, 0, extra),
                (0, extra, CY + extra),
            ):
                if size:
                    at = c * FIELD + (FIRST - away) * PITCH + source
                    west = final[at : at + size]
                    at = c * FIELD + (FIRST + CX - 1 + away) * PITCH + source
                    east = final[at : at + size]
                    at = c * WIDE_ROWS + start + target
                    out_a[at : at + size] = jnp.where(even, east, west)
                    out_b[at : at + size] = jnp.where(even, west, east)


def add_x(ny, delta, picks, core, x_a, x_b, *rest):
    out_a, out_b, out_near, out_sums = rest[:4]
    out_others = rest[4:-2]
    merged = ny == 4
    field, sums = rest[-2:]
    even, _, _ = place_on("gy")
    total = picks.shape[1]
    rows = total * NC // ny
    field[...] = core[...]
    for c in range(NC):
        for away, start, extra in WIDE:
            for source, target, size in (
                (0, PITCH - extra, extra),
                (extra, 0, CY + extra),
            ):
                if size:
                    at = c * WIDE_ROWS + start + source
                    west, east = x_sides(x_a, x_b, pl.ds(at, size))
                    at = c * CORE + (away - 1) * PITCH + target
                    field[at : at + size] += west
                    at = c * CORE + (CX - away) * PITCH + target
                    field[at : at + size] += east
    for c in range(NC):
        for away in range(1, RIM + 1):
            north = field[pl.ds(c * CORE + CY - 1 + away, CX, stride=PITCH)]
            south = field[pl.ds(c * CORE + PITCH - away, CX, stride=PITCH)]
            at = (c * RIM + away - 1) * CX
            out_a[at : at + CX] = jnp.where(even, north, south)
            out_b[at : at + CX] = jnp.where(even, south, north)
        for x in range(CX):
            at = c * CORE + x * PITCH
            here = slice(x * CY, (x + 1) * CY)
            out_near[c, here] = delta[c, here] + field[at : at + CY]
    adjoint = jnp.concatenate([field[c * CORE : (c + 1) * CORE] for c in range(NC)], axis=1)
    tile_sums = two_part_dot(jnp.transpose(picks[...]).astype(bf16), adjoint)
    for c in range(NC):
        sums[pl.ds(c, total, stride=NC)] = tile_sums[:, c * 128 : (c + 1) * 128]
    out_sums[...] = sums[0:rows]
    out_a[Y_COEF:] = sums[rows : 2 * rows]
    if merged:
        out_b[Y_COEF:] = sums[3 * rows : 4 * rows]
    for s, other in enumerate(out_others):
        other[...] = sums[(2 + s) * rows : (3 + s) * rows]


def add_y(alpha, near, sums, y_a, y_b, *rest):
    others = rest[:-2]
    out_delta, out_alpha = rest[-2:]
    out_delta[...] = near[...]
    for c in range(NC):
        for away in range(1, RIM + 1):
            north, south = y_sides(y_a, y_b, pl.ds((c * RIM + away - 1) * CX, CX))
            high = pl.ds(CY - away, CX, stride=CY)
            low = pl.ds(away - 1, CX, stride=CY)
            out_delta[c, high] = out_delta[c, high] + north
            out_delta[c, low] = out_delta[c, low] + south
    total = sums[...] + y_a[Y_COEF:]
    if y_b.shape[0] > Y_COEF:
        total = total + y_b[Y_COEF:]
    for other in others:
        total = total + other[...]
    out_alpha[...] = alpha[...] + profile_weight * total


def on_device(
    delta,
    alpha,
    eddy,
    courant,
    tile_map,
    obs_rows,
    gate_beam,
    gate_index,
    gate_column,
    gate_live,
    obs_weight,
    obs_precision,
):
    nx = lax.axis_size("gx")
    ny = lax.axis_size("gy")
    owned = alpha.shape[1]
    slots = gate_column.shape[2]
    fine = delta.reshape(NC, CX * CY, 128)
    eddy = eddy.reshape(CX * CY, 128)
    courant = courant.reshape(2, CX * CY, 128)
    control = alpha.reshape(owned * NC, 128)
    weights = obs_weight.reshape(slots * NC, 128)
    gates = [
        value.reshape(1, slots)
        for value in (gate_beam, gate_index, gate_column, gate_live, obs_precision)
    ]
    own_beams = jnp.transpose(obs_rows, (1, 0, 2)).reshape(STEPS * OWN_BEAMS, 128)
    beam_count = nx * OWN_BEAMS
    rows = owned * NC
    total = ny * owned

    y_a, y_b, fine, coefs, control_near, near_tiles, meta, near_beams = call(
        pack_y,
        [
            (Y_HALO + rows, 128),
            (Y_HALO, 128),
            fine.shape,
            (3, CX * CY, 128),
            control.shape,
            (CX, 128),
            (8, slots),
            own_beams.shape,
        ],
        [
            pltpu.with_memory_space_constraint(value, pltpu.HBM)
            for value in (fine, eddy, courant, control, tile_map, *gates, own_beams)
        ],
        [
            pltpu.VMEM(tile_map.shape, jnp.int32),
            pltpu.VMEM((4, 1, slots), jnp.int32),
            pltpu.VMEM((1, slots), f32),
            pltpu.SemaphoreType.DMA((12,)),
        ],
        in_specs=[HBM] * 11,
    )
    y_a = swap(y_a, "gy", 1)
    y_b = pair_b(y_b, "gy", "gx")
    others = [swap(control, "gy", xor) for xor in range(2, ny)]

    x_a, x_b, beams = call(
        lambda *refs: pack_x(ny, *refs),
        [(X_HALO, 128), (X_HALO, 128), (nx * own_beams.shape[0], 128)],
        [fine, coefs, control_near, near_tiles, y_a, y_b, near_beams, *others],
        [
            pltpu.VMEM((2 * RIM * PITCH, 128), f32),
            pltpu.VMEM((2 * RIM * PITCH, total), f32),
            pltpu.VMEM((total * NC, 128), f32),
            pltpu.VMEM((128, 128), f32),
        ],
    )
    x_a = swap(x_a, "gx", 1)
    x_b = pair_b(x_b, "gx", "gy")

    core, coef, picks, wide, slot_pick, slot_push, beam_pick, columns = call(
        lambda *refs: prepare(ny, *refs),
        [
            (NC * CORE, 128),
            (5 * CORE, 128),
            (CORE, total),
            (slots, NC * 128),
            jax.ShapeDtypeStruct((slots, CX * CY), bf16),
            jax.ShapeDtypeStruct((CX * CY, slots), bf16),
            jax.ShapeDtypeStruct((slots, beam_count), bf16),
            (slots, 8),
        ],
        [fine, coefs, control_near, near_tiles, meta, weights, y_a, y_b, *others],
        [
            pltpu.VMEM((total * NC, 128), f32),
            pltpu.VMEM((128, 128), f32),
        ],
        flops=3000000,
    )

    beams = [lax.all_to_all(beams, "gx", 0, 0, tiled=True)]
    tops, lows, coef = call(
        forecast,
        [
            jax.ShapeDtypeStruct((STEPS * CX * CY, NC * 128), bf16),
            jax.ShapeDtypeStruct((STEPS * CX * CY, NC * 128), bf16),
            (5 * FIELD, 128),
        ],
        [core, coef, x_a, x_b],
        [
            pltpu.VMEM((NC * FIELD, 128), f32),
            pltpu.VMEM((NC * FIELD, 128), f32),
            pltpu.VMEM((3 * FIELD, 128), f32),
        ],
        flops=10000000,
    )
    back_a, back_b, core = call(
        main,
        [(X_COEF, 128), (X_COEF, 128), (NC * CORE, 128)],
        [coef, tops, lows, wide, slot_pick, slot_push, beam_pick, columns, *beams],
        [
            pltpu.VMEM((NC * FIELD, 128), f32),
            pltpu.VMEM((NC * FIELD, 128), f32),
            pltpu.VMEM((STEPS * CX * CY, NC * 128), f32),
        ],
        flops=20000000,
    )
    x_a = swap(back_a, "gx", 1)
    x_b = pair_b(back_b, "gx", "gy")
    loose = [xor for xor in range(2, ny) if ny != 4 or xor != 3]
    back_a, back_b, near, sums, *back = call(
        lambda *refs: add_x(ny, *refs),
        [
            (Y_COEF + rows, 128),
            (Y_COEF + (rows if ny == 4 else 0), 128),
            fine.shape,
            (rows, 128),
        ]
        + [(rows, 128)] * len(loose),
        [fine, picks, core, x_a, x_b],
        [pltpu.VMEM((NC * CORE, 128), f32), pltpu.VMEM((total * NC, 128), f32)],
    )
    y_a = swap(back_a, "gy", 1)
    y_b = ring_b(back_b, "gy")
    others = [swap(value, "gy", xor) for xor, value in zip(loose, back)]
    grad_delta, grad_alpha = call(
        add_y,
        [fine.shape, control.shape],
        [control_near, near, sums, y_a, y_b, *others],
    )
    return grad_delta.reshape(delta.shape), grad_alpha.reshape(alpha.shape)


def solution(mesh):
    return jax.shard_map(
        on_device,
        mesh=mesh,
        in_specs=(
            P(None, "gx", "gy", None),
            P("gx", "gy", None, None),
            P("gx", "gy", None),
            P(None, "gx", "gy", None),
            P("gx", "gy"),
            P(("gx", "gy"), None, None),
            P("gx", "gy", None),
            P("gx", "gy", None),
            P("gx", "gy", None),
            P("gx", "gy", None),
            P("gx", "gy", None, None, None),
            P("gx", "gy", None),
        ),
        out_specs=(P(None, "gx", "gy", None), P("gx", "gy", None, None)),
        check_vma=False,
    )
```

```python
import jax
import jax.numpy as jnp
from jax import lax
from jax.experimental import pallas as pl
from jax.experimental.pallas import tpu as pltpu
from jax.sharding import PartitionSpec as P

STEPS = 3
RIM = 3
INNER = RIM - 1
NC = 4
CX = 16
CY = 16
BLOCKS = CX + 8
PITCH = CY + 8
FIRST = 4
FIELD = BLOCKS * PITCH
CORE = CX * PITCH
OWN_BEAMS = 8
BEAM_BITS = 3

profile_weight = 0.125
f32 = jnp.float32
bf16 = jnp.bfloat16

VMEM = pl.BlockSpec(memory_space=pltpu.VMEM)
HBM = pl.BlockSpec(memory_space=pltpu.HBM)


def call(body, outs, ins, scratch=(), in_specs=None, flops=1000000, limit=40 * 2**20):
    shapes = [
        out if isinstance(out, jax.ShapeDtypeStruct) else jax.ShapeDtypeStruct(out, f32)
        for out in outs
    ]
    size = sum(4 * value.size for value in ins)
    return pl.pallas_call(
        body,
        out_shape=shapes,
        in_specs=in_specs or [VMEM] * len(ins),
        out_specs=[VMEM] * len(shapes),
        scratch_shapes=list(scratch),
        compiler_params=pltpu.CompilerParams(vmem_limit_bytes=limit),
        cost_estimate=pl.CostEstimate(flops=flops, bytes_accessed=size, transcendentals=0),
    )(*ins)


def swap(block, axis, xor):
    return lax.ppermute(block, axis, [(i, i ^ xor) for i in range(lax.axis_size(axis))])


def pair_b(block, axis, other):
    count, across = lax.axis_size(axis), lax.axis_size(other)

    def place(i, j):
        return i * across + j if axis == "gx" else j * count + i

    pairs = []
    for j in range(across):
        for i in range(count):
            if i in (0, count - 1):
                pairs.append((place(i, j), place(i, j ^ 1)))
            else:
                pairs.append((place(i, j), place(i + 1 if i % 2 else i - 1, j)))
    return lax.ppermute(block, ("gx", "gy"), pairs)


def ring_b(block, axis):
    count = lax.axis_size(axis)
    pairs = [(i, (i + 1 if i % 2 else i - 1) % count) for i in range(count)]
    return lax.ppermute(block, axis, pairs)


def place_on(axis):
    me = lax.axis_index(axis)
    return lax.rem(me, 2) == 0, me > 0, me < lax.axis_size(axis) - 1


def split(value):
    top = value.astype(bf16)
    return top, (value - top.astype(f32)).astype(bf16)


def two_part_dot(left, value):
    top, low = split(value)
    return jnp.dot(left, top, preferred_element_type=f32) + jnp.dot(
        left, low, preferred_element_type=f32
    )


def layers(reach):
    found, at = [], 0
    for away in range(1, reach + 1):
        found.append((away, at, reach - away))
        at += CY + 2 * (reach - away)
    return found, at


WIDE, WIDE_ROWS = layers(RIM)
SLIM, SLIM_ROWS = layers(INNER)
X_COEF = NC * WIDE_ROWS
X_HALO = X_COEF + 3 * SLIM_ROWS

Y_COEF = NC * RIM * CX
Y_TILE = Y_COEF + 3 * INNER * CX
Y_HALO = Y_TILE + CX


def pack_y(
    delta,
    eddy,
    courant,
    alpha,
    tile_map,
    gate_beam,
    gate_index,
    gate_column,
    gate_live,
    precision,
    beam_rows,
    out_a,
    out_b,
    fine,
    coefs,
    profiles,
    near_tiles,
    meta,
    beams,
    tiles,
    gates,
    values,
    sems,
):
    even, _, _ = place_on("gy")
    moves = [
        pltpu.make_async_copy(source, target, sems.at[i])
        for i, (source, target) in enumerate(
            [
                (delta, fine),
                (eddy, coefs.at[0]),
                (courant.at[0], coefs.at[1]),
                (courant.at[1], coefs.at[2]),
                (tile_map, tiles),
                (alpha, profiles),
                (gate_beam, gates.at[0]),
                (gate_index, gates.at[1]),
                (gate_column, gates.at[2]),
                (gate_live, gates.at[3]),
                (precision, values),
                (beam_rows, beams),
            ]
        )
    ]
    for move in moves:
        move.start()
    for move in moves:
        move.wait()

    def put(at, field, away):
        north = field[pl.ds(CY - away, CX, stride=CY)]
        south = field[pl.ds(away - 1, CX, stride=CY)]
        out_a[at : at + CX] = jnp.where(even, north, south)
        out_b[at : at + CX] = jnp.where(even, south, north)

    for c in range(NC):
        for away in range(1, RIM + 1):
            put((c * RIM + away - 1) * CX, fine.at[c], away)
    for f in range(3):
        for away in range(1, INNER + 1):
            put(Y_COEF + (f * INNER + away - 1) * CX, coefs.at[f], away)
    near_tiles[...] = jnp.full((CX, 128), -1.0, f32)
    near_tiles[:, 0:CY] = tiles[...].astype(f32)
    for out in (out_a, out_b):
        out[Y_TILE : Y_TILE + CX] = near_tiles[...]
    out_a[Y_HALO:] = profiles[...]
    held = BEAM_BITS
    beam = gates[0]
    owner = jnp.bitwise_xor(beam >> held, lax.axis_index("gx"))
    block = (owner >> 1) + (owner & 1) * (lax.axis_size("gx") // 2)
    meta[...] = jnp.zeros(meta.shape, f32)
    meta[0:1] = gates[2].astype(f32)
    meta[1:2] = ((block << held) | (beam & ((1 << held) - 1))).astype(f32)
    meta[2:3] = gates[1].astype(f32)
    meta[3:4] = gates[3].astype(f32) * values[...]


def y_sides(got_a, got_b, rows, fill=0.0):
    even, low, high = place_on("gy")
    first, second = got_a[rows], got_b[rows]
    north, south = jnp.where(even, first, second), jnp.where(even, second, first)
    return jnp.where(high, north, fill), jnp.where(low, south, fill)


def x_sides(got_a, got_b, rows):
    even, low, high = place_on("gx")
    first, second = got_a[rows], got_b[rows]
    west, east = jnp.where(even, second, first), jnp.where(even, first, second)
    return jnp.where(low, west, 0.0), jnp.where(high, east, 0.0)


def gather_known(alpha, got_a, others, known):
    owned = alpha.shape[0]
    known[0:owned] = alpha[...]
    known[owned : 2 * owned] = got_a[Y_HALO:]
    for s, other in enumerate(others):
        known[(2 + s) * owned : (3 + s) * owned] = other[...]


def tile_numbers(near_tiles, got_a, got_b, tiles):
    spot = lax.broadcasted_iota(jnp.int32, (CX, 128), 1)
    north, south = y_sides(got_a, got_b, pl.ds(Y_TILE, CX), -1.0)
    near = jnp.where(
        (spot >= CY) & (spot < CY + RIM),
        pltpu.roll(north, CY, 1),
        jnp.where((spot >= PITCH - RIM) & (spot < PITCH), pltpu.roll(south, PITCH - CY, 1), -1.0),
    )
    tiles[...] = jnp.full(tiles.shape, -1.0, f32)
    tiles[0:CX] = jnp.where(spot < CY, near_tiles[...], near)
    return jnp.transpose(tiles[...])[0:PITCH]


def tile_ids(ny, owned):
    me = lax.axis_index("gy")
    lane = lax.broadcasted_iota(jnp.int32, (1, ny * owned), 1)
    ids = lane
    for s in range(ny):
        here = (lane >= s * owned) & (lane < (s + 1) * owned)
        ids = jnp.where(here, jnp.bitwise_xor(me, s) * owned + lane - s * owned, ids)
    return ids.astype(f32)


def by_variable(ref, count):
    return jnp.concatenate([ref[pl.ds(c, count, stride=NC)] for c in range(NC)], axis=1)


def pack_x(ny, delta, coefs, alpha, near_tiles, y_a, y_b, beams, *rest):
    others = rest[: ny - 2]
    out_a, out_b, field, picks, known, tiles = rest[ny - 2 :]
    even, _, _ = place_on("gx")
    owned = alpha.shape[0] // NC
    gather_known(alpha, y_a, others, known)
    turned = tile_numbers(near_tiles, y_a, y_b, tiles)
    ids = tile_ids(ny, owned)
    columns = [x for x in range(RIM)] + [CX - RIM + x for x in range(RIM)]
    for i, x in enumerate(columns):
        picks[i * PITCH : (i + 1) * PITCH] = (turned[:, x : x + 1] == ids).astype(f32)
    fine = two_part_dot(picks[...].astype(bf16), by_variable(known, ny * owned))

    def fill(own, y_base, reach, c):
        for i, x in enumerate(columns):
            at = i * PITCH
            field[at + CY : at + PITCH] = jnp.zeros((PITCH - CY, 128), f32)
            field[at : at + CY] = own[x * CY : (x + 1) * CY]
        for away in range(1, reach + 1):
            for first, base in ((0, 0), (CX - RIM, RIM * PITCH)):
                rows = pl.ds(y_base + (away - 1) * CX + first, RIM)
                north, south = y_sides(y_a, y_b, rows)
                field[pl.ds(base + CY - 1 + away, RIM, stride=PITCH)] = north
                field[pl.ds(base + PITCH - away, RIM, stride=PITCH)] = south
        if c is not None:
            field[...] += profile_weight * fine[:, c * 128 : (c + 1) * 128]

    def put(at, found):
        for away, start, extra in found:
            east, west = (2 * RIM - away) * PITCH, (away - 1) * PITCH
            here = at + start
            for source, target, size in (
                (PITCH - extra, 0, extra),
                (0, extra, CY + extra),
            ):
                if size:
                    first = field[east + source : east + source + size]
                    second = field[west + source : west + source + size]
                    rows = slice(here + target, here + target + size)
                    out_a[rows] = jnp.where(even, first, second)
                    out_b[rows] = jnp.where(even, second, first)

    for c in range(NC):
        fill(delta.at[c], c * RIM * CX, RIM, c)
        put(c * WIDE_ROWS, WIDE)
    for f in range(3):
        fill(coefs.at[f], Y_COEF + f * INNER * CX, INNER, None)
        put(X_COEF + f * SLIM_ROWS, SLIM)
    out_a[X_HALO:] = beams[...]


def prepare(ny, delta, coefs, alpha, near_tiles, meta, weights, y_a, y_b, *rest):
    others = rest[: ny - 2]
    core, coef, picks, wide, slot_pick, slot_push, beam_pick, columns = rest[ny - 2 : ny + 6]
    known, tiles = rest[ny + 6 :]
    owned = alpha.shape[0] // NC

    def fill(ref, base, own, y_base, reach):
        for x in range(CX):
            at = base + x * PITCH
            ref[at : at + CY] = own[x * CY : (x + 1) * CY]
            ref[at + CY : at + PITCH] = jnp.zeros((PITCH - CY, 128), f32)
        for away in range(1, reach + 1):
            north, south = y_sides(y_a, y_b, pl.ds(y_base + (away - 1) * CX, CX))
            ref[pl.ds(base + CY - 1 + away, CX, stride=PITCH)] = north
            ref[pl.ds(base + PITCH - away, CX, stride=PITCH)] = south

    for c in range(NC):
        fill(core, c * CORE, delta.at[c], c * RIM * CX, RIM)
    for f in range(3):
        fill(coef, f * CORE, coefs.at[f], Y_COEF + f * INNER * CX, INNER)

    def combine(b, carry):
        at = pl.multiple_of(b * PITCH, 8)
        combined = combine_coefs(*[coef[pl.ds(f * CORE + at, PITCH)] for f in range(3)])
        for f, value in enumerate(combined):
            coef[pl.ds(f * CORE + at, PITCH)] = value
        return carry

    lax.fori_loop(0, CX, combine, 0)

    gather_known(alpha, y_a, others, known)
    turned = tile_numbers(near_tiles, y_a, y_b, tiles)
    ids = tile_ids(ny, owned)
    for x in range(CX):
        picks[x * PITCH : (x + 1) * PITCH] = (turned[:, x : x + 1] == ids).astype(f32)
    fine = two_part_dot(picks[...].astype(bf16), by_variable(known, ny * owned))
    for c in range(NC):
        core[c * CORE : (c + 1) * CORE] += profile_weight * fine[:, c * 128 : (c + 1) * 128]

    slots = meta.shape[1]
    for c in range(NC):
        wide[:, c * 128 : (c + 1) * 128] = weights[pl.ds(c, slots, stride=NC)]
    per_beam = beam_pick.shape[1]
    turned = jnp.transpose(meta[...])
    columns[...] = turned
    slot_lane = lax.broadcasted_iota(jnp.int32, (slots, CX * CY), 1).astype(f32)
    slot_pick[...] = (slot_lane == turned[:, 0:1]).astype(f32).astype(bf16)
    column_row = lax.broadcasted_iota(jnp.int32, (CX * CY, slots), 0).astype(f32)
    slot_push[...] = (column_row == meta[0:1]).astype(f32).astype(bf16)
    beam_lane = lax.broadcasted_iota(jnp.int32, (slots, per_beam), 1).astype(f32)
    beam_pick[...] = (beam_lane == turned[:, 1:2]).astype(f32).astype(bf16)


def combine_coefs(viscous, along_x, along_y):
    half_x, half_y = 0.5 * along_x, 0.5 * along_y
    return (
        1.0 - 4.0 * viscous,
        viscous - half_x,
        viscous + half_x,
        viscous - half_y,
        viscous + half_y,
    )


def clear(ref, base, blocks):
    for b in blocks:
        at = base + b * PITCH
        ref[at : at + PITCH] = jnp.zeros((PITCH, 128), f32)


def forecast(core, coef_core, x_a, x_b, tops, lows, coef, state_0, state_1, raw):
    def fill(ref, base, x_base, found):
        for away, start, extra in found:
            for source, target, size in (
                (0, PITCH - extra, extra),
                (extra, 0, CY + extra),
            ):
                if size:
                    at = x_base + start + source
                    west, east = x_sides(x_a, x_b, pl.ds(at, size))
                    at = base + (FIRST - away) * PITCH + target
                    ref[at : at + size] = west
                    at = base + (FIRST + CX - 1 + away) * PITCH + target
                    ref[at : at + size] = east

    rim = [FIRST - 3, FIRST - 2, FIRST - 1, FIRST + CX, FIRST + CX + 1, FIRST + CX + 2]
    for c in range(NC):
        at = c * FIELD + FIRST * PITCH
        state_0[at : at + CORE] = core[c * CORE : (c + 1) * CORE]
        clear(state_0, c * FIELD, rim)
        fill(state_0, c * FIELD, c * WIDE_ROWS, WIDE)
    for f in range(3):
        clear(raw, f * FIELD, rim[1:5])
        fill(raw, f * FIELD, X_COEF + f * SLIM_ROWS, SLIM)
    for f in range(5):
        at = f * FIELD + FIRST * PITCH
        coef[at : at + CORE] = coef_core[f * CORE : (f + 1) * CORE]
        clear(coef, f * FIELD, [0, 1, BLOCKS - 2, BLOCKS - 1])
    for b in rim[1:5]:
        rows = [slice(f * FIELD + b * PITCH, f * FIELD + (b + 1) * PITCH) for f in range(5)]
        for f, value in enumerate(combine_coefs(*[raw[rows[f]] for f in range(3)])):
            coef[rows[f]] = value

    def forward(source, target, low, high):
        def body(b, carry):
            at = pl.multiple_of(b * PITCH, 8)
            k = [coef[pl.ds(f * FIELD + at, PITCH)] for f in range(5)]
            for c in range(NC):
                base = c * FIELD + at
                here = source[pl.ds(base, PITCH)]
                target[pl.ds(base, PITCH)] = (
                    k[0] * here
                    + k[1] * source[pl.ds(base + PITCH, PITCH)]
                    + k[2] * source[pl.ds(base - PITCH, PITCH)]
                    + k[3] * pltpu.roll(here, PITCH - 1, 0)
                    + k[4] * pltpu.roll(here, 1, 0)
                )
            return carry

        lax.fori_loop(low, high, body, 0)

    buffers = [state_0, state_1]
    for step in range(STEPS):
        source, target = buffers[step % 2], buffers[(step + 1) % 2]
        forward(source, target, 2 + step, BLOCKS - 2 - step)
        own = jnp.concatenate(
            [
                jnp.concatenate(
                    [
                        target[c * FIELD + b * PITCH : c * FIELD + b * PITCH + CY]
                        for b in range(FIRST, FIRST + CX)
                    ],
                    axis=0,
                )
                for c in range(NC)
            ],
            axis=1,
        )
        rows = slice(step * CX * CY, (step + 1) * CX * CY)
        tops[rows], lows[rows] = split(own)


def main(
    coef,
    tops,
    lows,
    wide,
    slot_pick,
    slot_push,
    beam_pick,
    columns,
    *rest,
):
    beams, x_a = rest[:-6]
    out_a, out_b, out_core, state_0, state_1, forcing = rest[-6:]
    even, _, _ = place_on("gx")
    slots = columns.shape[0]
    gate_lane = lax.broadcasted_iota(jnp.int32, (slots, 128), 1).astype(f32)
    gate_here = gate_lane == columns[:, 2:3]
    scaled = columns[:, 3:4]
    for step in range(STEPS):
        rows = slice(step * CX * CY, (step + 1) * CX * CY)
        picked = jnp.dot(slot_pick[...], tops[rows], preferred_element_type=f32)
        picked = picked + jnp.dot(slot_pick[...], lows[rows], preferred_element_type=f32)
        picked = picked * wide[...]
        table = []
        for part, low in ((beams, 0), (x_a, X_HALO)):
            for at in range(low, part.shape[0], STEPS * OWN_BEAMS):
                first = at + step * OWN_BEAMS
                table.append(part[first : first + OWN_BEAMS])
        table = two_part_dot(beam_pick[...], jnp.concatenate(table, axis=0))
        tally = -jnp.where(gate_here, table, 0.0)
        for c in range(NC):
            tally = tally + picked[:, c * 128 : (c + 1) * 128]
        misfit = scaled * jnp.sum(tally, axis=1, keepdims=True)
        forcing[rows] = two_part_dot(slot_push[...], misfit * wide[...])

    buffers = [state_0, state_1]

    for c in range(NC):
        clear(state_0, c * FIELD, [0, 1, 2, 3, BLOCKS - 4, BLOCKS - 3, BLOCKS - 2, BLOCKS - 1])
        clear(state_1, c * FIELD, [1, 2, BLOCKS - 3, BLOCKS - 2])

    def add_forcing(ref, step):
        for c in range(NC):
            for x in range(CX):
                at = c * FIELD + (FIRST + x) * PITCH
                first = step * CX * CY + x * CY
                value = forcing[first : first + CY, c * 128 : (c + 1) * 128]
                if step == STEPS - 1:
                    ref[at : at + CY] = value
                    ref[at + CY : at + PITCH] = jnp.zeros((PITCH - CY, 128), f32)
                else:
                    ref[at : at + CY] += value

    def backward(source, target, low, high):
        def body(b, carry):
            at = pl.multiple_of(b * PITCH, 8)
            k = [
                coef[pl.ds(at, PITCH)],
                coef[pl.ds(FIELD + at - PITCH, PITCH)],
                coef[pl.ds(2 * FIELD + at + PITCH, PITCH)],
                coef[pl.ds(3 * FIELD + at, PITCH)],
                coef[pl.ds(4 * FIELD + at, PITCH)],
            ]
            for c in range(NC):
                base = c * FIELD + at
                here = source[pl.ds(base, PITCH)]
                target[pl.ds(base, PITCH)] = (
                    k[0] * here
                    + k[1] * source[pl.ds(base - PITCH, PITCH)]
                    + k[2] * source[pl.ds(base + PITCH, PITCH)]
                    + pltpu.roll(k[3] * here, 1, 0)
                    + pltpu.roll(k[4] * here, PITCH - 1, 0)
                )
            return carry

        lax.fori_loop(low, high, body, 0)

    for step in range(STEPS):
        source, target = buffers[step % 2], buffers[(step + 1) % 2]
        add_forcing(source, STEPS - 1 - step)
        backward(source, target, FIRST - 1 - step, FIRST + CX + 1 + step)
    final = buffers[STEPS % 2]

    for c in range(NC):
        at = c * FIELD + FIRST * PITCH
        out_core[c * CORE : (c + 1) * CORE] = final[at : at + CORE]
        for away, start, extra in WIDE:
            for source, target, size in (
                (PITCH - extra, 0, extra),
                (0, extra, CY + extra),
            ):
                if size:
                    at = c * FIELD + (FIRST - away) * PITCH + source
                    west = final[at : at + size]
                    at = c * FIELD + (FIRST + CX - 1 + away) * PITCH + source
                    east = final[at : at + size]
                    at = c * WIDE_ROWS + start + target
                    out_a[at : at + size] = jnp.where(even, east, west)
                    out_b[at : at + size] = jnp.where(even, west, east)


def add_x(ny, delta, picks, core, x_a, x_b, *rest):
    out_a, out_b, out_near, out_sums = rest[:4]
    out_others = rest[4:-2]
    merged = ny == 4
    field, sums = rest[-2:]
    even, _, _ = place_on("gy")
    total = picks.shape[1]
    rows = total * NC // ny
    field[...] = core[...]
    for c in range(NC):
        for away, start, extra in WIDE:
            for source, target, size in (
                (0, PITCH - extra, extra),
                (extra, 0, CY + extra),
            ):
                if size:
                    at = c * WIDE_ROWS + start + source
                    west, east = x_sides(x_a, x_b, pl.ds(at, size))
                    at = c * CORE + (away - 1) * PITCH + target
                    field[at : at + size] += west
                    at = c * CORE + (CX - away) * PITCH + target
                    field[at : at + size] += east
    for c in range(NC):
        for away in range(1, RIM + 1):
            north = field[pl.ds(c * CORE + CY - 1 + away, CX, stride=PITCH)]
            south = field[pl.ds(c * CORE + PITCH - away, CX, stride=PITCH)]
            at = (c * RIM + away - 1) * CX
            out_a[at : at + CX] = jnp.where(even, north, south)
            out_b[at : at + CX] = jnp.where(even, south, north)
        for x in range(CX):
            at = c * CORE + x * PITCH
            here = slice(x * CY, (x + 1) * CY)
            out_near[c, here] = delta[c, here] + field[at : at + CY]
    adjoint = jnp.concatenate([field[c * CORE : (c + 1) * CORE] for c in range(NC)], axis=1)
    tile_sums = two_part_dot(jnp.transpose(picks[...]).astype(bf16), adjoint)
    for c in range(NC):
        sums[pl.ds(c, total, stride=NC)] = tile_sums[:, c * 128 : (c + 1) * 128]
    out_sums[...] = sums[0:rows]
    out_a[Y_COEF:] = sums[rows : 2 * rows]
    if merged:
        out_b[Y_COEF:] = sums[3 * rows : 4 * rows]
    for s, other in enumerate(out_others):
        other[...] = sums[(2 + s) * rows : (3 + s) * rows]


def add_y(alpha, near, sums, y_a, y_b, *rest):
    others = rest[:-2]
    out_delta, out_alpha = rest[-2:]
    out_delta[...] = near[...]
    for c in range(NC):
        for away in range(1, RIM + 1):
            north, south = y_sides(y_a, y_b, pl.ds((c * RIM + away - 1) * CX, CX))
            high = pl.ds(CY - away, CX, stride=CY)
            low = pl.ds(away - 1, CX, stride=CY)
            out_delta[c, high] = out_delta[c, high] + north
            out_delta[c, low] = out_delta[c, low] + south
    total = sums[...] + y_a[Y_COEF:]
    if y_b.shape[0] > Y_COEF:
        total = total + y_b[Y_COEF:]
    for other in others:
        total = total + other[...]
    out_alpha[...] = alpha[...] + profile_weight * total


def on_device(
    delta,
    alpha,
    eddy,
    courant,
    tile_map,
    obs_rows,
    gate_beam,
    gate_index,
    gate_column,
    gate_live,
    obs_weight,
    obs_precision,
):
    nx = lax.axis_size("gx")
    ny = lax.axis_size("gy")
    owned = alpha.shape[1]
    slots = gate_column.shape[2]
    fine = delta.reshape(NC, CX * CY, 128)
    eddy = eddy.reshape(CX * CY, 128)
    courant = courant.reshape(2, CX * CY, 128)
    control = alpha.reshape(owned * NC, 128)
    weights = obs_weight.reshape(slots * NC, 128)
    gates = [
        value.reshape(1, slots)
        for value in (gate_beam, gate_index, gate_column, gate_live, obs_precision)
    ]
    own_beams = jnp.transpose(obs_rows, (1, 0, 2)).reshape(STEPS * OWN_BEAMS, 128)
    beam_count = nx * OWN_BEAMS
    rows = owned * NC
    total = ny * owned

    y_a, y_b, fine, coefs, control_near, near_tiles, meta, near_beams = call(
        pack_y,
        [
            (Y_HALO + rows, 128),
            (Y_HALO, 128),
            fine.shape,
            (3, CX * CY, 128),
            control.shape,
            (CX, 128),
            (8, slots),
            own_beams.shape,
        ],
        [
            pltpu.with_memory_space_constraint(value, pltpu.HBM)
            for value in (fine, eddy, courant, control, tile_map, *gates, own_beams)
        ],
        [
            pltpu.VMEM(tile_map.shape, jnp.int32),
            pltpu.VMEM((4, 1, slots), jnp.int32),
            pltpu.VMEM((1, slots), f32),
            pltpu.SemaphoreType.DMA((12,)),
        ],
        in_specs=[HBM] * 11,
    )
    y_a = swap(y_a, "gy", 1)
    y_b = pair_b(y_b, "gy", "gx")
    others = [swap(control, "gy", xor) for xor in range(2, ny)]
    beams, xor = near_beams, 2
    while xor < nx:
        beams = jnp.concatenate([beams, swap(beams, "gx", xor)])
        xor *= 2

    x_a, x_b = call(
        lambda *refs: pack_x(ny, *refs),
        [(X_HALO + beams.shape[0], 128), (X_HALO, 128)],
        [fine, coefs, control_near, near_tiles, y_a, y_b, beams, *others],
        [
            pltpu.VMEM((2 * RIM * PITCH, 128), f32),
            pltpu.VMEM((2 * RIM * PITCH, total), f32),
            pltpu.VMEM((total * NC, 128), f32),
            pltpu.VMEM((128, 128), f32),
        ],
    )
    x_a = swap(x_a, "gx", 1)
    x_b = pair_b(x_b, "gx", "gy")

    core, coef, picks, wide, slot_pick, slot_push, beam_pick, columns = call(
        lambda *refs: prepare(ny, *refs),
        [
            (NC * CORE, 128),
            (5 * CORE, 128),
            (CORE, total),
            (slots, NC * 128),
            jax.ShapeDtypeStruct((slots, CX * CY), bf16),
            jax.ShapeDtypeStruct((CX * CY, slots), bf16),
            jax.ShapeDtypeStruct((slots, beam_count), bf16),
            (slots, 8),
        ],
        [fine, coefs, control_near, near_tiles, meta, weights, y_a, y_b, *others],
        [
            pltpu.VMEM((total * NC, 128), f32),
            pltpu.VMEM((128, 128), f32),
        ],
        flops=3000000,
    )


    tops, lows, coef = call(
        forecast,
        [
            jax.ShapeDtypeStruct((STEPS * CX * CY, NC * 128), bf16),
            jax.ShapeDtypeStruct((STEPS * CX * CY, NC * 128), bf16),
            (5 * FIELD, 128),
        ],
        [core, coef, x_a, x_b],
        [
            pltpu.VMEM((NC * FIELD, 128), f32),
            pltpu.VMEM((NC * FIELD, 128), f32),
            pltpu.VMEM((3 * FIELD, 128), f32),
        ],
        flops=10000000,
    )
    back_a, back_b, core = call(
        main,
        [(X_COEF, 128), (X_COEF, 128), (NC * CORE, 128)],
        [coef, tops, lows, wide, slot_pick, slot_push, beam_pick, columns, beams, x_a],
        [
            pltpu.VMEM((NC * FIELD, 128), f32),
            pltpu.VMEM((NC * FIELD, 128), f32),
            pltpu.VMEM((STEPS * CX * CY, NC * 128), f32),
        ],
        flops=20000000,
    )
    x_a = swap(back_a, "gx", 1)
    x_b = pair_b(back_b, "gx", "gy")
    loose = [xor for xor in range(2, ny) if ny != 4 or xor != 3]
    back_a, back_b, near, sums, *back = call(
        lambda *refs: add_x(ny, *refs),
        [
            (Y_COEF + rows, 128),
            (Y_COEF + (rows if ny == 4 else 0), 128),
            fine.shape,
            (rows, 128),
        ]
        + [(rows, 128)] * len(loose),
        [fine, picks, core, x_a, x_b],
        [pltpu.VMEM((NC * CORE, 128), f32), pltpu.VMEM((total * NC, 128), f32)],
    )
    y_a = swap(back_a, "gy", 1)
    y_b = ring_b(back_b, "gy")
    others = [swap(value, "gy", xor) for xor, value in zip(loose, back)]
    grad_delta, grad_alpha = call(
        add_y,
        [fine.shape, control.shape],
        [control_near, near, sums, y_a, y_b, *others],
    )
    return grad_delta.reshape(delta.shape), grad_alpha.reshape(alpha.shape)


def solution(mesh):
    return jax.shard_map(
        on_device,
        mesh=mesh,
        in_specs=(
            P(None, "gx", "gy", None),
            P("gx", "gy", None, None),
            P("gx", "gy", None),
            P(None, "gx", "gy", None),
            P("gx", "gy"),
            P(("gx", "gy"), None, None),
            P("gx", "gy", None),
            P("gx", "gy", None),
            P("gx", "gy", None),
            P("gx", "gy", None),
            P("gx", "gy", None, None, None),
            P("gx", "gy", None),
        ),
        out_specs=(P(None, "gx", "gy", None), P("gx", "gy", None, None)),
        check_vma=False,
    )
```

```python
import jax
import jax.numpy as jnp
from jax import lax
from jax.experimental import pallas as pl
from jax.experimental.pallas import tpu as pltpu
from jax.sharding import PartitionSpec as P

STEPS = 3
RIM = 3
INNER = RIM - 1
NC = 4
CX = 16
CY = 16
BLOCKS = CX + 8
PITCH = CY + 8
FIRST = 4
FIELD = BLOCKS * PITCH
CORE = CX * PITCH
OWN_BEAMS = 8
BEAM_BITS = 3

profile_weight = 0.125
f32 = jnp.float32
bf16 = jnp.bfloat16

VMEM = pl.BlockSpec(memory_space=pltpu.VMEM)
HBM = pl.BlockSpec(memory_space=pltpu.HBM)


def call(body, outs, ins, scratch=(), in_specs=None, flops=1000000, limit=40 * 2**20):
    shapes = [
        out if isinstance(out, jax.ShapeDtypeStruct) else jax.ShapeDtypeStruct(out, f32)
        for out in outs
    ]
    size = sum(4 * value.size for value in ins)
    return pl.pallas_call(
        body,
        out_shape=shapes,
        in_specs=in_specs or [VMEM] * len(ins),
        out_specs=[VMEM] * len(shapes),
        scratch_shapes=list(scratch),
        compiler_params=pltpu.CompilerParams(vmem_limit_bytes=limit),
        cost_estimate=pl.CostEstimate(flops=flops, bytes_accessed=size, transcendentals=0),
    )(*ins)


def swap(block, axis, xor):
    return lax.ppermute(block, axis, [(i, i ^ xor) for i in range(lax.axis_size(axis))])


def pair_b(block, axis, other):
    count, across = lax.axis_size(axis), lax.axis_size(other)

    def place(i, j):
        return i * across + j if axis == "gx" else j * count + i

    pairs = []
    for j in range(across):
        for i in range(count):
            if i in (0, count - 1):
                pairs.append((place(i, j), place(i, j ^ 1)))
            else:
                pairs.append((place(i, j), place(i + 1 if i % 2 else i - 1, j)))
    return lax.ppermute(block, ("gx", "gy"), pairs)


def ring_b(block, axis):
    count = lax.axis_size(axis)
    pairs = [(i, (i + 1 if i % 2 else i - 1) % count) for i in range(count)]
    return lax.ppermute(block, axis, pairs)


def place_on(axis):
    me = lax.axis_index(axis)
    return lax.rem(me, 2) == 0, me > 0, me < lax.axis_size(axis) - 1


def split(value):
    top = value.astype(bf16)
    return top, (value - top.astype(f32)).astype(bf16)


def two_part_dot(left, value):
    top, low = split(value)
    return jnp.dot(left, top, preferred_element_type=f32) + jnp.dot(
        left, low, preferred_element_type=f32
    )


def layers(reach):
    found, at = [], 0
    for away in range(1, reach + 1):
        found.append((away, at, reach - away))
        at += CY + 2 * (reach - away)
    return found, at


WIDE, WIDE_ROWS = layers(RIM)
SLIM, SLIM_ROWS = layers(INNER)
X_COEF = NC * WIDE_ROWS
X_HALO = X_COEF + 3 * SLIM_ROWS

Y_COEF = NC * RIM * CX
Y_TILE = Y_COEF + 3 * INNER * CX
Y_HALO = Y_TILE + CX


def pack_y(
    delta,
    eddy,
    courant,
    alpha,
    tile_map,
    gate_beam,
    gate_index,
    gate_column,
    gate_live,
    precision,
    beam_rows,
    out_a,
    out_b,
    fine,
    coefs,
    profiles,
    near_tiles,
    meta,
    beams,
    tiles,
    gates,
    values,
    sems,
):
    even, _, _ = place_on("gy")
    moves = [
        pltpu.make_async_copy(source, target, sems.at[i])
        for i, (source, target) in enumerate(
            [
                (delta, fine),
                (eddy, coefs.at[0]),
                (courant.at[0], coefs.at[1]),
                (courant.at[1], coefs.at[2]),
                (tile_map, tiles),
                (alpha, profiles),
                (gate_beam, gates.at[0]),
                (gate_index, gates.at[1]),
                (gate_column, gates.at[2]),
                (gate_live, gates.at[3]),
                (precision, values),
                (beam_rows, beams),
            ]
        )
    ]
    for move in moves:
        move.start()
    for move in moves:
        move.wait()

    def put(at, field, away):
        north = field[pl.ds(CY - away, CX, stride=CY)]
        south = field[pl.ds(away - 1, CX, stride=CY)]
        out_a[at : at + CX] = jnp.where(even, north, south)
        out_b[at : at + CX] = jnp.where(even, south, north)

    for c in range(NC):
        for away in range(1, RIM + 1):
            put((c * RIM + away - 1) * CX, fine.at[c], away)
    for f in range(3):
        for away in range(1, INNER + 1):
            put(Y_COEF + (f * INNER + away - 1) * CX, coefs.at[f], away)
    near_tiles[...] = jnp.full((CX, 128), -1.0, f32)
    near_tiles[:, 0:CY] = tiles[...].astype(f32)
    for out in (out_a, out_b):
        out[Y_TILE : Y_TILE + CX] = near_tiles[...]
    out_a[Y_HALO:] = profiles[...]
    held = BEAM_BITS
    beam = gates[0]
    owner = jnp.bitwise_xor(beam >> held, lax.axis_index("gx"))
    block = (owner & -4) | ((owner & 1) << 1) | ((owner >> 1) & 1)
    meta[...] = jnp.zeros(meta.shape, f32)
    meta[0:1] = gates[2].astype(f32)
    meta[1:2] = ((block << held) | (beam & ((1 << held) - 1))).astype(f32)
    meta[2:3] = gates[1].astype(f32)
    meta[3:4] = gates[3].astype(f32) * values[...]


def y_sides(got_a, got_b, rows, fill=0.0):
    even, low, high = place_on("gy")
    first, second = got_a[rows], got_b[rows]
    north, south = jnp.where(even, first, second), jnp.where(even, second, first)
    return jnp.where(high, north, fill), jnp.where(low, south, fill)


def x_sides(got_a, got_b, rows):
    even, low, high = place_on("gx")
    first, second = got_a[rows], got_b[rows]
    west, east = jnp.where(even, second, first), jnp.where(even, first, second)
    return jnp.where(low, west, 0.0), jnp.where(high, east, 0.0)


def gather_known(alpha, got_a, others, known):
    owned = alpha.shape[0]
    known[0:owned] = alpha[...]
    known[owned : 2 * owned] = got_a[Y_HALO:]
    for s, other in enumerate(others):
        known[(2 + s) * owned : (3 + s) * owned] = other[...]


def tile_numbers(near_tiles, got_a, got_b, tiles):
    spot = lax.broadcasted_iota(jnp.int32, (CX, 128), 1)
    north, south = y_sides(got_a, got_b, pl.ds(Y_TILE, CX), -1.0)
    near = jnp.where(
        (spot >= CY) & (spot < CY + RIM),
        pltpu.roll(north, CY, 1),
        jnp.where((spot >= PITCH - RIM) & (spot < PITCH), pltpu.roll(south, PITCH - CY, 1), -1.0),
    )
    tiles[...] = jnp.full(tiles.shape, -1.0, f32)
    tiles[0:CX] = jnp.where(spot < CY, near_tiles[...], near)
    return jnp.transpose(tiles[...])[0:PITCH]


def tile_ids(ny, owned):
    me = lax.axis_index("gy")
    lane = lax.broadcasted_iota(jnp.int32, (1, ny * owned), 1)
    ids = lane
    for s in range(ny):
        here = (lane >= s * owned) & (lane < (s + 1) * owned)
        ids = jnp.where(here, jnp.bitwise_xor(me, s) * owned + lane - s * owned, ids)
    return ids.astype(f32)


def by_variable(ref, count):
    return jnp.concatenate([ref[pl.ds(c, count, stride=NC)] for c in range(NC)], axis=1)


def pack_x(ny, delta, coefs, alpha, near_tiles, y_a, y_b, *rest):
    others = rest[: ny - 2]
    out_a, out_b, field, picks, known, tiles = rest[ny - 2 :]
    even, _, _ = place_on("gx")
    owned = alpha.shape[0] // NC
    gather_known(alpha, y_a, others, known)
    turned = tile_numbers(near_tiles, y_a, y_b, tiles)
    ids = tile_ids(ny, owned)
    columns = [x for x in range(RIM)] + [CX - RIM + x for x in range(RIM)]
    for i, x in enumerate(columns):
        picks[i * PITCH : (i + 1) * PITCH] = (turned[:, x : x + 1] == ids).astype(f32)
    fine = two_part_dot(picks[...].astype(bf16), by_variable(known, ny * owned))

    def fill(own, y_base, reach, c):
        for i, x in enumerate(columns):
            at = i * PITCH
            field[at + CY : at + PITCH] = jnp.zeros((PITCH - CY, 128), f32)
            field[at : at + CY] = own[x * CY : (x + 1) * CY]
        for away in range(1, reach + 1):
            for first, base in ((0, 0), (CX - RIM, RIM * PITCH)):
                rows = pl.ds(y_base + (away - 1) * CX + first, RIM)
                north, south = y_sides(y_a, y_b, rows)
                field[pl.ds(base + CY - 1 + away, RIM, stride=PITCH)] = north
                field[pl.ds(base + PITCH - away, RIM, stride=PITCH)] = south
        if c is not None:
            field[...] += profile_weight * fine[:, c * 128 : (c + 1) * 128]

    def put(at, found):
        for away, start, extra in found:
            east, west = (2 * RIM - away) * PITCH, (away - 1) * PITCH
            here = at + start
            for source, target, size in (
                (PITCH - extra, 0, extra),
                (0, extra, CY + extra),
            ):
                if size:
                    first = field[east + source : east + source + size]
                    second = field[west + source : west + source + size]
                    rows = slice(here + target, here + target + size)
                    out_a[rows] = jnp.where(even, first, second)
                    out_b[rows] = jnp.where(even, second, first)

    for c in range(NC):
        fill(delta.at[c], c * RIM * CX, RIM, c)
        put(c * WIDE_ROWS, WIDE)
    for f in range(3):
        fill(coefs.at[f], Y_COEF + f * INNER * CX, INNER, None)
        put(X_COEF + f * SLIM_ROWS, SLIM)


def prepare(ny, delta, coefs, alpha, near_tiles, meta, weights, y_a, y_b, *rest):
    others = rest[: ny - 2]
    core, coef, picks, wide, slot_pick, slot_push, beam_pick, columns = rest[ny - 2 : ny + 6]
    known, tiles = rest[ny + 6 :]
    owned = alpha.shape[0] // NC

    def fill(ref, base, own, y_base, reach):
        for x in range(CX):
            at = base + x * PITCH
            ref[at : at + CY] = own[x * CY : (x + 1) * CY]
            ref[at + CY : at + PITCH] = jnp.zeros((PITCH - CY, 128), f32)
        for away in range(1, reach + 1):
            north, south = y_sides(y_a, y_b, pl.ds(y_base + (away - 1) * CX, CX))
            ref[pl.ds(base + CY - 1 + away, CX, stride=PITCH)] = north
            ref[pl.ds(base + PITCH - away, CX, stride=PITCH)] = south

    for c in range(NC):
        fill(core, c * CORE, delta.at[c], c * RIM * CX, RIM)
    for f in range(3):
        fill(coef, f * CORE, coefs.at[f], Y_COEF + f * INNER * CX, INNER)

    def combine(b, carry):
        at = pl.multiple_of(b * PITCH, 8)
        combined = combine_coefs(*[coef[pl.ds(f * CORE + at, PITCH)] for f in range(3)])
        for f, value in enumerate(combined):
            coef[pl.ds(f * CORE + at, PITCH)] = value
        return carry

    lax.fori_loop(0, CX, combine, 0)

    gather_known(alpha, y_a, others, known)
    turned = tile_numbers(near_tiles, y_a, y_b, tiles)
    ids = tile_ids(ny, owned)
    for x in range(CX):
        picks[x * PITCH : (x + 1) * PITCH] = (turned[:, x : x + 1] == ids).astype(f32)
    fine = two_part_dot(picks[...].astype(bf16), by_variable(known, ny * owned))
    for c in range(NC):
        core[c * CORE : (c + 1) * CORE] += profile_weight * fine[:, c * 128 : (c + 1) * 128]

    slots = meta.shape[1]
    for c in range(NC):
        wide[:, c * 128 : (c + 1) * 128] = weights[pl.ds(c, slots, stride=NC)]
    per_beam = beam_pick.shape[1]
    turned = jnp.transpose(meta[...])
    columns[...] = turned
    slot_lane = lax.broadcasted_iota(jnp.int32, (slots, CX * CY), 1).astype(f32)
    slot_pick[...] = (slot_lane == turned[:, 0:1]).astype(f32).astype(bf16)
    column_row = lax.broadcasted_iota(jnp.int32, (CX * CY, slots), 0).astype(f32)
    slot_push[...] = (column_row == meta[0:1]).astype(f32).astype(bf16)
    beam_lane = lax.broadcasted_iota(jnp.int32, (slots, per_beam), 1).astype(f32)
    beam_pick[...] = (beam_lane == turned[:, 1:2]).astype(f32).astype(bf16)


def combine_coefs(viscous, along_x, along_y):
    half_x, half_y = 0.5 * along_x, 0.5 * along_y
    return (
        1.0 - 4.0 * viscous,
        viscous - half_x,
        viscous + half_x,
        viscous - half_y,
        viscous + half_y,
    )


def clear(ref, base, blocks):
    for b in blocks:
        at = base + b * PITCH
        ref[at : at + PITCH] = jnp.zeros((PITCH, 128), f32)


def forecast(core, coef_core, x_a, x_b, tops, lows, coef, state_0, state_1, raw):
    def fill(ref, base, x_base, found):
        for away, start, extra in found:
            for source, target, size in (
                (0, PITCH - extra, extra),
                (extra, 0, CY + extra),
            ):
                if size:
                    at = x_base + start + source
                    west, east = x_sides(x_a, x_b, pl.ds(at, size))
                    at = base + (FIRST - away) * PITCH + target
                    ref[at : at + size] = west
                    at = base + (FIRST + CX - 1 + away) * PITCH + target
                    ref[at : at + size] = east

    rim = [FIRST - 3, FIRST - 2, FIRST - 1, FIRST + CX, FIRST + CX + 1, FIRST + CX + 2]
    for c in range(NC):
        at = c * FIELD + FIRST * PITCH
        state_0[at : at + CORE] = core[c * CORE : (c + 1) * CORE]
        clear(state_0, c * FIELD, rim)
        fill(state_0, c * FIELD, c * WIDE_ROWS, WIDE)
    for f in range(3):
        clear(raw, f * FIELD, rim[1:5])
        fill(raw, f * FIELD, X_COEF + f * SLIM_ROWS, SLIM)
    for f in range(5):
        at = f * FIELD + FIRST * PITCH
        coef[at : at + CORE] = coef_core[f * CORE : (f + 1) * CORE]
        clear(coef, f * FIELD, [0, 1, BLOCKS - 2, BLOCKS - 1])
    for b in rim[1:5]:
        rows = [slice(f * FIELD + b * PITCH, f * FIELD + (b + 1) * PITCH) for f in range(5)]
        for f, value in enumerate(combine_coefs(*[raw[rows[f]] for f in range(3)])):
            coef[rows[f]] = value

    def forward(source, target, low, high):
        def body(b, carry):
            at = pl.multiple_of(b * PITCH, 8)
            k = [coef[pl.ds(f * FIELD + at, PITCH)] for f in range(5)]
            for c in range(NC):
                base = c * FIELD + at
                here = source[pl.ds(base, PITCH)]
                target[pl.ds(base, PITCH)] = (
                    k[0] * here
                    + k[1] * source[pl.ds(base + PITCH, PITCH)]
                    + k[2] * source[pl.ds(base - PITCH, PITCH)]
                    + k[3] * pltpu.roll(here, PITCH - 1, 0)
                    + k[4] * pltpu.roll(here, 1, 0)
                )
            return carry

        lax.fori_loop(low, high, body, 0)

    buffers = [state_0, state_1]
    for step in range(STEPS):
        source, target = buffers[step % 2], buffers[(step + 1) % 2]
        forward(source, target, 2 + step, BLOCKS - 2 - step)
        own = jnp.concatenate(
            [
                jnp.concatenate(
                    [
                        target[c * FIELD + b * PITCH : c * FIELD + b * PITCH + CY]
                        for b in range(FIRST, FIRST + CX)
                    ],
                    axis=0,
                )
                for c in range(NC)
            ],
            axis=1,
        )
        rows = slice(step * CX * CY, (step + 1) * CX * CY)
        tops[rows], lows[rows] = split(own)


def main(
    coef,
    tops,
    lows,
    wide,
    slot_pick,
    slot_push,
    beam_pick,
    columns,
    *rest,
):
    beams = rest[:-6]
    out_a, out_b, out_core, state_0, state_1, forcing = rest[-6:]
    even, _, _ = place_on("gx")
    slots = columns.shape[0]
    gate_lane = lax.broadcasted_iota(jnp.int32, (slots, 128), 1).astype(f32)
    gate_here = gate_lane == columns[:, 2:3]
    scaled = columns[:, 3:4]
    for step in range(STEPS):
        rows = slice(step * CX * CY, (step + 1) * CX * CY)
        picked = jnp.dot(slot_pick[...], tops[rows], preferred_element_type=f32)
        picked = picked + jnp.dot(slot_pick[...], lows[rows], preferred_element_type=f32)
        picked = picked * wide[...]
        table = []
        for part in beams:
            for at in range(0, part.shape[0], STEPS * OWN_BEAMS):
                first = at + step * OWN_BEAMS
                table.append(part[first : first + OWN_BEAMS])
        table = two_part_dot(beam_pick[...], jnp.concatenate(table, axis=0))
        tally = -jnp.where(gate_here, table, 0.0)
        for c in range(NC):
            tally = tally + picked[:, c * 128 : (c + 1) * 128]
        misfit = scaled * jnp.sum(tally, axis=1, keepdims=True)
        forcing[rows] = two_part_dot(slot_push[...], misfit * wide[...])

    buffers = [state_0, state_1]

    for c in range(NC):
        clear(state_0, c * FIELD, [0, 1, 2, 3, BLOCKS - 4, BLOCKS - 3, BLOCKS - 2, BLOCKS - 1])
        clear(state_1, c * FIELD, [1, 2, BLOCKS - 3, BLOCKS - 2])

    def add_forcing(ref, step):
        for c in range(NC):
            for x in range(CX):
                at = c * FIELD + (FIRST + x) * PITCH
                first = step * CX * CY + x * CY
                value = forcing[first : first + CY, c * 128 : (c + 1) * 128]
                if step == STEPS - 1:
                    ref[at : at + CY] = value
                    ref[at + CY : at + PITCH] = jnp.zeros((PITCH - CY, 128), f32)
                else:
                    ref[at : at + CY] += value

    def backward(source, target, low, high):
        def body(b, carry):
            at = pl.multiple_of(b * PITCH, 8)
            k = [
                coef[pl.ds(at, PITCH)],
                coef[pl.ds(FIELD + at - PITCH, PITCH)],
                coef[pl.ds(2 * FIELD + at + PITCH, PITCH)],
                coef[pl.ds(3 * FIELD + at, PITCH)],
                coef[pl.ds(4 * FIELD + at, PITCH)],
            ]
            for c in range(NC):
                base = c * FIELD + at
                here = source[pl.ds(base, PITCH)]
                target[pl.ds(base, PITCH)] = (
                    k[0] * here
                    + k[1] * source[pl.ds(base - PITCH, PITCH)]
                    + k[2] * source[pl.ds(base + PITCH, PITCH)]
                    + pltpu.roll(k[3] * here, 1, 0)
                    + pltpu.roll(k[4] * here, PITCH - 1, 0)
                )
            return carry

        lax.fori_loop(low, high, body, 0)

    for step in range(STEPS):
        source, target = buffers[step % 2], buffers[(step + 1) % 2]
        add_forcing(source, STEPS - 1 - step)
        backward(source, target, FIRST - 1 - step, FIRST + CX + 1 + step)
    final = buffers[STEPS % 2]

    for c in range(NC):
        at = c * FIELD + FIRST * PITCH
        out_core[c * CORE : (c + 1) * CORE] = final[at : at + CORE]
        for away, start, extra in WIDE:
            for source, target, size in (
                (PITCH - extra, 0, extra),
                (0, extra, CY + extra),
            ):
                if size:
                    at = c * FIELD + (FIRST - away) * PITCH + source
                    west = final[at : at + size]
                    at = c * FIELD + (FIRST + CX - 1 + away) * PITCH + source
                    east = final[at : at + size]
                    at = c * WIDE_ROWS + start + target
                    out_a[at : at + size] = jnp.where(even, east, west)
                    out_b[at : at + size] = jnp.where(even, west, east)


def add_x(ny, delta, picks, core, x_a, x_b, *rest):
    out_a, out_b, out_near, out_sums = rest[:4]
    out_others = rest[4:-2]
    merged = ny == 4
    field, sums = rest[-2:]
    even, _, _ = place_on("gy")
    total = picks.shape[1]
    rows = total * NC // ny
    field[...] = core[...]
    for c in range(NC):
        for away, start, extra in WIDE:
            for source, target, size in (
                (0, PITCH - extra, extra),
                (extra, 0, CY + extra),
            ):
                if size:
                    at = c * WIDE_ROWS + start + source
                    west, east = x_sides(x_a, x_b, pl.ds(at, size))
                    at = c * CORE + (away - 1) * PITCH + target
                    field[at : at + size] += west
                    at = c * CORE + (CX - away) * PITCH + target
                    field[at : at + size] += east
    for c in range(NC):
        for away in range(1, RIM + 1):
            north = field[pl.ds(c * CORE + CY - 1 + away, CX, stride=PITCH)]
            south = field[pl.ds(c * CORE + PITCH - away, CX, stride=PITCH)]
            at = (c * RIM + away - 1) * CX
            out_a[at : at + CX] = jnp.where(even, north, south)
            out_b[at : at + CX] = jnp.where(even, south, north)
        for x in range(CX):
            at = c * CORE + x * PITCH
            here = slice(x * CY, (x + 1) * CY)
            out_near[c, here] = delta[c, here] + field[at : at + CY]
    adjoint = jnp.concatenate([field[c * CORE : (c + 1) * CORE] for c in range(NC)], axis=1)
    tile_sums = two_part_dot(jnp.transpose(picks[...]).astype(bf16), adjoint)
    for c in range(NC):
        sums[pl.ds(c, total, stride=NC)] = tile_sums[:, c * 128 : (c + 1) * 128]
    out_sums[...] = sums[0:rows]
    out_a[Y_COEF:] = sums[rows : 2 * rows]
    if merged:
        out_b[Y_COEF:] = sums[3 * rows : 4 * rows]
    for s, other in enumerate(out_others):
        other[...] = sums[(2 + s) * rows : (3 + s) * rows]


def add_y(alpha, near, sums, y_a, y_b, *rest):
    others = rest[:-2]
    out_delta, out_alpha = rest[-2:]
    out_delta[...] = near[...]
    for c in range(NC):
        for away in range(1, RIM + 1):
            north, south = y_sides(y_a, y_b, pl.ds((c * RIM + away - 1) * CX, CX))
            high = pl.ds(CY - away, CX, stride=CY)
            low = pl.ds(away - 1, CX, stride=CY)
            out_delta[c, high] = out_delta[c, high] + north
            out_delta[c, low] = out_delta[c, low] + south
    total = sums[...] + y_a[Y_COEF:]
    if y_b.shape[0] > Y_COEF:
        total = total + y_b[Y_COEF:]
    for other in others:
        total = total + other[...]
    out_alpha[...] = alpha[...] + profile_weight * total


def on_device(
    delta,
    alpha,
    eddy,
    courant,
    tile_map,
    obs_rows,
    gate_beam,
    gate_index,
    gate_column,
    gate_live,
    obs_weight,
    obs_precision,
):
    nx = lax.axis_size("gx")
    ny = lax.axis_size("gy")
    owned = alpha.shape[1]
    slots = gate_column.shape[2]
    fine = delta.reshape(NC, CX * CY, 128)
    eddy = eddy.reshape(CX * CY, 128)
    courant = courant.reshape(2, CX * CY, 128)
    control = alpha.reshape(owned * NC, 128)
    weights = obs_weight.reshape(slots * NC, 128)
    gates = [
        value.reshape(1, slots)
        for value in (gate_beam, gate_index, gate_column, gate_live, obs_precision)
    ]
    own_beams = jnp.transpose(obs_rows, (1, 0, 2)).reshape(STEPS * OWN_BEAMS, 128)
    beam_count = nx * OWN_BEAMS
    rows = owned * NC
    total = ny * owned

    y_a, y_b, fine, coefs, control_near, near_tiles, meta, near_beams = call(
        pack_y,
        [
            (Y_HALO + rows, 128),
            (Y_HALO, 128),
            fine.shape,
            (3, CX * CY, 128),
            control.shape,
            (CX, 128),
            (8, slots),
            own_beams.shape,
        ],
        [
            pltpu.with_memory_space_constraint(value, pltpu.HBM)
            for value in (fine, eddy, courant, control, tile_map, *gates, own_beams)
        ],
        [
            pltpu.VMEM(tile_map.shape, jnp.int32),
            pltpu.VMEM((4, 1, slots), jnp.int32),
            pltpu.VMEM((1, slots), f32),
            pltpu.SemaphoreType.DMA((12,)),
        ],
        in_specs=[HBM] * 11,
    )
    y_a = swap(y_a, "gy", 1)
    y_b = pair_b(y_b, "gy", "gx")
    others = [swap(control, "gy", xor) for xor in range(2, ny)]
    beams = jnp.concatenate([near_beams, swap(own_beams, "gx", 2)])
    beams = [beams] + [swap(beams, "gx", xor) for xor in range(1, nx) if xor % 4 < 2]

    x_a, x_b = call(
        lambda *refs: pack_x(ny, *refs),
        [(X_HALO, 128), (X_HALO, 128)],
        [fine, coefs, control_near, near_tiles, y_a, y_b, *others],
        [
            pltpu.VMEM((2 * RIM * PITCH, 128), f32),
            pltpu.VMEM((2 * RIM * PITCH, total), f32),
            pltpu.VMEM((total * NC, 128), f32),
            pltpu.VMEM((128, 128), f32),
        ],
    )
    x_a = swap(x_a, "gx", 1)
    x_b = pair_b(x_b, "gx", "gy")

    core, coef, picks, wide, slot_pick, slot_push, beam_pick, columns = call(
        lambda *refs: prepare(ny, *refs),
        [
            (NC * CORE, 128),
            (5 * CORE, 128),
            (CORE, total),
            (slots, NC * 128),
            jax.ShapeDtypeStruct((slots, CX * CY), bf16),
            jax.ShapeDtypeStruct((CX * CY, slots), bf16),
            jax.ShapeDtypeStruct((slots, beam_count), bf16),
            (slots, 8),
        ],
        [fine, coefs, control_near, near_tiles, meta, weights, y_a, y_b, *others],
        [
            pltpu.VMEM((total * NC, 128), f32),
            pltpu.VMEM((128, 128), f32),
        ],
        flops=3000000,
    )


    tops, lows, coef = call(
        forecast,
        [
            jax.ShapeDtypeStruct((STEPS * CX * CY, NC * 128), bf16),
            jax.ShapeDtypeStruct((STEPS * CX * CY, NC * 128), bf16),
            (5 * FIELD, 128),
        ],
        [core, coef, x_a, x_b],
        [
            pltpu.VMEM((NC * FIELD, 128), f32),
            pltpu.VMEM((NC * FIELD, 128), f32),
            pltpu.VMEM((3 * FIELD, 128), f32),
        ],
        flops=10000000,
    )
    back_a, back_b, core = call(
        main,
        [(X_COEF, 128), (X_COEF, 128), (NC * CORE, 128)],
        [coef, tops, lows, wide, slot_pick, slot_push, beam_pick, columns, *beams],
        [
            pltpu.VMEM((NC * FIELD, 128), f32),
            pltpu.VMEM((NC * FIELD, 128), f32),
            pltpu.VMEM((STEPS * CX * CY, NC * 128), f32),
        ],
        flops=20000000,
    )
    x_a = swap(back_a, "gx", 1)
    x_b = pair_b(back_b, "gx", "gy")
    loose = [xor for xor in range(2, ny) if ny != 4 or xor != 3]
    back_a, back_b, near, sums, *back = call(
        lambda *refs: add_x(ny, *refs),
        [
            (Y_COEF + rows, 128),
            (Y_COEF + (rows if ny == 4 else 0), 128),
            fine.shape,
            (rows, 128),
        ]
        + [(rows, 128)] * len(loose),
        [fine, picks, core, x_a, x_b],
        [pltpu.VMEM((NC * CORE, 128), f32), pltpu.VMEM((total * NC, 128), f32)],
    )
    y_a = swap(back_a, "gy", 1)
    y_b = ring_b(back_b, "gy")
    others = [swap(value, "gy", xor) for xor, value in zip(loose, back)]
    grad_delta, grad_alpha = call(
        add_y,
        [fine.shape, control.shape],
        [control_near, near, sums, y_a, y_b, *others],
    )
    return grad_delta.reshape(delta.shape), grad_alpha.reshape(alpha.shape)


def solution(mesh):
    return jax.shard_map(
        on_device,
        mesh=mesh,
        in_specs=(
            P(None, "gx", "gy", None),
            P("gx", "gy", None, None),
            P("gx", "gy", None),
            P(None, "gx", "gy", None),
            P("gx", "gy"),
            P(("gx", "gy"), None, None),
            P("gx", "gy", None),
            P("gx", "gy", None),
            P("gx", "gy", None),
            P("gx", "gy", None),
            P("gx", "gy", None, None, None),
            P("gx", "gy", None),
        ),
        out_specs=(P(None, "gx", "gy", None), P("gx", "gy", None, None)),
        check_vma=False,
    )
```

```python
import jax
import jax.numpy as jnp
from jax import lax
from jax.experimental import pallas as pl
from jax.experimental.pallas import tpu as pltpu
from jax.sharding import PartitionSpec as P

STEPS = 3
RIM = 3
INNER = RIM - 1
NC = 4
CX = 16
CY = 16
BLOCKS = CX + 8
PITCH = CY + 8
FIRST = 4
FIELD = BLOCKS * PITCH
CORE = CX * PITCH
OWN_BEAMS = 8
BEAM_BITS = 3

profile_weight = 0.125
f32 = jnp.float32
bf16 = jnp.bfloat16

VMEM = pl.BlockSpec(memory_space=pltpu.VMEM)
HBM = pl.BlockSpec(memory_space=pltpu.HBM)


def call(body, outs, ins, scratch=(), in_specs=None, flops=1000000, limit=40 * 2**20):
    shapes = [
        out if isinstance(out, jax.ShapeDtypeStruct) else jax.ShapeDtypeStruct(out, f32)
        for out in outs
    ]
    size = sum(4 * value.size for value in ins)
    return pl.pallas_call(
        body,
        out_shape=shapes,
        in_specs=in_specs or [VMEM] * len(ins),
        out_specs=[VMEM] * len(shapes),
        scratch_shapes=list(scratch),
        compiler_params=pltpu.CompilerParams(vmem_limit_bytes=limit),
        cost_estimate=pl.CostEstimate(flops=flops, bytes_accessed=size, transcendentals=0),
    )(*ins)


def swap(block, axis, xor):
    return lax.ppermute(block, axis, [(i, i ^ xor) for i in range(lax.axis_size(axis))])


def pair_b(block, axis, other):
    count, across = lax.axis_size(axis), lax.axis_size(other)

    def place(i, j):
        return i * across + j if axis == "gx" else j * count + i

    pairs = []
    for j in range(across):
        for i in range(count):
            if i in (0, count - 1):
                pairs.append((place(i, j), place(i, j ^ 1)))
            else:
                pairs.append((place(i, j), place(i + 1 if i % 2 else i - 1, j)))
    return lax.ppermute(block, ("gx", "gy"), pairs)


def place_on(axis):
    me = lax.axis_index(axis)
    return lax.rem(me, 2) == 0, me > 0, me < lax.axis_size(axis) - 1


def split(value):
    top = value.astype(bf16)
    return top, (value - top.astype(f32)).astype(bf16)


def two_part_dot(left, value):
    top, low = split(value)
    return jnp.dot(left, top, preferred_element_type=f32) + jnp.dot(
        left, low, preferred_element_type=f32
    )


def layers(reach):
    found, at = [], 0
    for away in range(1, reach + 1):
        found.append((away, at, reach - away))
        at += CY + 2 * (reach - away)
    return found, at


WIDE, WIDE_ROWS = layers(RIM)
SLIM, SLIM_ROWS = layers(INNER)
X_COEF = NC * WIDE_ROWS
X_CORNERS = 2 * INNER - 2
X_EXTRA = X_COEF + 3 * X_CORNERS
X_HALO = X_COEF + 3 * SLIM_ROWS

EARLY_BEAMS = 3 * INNER * CY
EARLY = EARLY_BEAMS + STEPS * OWN_BEAMS

Y_COEF = NC * RIM * CX
Y_TILE = Y_COEF + 3 * INNER * CX
Y_HALO = Y_TILE + CX


def pack_y(
    delta,
    eddy,
    courant,
    alpha,
    tile_map,
    gate_beam,
    gate_index,
    gate_column,
    gate_live,
    precision,
    beam_rows,
    out_a,
    out_b,
    early,
    fine,
    coefs,
    profiles,
    near_tiles,
    meta,
    tiles,
    gates,
    values,
    sems,
):
    even, _, _ = place_on("gy")
    moves = [
        pltpu.make_async_copy(source, target, sems.at[i])
        for i, (source, target) in enumerate(
            [
                (delta, fine),
                (eddy, coefs.at[0]),
                (courant.at[0], coefs.at[1]),
                (courant.at[1], coefs.at[2]),
                (tile_map, tiles),
                (alpha, profiles),
                (gate_beam, gates.at[0]),
                (gate_index, gates.at[1]),
                (gate_column, gates.at[2]),
                (gate_live, gates.at[3]),
                (precision, values),
                (beam_rows, early.at[pl.ds(EARLY_BEAMS, STEPS * OWN_BEAMS)]),
            ]
        )
    ]
    for move in moves:
        move.start()
    for move in moves:
        move.wait()

    def put(at, field, away):
        north = field[pl.ds(CY - away, CX, stride=CY)]
        south = field[pl.ds(away - 1, CX, stride=CY)]
        out_a[at : at + CX] = jnp.where(even, north, south)
        out_b[at : at + CX] = jnp.where(even, south, north)

    for c in range(NC):
        for away in range(1, RIM + 1):
            put((c * RIM + away - 1) * CX, fine.at[c], away)
    for f in range(3):
        for away in range(1, INNER + 1):
            put(Y_COEF + (f * INNER + away - 1) * CX, coefs.at[f], away)
    near_tiles[...] = jnp.full((CX, 128), -1.0, f32)
    near_tiles[:, 0:CY] = tiles[...].astype(f32)
    for out in (out_a, out_b):
        out[Y_TILE : Y_TILE + CX] = near_tiles[...]
    even_x, _, _ = place_on("gx")
    slim = INNER * CY
    for f in range(3):
        east, west = coefs[f, CX * CY - slim :], coefs[f, :slim]
        early[f * slim : (f + 1) * slim] = jnp.where(even_x, east, west)
    out_a[Y_HALO:] = profiles[...]
    held = BEAM_BITS
    beam = gates[0]
    owner = jnp.bitwise_xor(beam >> held, lax.axis_index("gx"))
    meta[...] = jnp.zeros(meta.shape, f32)
    meta[0:1] = gates[2].astype(f32)
    meta[1:2] = ((owner << held) | (beam & ((1 << held) - 1))).astype(f32)
    meta[2:3] = gates[1].astype(f32)
    meta[3:4] = gates[3].astype(f32) * values[...]


def y_sides(got_a, got_b, rows, fill=0.0):
    even, low, high = place_on("gy")
    first, second = got_a[rows], got_b[rows]
    north, south = jnp.where(even, first, second), jnp.where(even, second, first)
    return jnp.where(high, north, fill), jnp.where(low, south, fill)


def x_sides(got_a, got_b, rows):
    even, low, high = place_on("gx")
    first, second = got_a[rows], got_b[rows]
    west, east = jnp.where(even, second, first), jnp.where(even, first, second)
    return jnp.where(low, west, 0.0), jnp.where(high, east, 0.0)


def gather_known(alpha, got_a, others, known):
    owned = alpha.shape[0]
    known[0:owned] = alpha[...]
    known[owned : 2 * owned] = got_a[Y_HALO:]
    for s, other in enumerate(others):
        known[(2 + s) * owned : (3 + s) * owned] = other[...]


def tile_numbers(near_tiles, got_a, got_b, tiles):
    spot = lax.broadcasted_iota(jnp.int32, (CX, 128), 1)
    north, south = y_sides(got_a, got_b, pl.ds(Y_TILE, CX), -1.0)
    near = jnp.where(
        (spot >= CY) & (spot < CY + RIM),
        pltpu.roll(north, CY, 1),
        jnp.where((spot >= PITCH - RIM) & (spot < PITCH), pltpu.roll(south, PITCH - CY, 1), -1.0),
    )
    tiles[...] = jnp.full(tiles.shape, -1.0, f32)
    tiles[0:CX] = jnp.where(spot < CY, near_tiles[...], near)
    return jnp.transpose(tiles[...])[0:PITCH]


def tile_ids(ny, owned):
    me = lax.axis_index("gy")
    lane = lax.broadcasted_iota(jnp.int32, (1, ny * owned), 1)
    ids = lane
    for s in range(ny):
        here = (lane >= s * owned) & (lane < (s + 1) * owned)
        ids = jnp.where(here, jnp.bitwise_xor(me, s) * owned + lane - s * owned, ids)
    return ids.astype(f32)


def by_variable(ref, count):
    return jnp.concatenate([ref[pl.ds(c, count, stride=NC)] for c in range(NC)], axis=1)


def pack_x(ny, delta, coefs, alpha, near_tiles, y_a, y_b, *rest):
    others = rest[: ny - 2]
    out_a, out_b, field, picks, known, tiles = rest[ny - 2 :]
    even, _, _ = place_on("gx")
    owned = alpha.shape[0] // NC
    gather_known(alpha, y_a, others, known)
    turned = tile_numbers(near_tiles, y_a, y_b, tiles)
    ids = tile_ids(ny, owned)
    columns = [x for x in range(RIM)] + [CX - RIM + x for x in range(RIM)]
    for i, x in enumerate(columns):
        picks[i * PITCH : (i + 1) * PITCH] = (turned[:, x : x + 1] == ids).astype(f32)
    fine = two_part_dot(picks[...].astype(bf16), by_variable(known, ny * owned))

    def fill(own, y_base, reach, c):
        for i, x in enumerate(columns):
            at = i * PITCH
            field[at + CY : at + PITCH] = jnp.zeros((PITCH - CY, 128), f32)
            field[at : at + CY] = own[x * CY : (x + 1) * CY]
        for away in range(1, reach + 1):
            for first, base in ((0, 0), (CX - RIM, RIM * PITCH)):
                rows = pl.ds(y_base + (away - 1) * CX + first, RIM)
                north, south = y_sides(y_a, y_b, rows)
                field[pl.ds(base + CY - 1 + away, RIM, stride=PITCH)] = north
                field[pl.ds(base + PITCH - away, RIM, stride=PITCH)] = south
        if c is not None:
            field[...] += profile_weight * fine[:, c * 128 : (c + 1) * 128]

    def put(at, found, at_a=None):
        for away, start, extra in found:
            east, west = (2 * RIM - away) * PITCH, (away - 1) * PITCH
            here = at + start
            for source, target, size in (
                (PITCH - extra, 0, extra),
                (0, extra, CY + extra),
            ):
                if size:
                    first = field[east + source : east + source + size]
                    second = field[west + source : west + source + size]
                    rows = slice(here + target, here + target + size)
                    out_b[rows] = jnp.where(even, second, first)
                    if at_a is None:
                        out_a[rows] = jnp.where(even, first, second)
            if at_a is not None and extra:
                for row in (PITCH - extra, CY):
                    first = field[east + row : east + row + extra]
                    second = field[west + row : west + row + extra]
                    out_a[at_a : at_a + extra] = jnp.where(even, first, second)
                    at_a += extra

    for c in range(NC):
        fill(delta.at[c], c * RIM * CX, RIM, c)
        put(c * WIDE_ROWS, WIDE)
    for f in range(3):
        fill(coefs.at[f], Y_COEF + f * INNER * CX, INNER, None)
        put(X_COEF + f * SLIM_ROWS, SLIM, X_COEF + f * X_CORNERS)


def prepare(ny, delta, coefs, alpha, near_tiles, meta, weights, y_a, y_b, *rest):
    others = rest[: ny - 2]
    core, coef, picks, wide, slot_pick, slot_push, beam_pick, columns = rest[ny - 2 : ny + 6]
    known, tiles = rest[ny + 6 :]
    owned = alpha.shape[0] // NC

    def fill(ref, base, own, y_base, reach):
        for x in range(CX):
            at = base + x * PITCH
            ref[at : at + CY] = own[x * CY : (x + 1) * CY]
            ref[at + CY : at + PITCH] = jnp.zeros((PITCH - CY, 128), f32)
        for away in range(1, reach + 1):
            north, south = y_sides(y_a, y_b, pl.ds(y_base + (away - 1) * CX, CX))
            ref[pl.ds(base + CY - 1 + away, CX, stride=PITCH)] = north
            ref[pl.ds(base + PITCH - away, CX, stride=PITCH)] = south

    for c in range(NC):
        fill(core, c * CORE, delta.at[c], c * RIM * CX, RIM)
    for f in range(3):
        fill(coef, f * CORE, coefs.at[f], Y_COEF + f * INNER * CX, INNER)

    def combine(b, carry):
        at = pl.multiple_of(b * PITCH, 8)
        combined = combine_coefs(*[coef[pl.ds(f * CORE + at, PITCH)] for f in range(3)])
        for f, value in enumerate(combined):
            coef[pl.ds(f * CORE + at, PITCH)] = value
        return carry

    lax.fori_loop(0, CX, combine, 0)

    gather_known(alpha, y_a, others, known)
    turned = tile_numbers(near_tiles, y_a, y_b, tiles)
    ids = tile_ids(ny, owned)
    for x in range(CX):
        picks[x * PITCH : (x + 1) * PITCH] = (turned[:, x : x + 1] == ids).astype(f32)
    fine = two_part_dot(picks[...].astype(bf16), by_variable(known, ny * owned))
    for c in range(NC):
        core[c * CORE : (c + 1) * CORE] += profile_weight * fine[:, c * 128 : (c + 1) * 128]

    slots = meta.shape[1]
    for c in range(NC):
        wide[:, c * 128 : (c + 1) * 128] = weights[pl.ds(c, slots, stride=NC)]
    per_beam = beam_pick.shape[1]
    turned = jnp.transpose(meta[...])
    columns[...] = turned
    slot_lane = lax.broadcasted_iota(jnp.int32, (slots, CX * CY), 1).astype(f32)
    slot_pick[...] = (slot_lane == turned[:, 0:1]).astype(f32).astype(bf16)
    column_row = lax.broadcasted_iota(jnp.int32, (CX * CY, slots), 0).astype(f32)
    slot_push[...] = (column_row == meta[0:1]).astype(f32).astype(bf16)
    beam_lane = lax.broadcasted_iota(jnp.int32, (slots, per_beam), 1).astype(f32)
    beam_pick[...] = (beam_lane == turned[:, 1:2]).astype(f32).astype(bf16)


def combine_coefs(viscous, along_x, along_y):
    half_x, half_y = 0.5 * along_x, 0.5 * along_y
    return (
        1.0 - 4.0 * viscous,
        viscous - half_x,
        viscous + half_x,
        viscous - half_y,
        viscous + half_y,
    )


def clear(ref, base, blocks):
    for b in blocks:
        at = base + b * PITCH
        ref[at : at + PITCH] = jnp.zeros((PITCH, 128), f32)


def forecast(core, coef_core, early, x_a, x_b, tops, lows, coef, state_0, state_1, raw):
    def fill(ref, base, x_base, found):
        for away, start, extra in found:
            for source, target, size in (
                (0, PITCH - extra, extra),
                (extra, 0, CY + extra),
            ):
                if size:
                    at = x_base + start + source
                    west, east = x_sides(x_a, x_b, pl.ds(at, size))
                    at = base + (FIRST - away) * PITCH + target
                    ref[at : at + size] = west
                    at = base + (FIRST + CX - 1 + away) * PITCH + target
                    ref[at : at + size] = east

    even, has_west, has_east = place_on("gx")
    rim = [FIRST - 3, FIRST - 2, FIRST - 1, FIRST + CX, FIRST + CX + 1, FIRST + CX + 2]
    for c in range(NC):
        at = c * FIELD + FIRST * PITCH
        state_0[at : at + CORE] = core[c * CORE : (c + 1) * CORE]
        clear(state_0, c * FIELD, rim)
        fill(state_0, c * FIELD, c * WIDE_ROWS, WIDE)
    for f in range(3):
        clear(raw, f * FIELD, rim[1:5])
        at_a = X_COEF + f * X_CORNERS
        for away, start, extra in SLIM:
            inner = f * INNER * CY
            west_a = early[pl.ds(inner + (INNER - away) * CY, CY)]
            east_a = early[pl.ds(inner + (away - 1) * CY, CY)]
            pieces = [(0, extra, CY, west_a, east_a)]
            if extra:
                for row, source in ((PITCH - extra, 0), (CY, extra + CY)):
                    value = x_a[at_a : at_a + extra]
                    pieces.append((row, source, extra, value, value))
                    at_a += extra
            for row, source, size, west_a, east_a in pieces:
                at = X_COEF + f * SLIM_ROWS + start + source
                value = x_b[at : at + size]
                west, east = jnp.where(even, value, west_a), jnp.where(even, east_a, value)
                at = f * FIELD + (FIRST - away) * PITCH + row
                raw[at : at + size] = jnp.where(has_west, west, 0.0)
                at = f * FIELD + (FIRST + CX - 1 + away) * PITCH + row
                raw[at : at + size] = jnp.where(has_east, east, 0.0)
    for f in range(5):
        at = f * FIELD + FIRST * PITCH
        coef[at : at + CORE] = coef_core[f * CORE : (f + 1) * CORE]
        clear(coef, f * FIELD, [0, 1, BLOCKS - 2, BLOCKS - 1])
    for b in rim[1:5]:
        rows = [slice(f * FIELD + b * PITCH, f * FIELD + (b + 1) * PITCH) for f in range(5)]
        for f, value in enumerate(combine_coefs(*[raw[rows[f]] for f in range(3)])):
            coef[rows[f]] = value

    def forward(source, target, low, high):
        def body(b, carry):
            at = pl.multiple_of(b * PITCH, 8)
            k = [coef[pl.ds(f * FIELD + at, PITCH)] for f in range(5)]
            for c in range(NC):
                base = c * FIELD + at
                here = source[pl.ds(base, PITCH)]
                target[pl.ds(base, PITCH)] = (
                    k[0] * here
                    + k[1] * source[pl.ds(base + PITCH, PITCH)]
                    + k[2] * source[pl.ds(base - PITCH, PITCH)]
                    + k[3] * pltpu.roll(here, PITCH - 1, 0)
                    + k[4] * pltpu.roll(here, 1, 0)
                )
            return carry

        lax.fori_loop(low, high, body, 0)

    buffers = [state_0, state_1]
    for step in range(STEPS):
        source, target = buffers[step % 2], buffers[(step + 1) % 2]
        forward(source, target, 2 + step, BLOCKS - 2 - step)
        own = jnp.concatenate(
            [
                jnp.concatenate(
                    [
                        target[c * FIELD + b * PITCH : c * FIELD + b * PITCH + CY]
                        for b in range(FIRST, FIRST + CX)
                    ],
                    axis=0,
                )
                for c in range(NC)
            ],
            axis=1,
        )
        rows = slice(step * CX * CY, (step + 1) * CX * CY)
        tops[rows], lows[rows] = split(own)


def main(
    coef,
    tops,
    lows,
    wide,
    slot_pick,
    slot_push,
    beam_pick,
    columns,
    *rest,
):
    beams = rest[:-6]
    out_a, out_b, out_core, state_0, state_1, forcing = rest[-6:]
    even, _, _ = place_on("gx")
    slots = columns.shape[0]
    gate_lane = lax.broadcasted_iota(jnp.int32, (slots, 128), 1).astype(f32)
    gate_here = gate_lane == columns[:, 2:3]
    scaled = columns[:, 3:4]
    for step in range(STEPS):
        rows = slice(step * CX * CY, (step + 1) * CX * CY)
        picked = jnp.dot(slot_pick[...], tops[rows], preferred_element_type=f32)
        picked = picked + jnp.dot(slot_pick[...], lows[rows], preferred_element_type=f32)
        picked = picked * wide[...]
        table = []
        for part in beams:
            for at in range(0, part.shape[0], STEPS * OWN_BEAMS):
                first = at + step * OWN_BEAMS
                table.append(part[first : first + OWN_BEAMS])
        table = two_part_dot(beam_pick[...], jnp.concatenate(table, axis=0))
        tally = -jnp.where(gate_here, table, 0.0)
        for c in range(NC):
            tally = tally + picked[:, c * 128 : (c + 1) * 128]
        misfit = scaled * jnp.sum(tally, axis=1, keepdims=True)
        forcing[rows] = two_part_dot(slot_push[...], misfit * wide[...])

    buffers = [state_0, state_1]

    for c in range(NC):
        clear(state_0, c * FIELD, [0, 1, 2, 3, BLOCKS - 4, BLOCKS - 3, BLOCKS - 2, BLOCKS - 1])
        clear(state_1, c * FIELD, [1, 2, BLOCKS - 3, BLOCKS - 2])

    def add_forcing(ref, step):
        for c in range(NC):
            for x in range(CX):
                at = c * FIELD + (FIRST + x) * PITCH
                first = step * CX * CY + x * CY
                value = forcing[first : first + CY, c * 128 : (c + 1) * 128]
                if step == STEPS - 1:
                    ref[at : at + CY] = value
                    ref[at + CY : at + PITCH] = jnp.zeros((PITCH - CY, 128), f32)
                else:
                    ref[at : at + CY] += value

    def backward(source, target, low, high):
        def body(b, carry):
            at = pl.multiple_of(b * PITCH, 8)
            k = [
                coef[pl.ds(at, PITCH)],
                coef[pl.ds(FIELD + at - PITCH, PITCH)],
                coef[pl.ds(2 * FIELD + at + PITCH, PITCH)],
                coef[pl.ds(3 * FIELD + at, PITCH)],
                coef[pl.ds(4 * FIELD + at, PITCH)],
            ]
            for c in range(NC):
                base = c * FIELD + at
                here = source[pl.ds(base, PITCH)]
                target[pl.ds(base, PITCH)] = (
                    k[0] * here
                    + k[1] * source[pl.ds(base - PITCH, PITCH)]
                    + k[2] * source[pl.ds(base + PITCH, PITCH)]
                    + pltpu.roll(k[3] * here, 1, 0)
                    + pltpu.roll(k[4] * here, PITCH - 1, 0)
                )
            return carry

        lax.fori_loop(low, high, body, 0)

    for step in range(STEPS):
        source, target = buffers[step % 2], buffers[(step + 1) % 2]
        add_forcing(source, STEPS - 1 - step)
        backward(source, target, FIRST - 1 - step, FIRST + CX + 1 + step)
    final = buffers[STEPS % 2]

    for c in range(NC):
        at = c * FIELD + FIRST * PITCH
        out_core[c * CORE : (c + 1) * CORE] = final[at : at + CORE]
        for away, start, extra in WIDE:
            for source, target, size in (
                (PITCH - extra, 0, extra),
                (0, extra, CY + extra),
            ):
                if size:
                    at = c * FIELD + (FIRST - away) * PITCH + source
                    west = final[at : at + size]
                    at = c * FIELD + (FIRST + CX - 1 + away) * PITCH + source
                    east = final[at : at + size]
                    at = c * WIDE_ROWS + start + target
                    out_a[at : at + size] = jnp.where(even, east, west)
                    out_b[at : at + size] = jnp.where(even, west, east)


def add_x(ny, delta, picks, core, x_a, x_b, *rest):
    out_a, out_b, out_near, out_sums = rest[:4]
    out_others = rest[4:-2]
    field, sums = rest[-2:]
    even, _, _ = place_on("gy")
    total = picks.shape[1]
    rows = total * NC // ny
    field[...] = core[...]
    for c in range(NC):
        for away, start, extra in WIDE:
            for source, target, size in (
                (0, PITCH - extra, extra),
                (extra, 0, CY + extra),
            ):
                if size:
                    at = c * WIDE_ROWS + start + source
                    west, east = x_sides(x_a, x_b, pl.ds(at, size))
                    at = c * CORE + (away - 1) * PITCH + target
                    field[at : at + size] += west
                    at = c * CORE + (CX - away) * PITCH + target
                    field[at : at + size] += east
    for c in range(NC):
        for away in range(1, RIM + 1):
            north = field[pl.ds(c * CORE + CY - 1 + away, CX, stride=PITCH)]
            south = field[pl.ds(c * CORE + PITCH - away, CX, stride=PITCH)]
            at = (c * RIM + away - 1) * CX
            out_a[at : at + CX] = jnp.where(even, north, south)
            out_b[at : at + CX] = jnp.where(even, south, north)
        for x in range(CX):
            at = c * CORE + x * PITCH
            here = slice(x * CY, (x + 1) * CY)
            out_near[c, here] = delta[c, here] + field[at : at + CY]
    adjoint = jnp.concatenate([field[c * CORE : (c + 1) * CORE] for c in range(NC)], axis=1)
    tile_sums = two_part_dot(jnp.transpose(picks[...]).astype(bf16), adjoint)
    for c in range(NC):
        sums[pl.ds(c, total, stride=NC)] = tile_sums[:, c * 128 : (c + 1) * 128]
    out_sums[...] = sums[0:rows]
    out_a[Y_COEF:] = sums[rows : 2 * rows]
    for s, other in enumerate(out_others):
        other[...] = sums[(2 + s) * rows : (3 + s) * rows]


def add_y(alpha, near, sums, y_a, y_b, *rest):
    others = rest[:-2]
    out_delta, out_alpha = rest[-2:]
    out_delta[...] = near[...]
    for c in range(NC):
        for away in range(1, RIM + 1):
            north, south = y_sides(y_a, y_b, pl.ds((c * RIM + away - 1) * CX, CX))
            high = pl.ds(CY - away, CX, stride=CY)
            low = pl.ds(away - 1, CX, stride=CY)
            out_delta[c, high] = out_delta[c, high] + north
            out_delta[c, low] = out_delta[c, low] + south
    total = sums[...] + y_a[Y_COEF:]
    for other in others:
        total = total + other[...]
    out_alpha[...] = alpha[...] + profile_weight * total


def on_device(
    delta,
    alpha,
    eddy,
    courant,
    tile_map,
    obs_rows,
    gate_beam,
    gate_index,
    gate_column,
    gate_live,
    obs_weight,
    obs_precision,
):
    nx = lax.axis_size("gx")
    ny = lax.axis_size("gy")
    owned = alpha.shape[1]
    slots = gate_column.shape[2]
    fine = delta.reshape(NC, CX * CY, 128)
    eddy = eddy.reshape(CX * CY, 128)
    courant = courant.reshape(2, CX * CY, 128)
    control = alpha.reshape(owned * NC, 128)
    weights = obs_weight.reshape(slots * NC, 128)
    gates = [
        value.reshape(1, slots)
        for value in (gate_beam, gate_index, gate_column, gate_live, obs_precision)
    ]
    own_beams = jnp.transpose(obs_rows, (1, 0, 2)).reshape(STEPS * OWN_BEAMS, 128)
    beam_count = nx * OWN_BEAMS
    rows = owned * NC
    total = ny * owned

    y_a, y_b, early, fine, coefs, control_near, near_tiles, meta = call(
        pack_y,
        [
            (Y_HALO + rows, 128),
            (Y_HALO, 128),
            (EARLY, 128),
            fine.shape,
            (3, CX * CY, 128),
            control.shape,
            (CX, 128),
            (8, slots),
        ],
        [
            pltpu.with_memory_space_constraint(value, pltpu.HBM)
            for value in (fine, eddy, courant, control, tile_map, *gates, own_beams)
        ],
        [
            pltpu.VMEM(tile_map.shape, jnp.int32),
            pltpu.VMEM((4, 1, slots), jnp.int32),
            pltpu.VMEM((1, slots), f32),
            pltpu.SemaphoreType.DMA((12,)),
        ],
        in_specs=[HBM] * 11,
    )
    y_a = swap(y_a, "gy", 1)
    y_b = pair_b(y_b, "gy", "gx")
    others = [swap(control, "gy", xor) for xor in range(2, ny)]
    got_early = swap(early, "gx", 1)
    beams = jnp.concatenate([early[EARLY_BEAMS:], got_early[EARLY_BEAMS:]])
    beams = [beams] + [swap(beams, "gx", xor) for xor in range(2, nx, 2)]

    x_a, x_b = call(
        lambda *refs: pack_x(ny, *refs),
        [(X_EXTRA, 128), (X_HALO, 128)],
        [fine, coefs, control_near, near_tiles, y_a, y_b, *others],
        [
            pltpu.VMEM((2 * RIM * PITCH, 128), f32),
            pltpu.VMEM((2 * RIM * PITCH, total), f32),
            pltpu.VMEM((total * NC, 128), f32),
            pltpu.VMEM((128, 128), f32),
        ],
    )
    x_a = swap(x_a, "gx", 1)
    x_b = pair_b(x_b, "gx", "gy")

    core, coef, picks, wide, slot_pick, slot_push, beam_pick, columns = call(
        lambda *refs: prepare(ny, *refs),
        [
            (NC * CORE, 128),
            (5 * CORE, 128),
            (CORE, total),
            (slots, NC * 128),
            jax.ShapeDtypeStruct((slots, CX * CY), bf16),
            jax.ShapeDtypeStruct((CX * CY, slots), bf16),
            jax.ShapeDtypeStruct((slots, beam_count), bf16),
            (slots, 8),
        ],
        [fine, coefs, control_near, near_tiles, meta, weights, y_a, y_b, *others],
        [
            pltpu.VMEM((total * NC, 128), f32),
            pltpu.VMEM((128, 128), f32),
        ],
        flops=3000000,
    )


    tops, lows, coef = call(
        forecast,
        [
            jax.ShapeDtypeStruct((STEPS * CX * CY, NC * 128), bf16),
            jax.ShapeDtypeStruct((STEPS * CX * CY, NC * 128), bf16),
            (5 * FIELD, 128),
        ],
        [core, coef, got_early, x_a, x_b],
        [
            pltpu.VMEM((NC * FIELD, 128), f32),
            pltpu.VMEM((NC * FIELD, 128), f32),
            pltpu.VMEM((3 * FIELD, 128), f32),
        ],
        flops=10000000,
    )
    back_a, back_b, core = call(
        main,
        [(X_COEF, 128), (X_COEF, 128), (NC * CORE, 128)],
        [coef, tops, lows, wide, slot_pick, slot_push, beam_pick, columns, *beams],
        [
            pltpu.VMEM((NC * FIELD, 128), f32),
            pltpu.VMEM((NC * FIELD, 128), f32),
            pltpu.VMEM((STEPS * CX * CY, NC * 128), f32),
        ],
        flops=20000000,
    )
    x_a = swap(back_a, "gx", 1)
    x_b = pair_b(back_b, "gx", "gy")
    back_a, back_b, near, sums, *back = call(
        lambda *refs: add_x(ny, *refs),
        [
            (Y_COEF + rows, 128),
            (Y_COEF, 128),
            fine.shape,
            (rows, 128),
        ]
        + [(rows, 128)] * (ny - 2),
        [fine, picks, core, x_a, x_b],
        [pltpu.VMEM((NC * CORE, 128), f32), pltpu.VMEM((total * NC, 128), f32)],
    )
    y_a = swap(back_a, "gy", 1)
    y_b = pair_b(back_b, "gy", "gx")
    others = [swap(value, "gy", xor) for xor, value in zip(range(2, ny), back)]
    grad_delta, grad_alpha = call(
        add_y,
        [fine.shape, control.shape],
        [control_near, near, sums, y_a, y_b, *others],
    )
    return grad_delta.reshape(delta.shape), grad_alpha.reshape(alpha.shape)


def solution(mesh):
    return jax.shard_map(
        on_device,
        mesh=mesh,
        in_specs=(
            P(None, "gx", "gy", None),
            P("gx", "gy", None, None),
            P("gx", "gy", None),
            P(None, "gx", "gy", None),
            P("gx", "gy"),
            P(("gx", "gy"), None, None),
            P("gx", "gy", None),
            P("gx", "gy", None),
            P("gx", "gy", None),
            P("gx", "gy", None),
            P("gx", "gy", None, None, None),
            P("gx", "gy", None),
        ),
        out_specs=(P(None, "gx", "gy", None), P("gx", "gy", None, None)),
        check_vma=False,
    )
```

```python
import jax
import jax.numpy as jnp
from jax import lax
from jax.experimental import pallas as pl
from jax.experimental.pallas import tpu as pltpu
from jax.sharding import PartitionSpec as P

STEPS = 3
RIM = 3
INNER = RIM - 1
NC = 4
CX = 16
CY = 16
BLOCKS = CX + 8
PITCH = CY + 8
FIRST = 4
FIELD = BLOCKS * PITCH
CORE = CX * PITCH
OWN_BEAMS = 8
BEAM_BITS = 3

profile_weight = 0.125
f32 = jnp.float32
bf16 = jnp.bfloat16

VMEM = pl.BlockSpec(memory_space=pltpu.VMEM)
HBM = pl.BlockSpec(memory_space=pltpu.HBM)


def call(body, outs, ins, scratch=(), in_specs=None, flops=1000000, limit=40 * 2**20):
    shapes = [
        out if isinstance(out, jax.ShapeDtypeStruct) else jax.ShapeDtypeStruct(out, f32)
        for out in outs
    ]
    size = sum(4 * value.size for value in ins)
    return pl.pallas_call(
        body,
        out_shape=shapes,
        in_specs=in_specs or [VMEM] * len(ins),
        out_specs=[VMEM] * len(shapes),
        scratch_shapes=list(scratch),
        compiler_params=pltpu.CompilerParams(vmem_limit_bytes=limit),
        cost_estimate=pl.CostEstimate(flops=flops, bytes_accessed=size, transcendentals=0),
    )(*ins)


def swap(block, axis, xor):
    return lax.ppermute(block, axis, [(i, i ^ xor) for i in range(lax.axis_size(axis))])


def pair_b(block, axis, other):
    count, across = lax.axis_size(axis), lax.axis_size(other)

    def place(i, j):
        return i * across + j if axis == "gx" else j * count + i

    pairs = []
    for j in range(across):
        for i in range(count):
            if i in (0, count - 1):
                pairs.append((place(i, j), place(i, j ^ 1)))
            else:
                pairs.append((place(i, j), place(i + 1 if i % 2 else i - 1, j)))
    return lax.ppermute(block, ("gx", "gy"), pairs)


def ring_b(block, axis):
    count = lax.axis_size(axis)
    pairs = [(i, (i + 1 if i % 2 else i - 1) % count) for i in range(count)]
    return lax.ppermute(block, axis, pairs)


def place_on(axis):
    me = lax.axis_index(axis)
    return lax.rem(me, 2) == 0, me > 0, me < lax.axis_size(axis) - 1


def split(value):
    top = value.astype(bf16)
    return top, (value - top.astype(f32)).astype(bf16)


def two_part_dot(left, value):
    top, low = split(value)
    return jnp.dot(left, top, preferred_element_type=f32) + jnp.dot(
        left, low, preferred_element_type=f32
    )


def layers(reach):
    found, at = [], 0
    for away in range(1, reach + 1):
        found.append((away, at, reach - away))
        at += CY + 2 * (reach - away)
    return found, at


WIDE, WIDE_ROWS = layers(RIM)
SLIM, SLIM_ROWS = layers(INNER)
X_COEF = NC * WIDE_ROWS
X_CORNERS = 2 * INNER - 2
X_EXTRA = X_COEF + 3 * X_CORNERS
X_HALO = X_COEF + 3 * SLIM_ROWS

EARLY_BEAMS = 3 * INNER * CY
EARLY = EARLY_BEAMS + STEPS * OWN_BEAMS

Y_COEF = NC * RIM * CX
Y_TILE = Y_COEF + 3 * INNER * CX
Y_HALO = Y_TILE + CX


def pack_y(
    delta,
    eddy,
    courant,
    alpha,
    tile_map,
    gate_beam,
    gate_index,
    gate_column,
    gate_live,
    precision,
    beam_rows,
    out_a,
    out_b,
    early,
    fine,
    coefs,
    profiles,
    near_tiles,
    meta,
    tiles,
    gates,
    values,
    sems,
):
    even, _, _ = place_on("gy")
    moves = [
        pltpu.make_async_copy(source, target, sems.at[i])
        for i, (source, target) in enumerate(
            [
                (delta, fine),
                (eddy, coefs.at[0]),
                (courant.at[0], coefs.at[1]),
                (courant.at[1], coefs.at[2]),
                (tile_map, tiles),
                (alpha, profiles),
                (gate_beam, gates.at[0]),
                (gate_index, gates.at[1]),
                (gate_column, gates.at[2]),
                (gate_live, gates.at[3]),
                (precision, values),
                (beam_rows, early.at[pl.ds(EARLY_BEAMS, STEPS * OWN_BEAMS)]),
            ]
        )
    ]
    for move in moves:
        move.start()
    for move in moves:
        move.wait()

    def put(at, field, away):
        north = field[pl.ds(CY - away, CX, stride=CY)]
        south = field[pl.ds(away - 1, CX, stride=CY)]
        out_a[at : at + CX] = jnp.where(even, north, south)
        out_b[at : at + CX] = jnp.where(even, south, north)

    for c in range(NC):
        for away in range(1, RIM + 1):
            put((c * RIM + away - 1) * CX, fine.at[c], away)
    for f in range(3):
        for away in range(1, INNER + 1):
            put(Y_COEF + (f * INNER + away - 1) * CX, coefs.at[f], away)
    near_tiles[...] = jnp.full((CX, 128), -1.0, f32)
    near_tiles[:, 0:CY] = tiles[...].astype(f32)
    for out in (out_a, out_b):
        out[Y_TILE : Y_TILE + CX] = near_tiles[...]
    even_x, _, _ = place_on("gx")
    slim = INNER * CY
    for f in range(3):
        east, west = coefs[f, CX * CY - slim :], coefs[f, :slim]
        early[f * slim : (f + 1) * slim] = jnp.where(even_x, east, west)
    out_a[Y_HALO:] = profiles[...]
    held = BEAM_BITS
    beam = gates[0]
    owner = jnp.bitwise_xor(beam >> held, lax.axis_index("gx"))
    meta[...] = jnp.zeros(meta.shape, f32)
    meta[0:1] = gates[2].astype(f32)
    meta[1:2] = ((owner << held) | (beam & ((1 << held) - 1))).astype(f32)
    meta[2:3] = gates[1].astype(f32)
    meta[3:4] = gates[3].astype(f32) * values[...]


def y_sides(got_a, got_b, rows, fill=0.0):
    even, low, high = place_on("gy")
    first, second = got_a[rows], got_b[rows]
    north, south = jnp.where(even, first, second), jnp.where(even, second, first)
    return jnp.where(high, north, fill), jnp.where(low, south, fill)


def x_sides(got_a, got_b, rows):
    even, low, high = place_on("gx")
    first, second = got_a[rows], got_b[rows]
    west, east = jnp.where(even, second, first), jnp.where(even, first, second)
    return jnp.where(low, west, 0.0), jnp.where(high, east, 0.0)


def gather_known(alpha, got_a, others, known):
    owned = alpha.shape[0]
    known[0:owned] = alpha[...]
    known[owned : 2 * owned] = got_a[Y_HALO:]
    known[2 * owned :] = others[0][...]


def tile_numbers(near_tiles, got_a, got_b, tiles):
    spot = lax.broadcasted_iota(jnp.int32, (CX, 128), 1)
    north, south = y_sides(got_a, got_b, pl.ds(Y_TILE, CX), -1.0)
    near = jnp.where(
        (spot >= CY) & (spot < CY + RIM),
        pltpu.roll(north, CY, 1),
        jnp.where((spot >= PITCH - RIM) & (spot < PITCH), pltpu.roll(south, PITCH - CY, 1), -1.0),
    )
    tiles[...] = jnp.full(tiles.shape, -1.0, f32)
    tiles[0:CX] = jnp.where(spot < CY, near_tiles[...], near)
    return jnp.transpose(tiles[...])[0:PITCH]


def tile_ids(ny, owned):
    me = lax.axis_index("gy")
    lane = lax.broadcasted_iota(jnp.int32, (1, ny * owned), 1)
    ids = lane
    for s in range(ny):
        here = (lane >= s * owned) & (lane < (s + 1) * owned)
        ids = jnp.where(here, jnp.bitwise_xor(me, s) * owned + lane - s * owned, ids)
    return ids.astype(f32)


def by_variable(ref, count):
    return jnp.concatenate([ref[pl.ds(c, count, stride=NC)] for c in range(NC)], axis=1)


def pack_x(ny, delta, coefs, alpha, near_tiles, y_a, y_b, *rest):
    others = rest[:1]
    out_a, out_b, field, picks, known, tiles = rest[1:]
    even, _, _ = place_on("gx")
    owned = alpha.shape[0] // NC
    gather_known(alpha, y_a, others, known)
    turned = tile_numbers(near_tiles, y_a, y_b, tiles)
    ids = tile_ids(ny, owned)
    columns = [x for x in range(RIM)] + [CX - RIM + x for x in range(RIM)]
    for i, x in enumerate(columns):
        picks[i * PITCH : (i + 1) * PITCH] = (turned[:, x : x + 1] == ids).astype(f32)
    fine = two_part_dot(picks[...].astype(bf16), by_variable(known, ny * owned))

    def fill(own, y_base, reach, c):
        for i, x in enumerate(columns):
            at = i * PITCH
            field[at + CY : at + PITCH] = jnp.zeros((PITCH - CY, 128), f32)
            field[at : at + CY] = own[x * CY : (x + 1) * CY]
        for away in range(1, reach + 1):
            for first, base in ((0, 0), (CX - RIM, RIM * PITCH)):
                rows = pl.ds(y_base + (away - 1) * CX + first, RIM)
                north, south = y_sides(y_a, y_b, rows)
                field[pl.ds(base + CY - 1 + away, RIM, stride=PITCH)] = north
                field[pl.ds(base + PITCH - away, RIM, stride=PITCH)] = south
        if c is not None:
            field[...] += profile_weight * fine[:, c * 128 : (c + 1) * 128]

    def put(at, found, at_a=None):
        for away, start, extra in found:
            east, west = (2 * RIM - away) * PITCH, (away - 1) * PITCH
            here = at + start
            for source, target, size in (
                (PITCH - extra, 0, extra),
                (0, extra, CY + extra),
            ):
                if size:
                    first = field[east + source : east + source + size]
                    second = field[west + source : west + source + size]
                    rows = slice(here + target, here + target + size)
                    out_b[rows] = jnp.where(even, second, first)
                    if at_a is None:
                        out_a[rows] = jnp.where(even, first, second)
            if at_a is not None and extra:
                for row in (PITCH - extra, CY):
                    first = field[east + row : east + row + extra]
                    second = field[west + row : west + row + extra]
                    out_a[at_a : at_a + extra] = jnp.where(even, first, second)
                    at_a += extra

    for c in range(NC):
        fill(delta.at[c], c * RIM * CX, RIM, c)
        put(c * WIDE_ROWS, WIDE)
    for f in range(3):
        fill(coefs.at[f], Y_COEF + f * INNER * CX, INNER, None)
        put(X_COEF + f * SLIM_ROWS, SLIM, X_COEF + f * X_CORNERS)


def prepare(ny, delta, coefs, alpha, near_tiles, meta, weights, y_a, y_b, *rest):
    others = rest[:1]
    core, coef, picks, wide, slot_pick, slot_push, beam_pick, columns = rest[1:9]
    known, tiles = rest[9:]
    owned = alpha.shape[0] // NC

    def fill(ref, base, own, y_base, reach):
        for x in range(CX):
            at = base + x * PITCH
            ref[at : at + CY] = own[x * CY : (x + 1) * CY]
            ref[at + CY : at + PITCH] = jnp.zeros((PITCH - CY, 128), f32)
        for away in range(1, reach + 1):
            north, south = y_sides(y_a, y_b, pl.ds(y_base + (away - 1) * CX, CX))
            ref[pl.ds(base + CY - 1 + away, CX, stride=PITCH)] = north
            ref[pl.ds(base + PITCH - away, CX, stride=PITCH)] = south

    for c in range(NC):
        fill(core, c * CORE, delta.at[c], c * RIM * CX, RIM)
    for f in range(3):
        fill(coef, f * CORE, coefs.at[f], Y_COEF + f * INNER * CX, INNER)

    def combine(b, carry):
        at = pl.multiple_of(b * PITCH, 8)
        combined = combine_coefs(*[coef[pl.ds(f * CORE + at, PITCH)] for f in range(3)])
        for f, value in enumerate(combined):
            coef[pl.ds(f * CORE + at, PITCH)] = value
        return carry

    lax.fori_loop(0, CX, combine, 0)

    gather_known(alpha, y_a, others, known)
    turned = tile_numbers(near_tiles, y_a, y_b, tiles)
    ids = tile_ids(ny, owned)
    for x in range(CX):
        picks[x * PITCH : (x + 1) * PITCH] = (turned[:, x : x + 1] == ids).astype(f32)
    fine = two_part_dot(picks[...].astype(bf16), by_variable(known, ny * owned))
    for c in range(NC):
        core[c * CORE : (c + 1) * CORE] += profile_weight * fine[:, c * 128 : (c + 1) * 128]

    slots = meta.shape[1]
    for c in range(NC):
        wide[:, c * 128 : (c + 1) * 128] = weights[pl.ds(c, slots, stride=NC)]
    per_beam = beam_pick.shape[1]
    turned = jnp.transpose(meta[...])
    columns[...] = turned
    slot_lane = lax.broadcasted_iota(jnp.int32, (slots, CX * CY), 1).astype(f32)
    slot_pick[...] = (slot_lane == turned[:, 0:1]).astype(f32).astype(bf16)
    column_row = lax.broadcasted_iota(jnp.int32, (CX * CY, slots), 0).astype(f32)
    slot_push[...] = (column_row == meta[0:1]).astype(f32).astype(bf16)
    beam_lane = lax.broadcasted_iota(jnp.int32, (slots, per_beam), 1).astype(f32)
    beam_pick[...] = (beam_lane == turned[:, 1:2]).astype(f32).astype(bf16)


def combine_coefs(viscous, along_x, along_y):
    half_x, half_y = 0.5 * along_x, 0.5 * along_y
    return (
        1.0 - 4.0 * viscous,
        viscous - half_x,
        viscous + half_x,
        viscous - half_y,
        viscous + half_y,
    )


def clear(ref, base, blocks):
    for b in blocks:
        at = base + b * PITCH
        ref[at : at + PITCH] = jnp.zeros((PITCH, 128), f32)


def forecast(core, coef_core, early, x_a, x_b, tops, lows, coef, state_0, state_1, raw):
    def fill(ref, base, x_base, found):
        for away, start, extra in found:
            for source, target, size in (
                (0, PITCH - extra, extra),
                (extra, 0, CY + extra),
            ):
                if size:
                    at = x_base + start + source
                    west, east = x_sides(x_a, x_b, pl.ds(at, size))
                    at = base + (FIRST - away) * PITCH + target
                    ref[at : at + size] = west
                    at = base + (FIRST + CX - 1 + away) * PITCH + target
                    ref[at : at + size] = east

    even, has_west, has_east = place_on("gx")
    rim = [FIRST - 3, FIRST - 2, FIRST - 1, FIRST + CX, FIRST + CX + 1, FIRST + CX + 2]
    for c in range(NC):
        at = c * FIELD + FIRST * PITCH
        state_0[at : at + CORE] = core[c * CORE : (c + 1) * CORE]
        clear(state_0, c * FIELD, rim)
        fill(state_0, c * FIELD, c * WIDE_ROWS, WIDE)
    for f in range(3):
        clear(raw, f * FIELD, rim[1:5])
        at_a = X_COEF + f * X_CORNERS
        for away, start, extra in SLIM:
            inner = f * INNER * CY
            west_a = early[pl.ds(inner + (INNER - away) * CY, CY)]
            east_a = early[pl.ds(inner + (away - 1) * CY, CY)]
            pieces = [(0, extra, CY, west_a, east_a)]
            if extra:
                for row, source in ((PITCH - extra, 0), (CY, extra + CY)):
                    value = x_a[at_a : at_a + extra]
                    pieces.append((row, source, extra, value, value))
                    at_a += extra
            for row, source, size, west_a, east_a in pieces:
                at = X_COEF + f * SLIM_ROWS + start + source
                value = x_b[at : at + size]
                west, east = jnp.where(even, value, west_a), jnp.where(even, east_a, value)
                at = f * FIELD + (FIRST - away) * PITCH + row
                raw[at : at + size] = jnp.where(has_west, west, 0.0)
                at = f * FIELD + (FIRST + CX - 1 + away) * PITCH + row
                raw[at : at + size] = jnp.where(has_east, east, 0.0)
    for f in range(5):
        at = f * FIELD + FIRST * PITCH
        coef[at : at + CORE] = coef_core[f * CORE : (f + 1) * CORE]
        clear(coef, f * FIELD, [0, 1, BLOCKS - 2, BLOCKS - 1])
    for b in rim[1:5]:
        rows = [slice(f * FIELD + b * PITCH, f * FIELD + (b + 1) * PITCH) for f in range(5)]
        for f, value in enumerate(combine_coefs(*[raw[rows[f]] for f in range(3)])):
            coef[rows[f]] = value

    def forward(source, target, low, high):
        def body(b, carry):
            at = pl.multiple_of(b * PITCH, 8)
            k = [coef[pl.ds(f * FIELD + at, PITCH)] for f in range(5)]
            for c in range(NC):
                base = c * FIELD + at
                here = source[pl.ds(base, PITCH)]
                target[pl.ds(base, PITCH)] = (
                    k[0] * here
                    + k[1] * source[pl.ds(base + PITCH, PITCH)]
                    + k[2] * source[pl.ds(base - PITCH, PITCH)]
                    + k[3] * pltpu.roll(here, PITCH - 1, 0)
                    + k[4] * pltpu.roll(here, 1, 0)
                )
            return carry

        lax.fori_loop(low, high, body, 0)

    buffers = [state_0, state_1]
    for step in range(STEPS):
        source, target = buffers[step % 2], buffers[(step + 1) % 2]
        forward(source, target, 2 + step, BLOCKS - 2 - step)
        own = jnp.concatenate(
            [
                jnp.concatenate(
                    [
                        target[c * FIELD + b * PITCH : c * FIELD + b * PITCH + CY]
                        for b in range(FIRST, FIRST + CX)
                    ],
                    axis=0,
                )
                for c in range(NC)
            ],
            axis=1,
        )
        rows = slice(step * CX * CY, (step + 1) * CX * CY)
        tops[rows], lows[rows] = split(own)


def main(
    coef,
    tops,
    lows,
    wide,
    slot_pick,
    slot_push,
    beam_pick,
    columns,
    *rest,
):
    beams = rest[:-6]
    out_a, out_b, out_core, state_0, state_1, forcing = rest[-6:]
    even, _, _ = place_on("gx")
    slots = columns.shape[0]
    gate_lane = lax.broadcasted_iota(jnp.int32, (slots, 128), 1).astype(f32)
    gate_here = gate_lane == columns[:, 2:3]
    scaled = columns[:, 3:4]
    for step in range(STEPS):
        rows = slice(step * CX * CY, (step + 1) * CX * CY)
        picked = jnp.dot(slot_pick[...], tops[rows], preferred_element_type=f32)
        picked = picked + jnp.dot(slot_pick[...], lows[rows], preferred_element_type=f32)
        picked = picked * wide[...]
        table = []
        for part in beams:
            for at in range(0, part.shape[0], STEPS * OWN_BEAMS):
                first = at + step * OWN_BEAMS
                table.append(part[first : first + OWN_BEAMS])
        table = two_part_dot(beam_pick[...], jnp.concatenate(table, axis=0))
        tally = -jnp.where(gate_here, table, 0.0)
        for c in range(NC):
            tally = tally + picked[:, c * 128 : (c + 1) * 128]
        misfit = scaled * jnp.sum(tally, axis=1, keepdims=True)
        forcing[rows] = two_part_dot(slot_push[...], misfit * wide[...])

    buffers = [state_0, state_1]

    for c in range(NC):
        clear(state_0, c * FIELD, [0, 1, 2, 3, BLOCKS - 4, BLOCKS - 3, BLOCKS - 2, BLOCKS - 1])
        clear(state_1, c * FIELD, [1, 2, BLOCKS - 3, BLOCKS - 2])

    def add_forcing(ref, step):
        for c in range(NC):
            for x in range(CX):
                at = c * FIELD + (FIRST + x) * PITCH
                first = step * CX * CY + x * CY
                value = forcing[first : first + CY, c * 128 : (c + 1) * 128]
                if step == STEPS - 1:
                    ref[at : at + CY] = value
                    ref[at + CY : at + PITCH] = jnp.zeros((PITCH - CY, 128), f32)
                else:
                    ref[at : at + CY] += value

    def backward(source, target, low, high):
        def body(b, carry):
            at = pl.multiple_of(b * PITCH, 8)
            k = [
                coef[pl.ds(at, PITCH)],
                coef[pl.ds(FIELD + at - PITCH, PITCH)],
                coef[pl.ds(2 * FIELD + at + PITCH, PITCH)],
                coef[pl.ds(3 * FIELD + at, PITCH)],
                coef[pl.ds(4 * FIELD + at, PITCH)],
            ]
            for c in range(NC):
                base = c * FIELD + at
                here = source[pl.ds(base, PITCH)]
                target[pl.ds(base, PITCH)] = (
                    k[0] * here
                    + k[1] * source[pl.ds(base - PITCH, PITCH)]
                    + k[2] * source[pl.ds(base + PITCH, PITCH)]
                    + pltpu.roll(k[3] * here, 1, 0)
                    + pltpu.roll(k[4] * here, PITCH - 1, 0)
                )
            return carry

        lax.fori_loop(low, high, body, 0)

    for step in range(STEPS):
        source, target = buffers[step % 2], buffers[(step + 1) % 2]
        add_forcing(source, STEPS - 1 - step)
        backward(source, target, FIRST - 1 - step, FIRST + CX + 1 + step)
    final = buffers[STEPS % 2]

    for c in range(NC):
        at = c * FIELD + FIRST * PITCH
        out_core[c * CORE : (c + 1) * CORE] = final[at : at + CORE]
        for away, start, extra in WIDE:
            for source, target, size in (
                (PITCH - extra, 0, extra),
                (0, extra, CY + extra),
            ):
                if size:
                    at = c * FIELD + (FIRST - away) * PITCH + source
                    west = final[at : at + size]
                    at = c * FIELD + (FIRST + CX - 1 + away) * PITCH + source
                    east = final[at : at + size]
                    at = c * WIDE_ROWS + start + target
                    out_a[at : at + size] = jnp.where(even, east, west)
                    out_b[at : at + size] = jnp.where(even, west, east)


def add_x(ny, delta, picks, core, x_a, x_b, *rest):
    out_a, out_b, out_near, out_sums = rest[:4]
    out_others = rest[4:-2]
    field, sums = rest[-2:]
    even, _, _ = place_on("gy")
    total = picks.shape[1]
    rows = total * NC // ny
    field[...] = core[...]
    for c in range(NC):
        for away, start, extra in WIDE:
            for source, target, size in (
                (0, PITCH - extra, extra),
                (extra, 0, CY + extra),
            ):
                if size:
                    at = c * WIDE_ROWS + start + source
                    west, east = x_sides(x_a, x_b, pl.ds(at, size))
                    at = c * CORE + (away - 1) * PITCH + target
                    field[at : at + size] += west
                    at = c * CORE + (CX - away) * PITCH + target
                    field[at : at + size] += east
    for c in range(NC):
        for away in range(1, RIM + 1):
            north = field[pl.ds(c * CORE + CY - 1 + away, CX, stride=PITCH)]
            south = field[pl.ds(c * CORE + PITCH - away, CX, stride=PITCH)]
            at = (c * RIM + away - 1) * CX
            out_a[at : at + CX] = jnp.where(even, north, south)
            out_b[at : at + CX] = jnp.where(even, south, north)
        for x in range(CX):
            at = c * CORE + x * PITCH
            here = slice(x * CY, (x + 1) * CY)
            out_near[c, here] = delta[c, here] + field[at : at + CY]
    adjoint = jnp.concatenate([field[c * CORE : (c + 1) * CORE] for c in range(NC)], axis=1)
    tile_sums = two_part_dot(jnp.transpose(picks[...]).astype(bf16), adjoint)
    for c in range(NC):
        sums[pl.ds(c, total, stride=NC)] = tile_sums[:, c * 128 : (c + 1) * 128]
    out_sums[...] = sums[0:rows]
    out_a[Y_COEF:] = sums[rows : 2 * rows]
    if ny == 4:
        out_b[Y_COEF:] = sums[3 * rows : 4 * rows]
    for s, other in enumerate(out_others):
        other[...] = sums[(2 + s) * rows : (3 + s) * rows]


def add_y(alpha, near, sums, y_a, y_b, *rest):
    others = rest[:-2]
    out_delta, out_alpha = rest[-2:]
    out_delta[...] = near[...]
    for c in range(NC):
        for away in range(1, RIM + 1):
            north, south = y_sides(y_a, y_b, pl.ds((c * RIM + away - 1) * CX, CX))
            high = pl.ds(CY - away, CX, stride=CY)
            low = pl.ds(away - 1, CX, stride=CY)
            out_delta[c, high] = out_delta[c, high] + north
            out_delta[c, low] = out_delta[c, low] + south
    total = sums[...] + y_a[Y_COEF:]
    if y_b.shape[0] > Y_COEF:
        total = total + y_b[Y_COEF:]
    for other in others:
        total = total + other[...]
    out_alpha[...] = alpha[...] + profile_weight * total


def on_device(
    delta,
    alpha,
    eddy,
    courant,
    tile_map,
    obs_rows,
    gate_beam,
    gate_index,
    gate_column,
    gate_live,
    obs_weight,
    obs_precision,
):
    nx = lax.axis_size("gx")
    ny = lax.axis_size("gy")
    owned = alpha.shape[1]
    slots = gate_column.shape[2]
    fine = delta.reshape(NC, CX * CY, 128)
    eddy = eddy.reshape(CX * CY, 128)
    courant = courant.reshape(2, CX * CY, 128)
    control = alpha.reshape(owned * NC, 128)
    weights = obs_weight.reshape(slots * NC, 128)
    gates = [
        value.reshape(1, slots)
        for value in (gate_beam, gate_index, gate_column, gate_live, obs_precision)
    ]
    own_beams = jnp.transpose(obs_rows, (1, 0, 2)).reshape(STEPS * OWN_BEAMS, 128)
    beam_count = nx * OWN_BEAMS
    rows = owned * NC
    total = ny * owned

    y_a, y_b, early, fine, coefs, control_near, near_tiles, meta = call(
        pack_y,
        [
            (Y_HALO + rows, 128),
            (Y_HALO, 128),
            (EARLY, 128),
            fine.shape,
            (3, CX * CY, 128),
            control.shape,
            (CX, 128),
            (8, slots),
        ],
        [
            pltpu.with_memory_space_constraint(value, pltpu.HBM)
            for value in (fine, eddy, courant, control, tile_map, *gates, own_beams)
        ],
        [
            pltpu.VMEM(tile_map.shape, jnp.int32),
            pltpu.VMEM((4, 1, slots), jnp.int32),
            pltpu.VMEM((1, slots), f32),
            pltpu.SemaphoreType.DMA((12,)),
        ],
        in_specs=[HBM] * 11,
    )
    y_a = swap(y_a, "gy", 1)
    y_b = pair_b(y_b, "gy", "gx")
    others = [jnp.concatenate([swap(control, "gy", xor) for xor in range(2, ny)])]
    got_early = swap(early, "gx", 1)
    beams = jnp.concatenate([early[EARLY_BEAMS:], got_early[EARLY_BEAMS:]])
    beams = [beams] + [swap(beams, "gx", xor) for xor in range(2, nx, 2)]

    x_a, x_b = call(
        lambda *refs: pack_x(ny, *refs),
        [(X_EXTRA, 128), (X_HALO, 128)],
        [fine, coefs, control_near, near_tiles, y_a, y_b, *others],
        [
            pltpu.VMEM((2 * RIM * PITCH, 128), f32),
            pltpu.VMEM((2 * RIM * PITCH, total), f32),
            pltpu.VMEM((total * NC, 128), f32),
            pltpu.VMEM((128, 128), f32),
        ],
    )
    x_a = swap(x_a, "gx", 1)
    x_b = pair_b(x_b, "gx", "gy")

    core, coef, picks, wide, slot_pick, slot_push, beam_pick, columns = call(
        lambda *refs: prepare(ny, *refs),
        [
            (NC * CORE, 128),
            (5 * CORE, 128),
            (CORE, total),
            (slots, NC * 128),
            jax.ShapeDtypeStruct((slots, CX * CY), bf16),
            jax.ShapeDtypeStruct((CX * CY, slots), bf16),
            jax.ShapeDtypeStruct((slots, beam_count), bf16),
            (slots, 8),
        ],
        [fine, coefs, control_near, near_tiles, meta, weights, y_a, y_b, *others],
        [
            pltpu.VMEM((total * NC, 128), f32),
            pltpu.VMEM((128, 128), f32),
        ],
        flops=3000000,
    )


    tops, lows, coef = call(
        forecast,
        [
            jax.ShapeDtypeStruct((STEPS * CX * CY, NC * 128), bf16),
            jax.ShapeDtypeStruct((STEPS * CX * CY, NC * 128), bf16),
            (5 * FIELD, 128),
        ],
        [core, coef, got_early, x_a, x_b],
        [
            pltpu.VMEM((NC * FIELD, 128), f32),
            pltpu.VMEM((NC * FIELD, 128), f32),
            pltpu.VMEM((3 * FIELD, 128), f32),
        ],
        flops=10000000,
    )
    back_a, back_b, core = call(
        main,
        [(X_COEF, 128), (X_COEF, 128), (NC * CORE, 128)],
        [coef, tops, lows, wide, slot_pick, slot_push, beam_pick, columns, *beams],
        [
            pltpu.VMEM((NC * FIELD, 128), f32),
            pltpu.VMEM((NC * FIELD, 128), f32),
            pltpu.VMEM((STEPS * CX * CY, NC * 128), f32),
        ],
        flops=20000000,
    )
    x_a = swap(back_a, "gx", 1)
    x_b = pair_b(back_b, "gx", "gy")
    loose = [xor for xor in range(2, ny) if ny != 4 or xor != 3]
    back_a, back_b, near, sums, *back = call(
        lambda *refs: add_x(ny, *refs),
        [
            (Y_COEF + rows, 128),
            (Y_COEF + (rows if ny == 4 else 0), 128),
            fine.shape,
            (rows, 128),
        ]
        + [(rows, 128)] * len(loose),
        [fine, picks, core, x_a, x_b],
        [pltpu.VMEM((NC * CORE, 128), f32), pltpu.VMEM((total * NC, 128), f32)],
    )
    y_a = swap(back_a, "gy", 1)
    y_b = ring_b(back_b, "gy")
    others = [swap(value, "gy", xor) for xor, value in zip(loose, back)]
    grad_delta, grad_alpha = call(
        add_y,
        [fine.shape, control.shape],
        [control_near, near, sums, y_a, y_b, *others],
    )
    return grad_delta.reshape(delta.shape), grad_alpha.reshape(alpha.shape)


def solution(mesh):
    return jax.shard_map(
        on_device,
        mesh=mesh,
        in_specs=(
            P(None, "gx", "gy", None),
            P("gx", "gy", None, None),
            P("gx", "gy", None),
            P(None, "gx", "gy", None),
            P("gx", "gy"),
            P(("gx", "gy"), None, None),
            P("gx", "gy", None),
            P("gx", "gy", None),
            P("gx", "gy", None),
            P("gx", "gy", None),
            P("gx", "gy", None, None, None),
            P("gx", "gy", None),
        ),
        out_specs=(P(None, "gx", "gy", None), P("gx", "gy", None, None)),
        check_vma=False,
    )
```

```python
import jax
import jax.numpy as jnp
from jax import lax
from jax.experimental import pallas as pl
from jax.experimental.pallas import tpu as pltpu
from jax.sharding import PartitionSpec as P

STEPS = 3
RIM = 3
INNER = RIM - 1
NC = 4
CX = 16
CY = 16
BLOCKS = CX + 8
PITCH = CY + 8
FIRST = 4
FIELD = BLOCKS * PITCH
CORE = CX * PITCH
OWN_BEAMS = 8
BEAM_BITS = 3

profile_weight = 0.125
f32 = jnp.float32
bf16 = jnp.bfloat16

VMEM = pl.BlockSpec(memory_space=pltpu.VMEM)
HBM = pl.BlockSpec(memory_space=pltpu.HBM)


def call(body, outs, ins, scratch=(), in_specs=None, flops=1000000, limit=40 * 2**20):
    shapes = [
        out if isinstance(out, jax.ShapeDtypeStruct) else jax.ShapeDtypeStruct(out, f32)
        for out in outs
    ]
    size = sum(4 * value.size for value in ins)
    return pl.pallas_call(
        body,
        out_shape=shapes,
        in_specs=in_specs or [VMEM] * len(ins),
        out_specs=[VMEM] * len(shapes),
        scratch_shapes=list(scratch),
        compiler_params=pltpu.CompilerParams(vmem_limit_bytes=limit),
        cost_estimate=pl.CostEstimate(flops=flops, bytes_accessed=size, transcendentals=0),
    )(*ins)


def swap(block, axis, xor):
    return lax.ppermute(block, axis, [(i, i ^ xor) for i in range(lax.axis_size(axis))])


def pair_b(block, axis, other):
    count, across = lax.axis_size(axis), lax.axis_size(other)

    def place(i, j):
        return i * across + j if axis == "gx" else j * count + i

    pairs = []
    for j in range(across):
        for i in range(count):
            if i in (0, count - 1):
                pairs.append((place(i, j), place(i, j ^ 1)))
            else:
                pairs.append((place(i, j), place(i + 1 if i % 2 else i - 1, j)))
    return lax.ppermute(block, ("gx", "gy"), pairs)


def ring_b(block, axis):
    count = lax.axis_size(axis)
    pairs = [(i, (i + 1 if i % 2 else i - 1) % count) for i in range(count)]
    return lax.ppermute(block, axis, pairs)


def place_on(axis):
    me = lax.axis_index(axis)
    return lax.rem(me, 2) == 0, me > 0, me < lax.axis_size(axis) - 1


def split(value):
    top = value.astype(bf16)
    return top, (value - top.astype(f32)).astype(bf16)


def two_part_dot(left, value):
    top, low = split(value)
    return jnp.dot(left, top, preferred_element_type=f32) + jnp.dot(
        left, low, preferred_element_type=f32
    )


def layers(reach):
    found, at = [], 0
    for away in range(1, reach + 1):
        found.append((away, at, reach - away))
        at += CY + 2 * (reach - away)
    return found, at


WIDE, WIDE_ROWS = layers(RIM)
SLIM, SLIM_ROWS = layers(INNER)
X_COEF = NC * WIDE_ROWS
X_HALO = X_COEF + 3 * SLIM_ROWS

Y_COEF = NC * RIM * CX
Y_TILE = Y_COEF + 3 * INNER * CX
Y_HALO = Y_TILE + CX


def pack_y(
    delta,
    eddy,
    courant,
    alpha,
    tile_map,
    gate_beam,
    gate_index,
    gate_column,
    gate_live,
    precision,
    beam_rows,
    out_a,
    out_b,
    fine,
    coefs,
    profiles,
    near_tiles,
    meta,
    beams,
    tiles,
    gates,
    values,
    sems,
):
    even, _, _ = place_on("gy")
    moves = [
        pltpu.make_async_copy(source, target, sems.at[i])
        for i, (source, target) in enumerate(
            [
                (delta, fine),
                (eddy, coefs.at[0]),
                (courant.at[0], coefs.at[1]),
                (courant.at[1], coefs.at[2]),
                (tile_map, tiles),
                (alpha, profiles),
                (gate_beam, gates.at[0]),
                (gate_index, gates.at[1]),
                (gate_column, gates.at[2]),
                (gate_live, gates.at[3]),
                (precision, values),
                (beam_rows, beams),
            ]
        )
    ]
    for move in moves:
        move.start()
    for move in moves:
        move.wait()

    def put(at, field, away):
        north = field[pl.ds(CY - away, CX, stride=CY)]
        south = field[pl.ds(away - 1, CX, stride=CY)]
        out_a[at : at + CX] = jnp.where(even, north, south)
        out_b[at : at + CX] = jnp.where(even, south, north)

    for c in range(NC):
        for away in range(1, RIM + 1):
            put((c * RIM + away - 1) * CX, fine.at[c], away)
    for f in range(3):
        for away in range(1, INNER + 1):
            put(Y_COEF + (f * INNER + away - 1) * CX, coefs.at[f], away)
    near_tiles[...] = jnp.full((CX, 128), -1.0, f32)
    near_tiles[:, 0:CY] = tiles[...].astype(f32)
    for out in (out_a, out_b):
        out[Y_TILE : Y_TILE + CX] = near_tiles[...]
    out_a[Y_HALO:] = profiles[...]
    held = BEAM_BITS
    beam = gates[0]
    owner = jnp.bitwise_xor(beam >> held, lax.axis_index("gx"))
    block = (owner & -4) | ((owner & 1) << 1) | ((owner >> 1) & 1)
    meta[...] = jnp.zeros(meta.shape, f32)
    meta[0:1] = gates[2].astype(f32)
    meta[1:2] = ((block << held) | (beam & ((1 << held) - 1))).astype(f32)
    meta[2:3] = gates[1].astype(f32)
    meta[3:4] = gates[3].astype(f32) * values[...]


def y_sides(got_a, got_b, rows, fill=0.0):
    even, low, high = place_on("gy")
    first, second = got_a[rows], got_b[rows]
    north, south = jnp.where(even, first, second), jnp.where(even, second, first)
    return jnp.where(high, north, fill), jnp.where(low, south, fill)


def x_sides(got_a, got_b, rows):
    even, low, high = place_on("gx")
    first, second = got_a[rows], got_b[rows]
    west, east = jnp.where(even, second, first), jnp.where(even, first, second)
    return jnp.where(low, west, 0.0), jnp.where(high, east, 0.0)


def gather_known(alpha, got_a, others, known):
    owned = alpha.shape[0]
    known[0:owned] = alpha[...]
    known[owned : 2 * owned] = got_a[Y_HALO:]
    for s, other in enumerate(others):
        known[(2 + s) * owned : (3 + s) * owned] = other[...]


def tile_numbers(near_tiles, got_a, got_b, tiles):
    spot = lax.broadcasted_iota(jnp.int32, (CX, 128), 1)
    north, south = y_sides(got_a, got_b, pl.ds(Y_TILE, CX), -1.0)
    near = jnp.where(
        (spot >= CY) & (spot < CY + RIM),
        pltpu.roll(north, CY, 1),
        jnp.where((spot >= PITCH - RIM) & (spot < PITCH), pltpu.roll(south, PITCH - CY, 1), -1.0),
    )
    tiles[...] = jnp.full(tiles.shape, -1.0, f32)
    tiles[0:CX] = jnp.where(spot < CY, near_tiles[...], near)
    return jnp.transpose(tiles[...])[0:PITCH]


def tile_ids(ny, owned):
    me = lax.axis_index("gy")
    lane = lax.broadcasted_iota(jnp.int32, (1, ny * owned), 1)
    ids = lane
    for s in range(ny):
        here = (lane >= s * owned) & (lane < (s + 1) * owned)
        ids = jnp.where(here, jnp.bitwise_xor(me, s) * owned + lane - s * owned, ids)
    return ids.astype(f32)


def by_variable(ref, count):
    return jnp.concatenate([ref[pl.ds(c, count, stride=NC)] for c in range(NC)], axis=1)


def pack_x(ny, delta, coefs, alpha, near_tiles, y_a, y_b, *rest):
    others = rest[: ny - 2]
    out_a, out_b, field, picks, known, tiles = rest[ny - 2 :]
    even, _, _ = place_on("gx")
    owned = alpha.shape[0] // NC
    gather_known(alpha, y_a, others, known)
    turned = tile_numbers(near_tiles, y_a, y_b, tiles)
    ids = tile_ids(ny, owned)
    columns = [x for x in range(RIM)] + [CX - RIM + x for x in range(RIM)]
    for i, x in enumerate(columns):
        picks[i * PITCH : (i + 1) * PITCH] = (turned[:, x : x + 1] == ids).astype(f32)
    fine = two_part_dot(picks[...].astype(bf16), by_variable(known, ny * owned))

    def fill(own, y_base, reach, c):
        for i, x in enumerate(columns):
            at = i * PITCH
            field[at + CY : at + PITCH] = jnp.zeros((PITCH - CY, 128), f32)
            field[at : at + CY] = own[x * CY : (x + 1) * CY]
        for away in range(1, reach + 1):
            for first, base in ((0, 0), (CX - RIM, RIM * PITCH)):
                rows = pl.ds(y_base + (away - 1) * CX + first, RIM)
                north, south = y_sides(y_a, y_b, rows)
                field[pl.ds(base + CY - 1 + away, RIM, stride=PITCH)] = north
                field[pl.ds(base + PITCH - away, RIM, stride=PITCH)] = south
        if c is not None:
            field[...] += profile_weight * fine[:, c * 128 : (c + 1) * 128]

    def put(at, found):
        for away, start, extra in found:
            east, west = (2 * RIM - away) * PITCH, (away - 1) * PITCH
            here = at + start
            for source, target, size in (
                (PITCH - extra, 0, extra),
                (0, extra, CY + extra),
            ):
                if size:
                    first = field[east + source : east + source + size]
                    second = field[west + source : west + source + size]
                    rows = slice(here + target, here + target + size)
                    out_a[rows] = jnp.where(even, first, second)
                    out_b[rows] = jnp.where(even, second, first)

    for c in range(NC):
        fill(delta.at[c], c * RIM * CX, RIM, c)
        put(c * WIDE_ROWS, WIDE)
    for f in range(3):
        fill(coefs.at[f], Y_COEF + f * INNER * CX, INNER, None)
        put(X_COEF + f * SLIM_ROWS, SLIM)


def prepare(ny, delta, coefs, alpha, near_tiles, meta, weights, y_a, y_b, *rest):
    others = rest[: ny - 2]
    core, coef, picks, wide, slot_push, beam_pick, columns = rest[ny - 2 : ny + 5]
    state_1, state_2, tally, edge_pick = rest[ny + 5 : ny + 9]
    state_3, known, tiles = rest[ny + 9 :]
    owned = alpha.shape[0] // NC

    def fill(ref, base, own, y_base, reach):
        for x in range(CX):
            at = base + x * PITCH
            ref[at : at + CY] = own[x * CY : (x + 1) * CY]
            ref[at + CY : at + PITCH] = jnp.zeros((PITCH - CY, 128), f32)
        for away in range(1, reach + 1):
            north, south = y_sides(y_a, y_b, pl.ds(y_base + (away - 1) * CX, CX))
            ref[pl.ds(base + CY - 1 + away, CX, stride=PITCH)] = north
            ref[pl.ds(base + PITCH - away, CX, stride=PITCH)] = south

    for c in range(NC):
        fill(core, c * CORE, delta.at[c], c * RIM * CX, RIM)
    for f in range(3):
        fill(coef, f * CORE, coefs.at[f], Y_COEF + f * INNER * CX, INNER)

    def combine(b, carry):
        at = pl.multiple_of(b * PITCH, 8)
        combined = combine_coefs(*[coef[pl.ds(f * CORE + at, PITCH)] for f in range(3)])
        for f, value in enumerate(combined):
            coef[pl.ds(f * CORE + at, PITCH)] = value
        return carry

    lax.fori_loop(0, CX, combine, 0)

    gather_known(alpha, y_a, others, known)
    turned = tile_numbers(near_tiles, y_a, y_b, tiles)
    ids = tile_ids(ny, owned)
    for x in range(CX):
        picks[x * PITCH : (x + 1) * PITCH] = (turned[:, x : x + 1] == ids).astype(f32)
    fine = two_part_dot(picks[...].astype(bf16), by_variable(known, ny * owned))
    for c in range(NC):
        core[c * CORE : (c + 1) * CORE] += profile_weight * fine[:, c * 128 : (c + 1) * 128]

    slots = meta.shape[1]
    for c in range(NC):
        wide[:, c * 128 : (c + 1) * 128] = weights[pl.ds(c, slots, stride=NC)]
    per_beam = beam_pick.shape[1]
    turned = jnp.transpose(meta[...])
    columns[...] = turned
    slot_lane = lax.broadcasted_iota(jnp.int32, (slots, CX * CY), 1).astype(f32)
    slot_pick = (slot_lane == turned[:, 0:1]).astype(f32).astype(bf16)
    edge_lane = lax.broadcasted_iota(jnp.int32, (slots, 128), 1)
    half = RIM * CY
    place = jnp.where(edge_lane < half, edge_lane, edge_lane + CX * CY - 2 * half)
    place = jnp.where(edge_lane < 2 * half, place, -1).astype(f32)
    near_edge = (place == turned[:, 0:1]).astype(f32).astype(bf16)
    edge_pick[:, 0:128] = near_edge
    edge_pick[:, 128:256] = near_edge
    column_row = lax.broadcasted_iota(jnp.int32, (CX * CY, slots), 0).astype(f32)
    slot_push[...] = (column_row == meta[0:1]).astype(f32).astype(bf16)
    beam_lane = lax.broadcasted_iota(jnp.int32, (slots, per_beam), 1).astype(f32)
    beam_pick[...] = (beam_lane == turned[:, 1:2]).astype(f32).astype(bf16)

    states = [core, state_1, state_2, state_3]
    for step in range(STEPS):
        source, target = states[step], states[step + 1]

        def body(x, carry, source=source, target=target):
            at = pl.multiple_of(x * PITCH, 8)
            k = [coef[pl.ds(f * CORE + at, PITCH)] for f in range(5)]
            for c in range(NC):
                base = c * CORE + at
                target[pl.ds(base, PITCH)] = forward_column(source, base, k)
            return carry

        lax.fori_loop(step + 1, CX - 1 - step, body, 0)
        own = []
        for c in range(NC):
            pieces = [jnp.zeros(((step + 1) * CY, 128), f32)]
            for x in range(step + 1, CX - 1 - step):
                at = c * CORE + x * PITCH
                pieces.append(target[at : at + CY])
            own.append(jnp.concatenate(pieces + pieces[:1], axis=0))
        seen = two_part_dot(slot_pick, jnp.concatenate(own, axis=1)) * wide[...]
        total = seen[:, 0:128]
        for c in range(1, NC):
            total = total + seen[:, c * 128 : (c + 1) * 128]
        tally[step * slots : (step + 1) * slots] = total


def forward_column(source, base, k):
    here = source[pl.ds(base, PITCH)]
    return (
        k[0] * here
        + k[1] * source[pl.ds(base + PITCH, PITCH)]
        + k[2] * source[pl.ds(base - PITCH, PITCH)]
        + k[3] * pltpu.roll(here, PITCH - 1, 0)
        + k[4] * pltpu.roll(here, 1, 0)
    )


def backward_column(source, base, coef, at):
    here = source[pl.ds(base, PITCH)]
    return (
        coef[pl.ds(at, PITCH)] * here
        + coef[pl.ds(FIELD + at - PITCH, PITCH)] * source[pl.ds(base - PITCH, PITCH)]
        + coef[pl.ds(2 * FIELD + at + PITCH, PITCH)] * source[pl.ds(base + PITCH, PITCH)]
        + pltpu.roll(coef[pl.ds(3 * FIELD + at, PITCH)] * here, 1, 0)
        + pltpu.roll(coef[pl.ds(4 * FIELD + at, PITCH)] * here, PITCH - 1, 0)
    )


def combine_coefs(viscous, along_x, along_y):
    half_x, half_y = 0.5 * along_x, 0.5 * along_y
    return (
        1.0 - 4.0 * viscous,
        viscous - half_x,
        viscous + half_x,
        viscous - half_y,
        viscous + half_y,
    )


def clear(ref, base, blocks):
    for b in blocks:
        at = base + b * PITCH
        ref[at : at + PITCH] = jnp.zeros((PITCH, 128), f32)


def edges(
    core,
    core_coef,
    near_1,
    near_2,
    tally,
    wide,
    edge_pick,
    slot_push,
    beam_pick,
    columns,
    x_a,
    x_b,
    *rest,
):
    beams = rest[:-13]
    out_a, out_b, back_2, back_1, coef, tops, lows = rest[-13:-6]
    state_0, state_1, state_2, state_3, raw, forcing = rest[-6:]
    even, _, _ = place_on("gx")
    slots = columns.shape[0]

    def fill(ref, base, x_base, found):
        for away, start, extra in found:
            for source, target, size in (
                (0, PITCH - extra, extra),
                (extra, 0, CY + extra),
            ):
                if size:
                    at = x_base + start + source
                    west, east = x_sides(x_a, x_b, pl.ds(at, size))
                    at = base + (FIRST - away) * PITCH + target
                    ref[at : at + size] = west
                    at = base + (FIRST + CX - 1 + away) * PITCH + target
                    ref[at : at + size] = east

    def copy(source, target, x, count):
        for c in range(NC):
            first = c * CORE + x * PITCH
            at = c * FIELD + (FIRST + x) * PITCH
            target[at : at + count * PITCH] = source[first : first + count * PITCH]

    rim = [FIRST - 3, FIRST - 2, FIRST - 1, FIRST + CX, FIRST + CX + 1, FIRST + CX + 2]
    for x, (source, target) in enumerate(((core, state_0), (near_1, state_1), (near_2, state_2))):
        copy(source, target, x, 2)
        copy(source, target, CX - 2 - x, 2)
    for c in range(NC):
        clear(state_0, c * FIELD, rim)
        fill(state_0, c * FIELD, c * WIDE_ROWS, WIDE)
    for f in range(3):
        clear(raw, f * FIELD, rim[1:5])
        fill(raw, f * FIELD, X_COEF + f * SLIM_ROWS, SLIM)
    for f in range(5):
        for x in (0, CX - RIM):
            first, at = f * CORE + x * PITCH, f * FIELD + (FIRST + x) * PITCH
            coef[at : at + RIM * PITCH] = core_coef[first : first + RIM * PITCH]
        clear(coef, f * FIELD, [0, 1, BLOCKS - 2, BLOCKS - 1])
    for b in rim[1:5]:
        rows = [slice(f * FIELD + b * PITCH, f * FIELD + (b + 1) * PITCH) for f in range(5)]
        for f, value in enumerate(combine_coefs(*[raw[rows[f]] for f in range(3)])):
            coef[rows[f]] = value

    gate_lane = lax.broadcasted_iota(jnp.int32, (slots, 128), 1).astype(f32)
    gate_here = gate_lane == columns[:, 2:3]
    scaled = columns[:, 3:4]
    outer = [*range(RIM), *range(CX - RIM, CX)]
    half = RIM * CY
    push = jnp.concatenate([slot_push[0:half], slot_push[CX * CY - half :]], axis=0)
    states = [state_0, state_1, state_2, state_3]
    for step in range(STEPS):
        source, target = states[step], states[step + 1]
        for x in range(step - 2, step + 1):
            for b in (FIRST + x, FIRST + CX - 1 - x):
                at = b * PITCH
                k = [coef[f * FIELD + at : f * FIELD + at + PITCH] for f in range(5)]
                for c in range(NC):
                    base = c * FIELD + at
                    target[base : base + PITCH] = forward_column(source, base, k)
        zero = jnp.zeros((CY, 128), f32)
        parts = []
        for c in range(NC):
            pieces = []
            for x in outer:
                at = c * FIELD + (FIRST + x) * PITCH
                known = x <= step or x >= CX - 1 - step
                pieces.append(target[at : at + CY] if known else zero)
            value = jnp.concatenate(pieces + [jnp.zeros((128 - 2 * half, 128), f32)], axis=0)
            parts.append(jnp.concatenate(split(value), axis=0))
        seen = jnp.dot(
            edge_pick[...], jnp.concatenate(parts, axis=1), preferred_element_type=f32
        )
        seen = seen * wide[...]
        table = []
        for part in beams:
            for at in range(0, part.shape[0], STEPS * OWN_BEAMS):
                first = at + step * OWN_BEAMS
                table.append(part[first : first + OWN_BEAMS])
        table = two_part_dot(beam_pick[...], jnp.concatenate(table, axis=0))
        rows = slice(step * slots, (step + 1) * slots)
        total = tally[rows] - jnp.where(gate_here, table, 0.0)
        for c in range(NC):
            total = total + seen[:, c * 128 : (c + 1) * 128]
        misfit = scaled * jnp.sum(total, axis=1, keepdims=True)
        top, low = split(misfit * wide[...])
        tops[rows] = top
        lows[rows] = low
        forcing[step * 2 * half : (step + 1) * 2 * half] = jnp.dot(
            push, top, preferred_element_type=f32
        ) + jnp.dot(push, low, preferred_element_type=f32)

    def forced(step, i, c):
        at = step * 2 * half + i * CY
        return forcing[at : at + CY, c * 128 : (c + 1) * 128]

    for c in range(NC):
        clear(state_0, c * FIELD, [2, 3, BLOCKS - 4, BLOCKS - 3])
        clear(back_2, c * FIELD, [1, 2, BLOCKS - 3, BLOCKS - 2])
        clear(back_1, c * FIELD, [0, 1, BLOCKS - 2, BLOCKS - 1])
        for i, x in enumerate(outer):
            at = c * FIELD + (FIRST + x) * PITCH
            state_0[at : at + CY] = forced(STEPS - 1, i, c)
            state_0[at + CY : at + PITCH] = jnp.zeros((PITCH - CY, 128), f32)
    fields = [state_0, back_2, back_1, state_3]
    for step in range(STEPS):
        source, target = fields[step], fields[step + 1]
        for x in range(-1 - step, 2 - step):
            for b in (FIRST + x, FIRST + CX - 1 - x):
                for c in range(NC):
                    base = c * FIELD + b * PITCH
                    target[base : base + PITCH] = backward_column(source, base, coef, b * PITCH)
        if step < STEPS - 1:
            for i, x in enumerate(outer):
                if x < 2 - step or x > CX - 3 + step:
                    for c in range(NC):
                        at = c * FIELD + (FIRST + x) * PITCH
                        target[at : at + CY] += forced(STEPS - 2 - step, i, c)
    for c in range(NC):
        for away, start, extra in WIDE:
            for source, target, size in (
                (PITCH - extra, 0, extra),
                (0, extra, CY + extra),
            ):
                if size:
                    at = c * FIELD + (FIRST - away) * PITCH + source
                    west = state_3[at : at + size]
                    at = c * FIELD + (FIRST + CX - 1 + away) * PITCH + source
                    east = state_3[at : at + size]
                    at = c * WIDE_ROWS + start + target
                    out_a[at : at + size] = jnp.where(even, east, west)
                    out_b[at : at + size] = jnp.where(even, west, east)


def interior(core_coef, edge_coef, back_2, back_1, tops, lows, slot_push, out, *scratch):
    coef, forced, field_2, field_1, forcing = scratch
    for f in range(5):
        at = f * FIELD + FIRST * PITCH
        coef[at : at + CORE] = core_coef[f * CORE : (f + 1) * CORE]
        for b in (FIRST - 1, FIRST + CX):
            at = f * FIELD + b * PITCH
            coef[at : at + PITCH] = edge_coef[at : at + PITCH]
    for step in range(STEPS):
        rows = slice(step * CX * CY, (step + 1) * CX * CY)
        forcing[rows] = jnp.dot(
            slot_push[...], tops[rows], preferred_element_type=f32
        ) + jnp.dot(slot_push[...], lows[rows], preferred_element_type=f32)

    def add_forcing(ref, step, columns):
        for c in range(NC):
            for x in columns:
                at = c * FIELD + (FIRST + x) * PITCH
                first = step * CX * CY + x * CY
                value = forcing[first : first + CY, c * 128 : (c + 1) * 128]
                if step == STEPS - 1:
                    ref[at : at + CY] = value
                    ref[at + CY : at + PITCH] = jnp.zeros((PITCH - CY, 128), f32)
                else:
                    ref[at : at + CY] += value

    def sweep(source, target, low, high):
        def body(x, carry):
            at = pl.multiple_of((x + FIRST) * PITCH, 8)
            for c in range(NC):
                value = backward_column(source, c * FIELD + at, coef, at)
                if target is out:
                    target[pl.ds(pl.multiple_of(c * CORE + x * PITCH, 8), PITCH)] = value
                else:
                    target[pl.ds(c * FIELD + at, PITCH)] = value
            return carry

        lax.fori_loop(low, high, body, 0)

    def copy(source, target, columns):
        for c in range(NC):
            for x in columns:
                at = c * FIELD + (FIRST + x) * PITCH
                target[at : at + PITCH] = source[at : at + PITCH]

    add_forcing(forced, STEPS - 1, range(CX))
    sweep(forced, field_2, 2, CX - 2)
    add_forcing(field_2, STEPS - 2, range(2, CX - 2))
    copy(back_2, field_2, (0, 1, CX - 2, CX - 1))
    sweep(field_2, field_1, 1, CX - 1)
    add_forcing(field_1, STEPS - 3, range(1, CX - 1))
    copy(back_1, field_1, (-1, 0, CX - 1, CX))
    sweep(field_1, out, 0, CX)


def add_x(ny, delta, picks, core, x_a, x_b, *rest):
    out_a, out_b, out_near, out_sums = rest[:4]
    out_others = rest[4:-2]
    merged = ny == 4
    field, sums = rest[-2:]
    even, _, _ = place_on("gy")
    total = picks.shape[1]
    rows = total * NC // ny
    field[...] = core[...]
    for c in range(NC):
        for away, start, extra in WIDE:
            for source, target, size in (
                (0, PITCH - extra, extra),
                (extra, 0, CY + extra),
            ):
                if size:
                    at = c * WIDE_ROWS + start + source
                    west, east = x_sides(x_a, x_b, pl.ds(at, size))
                    at = c * CORE + (away - 1) * PITCH + target
                    field[at : at + size] += west
                    at = c * CORE + (CX - away) * PITCH + target
                    field[at : at + size] += east
    for c in range(NC):
        for away in range(1, RIM + 1):
            north = field[pl.ds(c * CORE + CY - 1 + away, CX, stride=PITCH)]
            south = field[pl.ds(c * CORE + PITCH - away, CX, stride=PITCH)]
            at = (c * RIM + away - 1) * CX
            out_a[at : at + CX] = jnp.where(even, north, south)
            out_b[at : at + CX] = jnp.where(even, south, north)
        for x in range(CX):
            at = c * CORE + x * PITCH
            here = slice(x * CY, (x + 1) * CY)
            out_near[c, here] = delta[c, here] + field[at : at + CY]
    adjoint = jnp.concatenate([field[c * CORE : (c + 1) * CORE] for c in range(NC)], axis=1)
    tile_sums = two_part_dot(jnp.transpose(picks[...]).astype(bf16), adjoint)
    for c in range(NC):
        sums[pl.ds(c, total, stride=NC)] = tile_sums[:, c * 128 : (c + 1) * 128]
    out_sums[...] = sums[0:rows]
    out_a[Y_COEF:] = sums[rows : 2 * rows]
    if merged:
        out_b[Y_COEF:] = sums[3 * rows : 4 * rows]
    for s, other in enumerate(out_others):
        other[...] = sums[(2 + s) * rows : (3 + s) * rows]


def add_y(alpha, near, sums, y_a, y_b, *rest):
    others = rest[:-2]
    out_delta, out_alpha = rest[-2:]
    out_delta[...] = near[...]
    for c in range(NC):
        for away in range(1, RIM + 1):
            north, south = y_sides(y_a, y_b, pl.ds((c * RIM + away - 1) * CX, CX))
            high = pl.ds(CY - away, CX, stride=CY)
            low = pl.ds(away - 1, CX, stride=CY)
            out_delta[c, high] = out_delta[c, high] + north
            out_delta[c, low] = out_delta[c, low] + south
    total = sums[...] + y_a[Y_COEF:]
    if y_b.shape[0] > Y_COEF:
        total = total + y_b[Y_COEF:]
    for other in others:
        total = total + other[...]
    out_alpha[...] = alpha[...] + profile_weight * total


def on_device(
    delta,
    alpha,
    eddy,
    courant,
    tile_map,
    obs_rows,
    gate_beam,
    gate_index,
    gate_column,
    gate_live,
    obs_weight,
    obs_precision,
):
    nx = lax.axis_size("gx")
    ny = lax.axis_size("gy")
    owned = alpha.shape[1]
    slots = gate_column.shape[2]
    fine = delta.reshape(NC, CX * CY, 128)
    eddy = eddy.reshape(CX * CY, 128)
    courant = courant.reshape(2, CX * CY, 128)
    control = alpha.reshape(owned * NC, 128)
    weights = obs_weight.reshape(slots * NC, 128)
    gates = [
        value.reshape(1, slots)
        for value in (gate_beam, gate_index, gate_column, gate_live, obs_precision)
    ]
    own_beams = jnp.transpose(obs_rows, (1, 0, 2)).reshape(STEPS * OWN_BEAMS, 128)
    beam_count = nx * OWN_BEAMS
    rows = owned * NC
    total = ny * owned

    y_a, y_b, fine, coefs, control_near, near_tiles, meta, near_beams = call(
        pack_y,
        [
            (Y_HALO + rows, 128),
            (Y_HALO, 128),
            fine.shape,
            (3, CX * CY, 128),
            control.shape,
            (CX, 128),
            (8, slots),
            own_beams.shape,
        ],
        [
            pltpu.with_memory_space_constraint(value, pltpu.HBM)
            for value in (fine, eddy, courant, control, tile_map, *gates, own_beams)
        ],
        [
            pltpu.VMEM(tile_map.shape, jnp.int32),
            pltpu.VMEM((4, 1, slots), jnp.int32),
            pltpu.VMEM((1, slots), f32),
            pltpu.SemaphoreType.DMA((12,)),
        ],
        in_specs=[HBM] * 11,
    )
    y_a = swap(y_a, "gy", 1)
    y_b = pair_b(y_b, "gy", "gx")
    others = [swap(control, "gy", xor) for xor in range(2, ny)]
    beams = jnp.concatenate([near_beams, swap(own_beams, "gx", 2)])
    beams = [beams] + [swap(beams, "gx", xor) for xor in range(1, nx) if xor % 4 < 2]

    x_a, x_b = call(
        lambda *refs: pack_x(ny, *refs),
        [(X_HALO, 128), (X_HALO, 128)],
        [fine, coefs, control_near, near_tiles, y_a, y_b, *others],
        [
            pltpu.VMEM((2 * RIM * PITCH, 128), f32),
            pltpu.VMEM((2 * RIM * PITCH, total), f32),
            pltpu.VMEM((total * NC, 128), f32),
            pltpu.VMEM((128, 128), f32),
        ],
    )
    x_a = swap(x_a, "gx", 1)
    x_b = pair_b(x_b, "gx", "gy")

    big = (NC * FIELD, 128)
    (
        core,
        coef,
        picks,
        wide,
        slot_push,
        beam_pick,
        columns,
        state_1,
        state_2,
        tally,
        edge_pick,
    ) = call(
        lambda *refs: prepare(ny, *refs),
        [
            (NC * CORE, 128),
            (5 * CORE, 128),
            (CORE, total),
            (slots, NC * 128),
            jax.ShapeDtypeStruct((CX * CY, slots), bf16),
            jax.ShapeDtypeStruct((slots, beam_count), bf16),
            (slots, 8),
            (NC * CORE, 128),
            (NC * CORE, 128),
            (STEPS * slots, 128),
            jax.ShapeDtypeStruct((slots, 256), bf16),
        ],
        [fine, coefs, control_near, near_tiles, meta, weights, y_a, y_b, *others],
        [
            pltpu.VMEM((NC * CORE, 128), f32),
            pltpu.VMEM((total * NC, 128), f32),
            pltpu.VMEM((128, 128), f32),
        ],
        flops=3000000,
    )
    back_a, back_b, back_2, back_1, edge_coef, tops, lows = call(
        edges,
        [
            (X_COEF, 128),
            (X_COEF, 128),
            big,
            big,
            (5 * FIELD, 128),
            jax.ShapeDtypeStruct((STEPS * slots, NC * 128), bf16),
            jax.ShapeDtypeStruct((STEPS * slots, NC * 128), bf16),
        ],
        [
            core,
            coef,
            state_1,
            state_2,
            tally,
            wide,
            edge_pick,
            slot_push,
            beam_pick,
            columns,
            x_a,
            x_b,
            *beams,
        ],
        [pltpu.VMEM(big, f32)] * 4
        + [
            pltpu.VMEM((3 * FIELD, 128), f32),
            pltpu.VMEM((STEPS * 2 * RIM * CY, NC * 128), f32),
        ],
        flops=10000000,
    )
    (core,) = call(
        interior,
        [(NC * CORE, 128)],
        [coef, edge_coef, back_2, back_1, tops, lows, slot_push],
        [pltpu.VMEM((5 * FIELD, 128), f32)]
        + [pltpu.VMEM(big, f32)] * 3
        + [pltpu.VMEM((STEPS * CX * CY, NC * 128), f32)],
        flops=10000000,
    )
    x_a = swap(back_a, "gx", 1)
    x_b = pair_b(back_b, "gx", "gy")
    loose = [xor for xor in range(2, ny) if ny != 4 or xor != 3]
    back_a, back_b, near, sums, *back = call(
        lambda *refs: add_x(ny, *refs),
        [
            (Y_COEF + rows, 128),
            (Y_COEF + (rows if ny == 4 else 0), 128),
            fine.shape,
            (rows, 128),
        ]
        + [(rows, 128)] * len(loose),
        [fine, picks, core, x_a, x_b],
        [pltpu.VMEM((NC * CORE, 128), f32), pltpu.VMEM((total * NC, 128), f32)],
    )
    y_a = swap(back_a, "gy", 1)
    y_b = ring_b(back_b, "gy")
    others = [swap(value, "gy", xor) for xor, value in zip(loose, back)]
    grad_delta, grad_alpha = call(
        add_y,
        [fine.shape, control.shape],
        [control_near, near, sums, y_a, y_b, *others],
    )
    return grad_delta.reshape(delta.shape), grad_alpha.reshape(alpha.shape)


def solution(mesh):
    return jax.shard_map(
        on_device,
        mesh=mesh,
        in_specs=(
            P(None, "gx", "gy", None),
            P("gx", "gy", None, None),
            P("gx", "gy", None),
            P(None, "gx", "gy", None),
            P("gx", "gy"),
            P(("gx", "gy"), None, None),
            P("gx", "gy", None),
            P("gx", "gy", None),
            P("gx", "gy", None),
            P("gx", "gy", None),
            P("gx", "gy", None, None, None),
            P("gx", "gy", None),
        ),
        out_specs=(P(None, "gx", "gy", None), P("gx", "gy", None, None)),
        check_vma=False,
    )
```

```python
import jax
import jax.numpy as jnp
from jax import lax
from jax.experimental import pallas as pl
from jax.experimental.pallas import tpu as pltpu
from jax.sharding import PartitionSpec as P

STEPS = 3
RIM = 3
INNER = RIM - 1
NC = 4
CX = 16
CY = 16
BLOCKS = CX + 8
PITCH = CY + 8
FIRST = 4
FIELD = BLOCKS * PITCH
CORE = CX * PITCH
OWN_BEAMS = 8
BEAM_BITS = 3

profile_weight = 0.125
f32 = jnp.float32
bf16 = jnp.bfloat16

VMEM = pl.BlockSpec(memory_space=pltpu.VMEM)
HBM = pl.BlockSpec(memory_space=pltpu.HBM)


def call(body, outs, ins, scratch=(), in_specs=None, flops=1000000, limit=40 * 2**20):
    shapes = [
        out if isinstance(out, jax.ShapeDtypeStruct) else jax.ShapeDtypeStruct(out, f32)
        for out in outs
    ]
    size = sum(4 * value.size for value in ins)
    return pl.pallas_call(
        body,
        out_shape=shapes,
        in_specs=in_specs or [VMEM] * len(ins),
        out_specs=[VMEM] * len(shapes),
        scratch_shapes=list(scratch),
        compiler_params=pltpu.CompilerParams(vmem_limit_bytes=limit),
        cost_estimate=pl.CostEstimate(flops=flops, bytes_accessed=size, transcendentals=0),
    )(*ins)


def swap(block, axis, xor):
    return lax.ppermute(block, axis, [(i, i ^ xor) for i in range(lax.axis_size(axis))])


def pair_b(block, axis, other):
    count, across = lax.axis_size(axis), lax.axis_size(other)

    def place(i, j):
        return i * across + j if axis == "gx" else j * count + i

    pairs = []
    for j in range(across):
        for i in range(count):
            if i in (0, count - 1):
                pairs.append((place(i, j), place(i, j ^ 1)))
            else:
                pairs.append((place(i, j), place(i + 1 if i % 2 else i - 1, j)))
    return lax.ppermute(block, ("gx", "gy"), pairs)


def ring_b(block, axis):
    count = lax.axis_size(axis)
    pairs = [(i, (i + 1 if i % 2 else i - 1) % count) for i in range(count)]
    return lax.ppermute(block, axis, pairs)


def place_on(axis):
    me = lax.axis_index(axis)
    return lax.rem(me, 2) == 0, me > 0, me < lax.axis_size(axis) - 1


def split(value):
    top = value.astype(bf16)
    return top, (value - top.astype(f32)).astype(bf16)


def two_part_dot(left, value):
    top, low = split(value)
    return jnp.dot(left, top, preferred_element_type=f32) + jnp.dot(
        left, low, preferred_element_type=f32
    )


def layers(reach):
    found, at = [], 0
    for away in range(1, reach + 1):
        found.append((away, at, reach - away))
        at += CY + 2 * (reach - away)
    return found, at


WIDE, WIDE_ROWS = layers(RIM)
SLIM, SLIM_ROWS = layers(INNER)
X_COEF = NC * WIDE_ROWS
X_HALO = X_COEF + 3 * SLIM_ROWS

Y_COEF = NC * RIM * CX
Y_TILE = Y_COEF + 3 * INNER * CX
Y_HALO = Y_TILE + CX


def pack_y(
    delta,
    eddy,
    courant,
    alpha,
    tile_map,
    gate_beam,
    gate_index,
    gate_column,
    gate_live,
    precision,
    beam_rows,
    out_a,
    out_b,
    fine,
    coefs,
    profiles,
    near_tiles,
    meta,
    beams,
    tiles,
    gates,
    values,
    sems,
):
    even, _, _ = place_on("gy")
    moves = [
        pltpu.make_async_copy(source, target, sems.at[i])
        for i, (source, target) in enumerate(
            [
                (delta, fine),
                (eddy, coefs.at[0]),
                (courant.at[0], coefs.at[1]),
                (courant.at[1], coefs.at[2]),
                (tile_map, tiles),
                (alpha, profiles),
                (gate_beam, gates.at[0]),
                (gate_index, gates.at[1]),
                (gate_column, gates.at[2]),
                (gate_live, gates.at[3]),
                (precision, values),
                (beam_rows, beams),
            ]
        )
    ]
    for move in moves:
        move.start()
    for move in moves:
        move.wait()

    def put(at, field, away):
        north = field[pl.ds(CY - away, CX, stride=CY)]
        south = field[pl.ds(away - 1, CX, stride=CY)]
        out_a[at : at + CX] = jnp.where(even, north, south)
        out_b[at : at + CX] = jnp.where(even, south, north)

    for c in range(NC):
        for away in range(1, RIM + 1):
            put((c * RIM + away - 1) * CX, fine.at[c], away)
    for f in range(3):
        for away in range(1, INNER + 1):
            put(Y_COEF + (f * INNER + away - 1) * CX, coefs.at[f], away)
    near_tiles[...] = jnp.full((CX, 128), -1.0, f32)
    near_tiles[:, 0:CY] = tiles[...].astype(f32)
    for out in (out_a, out_b):
        out[Y_TILE : Y_TILE + CX] = near_tiles[...]
    out_a[Y_HALO:] = profiles[...]
    held = BEAM_BITS
    beam = gates[0]
    owner = jnp.bitwise_xor(beam >> held, lax.axis_index("gx"))
    block = (owner & -4) | ((owner & 1) << 1) | ((owner >> 1) & 1)
    meta[...] = jnp.zeros(meta.shape, f32)
    meta[0:1] = gates[2].astype(f32)
    meta[1:2] = ((block << held) | (beam & ((1 << held) - 1))).astype(f32)
    meta[2:3] = gates[1].astype(f32)
    meta[3:4] = gates[3].astype(f32) * values[...]


def y_sides(got_a, got_b, rows, fill=0.0):
    even, low, high = place_on("gy")
    first, second = got_a[rows], got_b[rows]
    north, south = jnp.where(even, first, second), jnp.where(even, second, first)
    return jnp.where(high, north, fill), jnp.where(low, south, fill)


def x_sides(got_a, got_b, rows):
    even, low, high = place_on("gx")
    first, second = got_a[rows], got_b[rows]
    west, east = jnp.where(even, second, first), jnp.where(even, first, second)
    return jnp.where(low, west, 0.0), jnp.where(high, east, 0.0)


def gather_known(alpha, got_a, others, known):
    owned = alpha.shape[0]
    known[0:owned] = alpha[...]
    known[owned : 2 * owned] = got_a[Y_HALO:]
    for s, other in enumerate(others):
        known[(2 + s) * owned : (3 + s) * owned] = other[...]


def tile_numbers(near_tiles, got_a, got_b, tiles):
    spot = lax.broadcasted_iota(jnp.int32, (CX, 128), 1)
    north, south = y_sides(got_a, got_b, pl.ds(Y_TILE, CX), -1.0)
    near = jnp.where(
        (spot >= CY) & (spot < CY + RIM),
        pltpu.roll(north, CY, 1),
        jnp.where((spot >= PITCH - RIM) & (spot < PITCH), pltpu.roll(south, PITCH - CY, 1), -1.0),
    )
    tiles[...] = jnp.full(tiles.shape, -1.0, f32)
    tiles[0:CX] = jnp.where(spot < CY, near_tiles[...], near)
    return jnp.transpose(tiles[...])[0:PITCH]


def tile_ids(ny, owned):
    me = lax.axis_index("gy")
    lane = lax.broadcasted_iota(jnp.int32, (1, ny * owned), 1)
    ids = lane
    for s in range(ny):
        here = (lane >= s * owned) & (lane < (s + 1) * owned)
        ids = jnp.where(here, jnp.bitwise_xor(me, s) * owned + lane - s * owned, ids)
    return ids.astype(f32)


def by_variable(ref, count):
    return jnp.concatenate([ref[pl.ds(c, count, stride=NC)] for c in range(NC)], axis=1)


def pack_x(ny, delta, coefs, alpha, near_tiles, _, y_a, y_b, *rest):
    others = rest[: ny - 2]
    out_a, out_b, field, picks, known, tiles = rest[ny - 2 :]
    even, _, _ = place_on("gx")
    out_b[X_HALO:] = jnp.zeros((8, 128), f32)
    owned = alpha.shape[0] // NC
    gather_known(alpha, y_a, others, known)
    turned = tile_numbers(near_tiles, y_a, y_b, tiles)
    ids = tile_ids(ny, owned)
    columns = [x for x in range(RIM)] + [CX - RIM + x for x in range(RIM)]
    for i, x in enumerate(columns):
        picks[i * PITCH : (i + 1) * PITCH] = (turned[:, x : x + 1] == ids).astype(f32)
    fine = two_part_dot(picks[...].astype(bf16), by_variable(known, ny * owned))

    def fill(own, y_base, reach, c):
        for i, x in enumerate(columns):
            at = i * PITCH
            field[at + CY : at + PITCH] = jnp.zeros((PITCH - CY, 128), f32)
            field[at : at + CY] = own[x * CY : (x + 1) * CY]
        for away in range(1, reach + 1):
            for first, base in ((0, 0), (CX - RIM, RIM * PITCH)):
                rows = pl.ds(y_base + (away - 1) * CX + first, RIM)
                north, south = y_sides(y_a, y_b, rows)
                field[pl.ds(base + CY - 1 + away, RIM, stride=PITCH)] = north
                field[pl.ds(base + PITCH - away, RIM, stride=PITCH)] = south
        if c is not None:
            field[...] += profile_weight * fine[:, c * 128 : (c + 1) * 128]

    def put(at, found):
        for away, start, extra in found:
            east, west = (2 * RIM - away) * PITCH, (away - 1) * PITCH
            here = at + start
            for source, target, size in (
                (PITCH - extra, 0, extra),
                (0, extra, CY + extra),
            ):
                if size:
                    first = field[east + source : east + source + size]
                    second = field[west + source : west + source + size]
                    rows = slice(here + target, here + target + size)
                    out_a[rows] = jnp.where(even, first, second)
                    out_b[rows] = jnp.where(even, second, first)

    for c in range(NC):
        fill(delta.at[c], c * RIM * CX, RIM, c)
        put(c * WIDE_ROWS, WIDE)
    for f in range(3):
        fill(coefs.at[f], Y_COEF + f * INNER * CX, INNER, None)
        put(X_COEF + f * SLIM_ROWS, SLIM)


def one_hots(meta, weights, wide, slot_pick, slot_push, beam_pick, columns, edge_pick):
    slots = meta.shape[1]
    for c in range(NC):
        wide[:, c * 128 : (c + 1) * 128] = weights[pl.ds(c, slots, stride=NC)]
    per_beam = beam_pick.shape[1]
    turned = jnp.transpose(meta[...])
    columns[...] = turned
    slot_lane = lax.broadcasted_iota(jnp.int32, (slots, CX * CY), 1).astype(f32)
    slot_pick[...] = (slot_lane == turned[:, 0:1]).astype(f32).astype(bf16)
    edge_lane = lax.broadcasted_iota(jnp.int32, (slots, 128), 1)
    half = RIM * CY
    place = jnp.where(edge_lane < half, edge_lane, edge_lane + CX * CY - 2 * half)
    place = jnp.where(edge_lane < 2 * half, place, -1).astype(f32)
    near_edge = (place == turned[:, 0:1]).astype(f32).astype(bf16)
    edge_pick[:, 0:128] = near_edge
    edge_pick[:, 128:256] = near_edge
    column_row = lax.broadcasted_iota(jnp.int32, (CX * CY, slots), 0).astype(f32)
    slot_push[...] = (column_row == meta[0:1]).astype(f32).astype(bf16)
    beam_lane = lax.broadcasted_iota(jnp.int32, (slots, per_beam), 1).astype(f32)
    beam_pick[...] = (beam_lane == turned[:, 1:2]).astype(f32).astype(bf16)


def prepare(ny, delta, coefs, alpha, near_tiles, columns, slot_pick, wide, y_a, y_b, *rest):
    others = rest[: ny - 2]
    core, coef, picks, state_1, state_2, tally, state_3, known, tiles = rest[ny - 2 :]
    owned = alpha.shape[0] // NC

    def fill(ref, base, own, y_base, reach):
        for x in range(CX):
            at = base + x * PITCH
            ref[at : at + CY] = own[x * CY : (x + 1) * CY]
            ref[at + CY : at + PITCH] = jnp.zeros((PITCH - CY, 128), f32)
        for away in range(1, reach + 1):
            north, south = y_sides(y_a, y_b, pl.ds(y_base + (away - 1) * CX, CX))
            ref[pl.ds(base + CY - 1 + away, CX, stride=PITCH)] = north
            ref[pl.ds(base + PITCH - away, CX, stride=PITCH)] = south

    for c in range(NC):
        fill(core, c * CORE, delta.at[c], c * RIM * CX, RIM)
    for f in range(3):
        fill(coef, f * CORE, coefs.at[f], Y_COEF + f * INNER * CX, INNER)

    def combine(b, carry):
        at = pl.multiple_of(b * PITCH, 8)
        combined = combine_coefs(*[coef[pl.ds(f * CORE + at, PITCH)] for f in range(3)])
        for f, value in enumerate(combined):
            coef[pl.ds(f * CORE + at, PITCH)] = value
        return carry

    lax.fori_loop(0, CX, combine, 0)

    gather_known(alpha, y_a, others, known)
    turned = tile_numbers(near_tiles, y_a, y_b, tiles)
    ids = tile_ids(ny, owned)
    for x in range(CX):
        picks[x * PITCH : (x + 1) * PITCH] = (turned[:, x : x + 1] == ids).astype(f32)
    fine = two_part_dot(picks[...].astype(bf16), by_variable(known, ny * owned))
    for c in range(NC):
        core[c * CORE : (c + 1) * CORE] += profile_weight * fine[:, c * 128 : (c + 1) * 128]

    slots = columns.shape[0]
    states = [core, state_1, state_2, state_3]
    for step in range(STEPS):
        source, target = states[step], states[step + 1]

        def body(x, carry, source=source, target=target):
            at = pl.multiple_of(x * PITCH, 8)
            k = [coef[pl.ds(f * CORE + at, PITCH)] for f in range(5)]
            for c in range(NC):
                base = c * CORE + at
                target[pl.ds(base, PITCH)] = forward_column(source, base, k)
            return carry

        lax.fori_loop(step + 1, CX - 1 - step, body, 0)
        own = []
        for c in range(NC):
            pieces = [jnp.zeros(((step + 1) * CY, 128), f32)]
            for x in range(step + 1, CX - 1 - step):
                at = c * CORE + x * PITCH
                pieces.append(target[at : at + CY])
            own.append(jnp.concatenate(pieces + pieces[:1], axis=0))
        seen = two_part_dot(slot_pick[...], jnp.concatenate(own, axis=1)) * wide[...]
        total = seen[:, 0:128]
        for c in range(1, NC):
            total = total + seen[:, c * 128 : (c + 1) * 128]
        tally[step * slots : (step + 1) * slots] = total


def forward_column(source, base, k):
    here = source[pl.ds(base, PITCH)]
    return (
        k[0] * here
        + k[1] * source[pl.ds(base + PITCH, PITCH)]
        + k[2] * source[pl.ds(base - PITCH, PITCH)]
        + k[3] * pltpu.roll(here, PITCH - 1, 0)
        + k[4] * pltpu.roll(here, 1, 0)
    )


def backward_column(source, base, coef, at):
    here = source[pl.ds(base, PITCH)]
    return (
        coef[pl.ds(at, PITCH)] * here
        + coef[pl.ds(FIELD + at - PITCH, PITCH)] * source[pl.ds(base - PITCH, PITCH)]
        + coef[pl.ds(2 * FIELD + at + PITCH, PITCH)] * source[pl.ds(base + PITCH, PITCH)]
        + pltpu.roll(coef[pl.ds(3 * FIELD + at, PITCH)] * here, 1, 0)
        + pltpu.roll(coef[pl.ds(4 * FIELD + at, PITCH)] * here, PITCH - 1, 0)
    )


def combine_coefs(viscous, along_x, along_y):
    half_x, half_y = 0.5 * along_x, 0.5 * along_y
    return (
        1.0 - 4.0 * viscous,
        viscous - half_x,
        viscous + half_x,
        viscous - half_y,
        viscous + half_y,
    )


def clear(ref, base, blocks):
    for b in blocks:
        at = base + b * PITCH
        ref[at : at + PITCH] = jnp.zeros((PITCH, 128), f32)


def edges(
    core,
    core_coef,
    near_1,
    near_2,
    tally,
    wide,
    edge_pick,
    slot_push,
    beam_pick,
    columns,
    x_a,
    x_b,
    *rest,
):
    beams = rest[:-13]
    out_a, out_b, back_2, back_1, coef, tops, lows = rest[-13:-6]
    state_0, state_1, state_2, state_3, raw, forcing = rest[-6:]
    even, _, _ = place_on("gx")
    out_b[X_COEF:] = jnp.zeros((8, 128), f32)
    slots = columns.shape[0]

    def fill(ref, base, x_base, found):
        for away, start, extra in found:
            for source, target, size in (
                (0, PITCH - extra, extra),
                (extra, 0, CY + extra),
            ):
                if size:
                    at = x_base + start + source
                    west, east = x_sides(x_a, x_b, pl.ds(at, size))
                    at = base + (FIRST - away) * PITCH + target
                    ref[at : at + size] = west
                    at = base + (FIRST + CX - 1 + away) * PITCH + target
                    ref[at : at + size] = east

    def copy(source, target, x, count):
        for c in range(NC):
            first = c * CORE + x * PITCH
            at = c * FIELD + (FIRST + x) * PITCH
            target[at : at + count * PITCH] = source[first : first + count * PITCH]

    rim = [FIRST - 3, FIRST - 2, FIRST - 1, FIRST + CX, FIRST + CX + 1, FIRST + CX + 2]
    for x, (source, target) in enumerate(((core, state_0), (near_1, state_1), (near_2, state_2))):
        copy(source, target, x, 2)
        copy(source, target, CX - 2 - x, 2)
    for c in range(NC):
        clear(state_0, c * FIELD, rim)
        fill(state_0, c * FIELD, c * WIDE_ROWS, WIDE)
    for f in range(3):
        clear(raw, f * FIELD, rim[1:5])
        fill(raw, f * FIELD, X_COEF + f * SLIM_ROWS, SLIM)
    for f in range(5):
        for x in (0, CX - RIM):
            first, at = f * CORE + x * PITCH, f * FIELD + (FIRST + x) * PITCH
            coef[at : at + RIM * PITCH] = core_coef[first : first + RIM * PITCH]
        clear(coef, f * FIELD, [0, 1, BLOCKS - 2, BLOCKS - 1])
    for b in rim[1:5]:
        rows = [slice(f * FIELD + b * PITCH, f * FIELD + (b + 1) * PITCH) for f in range(5)]
        for f, value in enumerate(combine_coefs(*[raw[rows[f]] for f in range(3)])):
            coef[rows[f]] = value

    gate_lane = lax.broadcasted_iota(jnp.int32, (slots, 128), 1).astype(f32)
    gate_here = gate_lane == columns[:, 2:3]
    scaled = columns[:, 3:4]
    outer = [*range(RIM), *range(CX - RIM, CX)]
    half = RIM * CY
    push = jnp.concatenate([slot_push[0:half], slot_push[CX * CY - half :]], axis=0)
    states = [state_0, state_1, state_2, state_3]
    for step in range(STEPS):
        source, target = states[step], states[step + 1]
        for x in range(step - 2, step + 1):
            for b in (FIRST + x, FIRST + CX - 1 - x):
                at = b * PITCH
                k = [coef[f * FIELD + at : f * FIELD + at + PITCH] for f in range(5)]
                for c in range(NC):
                    base = c * FIELD + at
                    target[base : base + PITCH] = forward_column(source, base, k)
        zero = jnp.zeros((CY, 128), f32)
        parts = []
        for c in range(NC):
            pieces = []
            for x in outer:
                at = c * FIELD + (FIRST + x) * PITCH
                known = x <= step or x >= CX - 1 - step
                pieces.append(target[at : at + CY] if known else zero)
            value = jnp.concatenate(pieces + [jnp.zeros((128 - 2 * half, 128), f32)], axis=0)
            parts.append(jnp.concatenate(split(value), axis=0))
        seen = jnp.dot(
            edge_pick[...], jnp.concatenate(parts, axis=1), preferred_element_type=f32
        )
        seen = seen * wide[...]
        table = []
        for part in beams:
            for at in range(0, part.shape[0], STEPS * OWN_BEAMS):
                first = at + step * OWN_BEAMS
                table.append(part[first : first + OWN_BEAMS])
        table = two_part_dot(beam_pick[...], jnp.concatenate(table, axis=0))
        rows = slice(step * slots, (step + 1) * slots)
        total = tally[rows] - jnp.where(gate_here, table, 0.0)
        for c in range(NC):
            total = total + seen[:, c * 128 : (c + 1) * 128]
        misfit = scaled * jnp.sum(total, axis=1, keepdims=True)
        top, low = split(misfit * wide[...])
        tops[rows] = top
        lows[rows] = low
        forcing[step * 2 * half : (step + 1) * 2 * half] = jnp.dot(
            push, top, preferred_element_type=f32
        ) + jnp.dot(push, low, preferred_element_type=f32)

    def forced(step, i, c):
        at = step * 2 * half + i * CY
        return forcing[at : at + CY, c * 128 : (c + 1) * 128]

    for c in range(NC):
        clear(state_0, c * FIELD, [2, 3, BLOCKS - 4, BLOCKS - 3])
        clear(back_2, c * FIELD, [1, 2, BLOCKS - 3, BLOCKS - 2])
        clear(back_1, c * FIELD, [0, 1, BLOCKS - 2, BLOCKS - 1])
        for i, x in enumerate(outer):
            at = c * FIELD + (FIRST + x) * PITCH
            state_0[at : at + CY] = forced(STEPS - 1, i, c)
            state_0[at + CY : at + PITCH] = jnp.zeros((PITCH - CY, 128), f32)
    fields = [state_0, back_2, back_1, state_3]
    for step in range(STEPS):
        source, target = fields[step], fields[step + 1]
        for x in range(-1 - step, 2 - step):
            for b in (FIRST + x, FIRST + CX - 1 - x):
                for c in range(NC):
                    base = c * FIELD + b * PITCH
                    target[base : base + PITCH] = backward_column(source, base, coef, b * PITCH)
        if step < STEPS - 1:
            for i, x in enumerate(outer):
                if x < 2 - step or x > CX - 3 + step:
                    for c in range(NC):
                        at = c * FIELD + (FIRST + x) * PITCH
                        target[at : at + CY] += forced(STEPS - 2 - step, i, c)
    for c in range(NC):
        for away, start, extra in WIDE:
            for source, target, size in (
                (PITCH - extra, 0, extra),
                (0, extra, CY + extra),
            ):
                if size:
                    at = c * FIELD + (FIRST - away) * PITCH + source
                    west = state_3[at : at + size]
                    at = c * FIELD + (FIRST + CX - 1 + away) * PITCH + source
                    east = state_3[at : at + size]
                    at = c * WIDE_ROWS + start + target
                    out_a[at : at + size] = jnp.where(even, east, west)
                    out_b[at : at + size] = jnp.where(even, west, east)


def interior(core_coef, edge_coef, back_2, back_1, tops, lows, slot_push, out, *scratch):
    coef, forced, field_2, field_1, forcing = scratch
    for f in range(5):
        at = f * FIELD + FIRST * PITCH
        coef[at : at + CORE] = core_coef[f * CORE : (f + 1) * CORE]
        for b in (FIRST - 1, FIRST + CX):
            at = f * FIELD + b * PITCH
            coef[at : at + PITCH] = edge_coef[at : at + PITCH]
    for step in range(STEPS):
        rows = slice(step * CX * CY, (step + 1) * CX * CY)
        forcing[rows] = jnp.dot(
            slot_push[...], tops[rows], preferred_element_type=f32
        ) + jnp.dot(slot_push[...], lows[rows], preferred_element_type=f32)

    def add_forcing(ref, step, columns):
        for c in range(NC):
            for x in columns:
                at = c * FIELD + (FIRST + x) * PITCH
                first = step * CX * CY + x * CY
                value = forcing[first : first + CY, c * 128 : (c + 1) * 128]
                if step == STEPS - 1:
                    ref[at : at + CY] = value
                    ref[at + CY : at + PITCH] = jnp.zeros((PITCH - CY, 128), f32)
                else:
                    ref[at : at + CY] += value

    def sweep(source, target, low, high):
        def body(x, carry):
            at = pl.multiple_of((x + FIRST) * PITCH, 8)
            for c in range(NC):
                value = backward_column(source, c * FIELD + at, coef, at)
                if target is out:
                    target[pl.ds(pl.multiple_of(c * CORE + x * PITCH, 8), PITCH)] = value
                else:
                    target[pl.ds(c * FIELD + at, PITCH)] = value
            return carry

        lax.fori_loop(low, high, body, 0)

    def copy(source, target, columns):
        for c in range(NC):
            for x in columns:
                at = c * FIELD + (FIRST + x) * PITCH
                target[at : at + PITCH] = source[at : at + PITCH]

    add_forcing(forced, STEPS - 1, range(CX))
    sweep(forced, field_2, 2, CX - 2)
    add_forcing(field_2, STEPS - 2, range(2, CX - 2))
    copy(back_2, field_2, (0, 1, CX - 2, CX - 1))
    sweep(field_2, field_1, 1, CX - 1)
    add_forcing(field_1, STEPS - 3, range(1, CX - 1))
    copy(back_1, field_1, (-1, 0, CX - 1, CX))
    sweep(field_1, out, 0, CX)


def add_x(ny, delta, picks, core, x_a, x_b, *rest):
    out_a, out_b, out_near, out_sums = rest[:4]
    out_others = rest[4:-2]
    merged = ny == 4
    field, sums = rest[-2:]
    even, _, _ = place_on("gy")
    total = picks.shape[1]
    rows = total * NC // ny
    field[...] = core[...]
    for c in range(NC):
        for away, start, extra in WIDE:
            for source, target, size in (
                (0, PITCH - extra, extra),
                (extra, 0, CY + extra),
            ):
                if size:
                    at = c * WIDE_ROWS + start + source
                    west, east = x_sides(x_a, x_b, pl.ds(at, size))
                    at = c * CORE + (away - 1) * PITCH + target
                    field[at : at + size] += west
                    at = c * CORE + (CX - away) * PITCH + target
                    field[at : at + size] += east
    for c in range(NC):
        for away in range(1, RIM + 1):
            north = field[pl.ds(c * CORE + CY - 1 + away, CX, stride=PITCH)]
            south = field[pl.ds(c * CORE + PITCH - away, CX, stride=PITCH)]
            at = (c * RIM + away - 1) * CX
            out_a[at : at + CX] = jnp.where(even, north, south)
            out_b[at : at + CX] = jnp.where(even, south, north)
        for x in range(CX):
            at = c * CORE + x * PITCH
            here = slice(x * CY, (x + 1) * CY)
            out_near[c, here] = delta[c, here] + field[at : at + CY]
    adjoint = jnp.concatenate([field[c * CORE : (c + 1) * CORE] for c in range(NC)], axis=1)
    tile_sums = two_part_dot(jnp.transpose(picks[...]).astype(bf16), adjoint)
    for c in range(NC):
        sums[pl.ds(c, total, stride=NC)] = tile_sums[:, c * 128 : (c + 1) * 128]
    out_sums[...] = sums[0:rows]
    out_a[Y_COEF:] = sums[rows : 2 * rows]
    if merged:
        out_b[Y_COEF:] = sums[3 * rows : 4 * rows]
    for s, other in enumerate(out_others):
        other[...] = sums[(2 + s) * rows : (3 + s) * rows]


def add_y(alpha, near, sums, y_a, y_b, *rest):
    others = rest[:-2]
    out_delta, out_alpha = rest[-2:]
    out_delta[...] = near[...]
    for c in range(NC):
        for away in range(1, RIM + 1):
            north, south = y_sides(y_a, y_b, pl.ds((c * RIM + away - 1) * CX, CX))
            high = pl.ds(CY - away, CX, stride=CY)
            low = pl.ds(away - 1, CX, stride=CY)
            out_delta[c, high] = out_delta[c, high] + north
            out_delta[c, low] = out_delta[c, low] + south
    total = sums[...] + y_a[Y_COEF:]
    if y_b.shape[0] > Y_COEF:
        total = total + y_b[Y_COEF:]
    for other in others:
        total = total + other[...]
    out_alpha[...] = alpha[...] + profile_weight * total


def on_device(
    delta,
    alpha,
    eddy,
    courant,
    tile_map,
    obs_rows,
    gate_beam,
    gate_index,
    gate_column,
    gate_live,
    obs_weight,
    obs_precision,
):
    nx = lax.axis_size("gx")
    ny = lax.axis_size("gy")
    owned = alpha.shape[1]
    slots = gate_column.shape[2]
    fine = delta.reshape(NC, CX * CY, 128)
    eddy = eddy.reshape(CX * CY, 128)
    courant = courant.reshape(2, CX * CY, 128)
    control = alpha.reshape(owned * NC, 128)
    weights = obs_weight.reshape(slots * NC, 128)
    gates = [
        value.reshape(1, slots)
        for value in (gate_beam, gate_index, gate_column, gate_live, obs_precision)
    ]
    own_beams = jnp.transpose(obs_rows, (1, 0, 2)).reshape(STEPS * OWN_BEAMS, 128)
    beam_count = nx * OWN_BEAMS
    rows = owned * NC
    total = ny * owned

    y_a, y_b, fine, coefs, control_near, near_tiles, meta, near_beams = call(
        pack_y,
        [
            (Y_HALO + rows, 128),
            (Y_HALO, 128),
            fine.shape,
            (3, CX * CY, 128),
            control.shape,
            (CX, 128),
            (8, slots),
            own_beams.shape,
        ],
        [
            pltpu.with_memory_space_constraint(value, pltpu.HBM)
            for value in (fine, eddy, courant, control, tile_map, *gates, own_beams)
        ],
        [
            pltpu.VMEM(tile_map.shape, jnp.int32),
            pltpu.VMEM((4, 1, slots), jnp.int32),
            pltpu.VMEM((1, slots), f32),
            pltpu.SemaphoreType.DMA((12,)),
        ],
        in_specs=[HBM] * 11,
    )
    y_a = swap(y_a, "gy", 1)
    y_b = pair_b(y_b, "gy", "gx")
    others = [swap(control, "gy", xor) for xor in range(2, ny)]
    beams = jnp.concatenate([near_beams, swap(own_beams, "gx", 2)])
    beams = [beams] + [swap(beams, "gx", xor) for xor in range(1, nx) if xor % 4 < 2]

    wide, slot_pick, slot_push, beam_pick, columns, edge_pick = call(
        one_hots,
        [
            (slots, NC * 128),
            jax.ShapeDtypeStruct((slots, CX * CY), bf16),
            jax.ShapeDtypeStruct((CX * CY, slots), bf16),
            jax.ShapeDtypeStruct((slots, beam_count), bf16),
            (slots, 8),
            jax.ShapeDtypeStruct((slots, 256), bf16),
        ],
        [meta, weights],
    )
    x_a, x_b = call(
        lambda *refs: pack_x(ny, *refs),
        [(X_HALO, 128), (X_HALO + 8, 128)],
        [fine, coefs, control_near, near_tiles, columns, y_a, y_b, *others],
        [
            pltpu.VMEM((2 * RIM * PITCH, 128), f32),
            pltpu.VMEM((2 * RIM * PITCH, total), f32),
            pltpu.VMEM((total * NC, 128), f32),
            pltpu.VMEM((128, 128), f32),
        ],
    )
    x_a = swap(x_a, "gx", 1)
    x_b = pair_b(x_b, "gx", "gy")

    big = (NC * FIELD, 128)
    core, coef, picks, state_1, state_2, tally = call(
        lambda *refs: prepare(ny, *refs),
        [
            (NC * CORE, 128),
            (5 * CORE, 128),
            (CORE, total),
            (NC * CORE, 128),
            (NC * CORE, 128),
            (STEPS * slots, 128),
        ],
        [fine, coefs, control_near, near_tiles, columns, slot_pick, wide, y_a, y_b, *others],
        [
            pltpu.VMEM((NC * CORE, 128), f32),
            pltpu.VMEM((total * NC, 128), f32),
            pltpu.VMEM((128, 128), f32),
        ],
        flops=3000000,
    )
    back_a, back_b, back_2, back_1, edge_coef, tops, lows = call(
        edges,
        [
            (X_COEF, 128),
            (X_COEF + 8, 128),
            big,
            big,
            (5 * FIELD, 128),
            jax.ShapeDtypeStruct((STEPS * slots, NC * 128), bf16),
            jax.ShapeDtypeStruct((STEPS * slots, NC * 128), bf16),
        ],
        [
            core,
            coef,
            state_1,
            state_2,
            tally,
            wide,
            edge_pick,
            slot_push,
            beam_pick,
            columns,
            x_a,
            x_b,
            *beams,
        ],
        [pltpu.VMEM(big, f32)] * 4
        + [
            pltpu.VMEM((3 * FIELD, 128), f32),
            pltpu.VMEM((STEPS * 2 * RIM * CY, NC * 128), f32),
        ],
        flops=10000000,
    )
    (core,) = call(
        interior,
        [(NC * CORE, 128)],
        [coef, edge_coef, back_2, back_1, tops, lows, slot_push],
        [pltpu.VMEM((5 * FIELD, 128), f32)]
        + [pltpu.VMEM(big, f32)] * 3
        + [pltpu.VMEM((STEPS * CX * CY, NC * 128), f32)],
        flops=10000000,
    )
    x_a = swap(back_a, "gx", 1)
    x_b = pair_b(back_b, "gx", "gy")
    loose = [xor for xor in range(2, ny) if ny != 4 or xor != 3]
    back_a, back_b, near, sums, *back = call(
        lambda *refs: add_x(ny, *refs),
        [
            (Y_COEF + rows, 128),
            (Y_COEF + (rows if ny == 4 else 0), 128),
            fine.shape,
            (rows, 128),
        ]
        + [(rows, 128)] * len(loose),
        [fine, picks, core, x_a, x_b],
        [pltpu.VMEM((NC * CORE, 128), f32), pltpu.VMEM((total * NC, 128), f32)],
    )
    y_a = swap(back_a, "gy", 1)
    y_b = ring_b(back_b, "gy")
    others = [swap(value, "gy", xor) for xor, value in zip(loose, back)]
    grad_delta, grad_alpha = call(
        add_y,
        [fine.shape, control.shape],
        [control_near, near, sums, y_a, y_b, *others],
    )
    return grad_delta.reshape(delta.shape), grad_alpha.reshape(alpha.shape)


def solution(mesh):
    return jax.shard_map(
        on_device,
        mesh=mesh,
        in_specs=(
            P(None, "gx", "gy", None),
            P("gx", "gy", None, None),
            P("gx", "gy", None),
            P(None, "gx", "gy", None),
            P("gx", "gy"),
            P(("gx", "gy"), None, None),
            P("gx", "gy", None),
            P("gx", "gy", None),
            P("gx", "gy", None),
            P("gx", "gy", None),
            P("gx", "gy", None, None, None),
            P("gx", "gy", None),
        ),
        out_specs=(P(None, "gx", "gy", None), P("gx", "gy", None, None)),
        check_vma=False,
    )
```

```python
import jax
import jax.numpy as jnp
from jax import lax
from jax.experimental import pallas as pl
from jax.experimental.pallas import tpu as pltpu
from jax.sharding import PartitionSpec as P

STEPS = 3
RIM = 3
INNER = RIM - 1
NC = 4
CX = 16
CY = 16
BLOCKS = CX + 8
PITCH = CY + 8
FIRST = 4
FIELD = BLOCKS * PITCH
CORE = CX * PITCH
OWN_BEAMS = 8
BEAM_BITS = 3

profile_weight = 0.125
f32 = jnp.float32
bf16 = jnp.bfloat16

VMEM = pl.BlockSpec(memory_space=pltpu.VMEM)
HBM = pl.BlockSpec(memory_space=pltpu.HBM)


def call(body, outs, ins, scratch=(), in_specs=None, flops=1000000, limit=40 * 2**20):
    shapes = [
        out if isinstance(out, jax.ShapeDtypeStruct) else jax.ShapeDtypeStruct(out, f32)
        for out in outs
    ]
    size = sum(4 * value.size for value in ins)
    return pl.pallas_call(
        body,
        out_shape=shapes,
        in_specs=in_specs or [VMEM] * len(ins),
        out_specs=[VMEM] * len(shapes),
        scratch_shapes=list(scratch),
        compiler_params=pltpu.CompilerParams(vmem_limit_bytes=limit),
        cost_estimate=pl.CostEstimate(flops=flops, bytes_accessed=size, transcendentals=0),
    )(*ins)


def swap(block, axis, xor):
    return lax.ppermute(block, axis, [(i, i ^ xor) for i in range(lax.axis_size(axis))])


def pair_b(block, axis, other):
    count, across = lax.axis_size(axis), lax.axis_size(other)

    def place(i, j):
        return i * across + j if axis == "gx" else j * count + i

    pairs = []
    for j in range(across):
        for i in range(count):
            if i in (0, count - 1):
                pairs.append((place(i, j), place(i, j ^ 1)))
            else:
                pairs.append((place(i, j), place(i + 1 if i % 2 else i - 1, j)))
    return lax.ppermute(block, ("gx", "gy"), pairs)


def ring_b(block, axis):
    count = lax.axis_size(axis)
    pairs = [(i, (i + 1 if i % 2 else i - 1) % count) for i in range(count)]
    return lax.ppermute(block, axis, pairs)


def place_on(axis):
    me = lax.axis_index(axis)
    return lax.rem(me, 2) == 0, me > 0, me < lax.axis_size(axis) - 1


def split(value):
    top = value.astype(bf16)
    return top, (value - top.astype(f32)).astype(bf16)


def two_part_dot(left, value):
    top, low = split(value)
    return jnp.dot(left, top, preferred_element_type=f32) + jnp.dot(
        left, low, preferred_element_type=f32
    )


def layers(reach):
    found, at = [], 0
    for away in range(1, reach + 1):
        found.append((away, at, reach - away))
        at += CY + 2 * (reach - away)
    return found, at


WIDE, WIDE_ROWS = layers(RIM)
SLIM, SLIM_ROWS = layers(INNER)
X_COEF = NC * WIDE_ROWS
X_HALO = X_COEF + 3 * SLIM_ROWS

Y_COEF = NC * RIM * CX
Y_TILE = Y_COEF + 3 * INNER * CX
Y_HALO = Y_TILE + CX


def pack_y(
    delta,
    eddy,
    courant,
    alpha,
    tile_map,
    gate_beam,
    gate_index,
    gate_column,
    gate_live,
    precision,
    beam_rows,
    out_a,
    out_b,
    fine,
    coefs,
    profiles,
    near_tiles,
    meta,
    beams,
    tiles,
    gates,
    values,
    sems,
):
    even, _, _ = place_on("gy")
    moves = [
        pltpu.make_async_copy(source, target, sems.at[i])
        for i, (source, target) in enumerate(
            [
                (delta, fine),
                (eddy, coefs.at[0]),
                (courant.at[0], coefs.at[1]),
                (courant.at[1], coefs.at[2]),
                (tile_map, tiles),
                (alpha, profiles),
                (gate_beam, gates.at[0]),
                (gate_index, gates.at[1]),
                (gate_column, gates.at[2]),
                (gate_live, gates.at[3]),
                (precision, values),
                (beam_rows, beams),
            ]
        )
    ]
    for move in moves:
        move.start()
    for move in moves:
        move.wait()

    def put(at, field, away):
        north = field[pl.ds(CY - away, CX, stride=CY)]
        south = field[pl.ds(away - 1, CX, stride=CY)]
        out_a[at : at + CX] = jnp.where(even, north, south)
        out_b[at : at + CX] = jnp.where(even, south, north)

    for c in range(NC):
        for away in range(1, RIM + 1):
            put((c * RIM + away - 1) * CX, fine.at[c], away)
    for f in range(3):
        for away in range(1, INNER + 1):
            put(Y_COEF + (f * INNER + away - 1) * CX, coefs.at[f], away)
    near_tiles[...] = jnp.full((CX, 128), -1.0, f32)
    near_tiles[:, 0:CY] = tiles[...].astype(f32)
    for out in (out_a, out_b):
        out[Y_TILE : Y_TILE + CX] = near_tiles[...]
    out_a[Y_HALO:] = profiles[...]
    held = BEAM_BITS
    beam = gates[0]
    owner = jnp.bitwise_xor(beam >> held, lax.axis_index("gx"))
    meta[...] = jnp.zeros(meta.shape, f32)
    meta[0:1] = gates[2].astype(f32)
    meta[1:2] = ((owner << held) | (beam & ((1 << held) - 1))).astype(f32)
    meta[2:3] = gates[1].astype(f32)
    meta[3:4] = gates[3].astype(f32) * values[...]


def y_sides(got_a, got_b, rows, fill=0.0):
    even, low, high = place_on("gy")
    first, second = got_a[rows], got_b[rows]
    north, south = jnp.where(even, first, second), jnp.where(even, second, first)
    return jnp.where(high, north, fill), jnp.where(low, south, fill)


def x_sides(got_a, got_b, rows):
    even, low, high = place_on("gx")
    first, second = got_a[rows], got_b[rows]
    west, east = jnp.where(even, second, first), jnp.where(even, first, second)
    return jnp.where(low, west, 0.0), jnp.where(high, east, 0.0)


def gather_known(alpha, got_a, others, known):
    owned = alpha.shape[0]
    known[0:owned] = alpha[...]
    known[owned : 2 * owned] = got_a[Y_HALO:]
    for s, other in enumerate(others):
        known[(2 + s) * owned : (3 + s) * owned] = other[...]


def tile_numbers(near_tiles, got_a, got_b, tiles):
    spot = lax.broadcasted_iota(jnp.int32, (CX, 128), 1)
    north, south = y_sides(got_a, got_b, pl.ds(Y_TILE, CX), -1.0)
    near = jnp.where(
        (spot >= CY) & (spot < CY + RIM),
        pltpu.roll(north, CY, 1),
        jnp.where((spot >= PITCH - RIM) & (spot < PITCH), pltpu.roll(south, PITCH - CY, 1), -1.0),
    )
    tiles[...] = jnp.full(tiles.shape, -1.0, f32)
    tiles[0:CX] = jnp.where(spot < CY, near_tiles[...], near)
    return jnp.transpose(tiles[...])[0:PITCH]


def tile_ids(ny, owned):
    me = lax.axis_index("gy")
    lane = lax.broadcasted_iota(jnp.int32, (1, ny * owned), 1)
    ids = lane
    for s in range(ny):
        here = (lane >= s * owned) & (lane < (s + 1) * owned)
        ids = jnp.where(here, jnp.bitwise_xor(me, s) * owned + lane - s * owned, ids)
    return ids.astype(f32)


def by_variable(ref, count):
    return jnp.concatenate([ref[pl.ds(c, count, stride=NC)] for c in range(NC)], axis=1)


def pack_x(ny, delta, coefs, alpha, near_tiles, _, y_a, y_b, *rest):
    others = rest[: ny - 2]
    out_a, out_b, field, picks, known, tiles = rest[ny - 2 :]
    even, _, _ = place_on("gx")
    owned = alpha.shape[0] // NC
    gather_known(alpha, y_a, others, known)
    turned = tile_numbers(near_tiles, y_a, y_b, tiles)
    ids = tile_ids(ny, owned)
    columns = [x for x in range(RIM)] + [CX - RIM + x for x in range(RIM)]
    for i, x in enumerate(columns):
        picks[i * PITCH : (i + 1) * PITCH] = (turned[:, x : x + 1] == ids).astype(f32)
    fine = two_part_dot(picks[...].astype(bf16), by_variable(known, ny * owned))

    def fill(own, y_base, reach, c):
        for i, x in enumerate(columns):
            at = i * PITCH
            field[at + CY : at + PITCH] = jnp.zeros((PITCH - CY, 128), f32)
            field[at : at + CY] = own[x * CY : (x + 1) * CY]
        for away in range(1, reach + 1):
            for first, base in ((0, 0), (CX - RIM, RIM * PITCH)):
                rows = pl.ds(y_base + (away - 1) * CX + first, RIM)
                north, south = y_sides(y_a, y_b, rows)
                field[pl.ds(base + CY - 1 + away, RIM, stride=PITCH)] = north
                field[pl.ds(base + PITCH - away, RIM, stride=PITCH)] = south
        if c is not None:
            field[...] += profile_weight * fine[:, c * 128 : (c + 1) * 128]

    def put(at, found):
        for away, start, extra in found:
            east, west = (2 * RIM - away) * PITCH, (away - 1) * PITCH
            here = at + start
            for source, target, size in (
                (PITCH - extra, 0, extra),
                (0, extra, CY + extra),
            ):
                if size:
                    first = field[east + source : east + source + size]
                    second = field[west + source : west + source + size]
                    rows = slice(here + target, here + target + size)
                    out_a[rows] = jnp.where(even, first, second)
                    out_b[rows] = jnp.where(even, second, first)

    for c in range(NC):
        fill(delta.at[c], c * RIM * CX, RIM, c)
        put(c * WIDE_ROWS, WIDE)
    for f in range(3):
        fill(coefs.at[f], Y_COEF + f * INNER * CX, INNER, None)
        put(X_COEF + f * SLIM_ROWS, SLIM)


def one_hots(meta, weights, wide, slot_pick, slot_push, beam_pick, columns, edge_pick):
    slots = meta.shape[1]
    for c in range(NC):
        wide[:, c * 128 : (c + 1) * 128] = weights[pl.ds(c, slots, stride=NC)]
    per_beam = beam_pick.shape[1]
    turned = jnp.transpose(meta[...])
    columns[...] = turned
    slot_lane = lax.broadcasted_iota(jnp.int32, (slots, CX * CY), 1).astype(f32)
    slot_pick[...] = (slot_lane == turned[:, 0:1]).astype(f32).astype(bf16)
    edge_lane = lax.broadcasted_iota(jnp.int32, (slots, 128), 1)
    half = RIM * CY
    place = jnp.where(edge_lane < half, edge_lane, edge_lane + CX * CY - 2 * half)
    place = jnp.where(edge_lane < 2 * half, place, -1).astype(f32)
    near_edge = (place == turned[:, 0:1]).astype(f32).astype(bf16)
    edge_pick[:, 0:128] = near_edge
    edge_pick[:, 128:256] = near_edge
    column_row = lax.broadcasted_iota(jnp.int32, (CX * CY, slots), 0).astype(f32)
    slot_push[...] = (column_row == meta[0:1]).astype(f32).astype(bf16)
    beam_lane = lax.broadcasted_iota(jnp.int32, (slots, per_beam), 1).astype(f32)
    beam_pick[...] = (beam_lane == turned[:, 1:2]).astype(f32).astype(bf16)


def prepare(ny, delta, coefs, alpha, near_tiles, columns, slot_pick, wide, y_a, y_b, *rest):
    others = rest[: ny - 2]
    core, coef, picks, state_1, state_2, tally, state_3, known, tiles = rest[ny - 2 :]
    owned = alpha.shape[0] // NC

    def fill(ref, base, own, y_base, reach):
        for x in range(CX):
            at = base + x * PITCH
            ref[at : at + CY] = own[x * CY : (x + 1) * CY]
            ref[at + CY : at + PITCH] = jnp.zeros((PITCH - CY, 128), f32)
        for away in range(1, reach + 1):
            north, south = y_sides(y_a, y_b, pl.ds(y_base + (away - 1) * CX, CX))
            ref[pl.ds(base + CY - 1 + away, CX, stride=PITCH)] = north
            ref[pl.ds(base + PITCH - away, CX, stride=PITCH)] = south

    for c in range(NC):
        fill(core, c * CORE, delta.at[c], c * RIM * CX, RIM)
    for f in range(3):
        fill(coef, f * CORE, coefs.at[f], Y_COEF + f * INNER * CX, INNER)

    def combine(b, carry):
        at = pl.multiple_of(b * PITCH, 8)
        combined = combine_coefs(*[coef[pl.ds(f * CORE + at, PITCH)] for f in range(3)])
        for f, value in enumerate(combined):
            coef[pl.ds(f * CORE + at, PITCH)] = value
        return carry

    lax.fori_loop(0, CX, combine, 0)

    gather_known(alpha, y_a, others, known)
    turned = tile_numbers(near_tiles, y_a, y_b, tiles)
    ids = tile_ids(ny, owned)
    for x in range(CX):
        picks[x * PITCH : (x + 1) * PITCH] = (turned[:, x : x + 1] == ids).astype(f32)
    fine = two_part_dot(picks[...].astype(bf16), by_variable(known, ny * owned))
    for c in range(NC):
        core[c * CORE : (c + 1) * CORE] += profile_weight * fine[:, c * 128 : (c + 1) * 128]

    slots = columns.shape[0]
    states = [core, state_1, state_2, state_3]
    for step in range(STEPS):
        source, target = states[step], states[step + 1]

        def body(x, carry, source=source, target=target):
            at = pl.multiple_of(x * PITCH, 8)
            k = [coef[pl.ds(f * CORE + at, PITCH)] for f in range(5)]
            for c in range(NC):
                base = c * CORE + at
                target[pl.ds(base, PITCH)] = forward_column(source, base, k)
            return carry

        lax.fori_loop(step + 1, CX - 1 - step, body, 0)
        own = []
        for c in range(NC):
            pieces = [jnp.zeros(((step + 1) * CY, 128), f32)]
            for x in range(step + 1, CX - 1 - step):
                at = c * CORE + x * PITCH
                pieces.append(target[at : at + CY])
            own.append(jnp.concatenate(pieces + pieces[:1], axis=0))
        seen = two_part_dot(slot_pick[...], jnp.concatenate(own, axis=1)) * wide[...]
        total = seen[:, 0:128]
        for c in range(1, NC):
            total = total + seen[:, c * 128 : (c + 1) * 128]
        tally[step * slots : (step + 1) * slots] = total


def forward_column(source, base, k):
    here = source[pl.ds(base, PITCH)]
    return (
        k[0] * here
        + k[1] * source[pl.ds(base + PITCH, PITCH)]
        + k[2] * source[pl.ds(base - PITCH, PITCH)]
        + k[3] * pltpu.roll(here, PITCH - 1, 0)
        + k[4] * pltpu.roll(here, 1, 0)
    )


def backward_column(source, base, coef, at):
    here = source[pl.ds(base, PITCH)]
    return (
        coef[pl.ds(at, PITCH)] * here
        + coef[pl.ds(FIELD + at - PITCH, PITCH)] * source[pl.ds(base - PITCH, PITCH)]
        + coef[pl.ds(2 * FIELD + at + PITCH, PITCH)] * source[pl.ds(base + PITCH, PITCH)]
        + pltpu.roll(coef[pl.ds(3 * FIELD + at, PITCH)] * here, 1, 0)
        + pltpu.roll(coef[pl.ds(4 * FIELD + at, PITCH)] * here, PITCH - 1, 0)
    )


def combine_coefs(viscous, along_x, along_y):
    half_x, half_y = 0.5 * along_x, 0.5 * along_y
    return (
        1.0 - 4.0 * viscous,
        viscous - half_x,
        viscous + half_x,
        viscous - half_y,
        viscous + half_y,
    )


def clear(ref, base, blocks):
    for b in blocks:
        at = base + b * PITCH
        ref[at : at + PITCH] = jnp.zeros((PITCH, 128), f32)


def edges(
    core,
    core_coef,
    near_1,
    near_2,
    tally,
    wide,
    edge_pick,
    slot_push,
    beam_pick,
    columns,
    x_a,
    x_b,
    *rest,
):
    beams = rest[:-13]
    out_a, out_b, back_2, back_1, coef, tops, lows = rest[-13:-6]
    state_0, state_1, state_2, state_3, raw, forcing = rest[-6:]
    even, _, _ = place_on("gx")
    slots = columns.shape[0]

    def fill(ref, base, x_base, found):
        for away, start, extra in found:
            for source, target, size in (
                (0, PITCH - extra, extra),
                (extra, 0, CY + extra),
            ):
                if size:
                    at = x_base + start + source
                    west, east = x_sides(x_a, x_b, pl.ds(at, size))
                    at = base + (FIRST - away) * PITCH + target
                    ref[at : at + size] = west
                    at = base + (FIRST + CX - 1 + away) * PITCH + target
                    ref[at : at + size] = east

    def copy(source, target, x, count):
        for c in range(NC):
            first = c * CORE + x * PITCH
            at = c * FIELD + (FIRST + x) * PITCH
            target[at : at + count * PITCH] = source[first : first + count * PITCH]

    rim = [FIRST - 3, FIRST - 2, FIRST - 1, FIRST + CX, FIRST + CX + 1, FIRST + CX + 2]
    for x, (source, target) in enumerate(((core, state_0), (near_1, state_1), (near_2, state_2))):
        copy(source, target, x, 2)
        copy(source, target, CX - 2 - x, 2)
    for c in range(NC):
        clear(state_0, c * FIELD, rim)
        fill(state_0, c * FIELD, c * WIDE_ROWS, WIDE)
    for f in range(3):
        clear(raw, f * FIELD, rim[1:5])
        fill(raw, f * FIELD, X_COEF + f * SLIM_ROWS, SLIM)
    for f in range(5):
        for x in (0, CX - RIM):
            first, at = f * CORE + x * PITCH, f * FIELD + (FIRST + x) * PITCH
            coef[at : at + RIM * PITCH] = core_coef[first : first + RIM * PITCH]
        clear(coef, f * FIELD, [0, 1, BLOCKS - 2, BLOCKS - 1])
    for b in rim[1:5]:
        rows = [slice(f * FIELD + b * PITCH, f * FIELD + (b + 1) * PITCH) for f in range(5)]
        for f, value in enumerate(combine_coefs(*[raw[rows[f]] for f in range(3)])):
            coef[rows[f]] = value

    gate_lane = lax.broadcasted_iota(jnp.int32, (slots, 128), 1).astype(f32)
    gate_here = gate_lane == columns[:, 2:3]
    scaled = columns[:, 3:4]
    outer = [*range(RIM), *range(CX - RIM, CX)]
    half = RIM * CY
    push = jnp.concatenate([slot_push[0:half], slot_push[CX * CY - half :]], axis=0)
    states = [state_0, state_1, state_2, state_3]
    for step in range(STEPS):
        source, target = states[step], states[step + 1]
        for x in range(step - 2, step + 1):
            for b in (FIRST + x, FIRST + CX - 1 - x):
                at = b * PITCH
                k = [coef[f * FIELD + at : f * FIELD + at + PITCH] for f in range(5)]
                for c in range(NC):
                    base = c * FIELD + at
                    target[base : base + PITCH] = forward_column(source, base, k)
        zero = jnp.zeros((CY, 128), f32)
        parts = []
        for c in range(NC):
            pieces = []
            for x in outer:
                at = c * FIELD + (FIRST + x) * PITCH
                known = x <= step or x >= CX - 1 - step
                pieces.append(target[at : at + CY] if known else zero)
            value = jnp.concatenate(pieces + [jnp.zeros((128 - 2 * half, 128), f32)], axis=0)
            parts.append(jnp.concatenate(split(value), axis=0))
        seen = jnp.dot(
            edge_pick[...], jnp.concatenate(parts, axis=1), preferred_element_type=f32
        )
        seen = seen * wide[...]
        table = []
        for part in beams:
            for at in range(0, part.shape[0], STEPS * OWN_BEAMS):
                first = at + step * OWN_BEAMS
                table.append(part[first : first + OWN_BEAMS])
        table = two_part_dot(beam_pick[...], jnp.concatenate(table, axis=0))
        rows = slice(step * slots, (step + 1) * slots)
        total = tally[rows] - jnp.where(gate_here, table, 0.0)
        for c in range(NC):
            total = total + seen[:, c * 128 : (c + 1) * 128]
        misfit = scaled * jnp.sum(total, axis=1, keepdims=True)
        top, low = split(misfit * wide[...])
        tops[rows] = top
        lows[rows] = low
        forcing[step * 2 * half : (step + 1) * 2 * half] = jnp.dot(
            push, top, preferred_element_type=f32
        ) + jnp.dot(push, low, preferred_element_type=f32)

    def forced(step, i, c):
        at = step * 2 * half + i * CY
        return forcing[at : at + CY, c * 128 : (c + 1) * 128]

    for c in range(NC):
        clear(state_0, c * FIELD, [2, 3, BLOCKS - 4, BLOCKS - 3])
        clear(back_2, c * FIELD, [1, 2, BLOCKS - 3, BLOCKS - 2])
        clear(back_1, c * FIELD, [0, 1, BLOCKS - 2, BLOCKS - 1])
        for i, x in enumerate(outer):
            at = c * FIELD + (FIRST + x) * PITCH
            state_0[at : at + CY] = forced(STEPS - 1, i, c)
            state_0[at + CY : at + PITCH] = jnp.zeros((PITCH - CY, 128), f32)
    fields = [state_0, back_2, back_1, state_3]
    for step in range(STEPS):
        source, target = fields[step], fields[step + 1]
        for x in range(-1 - step, 2 - step):
            for b in (FIRST + x, FIRST + CX - 1 - x):
                for c in range(NC):
                    base = c * FIELD + b * PITCH
                    target[base : base + PITCH] = backward_column(source, base, coef, b * PITCH)
        if step < STEPS - 1:
            for i, x in enumerate(outer):
                if x < 2 - step or x > CX - 3 + step:
                    for c in range(NC):
                        at = c * FIELD + (FIRST + x) * PITCH
                        target[at : at + CY] += forced(STEPS - 2 - step, i, c)
    for c in range(NC):
        for away, start, extra in WIDE:
            for source, target, size in (
                (PITCH - extra, 0, extra),
                (0, extra, CY + extra),
            ):
                if size:
                    at = c * FIELD + (FIRST - away) * PITCH + source
                    west = state_3[at : at + size]
                    at = c * FIELD + (FIRST + CX - 1 + away) * PITCH + source
                    east = state_3[at : at + size]
                    at = c * WIDE_ROWS + start + target
                    out_a[at : at + size] = jnp.where(even, east, west)
                    out_b[at : at + size] = jnp.where(even, west, east)


def interior(core_coef, edge_coef, back_2, back_1, tops, lows, slot_push, out, *scratch):
    coef, forced, field_2, field_1, forcing = scratch
    for f in range(5):
        at = f * FIELD + FIRST * PITCH
        coef[at : at + CORE] = core_coef[f * CORE : (f + 1) * CORE]
        for b in (FIRST - 1, FIRST + CX):
            at = f * FIELD + b * PITCH
            coef[at : at + PITCH] = edge_coef[at : at + PITCH]
    for step in range(STEPS):
        rows = slice(step * CX * CY, (step + 1) * CX * CY)
        forcing[rows] = jnp.dot(
            slot_push[...], tops[rows], preferred_element_type=f32
        ) + jnp.dot(slot_push[...], lows[rows], preferred_element_type=f32)

    def add_forcing(ref, step, columns):
        for c in range(NC):
            for x in columns:
                at = c * FIELD + (FIRST + x) * PITCH
                first = step * CX * CY + x * CY
                value = forcing[first : first + CY, c * 128 : (c + 1) * 128]
                if step == STEPS - 1:
                    ref[at : at + CY] = value
                    ref[at + CY : at + PITCH] = jnp.zeros((PITCH - CY, 128), f32)
                else:
                    ref[at : at + CY] += value

    def sweep(source, target, low, high):
        def body(x, carry):
            at = pl.multiple_of((x + FIRST) * PITCH, 8)
            for c in range(NC):
                value = backward_column(source, c * FIELD + at, coef, at)
                if target is out:
                    target[pl.ds(pl.multiple_of(c * CORE + x * PITCH, 8), PITCH)] = value
                else:
                    target[pl.ds(c * FIELD + at, PITCH)] = value
            return carry

        lax.fori_loop(low, high, body, 0)

    def copy(source, target, columns):
        for c in range(NC):
            for x in columns:
                at = c * FIELD + (FIRST + x) * PITCH
                target[at : at + PITCH] = source[at : at + PITCH]

    add_forcing(forced, STEPS - 1, range(CX))
    sweep(forced, field_2, 2, CX - 2)
    add_forcing(field_2, STEPS - 2, range(2, CX - 2))
    copy(back_2, field_2, (0, 1, CX - 2, CX - 1))
    sweep(field_2, field_1, 1, CX - 1)
    add_forcing(field_1, STEPS - 3, range(1, CX - 1))
    copy(back_1, field_1, (-1, 0, CX - 1, CX))
    sweep(field_1, out, 0, CX)


def add_x(ny, delta, picks, core, x_a, x_b, *rest):
    out_a, out_b, out_near, out_sums = rest[:4]
    out_others = rest[4:-2]
    merged = ny == 4
    field, sums = rest[-2:]
    even, _, _ = place_on("gy")
    total = picks.shape[1]
    rows = total * NC // ny
    field[...] = core[...]
    for c in range(NC):
        for away, start, extra in WIDE:
            for source, target, size in (
                (0, PITCH - extra, extra),
                (extra, 0, CY + extra),
            ):
                if size:
                    at = c * WIDE_ROWS + start + source
                    west, east = x_sides(x_a, x_b, pl.ds(at, size))
                    at = c * CORE + (away - 1) * PITCH + target
                    field[at : at + size] += west
                    at = c * CORE + (CX - away) * PITCH + target
                    field[at : at + size] += east
    for c in range(NC):
        for away in range(1, RIM + 1):
            north = field[pl.ds(c * CORE + CY - 1 + away, CX, stride=PITCH)]
            south = field[pl.ds(c * CORE + PITCH - away, CX, stride=PITCH)]
            at = (c * RIM + away - 1) * CX
            out_a[at : at + CX] = jnp.where(even, north, south)
            out_b[at : at + CX] = jnp.where(even, south, north)
        for x in range(CX):
            at = c * CORE + x * PITCH
            here = slice(x * CY, (x + 1) * CY)
            out_near[c, here] = delta[c, here] + field[at : at + CY]
    adjoint = jnp.concatenate([field[c * CORE : (c + 1) * CORE] for c in range(NC)], axis=1)
    tile_sums = two_part_dot(jnp.transpose(picks[...]).astype(bf16), adjoint)
    for c in range(NC):
        sums[pl.ds(c, total, stride=NC)] = tile_sums[:, c * 128 : (c + 1) * 128]
    out_sums[...] = sums[0:rows]
    out_a[Y_COEF:] = sums[rows : 2 * rows]
    if merged:
        out_b[Y_COEF:] = sums[3 * rows : 4 * rows]
    for s, other in enumerate(out_others):
        other[...] = sums[(2 + s) * rows : (3 + s) * rows]


def add_y(alpha, near, sums, y_a, y_b, *rest):
    others = rest[:-2]
    out_delta, out_alpha = rest[-2:]
    out_delta[...] = near[...]
    for c in range(NC):
        for away in range(1, RIM + 1):
            north, south = y_sides(y_a, y_b, pl.ds((c * RIM + away - 1) * CX, CX))
            high = pl.ds(CY - away, CX, stride=CY)
            low = pl.ds(away - 1, CX, stride=CY)
            out_delta[c, high] = out_delta[c, high] + north
            out_delta[c, low] = out_delta[c, low] + south
    total = sums[...] + y_a[Y_COEF:]
    if y_b.shape[0] > Y_COEF:
        total = total + y_b[Y_COEF:]
    for other in others:
        total = total + other[...]
    out_alpha[...] = alpha[...] + profile_weight * total


def on_device(
    delta,
    alpha,
    eddy,
    courant,
    tile_map,
    obs_rows,
    gate_beam,
    gate_index,
    gate_column,
    gate_live,
    obs_weight,
    obs_precision,
):
    nx = lax.axis_size("gx")
    ny = lax.axis_size("gy")
    owned = alpha.shape[1]
    slots = gate_column.shape[2]
    fine = delta.reshape(NC, CX * CY, 128)
    eddy = eddy.reshape(CX * CY, 128)
    courant = courant.reshape(2, CX * CY, 128)
    control = alpha.reshape(owned * NC, 128)
    weights = obs_weight.reshape(slots * NC, 128)
    gates = [
        value.reshape(1, slots)
        for value in (gate_beam, gate_index, gate_column, gate_live, obs_precision)
    ]
    own_beams = jnp.transpose(obs_rows, (1, 0, 2)).reshape(STEPS * OWN_BEAMS, 128)
    beam_count = nx * OWN_BEAMS
    rows = owned * NC
    total = ny * owned

    y_a, y_b, fine, coefs, control_near, near_tiles, meta, near_beams = call(
        pack_y,
        [
            (Y_HALO + rows, 128),
            (Y_HALO, 128),
            fine.shape,
            (3, CX * CY, 128),
            control.shape,
            (CX, 128),
            (8, slots),
            own_beams.shape,
        ],
        [
            pltpu.with_memory_space_constraint(value, pltpu.HBM)
            for value in (fine, eddy, courant, control, tile_map, *gates, own_beams)
        ],
        [
            pltpu.VMEM(tile_map.shape, jnp.int32),
            pltpu.VMEM((4, 1, slots), jnp.int32),
            pltpu.VMEM((1, slots), f32),
            pltpu.SemaphoreType.DMA((12,)),
        ],
        in_specs=[HBM] * 11,
    )
    y_a = swap(y_a, "gy", 1)
    y_b = pair_b(y_b, "gy", "gx")
    others = [swap(control, "gy", xor) for xor in range(2, ny)]
    beams = jnp.concatenate([near_beams, swap(own_beams, "gx", 1)])
    beams = [beams] + [swap(beams, "gx", xor) for xor in range(2, nx, 2)]

    wide, slot_pick, slot_push, beam_pick, columns, edge_pick = call(
        one_hots,
        [
            (slots, NC * 128),
            jax.ShapeDtypeStruct((slots, CX * CY), bf16),
            jax.ShapeDtypeStruct((CX * CY, slots), bf16),
            jax.ShapeDtypeStruct((slots, beam_count), bf16),
            (slots, 8),
            jax.ShapeDtypeStruct((slots, 256), bf16),
        ],
        [meta, weights],
    )
    x_a, x_b = call(
        lambda *refs: pack_x(ny, *refs),
        [(X_HALO, 128), (X_HALO, 128)],
        [fine, coefs, control_near, near_tiles, columns, y_a, y_b, *others],
        [
            pltpu.VMEM((2 * RIM * PITCH, 128), f32),
            pltpu.VMEM((2 * RIM * PITCH, total), f32),
            pltpu.VMEM((total * NC, 128), f32),
            pltpu.VMEM((128, 128), f32),
        ],
    )
    x_a = swap(x_a, "gx", 1)
    x_b = pair_b(x_b, "gx", "gy")

    big = (NC * FIELD, 128)
    core, coef, picks, state_1, state_2, tally = call(
        lambda *refs: prepare(ny, *refs),
        [
            (NC * CORE, 128),
            (5 * CORE, 128),
            (CORE, total),
            (NC * CORE, 128),
            (NC * CORE, 128),
            (STEPS * slots, 128),
        ],
        [fine, coefs, control_near, near_tiles, columns, slot_pick, wide, y_a, y_b, *others],
        [
            pltpu.VMEM((NC * CORE, 128), f32),
            pltpu.VMEM((total * NC, 128), f32),
            pltpu.VMEM((128, 128), f32),
        ],
        flops=3000000,
    )
    back_a, back_b, back_2, back_1, edge_coef, tops, lows = call(
        edges,
        [
            (X_COEF, 128),
            (X_COEF, 128),
            big,
            big,
            (5 * FIELD, 128),
            jax.ShapeDtypeStruct((STEPS * slots, NC * 128), bf16),
            jax.ShapeDtypeStruct((STEPS * slots, NC * 128), bf16),
        ],
        [
            core,
            coef,
            state_1,
            state_2,
            tally,
            wide,
            edge_pick,
            slot_push,
            beam_pick,
            columns,
            x_a,
            x_b,
            *beams,
        ],
        [pltpu.VMEM(big, f32)] * 4
        + [
            pltpu.VMEM((3 * FIELD, 128), f32),
            pltpu.VMEM((STEPS * 2 * RIM * CY, NC * 128), f32),
        ],
        flops=10000000,
    )
    (core,) = call(
        interior,
        [(NC * CORE, 128)],
        [coef, edge_coef, back_2, back_1, tops, lows, slot_push],
        [pltpu.VMEM((5 * FIELD, 128), f32)]
        + [pltpu.VMEM(big, f32)] * 3
        + [pltpu.VMEM((STEPS * CX * CY, NC * 128), f32)],
        flops=10000000,
    )
    x_a = swap(back_a, "gx", 1)
    x_b = pair_b(back_b, "gx", "gy")
    loose = [xor for xor in range(2, ny) if ny != 4 or xor != 3]
    back_a, back_b, near, sums, *back = call(
        lambda *refs: add_x(ny, *refs),
        [
            (Y_COEF + rows, 128),
            (Y_COEF + (rows if ny == 4 else 0), 128),
            fine.shape,
            (rows, 128),
        ]
        + [(rows, 128)] * len(loose),
        [fine, picks, core, x_a, x_b],
        [pltpu.VMEM((NC * CORE, 128), f32), pltpu.VMEM((total * NC, 128), f32)],
    )
    y_a = swap(back_a, "gy", 1)
    y_b = ring_b(back_b, "gy")
    others = [swap(value, "gy", xor) for xor, value in zip(loose, back)]
    grad_delta, grad_alpha = call(
        add_y,
        [fine.shape, control.shape],
        [control_near, near, sums, y_a, y_b, *others],
    )
    return grad_delta.reshape(delta.shape), grad_alpha.reshape(alpha.shape)


def solution(mesh):
    return jax.shard_map(
        on_device,
        mesh=mesh,
        in_specs=(
            P(None, "gx", "gy", None),
            P("gx", "gy", None, None),
            P("gx", "gy", None),
            P(None, "gx", "gy", None),
            P("gx", "gy"),
            P(("gx", "gy"), None, None),
            P("gx", "gy", None),
            P("gx", "gy", None),
            P("gx", "gy", None),
            P("gx", "gy", None),
            P("gx", "gy", None, None, None),
            P("gx", "gy", None),
        ),
        out_specs=(P(None, "gx", "gy", None), P("gx", "gy", None, None)),
        check_vma=False,
    )
```

```python
import jax
import jax.numpy as jnp
from jax import lax
from jax.experimental import pallas as pl
from jax.experimental.pallas import tpu as pltpu
from jax.sharding import PartitionSpec as P

STEPS = 3
RIM = 3
INNER = RIM - 1
NC = 4
CX = 16
CY = 16
BLOCKS = CX + 8
PITCH = CY + 8
FIRST = 4
FIELD = BLOCKS * PITCH
CORE = CX * PITCH
OWN_BEAMS = 8
BEAM_BITS = 3

profile_weight = 0.125
f32 = jnp.float32
bf16 = jnp.bfloat16

VMEM = pl.BlockSpec(memory_space=pltpu.VMEM)
HBM = pl.BlockSpec(memory_space=pltpu.HBM)


def call(body, outs, ins, scratch=(), in_specs=None, flops=1000000, limit=40 * 2**20):
    shapes = [
        out if isinstance(out, jax.ShapeDtypeStruct) else jax.ShapeDtypeStruct(out, f32)
        for out in outs
    ]
    size = sum(4 * value.size for value in ins)
    return pl.pallas_call(
        body,
        out_shape=shapes,
        in_specs=in_specs or [VMEM] * len(ins),
        out_specs=[VMEM] * len(shapes),
        scratch_shapes=list(scratch),
        compiler_params=pltpu.CompilerParams(vmem_limit_bytes=limit),
        cost_estimate=pl.CostEstimate(flops=flops, bytes_accessed=size, transcendentals=0),
    )(*ins)


def swap(block, axis, xor):
    return lax.ppermute(block, axis, [(i, i ^ xor) for i in range(lax.axis_size(axis))])


def pair_b(block, axis, other):
    count, across = lax.axis_size(axis), lax.axis_size(other)

    def place(i, j):
        return i * across + j if axis == "gx" else j * count + i

    pairs = []
    for j in range(across):
        for i in range(count):
            if i in (0, count - 1):
                pairs.append((place(i, j), place(i, j ^ 1)))
            else:
                pairs.append((place(i, j), place(i + 1 if i % 2 else i - 1, j)))
    return lax.ppermute(block, ("gx", "gy"), pairs)


def ring_b(block, axis):
    count = lax.axis_size(axis)
    pairs = [(i, (i + 1 if i % 2 else i - 1) % count) for i in range(count)]
    return lax.ppermute(block, axis, pairs)


def place_on(axis):
    me = lax.axis_index(axis)
    return lax.rem(me, 2) == 0, me > 0, me < lax.axis_size(axis) - 1


def split(value):
    top = value.astype(bf16)
    return top, (value - top.astype(f32)).astype(bf16)


def two_part_dot(left, value):
    top, low = split(value)
    return jnp.dot(left, top, preferred_element_type=f32) + jnp.dot(
        left, low, preferred_element_type=f32
    )


def layers(reach):
    found, at = [], 0
    for away in range(1, reach + 1):
        found.append((away, at, reach - away))
        at += CY + 2 * (reach - away)
    return found, at


WIDE, WIDE_ROWS = layers(RIM)
SLIM, SLIM_ROWS = layers(INNER)
X_COEF = NC * WIDE_ROWS
CORNERS = NC * 2 * sum(extra for _, _, extra in WIDE)
X_HALO = X_COEF + 3 * SLIM_ROWS

Y_COEF = NC * RIM * CX
Y_TILE = Y_COEF + 3 * INNER * CX
Y_HALO = Y_TILE + CX


def pack_y(
    delta,
    eddy,
    courant,
    alpha,
    tile_map,
    gate_beam,
    gate_index,
    gate_column,
    gate_live,
    precision,
    beam_rows,
    out_a,
    out_b,
    fine,
    coefs,
    profiles,
    near_tiles,
    meta,
    beams,
    tiles,
    gates,
    values,
    sems,
):
    even, _, _ = place_on("gy")
    moves = [
        pltpu.make_async_copy(source, target, sems.at[i])
        for i, (source, target) in enumerate(
            [
                (delta, fine),
                (eddy, coefs.at[0]),
                (courant.at[0], coefs.at[1]),
                (courant.at[1], coefs.at[2]),
                (tile_map, tiles),
                (alpha, profiles),
                (gate_beam, gates.at[0]),
                (gate_index, gates.at[1]),
                (gate_column, gates.at[2]),
                (gate_live, gates.at[3]),
                (precision, values),
                (beam_rows, beams),
            ]
        )
    ]
    for move in moves:
        move.start()
    for move in moves:
        move.wait()

    def put(at, field, away):
        north = field[pl.ds(CY - away, CX, stride=CY)]
        south = field[pl.ds(away - 1, CX, stride=CY)]
        out_a[at : at + CX] = jnp.where(even, north, south)
        out_b[at : at + CX] = jnp.where(even, south, north)

    for c in range(NC):
        for away in range(1, RIM + 1):
            put((c * RIM + away - 1) * CX, fine.at[c], away)
    for f in range(3):
        for away in range(1, INNER + 1):
            put(Y_COEF + (f * INNER + away - 1) * CX, coefs.at[f], away)
    near_tiles[...] = jnp.full((CX, 128), -1.0, f32)
    near_tiles[:, 0:CY] = tiles[...].astype(f32)
    for out in (out_a, out_b):
        out[Y_TILE : Y_TILE + CX] = near_tiles[...]
    out_a[Y_HALO:] = profiles[...]
    held = BEAM_BITS
    beam = gates[0]
    owner = jnp.bitwise_xor(beam >> held, lax.axis_index("gx"))
    meta[...] = jnp.zeros(meta.shape, f32)
    meta[0:1] = gates[2].astype(f32)
    meta[1:2] = ((owner << held) | (beam & ((1 << held) - 1))).astype(f32)
    meta[2:3] = gates[1].astype(f32)
    meta[3:4] = gates[3].astype(f32) * values[...]


def y_sides(got_a, got_b, rows, fill=0.0):
    even, low, high = place_on("gy")
    first, second = got_a[rows], got_b[rows]
    north, south = jnp.where(even, first, second), jnp.where(even, second, first)
    return jnp.where(high, north, fill), jnp.where(low, south, fill)


def x_sides(got_a, got_b, rows):
    even, low, high = place_on("gx")
    first, second = got_a[rows], got_b[rows]
    west, east = jnp.where(even, second, first), jnp.where(even, first, second)
    return jnp.where(low, west, 0.0), jnp.where(high, east, 0.0)


def gather_known(alpha, got_a, others, known):
    owned = alpha.shape[0]
    known[0:owned] = alpha[...]
    known[owned : 2 * owned] = got_a[Y_HALO:]
    for s, other in enumerate(others):
        known[(2 + s) * owned : (3 + s) * owned] = other[...]


def tile_numbers(near_tiles, got_a, got_b, tiles):
    spot = lax.broadcasted_iota(jnp.int32, (CX, 128), 1)
    north, south = y_sides(got_a, got_b, pl.ds(Y_TILE, CX), -1.0)
    near = jnp.where(
        (spot >= CY) & (spot < CY + RIM),
        pltpu.roll(north, CY, 1),
        jnp.where((spot >= PITCH - RIM) & (spot < PITCH), pltpu.roll(south, PITCH - CY, 1), -1.0),
    )
    tiles[...] = jnp.full(tiles.shape, -1.0, f32)
    tiles[0:CX] = jnp.where(spot < CY, near_tiles[...], near)
    return jnp.transpose(tiles[...])[0:PITCH]


def tile_ids(ny, owned):
    me = lax.axis_index("gy")
    lane = lax.broadcasted_iota(jnp.int32, (1, ny * owned), 1)
    ids = lane
    for s in range(ny):
        here = (lane >= s * owned) & (lane < (s + 1) * owned)
        ids = jnp.where(here, jnp.bitwise_xor(me, s) * owned + lane - s * owned, ids)
    return ids.astype(f32)


def by_variable(ref, count):
    return jnp.concatenate([ref[pl.ds(c, count, stride=NC)] for c in range(NC)], axis=1)


def pack_x(ny, delta, coefs, alpha, near_tiles, _, y_a, y_b, *rest):
    others = rest[: ny - 2]
    out_a, out_b, field, picks, known, tiles = rest[ny - 2 :]
    even, _, _ = place_on("gx")
    owned = alpha.shape[0] // NC
    gather_known(alpha, y_a, others, known)
    turned = tile_numbers(near_tiles, y_a, y_b, tiles)
    ids = tile_ids(ny, owned)
    columns = [x for x in range(RIM)] + [CX - RIM + x for x in range(RIM)]
    for i, x in enumerate(columns):
        picks[i * PITCH : (i + 1) * PITCH] = (turned[:, x : x + 1] == ids).astype(f32)
    fine = two_part_dot(picks[...].astype(bf16), by_variable(known, ny * owned))

    def fill(own, y_base, reach, c):
        for i, x in enumerate(columns):
            at = i * PITCH
            field[at + CY : at + PITCH] = jnp.zeros((PITCH - CY, 128), f32)
            field[at : at + CY] = own[x * CY : (x + 1) * CY]
        for away in range(1, reach + 1):
            for first, base in ((0, 0), (CX - RIM, RIM * PITCH)):
                rows = pl.ds(y_base + (away - 1) * CX + first, RIM)
                north, south = y_sides(y_a, y_b, rows)
                field[pl.ds(base + CY - 1 + away, RIM, stride=PITCH)] = north
                field[pl.ds(base + PITCH - away, RIM, stride=PITCH)] = south
        if c is not None:
            field[...] += profile_weight * fine[:, c * 128 : (c + 1) * 128]

    def put(at, found):
        for away, start, extra in found:
            east, west = (2 * RIM - away) * PITCH, (away - 1) * PITCH
            here = at + start
            for source, target, size in (
                (PITCH - extra, 0, extra),
                (0, extra, CY + extra),
            ):
                if size:
                    first = field[east + source : east + source + size]
                    second = field[west + source : west + source + size]
                    rows = slice(here + target, here + target + size)
                    out_a[rows] = jnp.where(even, first, second)
                    out_b[rows] = jnp.where(even, second, first)

    for c in range(NC):
        fill(delta.at[c], c * RIM * CX, RIM, c)
        put(c * WIDE_ROWS, WIDE)
    for f in range(3):
        fill(coefs.at[f], Y_COEF + f * INNER * CX, INNER, None)
        put(X_COEF + f * SLIM_ROWS, SLIM)


def one_hots(meta, weights, wide, slot_pick, slot_push, beam_pick, columns, edge_pick):
    slots = meta.shape[1]
    for c in range(NC):
        wide[:, c * 128 : (c + 1) * 128] = weights[pl.ds(c, slots, stride=NC)]
    per_beam = beam_pick.shape[1]
    turned = jnp.transpose(meta[...])
    columns[...] = turned
    slot_lane = lax.broadcasted_iota(jnp.int32, (slots, CX * CY), 1).astype(f32)
    slot_pick[...] = (slot_lane == turned[:, 0:1]).astype(f32).astype(bf16)
    edge_lane = lax.broadcasted_iota(jnp.int32, (slots, 128), 1)
    half = RIM * CY
    place = jnp.where(edge_lane < half, edge_lane, edge_lane + CX * CY - 2 * half)
    place = jnp.where(edge_lane < 2 * half, place, -1).astype(f32)
    near_edge = (place == turned[:, 0:1]).astype(f32).astype(bf16)
    edge_pick[:, 0:128] = near_edge
    edge_pick[:, 128:256] = near_edge
    column_row = lax.broadcasted_iota(jnp.int32, (CX * CY, slots), 0).astype(f32)
    slot_push[...] = (column_row == meta[0:1]).astype(f32).astype(bf16)
    beam_lane = lax.broadcasted_iota(jnp.int32, (slots, per_beam), 1).astype(f32)
    beam_pick[...] = (beam_lane == turned[:, 1:2]).astype(f32).astype(bf16)


def prepare(ny, delta, coefs, alpha, near_tiles, columns, slot_pick, wide, y_a, y_b, *rest):
    others = rest[: ny - 2]
    core, coef, picks, state_1, state_2, tally, state_3, known, tiles = rest[ny - 2 :]
    owned = alpha.shape[0] // NC

    def fill(ref, base, own, y_base, reach):
        for x in range(CX):
            at = base + x * PITCH
            ref[at : at + CY] = own[x * CY : (x + 1) * CY]
            ref[at + CY : at + PITCH] = jnp.zeros((PITCH - CY, 128), f32)
        for away in range(1, reach + 1):
            north, south = y_sides(y_a, y_b, pl.ds(y_base + (away - 1) * CX, CX))
            ref[pl.ds(base + CY - 1 + away, CX, stride=PITCH)] = north
            ref[pl.ds(base + PITCH - away, CX, stride=PITCH)] = south

    for c in range(NC):
        fill(core, c * CORE, delta.at[c], c * RIM * CX, RIM)
    for f in range(3):
        fill(coef, f * CORE, coefs.at[f], Y_COEF + f * INNER * CX, INNER)

    def combine(b, carry):
        at = pl.multiple_of(b * PITCH, 8)
        combined = combine_coefs(*[coef[pl.ds(f * CORE + at, PITCH)] for f in range(3)])
        for f, value in enumerate(combined):
            coef[pl.ds(f * CORE + at, PITCH)] = value
        return carry

    lax.fori_loop(0, CX, combine, 0)

    gather_known(alpha, y_a, others, known)
    turned = tile_numbers(near_tiles, y_a, y_b, tiles)
    ids = tile_ids(ny, owned)
    for x in range(CX):
        picks[x * PITCH : (x + 1) * PITCH] = (turned[:, x : x + 1] == ids).astype(f32)
    fine = two_part_dot(picks[...].astype(bf16), by_variable(known, ny * owned))
    for c in range(NC):
        core[c * CORE : (c + 1) * CORE] += profile_weight * fine[:, c * 128 : (c + 1) * 128]

    slots = columns.shape[0]
    states = [core, state_1, state_2, state_3]
    for step in range(STEPS):
        source, target = states[step], states[step + 1]

        def body(x, carry, source=source, target=target):
            at = pl.multiple_of(x * PITCH, 8)
            k = [coef[pl.ds(f * CORE + at, PITCH)] for f in range(5)]
            for c in range(NC):
                base = c * CORE + at
                target[pl.ds(base, PITCH)] = forward_column(source, base, k)
            return carry

        lax.fori_loop(step + 1, CX - 1 - step, body, 0)
        own = []
        for c in range(NC):
            pieces = [jnp.zeros(((step + 1) * CY, 128), f32)]
            for x in range(step + 1, CX - 1 - step):
                at = c * CORE + x * PITCH
                pieces.append(target[at : at + CY])
            own.append(jnp.concatenate(pieces + pieces[:1], axis=0))
        seen = two_part_dot(slot_pick[...], jnp.concatenate(own, axis=1)) * wide[...]
        total = seen[:, 0:128]
        for c in range(1, NC):
            total = total + seen[:, c * 128 : (c + 1) * 128]
        tally[step * slots : (step + 1) * slots] = total


def forward_column(source, base, k):
    here = source[pl.ds(base, PITCH)]
    return (
        k[0] * here
        + k[1] * source[pl.ds(base + PITCH, PITCH)]
        + k[2] * source[pl.ds(base - PITCH, PITCH)]
        + k[3] * pltpu.roll(here, PITCH - 1, 0)
        + k[4] * pltpu.roll(here, 1, 0)
    )


def backward_column(source, base, coef, at):
    here = source[pl.ds(base, PITCH)]
    return (
        coef[pl.ds(at, PITCH)] * here
        + coef[pl.ds(FIELD + at - PITCH, PITCH)] * source[pl.ds(base - PITCH, PITCH)]
        + coef[pl.ds(2 * FIELD + at + PITCH, PITCH)] * source[pl.ds(base + PITCH, PITCH)]
        + pltpu.roll(coef[pl.ds(3 * FIELD + at, PITCH)] * here, 1, 0)
        + pltpu.roll(coef[pl.ds(4 * FIELD + at, PITCH)] * here, PITCH - 1, 0)
    )


def combine_coefs(viscous, along_x, along_y):
    half_x, half_y = 0.5 * along_x, 0.5 * along_y
    return (
        1.0 - 4.0 * viscous,
        viscous - half_x,
        viscous + half_x,
        viscous - half_y,
        viscous + half_y,
    )


def clear(ref, base, blocks):
    for b in blocks:
        at = base + b * PITCH
        ref[at : at + PITCH] = jnp.zeros((PITCH, 128), f32)


def edges(
    core,
    core_coef,
    near_1,
    near_2,
    tally,
    wide,
    edge_pick,
    slot_push,
    beam_pick,
    columns,
    x_a,
    x_b,
    *rest,
):
    beams = rest[:-13]
    out_a, out_b, back_2, back_1, coef, tops, lows = rest[-13:-6]
    state_0, state_1, state_2, state_3, raw, forcing = rest[-6:]
    even, _, _ = place_on("gx")
    slots = columns.shape[0]

    def fill(ref, base, x_base, found):
        for away, start, extra in found:
            for source, target, size in (
                (0, PITCH - extra, extra),
                (extra, 0, CY + extra),
            ):
                if size:
                    at = x_base + start + source
                    west, east = x_sides(x_a, x_b, pl.ds(at, size))
                    at = base + (FIRST - away) * PITCH + target
                    ref[at : at + size] = west
                    at = base + (FIRST + CX - 1 + away) * PITCH + target
                    ref[at : at + size] = east

    def copy(source, target, x, count):
        for c in range(NC):
            first = c * CORE + x * PITCH
            at = c * FIELD + (FIRST + x) * PITCH
            target[at : at + count * PITCH] = source[first : first + count * PITCH]

    rim = [FIRST - 3, FIRST - 2, FIRST - 1, FIRST + CX, FIRST + CX + 1, FIRST + CX + 2]
    for x, (source, target) in enumerate(((core, state_0), (near_1, state_1), (near_2, state_2))):
        copy(source, target, x, 2)
        copy(source, target, CX - 2 - x, 2)
    for c in range(NC):
        clear(state_0, c * FIELD, rim)
        fill(state_0, c * FIELD, c * WIDE_ROWS, WIDE)
    for f in range(3):
        clear(raw, f * FIELD, rim[1:5])
        fill(raw, f * FIELD, X_COEF + f * SLIM_ROWS, SLIM)
    for f in range(5):
        for x in (0, CX - RIM):
            first, at = f * CORE + x * PITCH, f * FIELD + (FIRST + x) * PITCH
            coef[at : at + RIM * PITCH] = core_coef[first : first + RIM * PITCH]
        clear(coef, f * FIELD, [0, 1, BLOCKS - 2, BLOCKS - 1])
    for b in rim[1:5]:
        rows = [slice(f * FIELD + b * PITCH, f * FIELD + (b + 1) * PITCH) for f in range(5)]
        for f, value in enumerate(combine_coefs(*[raw[rows[f]] for f in range(3)])):
            coef[rows[f]] = value

    gate_lane = lax.broadcasted_iota(jnp.int32, (slots, 128), 1).astype(f32)
    gate_here = gate_lane == columns[:, 2:3]
    scaled = columns[:, 3:4]
    outer = [*range(RIM), *range(CX - RIM, CX)]
    half = RIM * CY
    push = jnp.concatenate([slot_push[0:half], slot_push[CX * CY - half :]], axis=0)
    states = [state_0, state_1, state_2, state_3]
    for step in range(STEPS):
        source, target = states[step], states[step + 1]
        for x in range(step - 2, step + 1):
            for b in (FIRST + x, FIRST + CX - 1 - x):
                at = b * PITCH
                k = [coef[f * FIELD + at : f * FIELD + at + PITCH] for f in range(5)]
                for c in range(NC):
                    base = c * FIELD + at
                    target[base : base + PITCH] = forward_column(source, base, k)
        zero = jnp.zeros((CY, 128), f32)
        parts = []
        for c in range(NC):
            pieces = []
            for x in outer:
                at = c * FIELD + (FIRST + x) * PITCH
                known = x <= step or x >= CX - 1 - step
                pieces.append(target[at : at + CY] if known else zero)
            value = jnp.concatenate(pieces + [jnp.zeros((128 - 2 * half, 128), f32)], axis=0)
            parts.append(jnp.concatenate(split(value), axis=0))
        seen = jnp.dot(
            edge_pick[...], jnp.concatenate(parts, axis=1), preferred_element_type=f32
        )
        seen = seen * wide[...]
        table = []
        for part in beams:
            for at in range(0, part.shape[0], STEPS * OWN_BEAMS):
                first = at + step * OWN_BEAMS
                table.append(part[first : first + OWN_BEAMS])
        table = two_part_dot(beam_pick[...], jnp.concatenate(table, axis=0))
        rows = slice(step * slots, (step + 1) * slots)
        total = tally[rows] - jnp.where(gate_here, table, 0.0)
        for c in range(NC):
            total = total + seen[:, c * 128 : (c + 1) * 128]
        misfit = scaled * jnp.sum(total, axis=1, keepdims=True)
        top, low = split(misfit * wide[...])
        tops[rows] = top
        lows[rows] = low
        forcing[step * 2 * half : (step + 1) * 2 * half] = jnp.dot(
            push, top, preferred_element_type=f32
        ) + jnp.dot(push, low, preferred_element_type=f32)

    def forced(step, i, c):
        at = step * 2 * half + i * CY
        return forcing[at : at + CY, c * 128 : (c + 1) * 128]

    for c in range(NC):
        clear(state_0, c * FIELD, [2, 3, BLOCKS - 4, BLOCKS - 3])
        clear(back_2, c * FIELD, [1, 2, BLOCKS - 3, BLOCKS - 2])
        clear(back_1, c * FIELD, [0, 1, BLOCKS - 2, BLOCKS - 1])
        for i, x in enumerate(outer):
            at = c * FIELD + (FIRST + x) * PITCH
            state_0[at : at + CY] = forced(STEPS - 1, i, c)
            state_0[at + CY : at + PITCH] = jnp.zeros((PITCH - CY, 128), f32)
    fields = [state_0, back_2, back_1, state_3]
    for step in range(STEPS):
        source, target = fields[step], fields[step + 1]
        for x in range(-1 - step, 2 - step):
            for b in (FIRST + x, FIRST + CX - 1 - x):
                for c in range(NC):
                    base = c * FIELD + b * PITCH
                    target[base : base + PITCH] = backward_column(source, base, coef, b * PITCH)
        if step < STEPS - 1:
            for i, x in enumerate(outer):
                if x < 2 - step or x > CX - 3 + step:
                    for c in range(NC):
                        at = c * FIELD + (FIRST + x) * PITCH
                        target[at : at + CY] += forced(STEPS - 2 - step, i, c)
    for c in range(NC):
        for away, start, extra in WIDE:
            for source, target, size in (
                (PITCH - extra, 0, extra),
                (0, extra, CY + extra),
            ):
                if size:
                    at = c * FIELD + (FIRST - away) * PITCH + source
                    west = state_3[at : at + size]
                    at = c * FIELD + (FIRST + CX - 1 + away) * PITCH + source
                    east = state_3[at : at + size]
                    at = c * WIDE_ROWS + start + target
                    out_a[at : at + size] = jnp.where(even, east, west)
                    out_b[at : at + size] = jnp.where(even, west, east)


def interior(
    core_coef, edge_coef, back_2, back_1, tops, lows, slot_push, out, out_a, out_b, *scratch
):
    coef, forced, field_2, field_1, forcing = scratch
    for f in range(5):
        at = f * FIELD + FIRST * PITCH
        coef[at : at + CORE] = core_coef[f * CORE : (f + 1) * CORE]
        for b in (FIRST - 1, FIRST + CX):
            at = f * FIELD + b * PITCH
            coef[at : at + PITCH] = edge_coef[at : at + PITCH]
    for step in range(STEPS):
        rows = slice(step * CX * CY, (step + 1) * CX * CY)
        forcing[rows] = jnp.dot(
            slot_push[...], tops[rows], preferred_element_type=f32
        ) + jnp.dot(slot_push[...], lows[rows], preferred_element_type=f32)

    def add_forcing(ref, step, columns):
        for c in range(NC):
            for x in columns:
                at = c * FIELD + (FIRST + x) * PITCH
                first = step * CX * CY + x * CY
                value = forcing[first : first + CY, c * 128 : (c + 1) * 128]
                if step == STEPS - 1:
                    ref[at : at + CY] = value
                    ref[at + CY : at + PITCH] = jnp.zeros((PITCH - CY, 128), f32)
                else:
                    ref[at : at + CY] += value

    def sweep(source, target, low, high):
        def body(x, carry):
            at = pl.multiple_of((x + FIRST) * PITCH, 8)
            for c in range(NC):
                value = backward_column(source, c * FIELD + at, coef, at)
                if target is out:
                    target[pl.ds(pl.multiple_of(c * CORE + x * PITCH, 8), PITCH)] = value
                else:
                    target[pl.ds(c * FIELD + at, PITCH)] = value
            return carry

        lax.fori_loop(low, high, body, 0)

    def copy(source, target, columns):
        for c in range(NC):
            for x in columns:
                at = c * FIELD + (FIRST + x) * PITCH
                target[at : at + PITCH] = source[at : at + PITCH]

    add_forcing(forced, STEPS - 1, range(CX))
    sweep(forced, field_2, 2, CX - 2)
    add_forcing(field_2, STEPS - 2, range(2, CX - 2))
    copy(back_2, field_2, (0, 1, CX - 2, CX - 1))
    sweep(field_2, field_1, 1, CX - 1)
    add_forcing(field_1, STEPS - 3, range(1, CX - 1))
    copy(back_1, field_1, (-1, 0, CX - 1, CX))
    sweep(field_1, out, 0, CX)
    even, _, _ = place_on("gy")
    for c in range(NC):
        for away in range(1, RIM + 1):
            north = out[pl.ds(c * CORE + CY - 1 + away, CX, stride=PITCH)]
            south = out[pl.ds(c * CORE + PITCH - away, CX, stride=PITCH)]
            at = (c * RIM + away - 1) * CX
            out_a[at : at + CX] = jnp.where(even, north, south)
            out_b[at : at + CX] = jnp.where(even, south, north)


def add_x(ny, delta, picks, core, x_a, x_b, *rest):
    out_a, out_b, out_near, out_sums = rest[:4]
    out_others = rest[4:-2]
    merged = ny == 4
    field, sums = rest[-2:]
    even, _, _ = place_on("gy")
    total = picks.shape[1]
    rows = total * NC // ny
    field[...] = core[...]
    for c in range(NC):
        for away, start, extra in WIDE:
            for source, target, size in (
                (0, PITCH - extra, extra),
                (extra, 0, CY + extra),
            ):
                if size:
                    at = c * WIDE_ROWS + start + source
                    west, east = x_sides(x_a, x_b, pl.ds(at, size))
                    at = c * CORE + (away - 1) * PITCH + target
                    field[at : at + size] += west
                    at = c * CORE + (CX - away) * PITCH + target
                    field[at : at + size] += east
    at = 0
    for c in range(NC):
        for away, start, extra in WIDE:
            if extra:
                first = c * WIDE_ROWS + start
                south = x_sides(x_a, x_b, pl.ds(first, extra))
                north = x_sides(x_a, x_b, pl.ds(first + extra + CY, extra))
                for side in range(2):
                    out_a[at : at + extra] = jnp.where(even, north[side], south[side])
                    out_b[at : at + extra] = jnp.where(even, south[side], north[side])
                    at += extra
    for c in range(NC):
        for x in range(CX):
            at = c * CORE + x * PITCH
            here = slice(x * CY, (x + 1) * CY)
            out_near[c, here] = delta[c, here] + field[at : at + CY]
    adjoint = jnp.concatenate([field[c * CORE : (c + 1) * CORE] for c in range(NC)], axis=1)
    tile_sums = two_part_dot(jnp.transpose(picks[...]).astype(bf16), adjoint)
    for c in range(NC):
        sums[pl.ds(c, total, stride=NC)] = tile_sums[:, c * 128 : (c + 1) * 128]
    out_sums[...] = sums[0:rows]
    out_a[CORNERS:] = sums[rows : 2 * rows]
    if merged:
        out_b[CORNERS:] = sums[3 * rows : 4 * rows]
    for s, other in enumerate(out_others):
        other[...] = sums[(2 + s) * rows : (3 + s) * rows]


def add_y(alpha, near, sums, y_a, y_b, small_a, small_b, *rest):
    others = rest[:-2]
    out_delta, out_alpha = rest[-2:]
    out_delta[...] = near[...]
    at = 0
    for c in range(NC):
        for away, start, extra in WIDE:
            north, south = y_sides(y_a, y_b, pl.ds((c * RIM + away - 1) * CX, CX))
            high = pl.ds(CY - away, CX, stride=CY)
            low = pl.ds(away - 1, CX, stride=CY)
            out_delta[c, high] = out_delta[c, high] + north
            out_delta[c, low] = out_delta[c, low] + south
            if extra:
                for x in (away - 1, CX - away):
                    north, south = y_sides(small_a, small_b, pl.ds(at, extra))
                    out_delta[c, (x + 1) * CY - extra : (x + 1) * CY] += north
                    out_delta[c, x * CY : x * CY + extra] += south
                    at += extra
    total = sums[...] + small_a[CORNERS:]
    if small_b.shape[0] > CORNERS:
        total = total + small_b[CORNERS:]
    for other in others:
        total = total + other[...]
    out_alpha[...] = alpha[...] + profile_weight * total


def on_device(
    delta,
    alpha,
    eddy,
    courant,
    tile_map,
    obs_rows,
    gate_beam,
    gate_index,
    gate_column,
    gate_live,
    obs_weight,
    obs_precision,
):
    nx = lax.axis_size("gx")
    ny = lax.axis_size("gy")
    owned = alpha.shape[1]
    slots = gate_column.shape[2]
    fine = delta.reshape(NC, CX * CY, 128)
    eddy = eddy.reshape(CX * CY, 128)
    courant = courant.reshape(2, CX * CY, 128)
    control = alpha.reshape(owned * NC, 128)
    weights = obs_weight.reshape(slots * NC, 128)
    gates = [
        value.reshape(1, slots)
        for value in (gate_beam, gate_index, gate_column, gate_live, obs_precision)
    ]
    own_beams = jnp.transpose(obs_rows, (1, 0, 2)).reshape(STEPS * OWN_BEAMS, 128)
    beam_count = nx * OWN_BEAMS
    rows = owned * NC
    total = ny * owned

    y_a, y_b, fine, coefs, control_near, near_tiles, meta, near_beams = call(
        pack_y,
        [
            (Y_HALO + rows, 128),
            (Y_HALO, 128),
            fine.shape,
            (3, CX * CY, 128),
            control.shape,
            (CX, 128),
            (8, slots),
            own_beams.shape,
        ],
        [
            pltpu.with_memory_space_constraint(value, pltpu.HBM)
            for value in (fine, eddy, courant, control, tile_map, *gates, own_beams)
        ],
        [
            pltpu.VMEM(tile_map.shape, jnp.int32),
            pltpu.VMEM((4, 1, slots), jnp.int32),
            pltpu.VMEM((1, slots), f32),
            pltpu.SemaphoreType.DMA((12,)),
        ],
        in_specs=[HBM] * 11,
    )
    y_a = swap(y_a, "gy", 1)
    y_b = pair_b(y_b, "gy", "gx")
    others = [swap(control, "gy", xor) for xor in range(2, ny)]
    beams = jnp.concatenate([near_beams, swap(own_beams, "gx", 1)])
    beams = [beams] + [swap(beams, "gx", xor) for xor in range(2, nx, 2)]

    wide, slot_pick, slot_push, beam_pick, columns, edge_pick = call(
        one_hots,
        [
            (slots, NC * 128),
            jax.ShapeDtypeStruct((slots, CX * CY), bf16),
            jax.ShapeDtypeStruct((CX * CY, slots), bf16),
            jax.ShapeDtypeStruct((slots, beam_count), bf16),
            (slots, 8),
            jax.ShapeDtypeStruct((slots, 256), bf16),
        ],
        [meta, weights],
    )
    x_a, x_b = call(
        lambda *refs: pack_x(ny, *refs),
        [(X_HALO, 128), (X_HALO, 128)],
        [fine, coefs, control_near, near_tiles, columns, y_a, y_b, *others],
        [
            pltpu.VMEM((2 * RIM * PITCH, 128), f32),
            pltpu.VMEM((2 * RIM * PITCH, total), f32),
            pltpu.VMEM((total * NC, 128), f32),
            pltpu.VMEM((128, 128), f32),
        ],
    )
    x_a = swap(x_a, "gx", 1)
    x_b = pair_b(x_b, "gx", "gy")

    big = (NC * FIELD, 128)
    core, coef, picks, state_1, state_2, tally = call(
        lambda *refs: prepare(ny, *refs),
        [
            (NC * CORE, 128),
            (5 * CORE, 128),
            (CORE, total),
            (NC * CORE, 128),
            (NC * CORE, 128),
            (STEPS * slots, 128),
        ],
        [fine, coefs, control_near, near_tiles, columns, slot_pick, wide, y_a, y_b, *others],
        [
            pltpu.VMEM((NC * CORE, 128), f32),
            pltpu.VMEM((total * NC, 128), f32),
            pltpu.VMEM((128, 128), f32),
        ],
        flops=3000000,
    )
    back_a, back_b, back_2, back_1, edge_coef, tops, lows = call(
        edges,
        [
            (X_COEF, 128),
            (X_COEF, 128),
            big,
            big,
            (5 * FIELD, 128),
            jax.ShapeDtypeStruct((STEPS * slots, NC * 128), bf16),
            jax.ShapeDtypeStruct((STEPS * slots, NC * 128), bf16),
        ],
        [
            core,
            coef,
            state_1,
            state_2,
            tally,
            wide,
            edge_pick,
            slot_push,
            beam_pick,
            columns,
            x_a,
            x_b,
            *beams,
        ],
        [pltpu.VMEM(big, f32)] * 4
        + [
            pltpu.VMEM((3 * FIELD, 128), f32),
            pltpu.VMEM((STEPS * 2 * RIM * CY, NC * 128), f32),
        ],
        flops=10000000,
    )
    core, rim_a, rim_b = call(
        interior,
        [(NC * CORE, 128), (Y_COEF, 128), (Y_COEF, 128)],
        [coef, edge_coef, back_2, back_1, tops, lows, slot_push],
        [pltpu.VMEM((5 * FIELD, 128), f32)]
        + [pltpu.VMEM(big, f32)] * 3
        + [pltpu.VMEM((STEPS * CX * CY, NC * 128), f32)],
        flops=10000000,
    )
    x_a = swap(back_a, "gx", 1)
    x_b = pair_b(back_b, "gx", "gy")
    loose = [xor for xor in range(2, ny) if ny != 4 or xor != 3]
    back_a, back_b, near, sums, *back = call(
        lambda *refs: add_x(ny, *refs),
        [
            (CORNERS + rows, 128),
            (CORNERS + (rows if ny == 4 else 0), 128),
            fine.shape,
            (rows, 128),
        ]
        + [(rows, 128)] * len(loose),
        [fine, picks, core, x_a, x_b],
        [pltpu.VMEM((NC * CORE, 128), f32), pltpu.VMEM((total * NC, 128), f32)],
    )
    y_a = swap(rim_a, "gy", 1)
    y_b = pair_b(rim_b, "gy", "gx")
    small_a = swap(back_a, "gy", 1)
    small_b = ring_b(back_b, "gy")
    others = [swap(value, "gy", xor) for xor, value in zip(loose, back)]
    grad_delta, grad_alpha = call(
        add_y,
        [fine.shape, control.shape],
        [control_near, near, sums, y_a, y_b, small_a, small_b, *others],
    )
    return grad_delta.reshape(delta.shape), grad_alpha.reshape(alpha.shape)


def solution(mesh):
    return jax.shard_map(
        on_device,
        mesh=mesh,
        in_specs=(
            P(None, "gx", "gy", None),
            P("gx", "gy", None, None),
            P("gx", "gy", None),
            P(None, "gx", "gy", None),
            P("gx", "gy"),
            P(("gx", "gy"), None, None),
            P("gx", "gy", None),
            P("gx", "gy", None),
            P("gx", "gy", None),
            P("gx", "gy", None),
            P("gx", "gy", None, None, None),
            P("gx", "gy", None),
        ),
        out_specs=(P(None, "gx", "gy", None), P("gx", "gy", None, None)),
        check_vma=False,
    )
```

```python
import jax
import jax.numpy as jnp
from jax import lax
from jax.experimental import pallas as pl
from jax.experimental.pallas import tpu as pltpu
from jax.sharding import PartitionSpec as P

STEPS = 3
RIM = 3
INNER = RIM - 1
NC = 4
CX = 16
CY = 16
BLOCKS = CX + 8
PITCH = CY + 8
FIRST = 4
FIELD = BLOCKS * PITCH
CORE = CX * PITCH
OWN_BEAMS = 8
BEAM_BITS = 3

profile_weight = 0.125
f32 = jnp.float32
bf16 = jnp.bfloat16

VMEM = pl.BlockSpec(memory_space=pltpu.VMEM)
HBM = pl.BlockSpec(memory_space=pltpu.HBM)


def call(body, outs, ins, scratch=(), in_specs=None, flops=1000000, limit=40 * 2**20):
    shapes = [
        out if isinstance(out, jax.ShapeDtypeStruct) else jax.ShapeDtypeStruct(out, f32)
        for out in outs
    ]
    size = sum(4 * value.size for value in ins)
    return pl.pallas_call(
        body,
        out_shape=shapes,
        in_specs=in_specs or [VMEM] * len(ins),
        out_specs=[VMEM] * len(shapes),
        scratch_shapes=list(scratch),
        compiler_params=pltpu.CompilerParams(vmem_limit_bytes=limit),
        cost_estimate=pl.CostEstimate(flops=flops, bytes_accessed=size, transcendentals=0),
    )(*ins)


def swap(block, axis, xor):
    return lax.ppermute(block, axis, [(i, i ^ xor) for i in range(lax.axis_size(axis))])


def pair_b(block, axis, other):
    count, across = lax.axis_size(axis), lax.axis_size(other)

    def place(i, j):
        return i * across + j if axis == "gx" else j * count + i

    pairs = []
    for j in range(across):
        for i in range(count):
            if i in (0, count - 1):
                pairs.append((place(i, j), place(i, j ^ 1)))
            else:
                pairs.append((place(i, j), place(i + 1 if i % 2 else i - 1, j)))
    return lax.ppermute(block, ("gx", "gy"), pairs)


def ring_b(block, axis):
    count = lax.axis_size(axis)
    pairs = [(i, (i + 1 if i % 2 else i - 1) % count) for i in range(count)]
    return lax.ppermute(block, axis, pairs)


def place_on(axis):
    me = lax.axis_index(axis)
    return lax.rem(me, 2) == 0, me > 0, me < lax.axis_size(axis) - 1


def split(value):
    top = value.astype(bf16)
    return top, (value - top.astype(f32)).astype(bf16)


def two_part_dot(left, value):
    top, low = split(value)
    return jnp.dot(left, top, preferred_element_type=f32) + jnp.dot(
        left, low, preferred_element_type=f32
    )


def layers(reach):
    found, at = [], 0
    for away in range(1, reach + 1):
        found.append((away, at, reach - away))
        at += CY + 2 * (reach - away)
    return found, at


WIDE, WIDE_ROWS = layers(RIM)
SLIM, SLIM_ROWS = layers(INNER)
X_COEF = NC * WIDE_ROWS
CORNERS = NC * 2 * sum(extra for _, _, extra in WIDE)
X_HALO = X_COEF + 3 * SLIM_ROWS

Y_COEF = NC * RIM * CX
Y_TILE = Y_COEF + 3 * INNER * CX
Y_HALO = Y_TILE + CX


def pack_y(
    delta,
    eddy,
    courant,
    alpha,
    tile_map,
    gate_beam,
    gate_index,
    gate_column,
    gate_live,
    precision,
    beam_rows,
    out_a,
    out_b,
    fine,
    coefs,
    profiles,
    near_tiles,
    meta,
    beams,
    tiles,
    gates,
    values,
    sems,
):
    even, _, _ = place_on("gy")
    moves = [
        pltpu.make_async_copy(source, target, sems.at[i])
        for i, (source, target) in enumerate(
            [
                (delta, fine),
                (eddy, coefs.at[0]),
                (courant.at[0], coefs.at[1]),
                (courant.at[1], coefs.at[2]),
                (tile_map, tiles),
                (alpha, profiles),
                (gate_beam, gates.at[0]),
                (gate_index, gates.at[1]),
                (gate_column, gates.at[2]),
                (gate_live, gates.at[3]),
                (precision, values),
                (beam_rows, beams),
            ]
        )
    ]
    for move in moves:
        move.start()
    for move in moves:
        move.wait()

    def put(at, field, away):
        north = field[pl.ds(CY - away, CX, stride=CY)]
        south = field[pl.ds(away - 1, CX, stride=CY)]
        out_a[at : at + CX] = jnp.where(even, north, south)
        out_b[at : at + CX] = jnp.where(even, south, north)

    for c in range(NC):
        for away in range(1, RIM + 1):
            put((c * RIM + away - 1) * CX, fine.at[c], away)
    for f in range(3):
        for away in range(1, INNER + 1):
            put(Y_COEF + (f * INNER + away - 1) * CX, coefs.at[f], away)
    near_tiles[...] = jnp.full((CX, 128), -1.0, f32)
    near_tiles[:, 0:CY] = tiles[...].astype(f32)
    for out in (out_a, out_b):
        out[Y_TILE : Y_TILE + CX] = near_tiles[...]
    out_a[Y_HALO:] = profiles[...]
    held = BEAM_BITS
    beam = gates[0]
    owner = jnp.bitwise_xor(beam >> held, lax.axis_index("gx"))
    meta[...] = jnp.zeros(meta.shape, f32)
    meta[0:1] = gates[2].astype(f32)
    meta[1:2] = ((owner << held) | (beam & ((1 << held) - 1))).astype(f32)
    meta[2:3] = gates[1].astype(f32)
    meta[3:4] = gates[3].astype(f32) * values[...]


def y_sides(got_a, got_b, rows, fill=0.0):
    even, low, high = place_on("gy")
    first, second = got_a[rows], got_b[rows]
    north, south = jnp.where(even, first, second), jnp.where(even, second, first)
    return jnp.where(high, north, fill), jnp.where(low, south, fill)


def x_sides(got_a, got_b, rows):
    even, low, high = place_on("gx")
    first, second = got_a[rows], got_b[rows]
    west, east = jnp.where(even, second, first), jnp.where(even, first, second)
    return jnp.where(low, west, 0.0), jnp.where(high, east, 0.0)


def gather_known(alpha, got_a, others, known):
    owned = alpha.shape[0]
    known[0:owned] = alpha[...]
    known[owned : 2 * owned] = got_a[Y_HALO:]
    for s, other in enumerate(others):
        known[(2 + s) * owned : (3 + s) * owned] = other[...]


def tile_numbers(near_tiles, got_a, got_b, tiles):
    spot = lax.broadcasted_iota(jnp.int32, (CX, 128), 1)
    north, south = y_sides(got_a, got_b, pl.ds(Y_TILE, CX), -1.0)
    near = jnp.where(
        (spot >= CY) & (spot < CY + RIM),
        pltpu.roll(north, CY, 1),
        jnp.where((spot >= PITCH - RIM) & (spot < PITCH), pltpu.roll(south, PITCH - CY, 1), -1.0),
    )
    tiles[...] = jnp.full(tiles.shape, -1.0, f32)
    tiles[0:CX] = jnp.where(spot < CY, near_tiles[...], near)
    return jnp.transpose(tiles[...])[0:PITCH]


def tile_ids(ny, owned):
    me = lax.axis_index("gy")
    lane = lax.broadcasted_iota(jnp.int32, (1, ny * owned), 1)
    ids = lane
    for s in range(ny):
        here = (lane >= s * owned) & (lane < (s + 1) * owned)
        ids = jnp.where(here, jnp.bitwise_xor(me, s) * owned + lane - s * owned, ids)
    return ids.astype(f32)


def by_variable(ref, count):
    return jnp.concatenate([ref[pl.ds(c, count, stride=NC)] for c in range(NC)], axis=1)


def pack_x(ny, delta, coefs, alpha, near_tiles, _, y_a, y_b, *rest):
    others = rest[: ny - 2]
    out_a, out_b, field, picks, known, tiles = rest[ny - 2 :]
    even, _, _ = place_on("gx")
    owned = alpha.shape[0] // NC
    gather_known(alpha, y_a, others, known)
    turned = tile_numbers(near_tiles, y_a, y_b, tiles)
    ids = tile_ids(ny, owned)
    columns = [x for x in range(RIM)] + [CX - RIM + x for x in range(RIM)]
    for i, x in enumerate(columns):
        picks[i * PITCH : (i + 1) * PITCH] = (turned[:, x : x + 1] == ids).astype(f32)
    fine = two_part_dot(picks[...].astype(bf16), by_variable(known, ny * owned))

    def fill(own, y_base, reach, c):
        for i, x in enumerate(columns):
            at = i * PITCH
            field[at + CY : at + PITCH] = jnp.zeros((PITCH - CY, 128), f32)
            field[at : at + CY] = own[x * CY : (x + 1) * CY]
        for away in range(1, reach + 1):
            for first, base in ((0, 0), (CX - RIM, RIM * PITCH)):
                rows = pl.ds(y_base + (away - 1) * CX + first, RIM)
                north, south = y_sides(y_a, y_b, rows)
                field[pl.ds(base + CY - 1 + away, RIM, stride=PITCH)] = north
                field[pl.ds(base + PITCH - away, RIM, stride=PITCH)] = south
        if c is not None:
            field[...] += profile_weight * fine[:, c * 128 : (c + 1) * 128]

    def put(at, found):
        for away, start, extra in found:
            east, west = (2 * RIM - away) * PITCH, (away - 1) * PITCH
            here = at + start
            for source, target, size in (
                (PITCH - extra, 0, extra),
                (0, extra, CY + extra),
            ):
                if size:
                    first = field[east + source : east + source + size]
                    second = field[west + source : west + source + size]
                    rows = slice(here + target, here + target + size)
                    out_a[rows] = jnp.where(even, first, second)
                    out_b[rows] = jnp.where(even, second, first)

    for c in range(NC):
        fill(delta.at[c], c * RIM * CX, RIM, c)
        put(c * WIDE_ROWS, WIDE)
    for f in range(3):
        fill(coefs.at[f], Y_COEF + f * INNER * CX, INNER, None)
        put(X_COEF + f * SLIM_ROWS, SLIM)


def one_hots(meta, weights, wide, slot_pick, slot_push, beam_pick, columns, edge_pick):
    slots = meta.shape[1]
    for c in range(NC):
        wide[:, c * 128 : (c + 1) * 128] = weights[pl.ds(c, slots, stride=NC)]
    per_beam = beam_pick.shape[1]
    turned = jnp.transpose(meta[...])
    columns[...] = turned
    slot_lane = lax.broadcasted_iota(jnp.int32, (slots, CX * CY), 1).astype(f32)
    slot_pick[...] = (slot_lane == turned[:, 0:1]).astype(f32).astype(bf16)
    edge_lane = lax.broadcasted_iota(jnp.int32, (slots, 128), 1)
    half = RIM * CY
    place = jnp.where(edge_lane < half, edge_lane, edge_lane + CX * CY - 2 * half)
    place = jnp.where(edge_lane < 2 * half, place, -1).astype(f32)
    near_edge = (place == turned[:, 0:1]).astype(f32).astype(bf16)
    edge_pick[:, 0:128] = near_edge
    edge_pick[:, 128:256] = near_edge
    column_row = lax.broadcasted_iota(jnp.int32, (CX * CY, slots), 0).astype(f32)
    slot_push[...] = (column_row == meta[0:1]).astype(f32).astype(bf16)
    beam_lane = lax.broadcasted_iota(jnp.int32, (slots, per_beam), 1).astype(f32)
    beam_pick[...] = (beam_lane == turned[:, 1:2]).astype(f32).astype(bf16)


def prepare(ny, delta, coefs, alpha, near_tiles, columns, slot_pick, wide, y_a, y_b, *rest):
    others = rest[: ny - 2]
    core, coef, picks, state_1, state_2, tally, state_3, known, tiles = rest[ny - 2 :]
    owned = alpha.shape[0] // NC

    def fill(ref, base, own, y_base, reach):
        for x in range(CX):
            at = base + x * PITCH
            ref[at : at + CY] = own[x * CY : (x + 1) * CY]
            ref[at + CY : at + PITCH] = jnp.zeros((PITCH - CY, 128), f32)
        for away in range(1, reach + 1):
            north, south = y_sides(y_a, y_b, pl.ds(y_base + (away - 1) * CX, CX))
            ref[pl.ds(base + CY - 1 + away, CX, stride=PITCH)] = north
            ref[pl.ds(base + PITCH - away, CX, stride=PITCH)] = south

    for c in range(NC):
        fill(core, c * CORE, delta.at[c], c * RIM * CX, RIM)
    for f in range(3):
        fill(coef, f * CORE, coefs.at[f], Y_COEF + f * INNER * CX, INNER)

    def combine(b, carry):
        at = pl.multiple_of(b * PITCH, 8)
        combined = combine_coefs(*[coef[pl.ds(f * CORE + at, PITCH)] for f in range(3)])
        for f, value in enumerate(combined):
            coef[pl.ds(f * CORE + at, PITCH)] = value
        return carry

    lax.fori_loop(0, CX, combine, 0)

    gather_known(alpha, y_a, others, known)
    turned = tile_numbers(near_tiles, y_a, y_b, tiles)
    ids = tile_ids(ny, owned)
    for x in range(CX):
        picks[x * PITCH : (x + 1) * PITCH] = (turned[:, x : x + 1] == ids).astype(f32)
    fine = two_part_dot(picks[...].astype(bf16), by_variable(known, ny * owned))
    for c in range(NC):
        core[c * CORE : (c + 1) * CORE] += profile_weight * fine[:, c * 128 : (c + 1) * 128]

    slots = columns.shape[0]
    states = [core, state_1, state_2, state_3]
    for step in range(STEPS):
        source, target = states[step], states[step + 1]

        def body(x, carry, source=source, target=target):
            at = pl.multiple_of(x * PITCH, 8)
            k = [coef[pl.ds(f * CORE + at, PITCH)] for f in range(5)]
            for c in range(NC):
                base = c * CORE + at
                target[pl.ds(base, PITCH)] = forward_column(source, base, k)
            return carry

        lax.fori_loop(step + 1, CX - 1 - step, body, 0, unroll=2)
        own = []
        for c in range(NC):
            pieces = [jnp.zeros(((step + 1) * CY, 128), f32)]
            for x in range(step + 1, CX - 1 - step):
                at = c * CORE + x * PITCH
                pieces.append(target[at : at + CY])
            own.append(jnp.concatenate(pieces + pieces[:1], axis=0))
        seen = two_part_dot(slot_pick[...], jnp.concatenate(own, axis=1)) * wide[...]
        total = seen[:, 0:128]
        for c in range(1, NC):
            total = total + seen[:, c * 128 : (c + 1) * 128]
        tally[step * slots : (step + 1) * slots] = total


def forward_column(source, base, k):
    here = source[pl.ds(base, PITCH)]
    return (
        k[0] * here
        + k[1] * source[pl.ds(base + PITCH, PITCH)]
        + k[2] * source[pl.ds(base - PITCH, PITCH)]
        + k[3] * pltpu.roll(here, PITCH - 1, 0)
        + k[4] * pltpu.roll(here, 1, 0)
    )


def backward_column(source, base, coef, at):
    here = source[pl.ds(base, PITCH)]
    return (
        coef[pl.ds(at, PITCH)] * here
        + coef[pl.ds(FIELD + at - PITCH, PITCH)] * source[pl.ds(base - PITCH, PITCH)]
        + coef[pl.ds(2 * FIELD + at + PITCH, PITCH)] * source[pl.ds(base + PITCH, PITCH)]
        + pltpu.roll(coef[pl.ds(3 * FIELD + at, PITCH)] * here, 1, 0)
        + pltpu.roll(coef[pl.ds(4 * FIELD + at, PITCH)] * here, PITCH - 1, 0)
    )


def combine_coefs(viscous, along_x, along_y):
    half_x, half_y = 0.5 * along_x, 0.5 * along_y
    return (
        1.0 - 4.0 * viscous,
        viscous - half_x,
        viscous + half_x,
        viscous - half_y,
        viscous + half_y,
    )


def clear(ref, base, blocks):
    for b in blocks:
        at = base + b * PITCH
        ref[at : at + PITCH] = jnp.zeros((PITCH, 128), f32)


def edges(
    core,
    core_coef,
    near_1,
    near_2,
    tally,
    wide,
    edge_pick,
    x_a,
    x_b,
    coef,
    totals,
    state_0,
    state_1,
    state_2,
    state_3,
    raw,
):
    slots = wide.shape[0]

    def fill(ref, base, x_base, found):
        for away, start, extra in found:
            for source, target, size in (
                (0, PITCH - extra, extra),
                (extra, 0, CY + extra),
            ):
                if size:
                    at = x_base + start + source
                    west, east = x_sides(x_a, x_b, pl.ds(at, size))
                    at = base + (FIRST - away) * PITCH + target
                    ref[at : at + size] = west
                    at = base + (FIRST + CX - 1 + away) * PITCH + target
                    ref[at : at + size] = east

    def copy(source, target, x, count):
        for c in range(NC):
            first = c * CORE + x * PITCH
            at = c * FIELD + (FIRST + x) * PITCH
            target[at : at + count * PITCH] = source[first : first + count * PITCH]

    rim = [FIRST - 3, FIRST - 2, FIRST - 1, FIRST + CX, FIRST + CX + 1, FIRST + CX + 2]
    for x, (source, target) in enumerate(((core, state_0), (near_1, state_1), (near_2, state_2))):
        copy(source, target, x, 2)
        copy(source, target, CX - 2 - x, 2)
    for c in range(NC):
        clear(state_0, c * FIELD, rim)
        fill(state_0, c * FIELD, c * WIDE_ROWS, WIDE)
    for f in range(3):
        clear(raw, f * FIELD, rim[1:5])
        fill(raw, f * FIELD, X_COEF + f * SLIM_ROWS, SLIM)
    for f in range(5):
        for x in (0, CX - RIM):
            first, at = f * CORE + x * PITCH, f * FIELD + (FIRST + x) * PITCH
            coef[at : at + RIM * PITCH] = core_coef[first : first + RIM * PITCH]
        clear(coef, f * FIELD, [0, 1, BLOCKS - 2, BLOCKS - 1])
    for b in rim[1:5]:
        rows = [slice(f * FIELD + b * PITCH, f * FIELD + (b + 1) * PITCH) for f in range(5)]
        for f, value in enumerate(combine_coefs(*[raw[rows[f]] for f in range(3)])):
            coef[rows[f]] = value

    outer = [*range(RIM), *range(CX - RIM, CX)]
    half = RIM * CY
    states = [state_0, state_1, state_2, state_3]
    for step in range(STEPS):
        source, target = states[step], states[step + 1]
        for x in range(step - 2, step + 1):
            for b in (FIRST + x, FIRST + CX - 1 - x):
                at = b * PITCH
                k = [coef[f * FIELD + at : f * FIELD + at + PITCH] for f in range(5)]
                for c in range(NC):
                    base = c * FIELD + at
                    target[base : base + PITCH] = forward_column(source, base, k)
        zero = jnp.zeros((CY, 128), f32)
        parts = []
        for c in range(NC):
            pieces = []
            for x in outer:
                at = c * FIELD + (FIRST + x) * PITCH
                known = x <= step or x >= CX - 1 - step
                pieces.append(target[at : at + CY] if known else zero)
            value = jnp.concatenate(pieces + [jnp.zeros((128 - 2 * half, 128), f32)], axis=0)
            parts.append(jnp.concatenate(split(value), axis=0))
        seen = jnp.dot(
            edge_pick[...], jnp.concatenate(parts, axis=1), preferred_element_type=f32
        )
        seen = seen * wide[...]
        rows = slice(step * slots, (step + 1) * slots)
        total = tally[rows]
        for c in range(NC):
            total = total + seen[:, c * 128 : (c + 1) * 128]
        totals[rows] = total


def push_edges(coef, totals, wide, slot_push, beam_pick, columns, *rest):
    beams = rest[:-9]
    out_a, out_b, back_2, back_1, tops, lows, state_0, state_3, forcing = rest[-9:]
    even, _, _ = place_on("gx")
    slots = columns.shape[0]
    gate_lane = lax.broadcasted_iota(jnp.int32, (slots, 128), 1).astype(f32)
    gate_here = gate_lane == columns[:, 2:3]
    scaled = columns[:, 3:4]
    outer = [*range(RIM), *range(CX - RIM, CX)]
    half = RIM * CY
    push = jnp.concatenate([slot_push[0:half], slot_push[CX * CY - half :]], axis=0)
    for step in range(STEPS):
        table = []
        for part in beams:
            for at in range(0, part.shape[0], STEPS * OWN_BEAMS):
                first = at + step * OWN_BEAMS
                table.append(part[first : first + OWN_BEAMS])
        table = two_part_dot(beam_pick[...], jnp.concatenate(table, axis=0))
        rows = slice(step * slots, (step + 1) * slots)
        total = totals[rows] - jnp.where(gate_here, table, 0.0)
        misfit = scaled * jnp.sum(total, axis=1, keepdims=True)
        top, low = split(misfit * wide[...])
        tops[rows] = top
        lows[rows] = low
        forcing[step * 2 * half : (step + 1) * 2 * half] = jnp.dot(
            push, top, preferred_element_type=f32
        ) + jnp.dot(push, low, preferred_element_type=f32)

    def forced(step, i, c):
        at = step * 2 * half + i * CY
        return forcing[at : at + CY, c * 128 : (c + 1) * 128]

    for c in range(NC):
        clear(state_0, c * FIELD, [2, 3, BLOCKS - 4, BLOCKS - 3])
        clear(back_2, c * FIELD, [1, 2, BLOCKS - 3, BLOCKS - 2])
        clear(back_1, c * FIELD, [0, 1, BLOCKS - 2, BLOCKS - 1])
        for i, x in enumerate(outer):
            at = c * FIELD + (FIRST + x) * PITCH
            state_0[at : at + CY] = forced(STEPS - 1, i, c)
            state_0[at + CY : at + PITCH] = jnp.zeros((PITCH - CY, 128), f32)
    fields = [state_0, back_2, back_1, state_3]
    for step in range(STEPS):
        source, target = fields[step], fields[step + 1]
        for x in range(-1 - step, 2 - step):
            for b in (FIRST + x, FIRST + CX - 1 - x):
                for c in range(NC):
                    base = c * FIELD + b * PITCH
                    target[base : base + PITCH] = backward_column(source, base, coef, b * PITCH)
        if step < STEPS - 1:
            for i, x in enumerate(outer):
                if x < 2 - step or x > CX - 3 + step:
                    for c in range(NC):
                        at = c * FIELD + (FIRST + x) * PITCH
                        target[at : at + CY] += forced(STEPS - 2 - step, i, c)
    for c in range(NC):
        for away, start, extra in WIDE:
            for source, target, size in (
                (PITCH - extra, 0, extra),
                (0, extra, CY + extra),
            ):
                if size:
                    at = c * FIELD + (FIRST - away) * PITCH + source
                    west = state_3[at : at + size]
                    at = c * FIELD + (FIRST + CX - 1 + away) * PITCH + source
                    east = state_3[at : at + size]
                    at = c * WIDE_ROWS + start + target
                    out_a[at : at + size] = jnp.where(even, east, west)
                    out_b[at : at + size] = jnp.where(even, west, east)


def interior(
    core_coef, edge_coef, back_2, back_1, tops, lows, slot_push, out, out_a, out_b, *scratch
):
    coef, forced, field_2, field_1, forcing = scratch
    for f in range(5):
        at = f * FIELD + FIRST * PITCH
        coef[at : at + CORE] = core_coef[f * CORE : (f + 1) * CORE]
        for b in (FIRST - 1, FIRST + CX):
            at = f * FIELD + b * PITCH
            coef[at : at + PITCH] = edge_coef[at : at + PITCH]
    for step in range(STEPS):
        rows = slice(step * CX * CY, (step + 1) * CX * CY)
        forcing[rows] = jnp.dot(
            slot_push[...], tops[rows], preferred_element_type=f32
        ) + jnp.dot(slot_push[...], lows[rows], preferred_element_type=f32)

    def add_forcing(ref, step, columns):
        for c in range(NC):
            for x in columns:
                at = c * FIELD + (FIRST + x) * PITCH
                first = step * CX * CY + x * CY
                value = forcing[first : first + CY, c * 128 : (c + 1) * 128]
                if step == STEPS - 1:
                    ref[at : at + CY] = value
                    ref[at + CY : at + PITCH] = jnp.zeros((PITCH - CY, 128), f32)
                else:
                    ref[at : at + CY] += value

    def sweep(source, target, low, high):
        def body(x, carry):
            at = pl.multiple_of((x + FIRST) * PITCH, 8)
            for c in range(NC):
                value = backward_column(source, c * FIELD + at, coef, at)
                if target is out:
                    target[pl.ds(pl.multiple_of(c * CORE + x * PITCH, 8), PITCH)] = value
                else:
                    target[pl.ds(c * FIELD + at, PITCH)] = value
            return carry

        lax.fori_loop(low, high, body, 0, unroll=2)

    def copy(source, target, columns):
        for c in range(NC):
            for x in columns:
                at = c * FIELD + (FIRST + x) * PITCH
                target[at : at + PITCH] = source[at : at + PITCH]

    add_forcing(forced, STEPS - 1, range(CX))
    sweep(forced, field_2, 2, CX - 2)
    add_forcing(field_2, STEPS - 2, range(2, CX - 2))
    copy(back_2, field_2, (0, 1, CX - 2, CX - 1))
    sweep(field_2, field_1, 1, CX - 1)
    add_forcing(field_1, STEPS - 3, range(1, CX - 1))
    copy(back_1, field_1, (-1, 0, CX - 1, CX))
    sweep(field_1, out, 0, CX)
    even, _, _ = place_on("gy")
    for c in range(NC):
        for away in range(1, RIM + 1):
            north = out[pl.ds(c * CORE + CY - 1 + away, CX, stride=PITCH)]
            south = out[pl.ds(c * CORE + PITCH - away, CX, stride=PITCH)]
            at = (c * RIM + away - 1) * CX
            out_a[at : at + CX] = jnp.where(even, north, south)
            out_b[at : at + CX] = jnp.where(even, south, north)


def add_x(ny, delta, picks, core, x_a, x_b, *rest):
    out_a, out_b, out_near, out_sums = rest[:4]
    out_others = rest[4:-2]
    merged = ny == 4
    field, sums = rest[-2:]
    even, _, _ = place_on("gy")
    total = picks.shape[1]
    rows = total * NC // ny
    field[...] = core[...]
    for c in range(NC):
        for away, start, extra in WIDE:
            for source, target, size in (
                (0, PITCH - extra, extra),
                (extra, 0, CY + extra),
            ):
                if size:
                    at = c * WIDE_ROWS + start + source
                    west, east = x_sides(x_a, x_b, pl.ds(at, size))
                    at = c * CORE + (away - 1) * PITCH + target
                    field[at : at + size] += west
                    at = c * CORE + (CX - away) * PITCH + target
                    field[at : at + size] += east
    at = 0
    for c in range(NC):
        for away, start, extra in WIDE:
            if extra:
                first = c * WIDE_ROWS + start
                south = x_sides(x_a, x_b, pl.ds(first, extra))
                north = x_sides(x_a, x_b, pl.ds(first + extra + CY, extra))
                for side in range(2):
                    out_a[at : at + extra] = jnp.where(even, north[side], south[side])
                    out_b[at : at + extra] = jnp.where(even, south[side], north[side])
                    at += extra
    for c in range(NC):
        for x in range(CX):
            at = c * CORE + x * PITCH
            here = slice(x * CY, (x + 1) * CY)
            out_near[c, here] = delta[c, here] + field[at : at + CY]
    adjoint = jnp.concatenate([field[c * CORE : (c + 1) * CORE] for c in range(NC)], axis=1)
    tile_sums = two_part_dot(jnp.transpose(picks[...]).astype(bf16), adjoint)
    for c in range(NC):
        sums[pl.ds(c, total, stride=NC)] = tile_sums[:, c * 128 : (c + 1) * 128]
    out_sums[...] = sums[0:rows]
    out_a[CORNERS:] = sums[rows : 2 * rows]
    if merged:
        out_b[CORNERS:] = sums[3 * rows : 4 * rows]
    for s, other in enumerate(out_others):
        other[...] = sums[(2 + s) * rows : (3 + s) * rows]


def add_y(alpha, near, sums, y_a, y_b, small_a, small_b, *rest):
    others = rest[:-2]
    out_delta, out_alpha = rest[-2:]
    out_delta[...] = near[...]
    at = 0
    for c in range(NC):
        for away, start, extra in WIDE:
            north, south = y_sides(y_a, y_b, pl.ds((c * RIM + away - 1) * CX, CX))
            high = pl.ds(CY - away, CX, stride=CY)
            low = pl.ds(away - 1, CX, stride=CY)
            out_delta[c, high] = out_delta[c, high] + north
            out_delta[c, low] = out_delta[c, low] + south
            if extra:
                for x in (away - 1, CX - away):
                    north, south = y_sides(small_a, small_b, pl.ds(at, extra))
                    out_delta[c, (x + 1) * CY - extra : (x + 1) * CY] += north
                    out_delta[c, x * CY : x * CY + extra] += south
                    at += extra
    total = sums[...] + small_a[CORNERS:]
    if small_b.shape[0] > CORNERS:
        total = total + small_b[CORNERS:]
    for other in others:
        total = total + other[...]
    out_alpha[...] = alpha[...] + profile_weight * total


def on_device(
    delta,
    alpha,
    eddy,
    courant,
    tile_map,
    obs_rows,
    gate_beam,
    gate_index,
    gate_column,
    gate_live,
    obs_weight,
    obs_precision,
):
    nx = lax.axis_size("gx")
    ny = lax.axis_size("gy")
    owned = alpha.shape[1]
    slots = gate_column.shape[2]
    fine = delta.reshape(NC, CX * CY, 128)
    eddy = eddy.reshape(CX * CY, 128)
    courant = courant.reshape(2, CX * CY, 128)
    control = alpha.reshape(owned * NC, 128)
    weights = obs_weight.reshape(slots * NC, 128)
    gates = [
        value.reshape(1, slots)
        for value in (gate_beam, gate_index, gate_column, gate_live, obs_precision)
    ]
    own_beams = jnp.transpose(obs_rows, (1, 0, 2)).reshape(STEPS * OWN_BEAMS, 128)
    beam_count = nx * OWN_BEAMS
    rows = owned * NC
    total = ny * owned

    y_a, y_b, fine, coefs, control_near, near_tiles, meta, near_beams = call(
        pack_y,
        [
            (Y_HALO + rows, 128),
            (Y_HALO, 128),
            fine.shape,
            (3, CX * CY, 128),
            control.shape,
            (CX, 128),
            (8, slots),
            own_beams.shape,
        ],
        [
            pltpu.with_memory_space_constraint(value, pltpu.HBM)
            for value in (fine, eddy, courant, control, tile_map, *gates, own_beams)
        ],
        [
            pltpu.VMEM(tile_map.shape, jnp.int32),
            pltpu.VMEM((4, 1, slots), jnp.int32),
            pltpu.VMEM((1, slots), f32),
            pltpu.SemaphoreType.DMA((12,)),
        ],
        in_specs=[HBM] * 11,
    )
    y_a = swap(y_a, "gy", 1)
    y_b = pair_b(y_b, "gy", "gx")
    others = [swap(control, "gy", xor) for xor in range(2, ny)]
    beams = jnp.concatenate([near_beams, swap(own_beams, "gx", 1)])
    beams = [beams] + [swap(beams, "gx", xor) for xor in range(2, nx, 2)]

    wide, slot_pick, slot_push, beam_pick, columns, edge_pick = call(
        one_hots,
        [
            (slots, NC * 128),
            jax.ShapeDtypeStruct((slots, CX * CY), bf16),
            jax.ShapeDtypeStruct((CX * CY, slots), bf16),
            jax.ShapeDtypeStruct((slots, beam_count), bf16),
            (slots, 8),
            jax.ShapeDtypeStruct((slots, 256), bf16),
        ],
        [meta, weights],
    )
    x_a, x_b = call(
        lambda *refs: pack_x(ny, *refs),
        [(X_HALO, 128), (X_HALO, 128)],
        [fine, coefs, control_near, near_tiles, columns, y_a, y_b, *others],
        [
            pltpu.VMEM((2 * RIM * PITCH, 128), f32),
            pltpu.VMEM((2 * RIM * PITCH, total), f32),
            pltpu.VMEM((total * NC, 128), f32),
            pltpu.VMEM((128, 128), f32),
        ],
    )
    x_a = swap(x_a, "gx", 1)
    x_b = pair_b(x_b, "gx", "gy")

    big = (NC * FIELD, 128)
    core, coef, picks, state_1, state_2, tally = call(
        lambda *refs: prepare(ny, *refs),
        [
            (NC * CORE, 128),
            (5 * CORE, 128),
            (CORE, total),
            (NC * CORE, 128),
            (NC * CORE, 128),
            (STEPS * slots, 128),
        ],
        [fine, coefs, control_near, near_tiles, columns, slot_pick, wide, y_a, y_b, *others],
        [
            pltpu.VMEM((NC * CORE, 128), f32),
            pltpu.VMEM((total * NC, 128), f32),
            pltpu.VMEM((128, 128), f32),
        ],
        flops=3000000,
    )
    edge_coef, totals = call(
        edges,
        [(5 * FIELD, 128), (STEPS * slots, 128)],
        [core, coef, state_1, state_2, tally, wide, edge_pick, x_a, x_b],
        [pltpu.VMEM(big, f32)] * 4 + [pltpu.VMEM((3 * FIELD, 128), f32)],
        flops=10000000,
    )
    back_a, back_b, back_2, back_1, tops, lows = call(
        push_edges,
        [
            (X_COEF, 128),
            (X_COEF, 128),
            big,
            big,
            jax.ShapeDtypeStruct((STEPS * slots, NC * 128), bf16),
            jax.ShapeDtypeStruct((STEPS * slots, NC * 128), bf16),
        ],
        [edge_coef, totals, wide, slot_push, beam_pick, columns, *beams],
        [
            pltpu.VMEM(big, f32),
            pltpu.VMEM(big, f32),
            pltpu.VMEM((STEPS * 2 * RIM * CY, NC * 128), f32),
        ],
        flops=10000000,
    )
    core, rim_a, rim_b = call(
        interior,
        [(NC * CORE, 128), (Y_COEF, 128), (Y_COEF, 128)],
        [coef, edge_coef, back_2, back_1, tops, lows, slot_push],
        [pltpu.VMEM((5 * FIELD, 128), f32)]
        + [pltpu.VMEM(big, f32)] * 3
        + [pltpu.VMEM((STEPS * CX * CY, NC * 128), f32)],
        flops=10000000,
    )
    x_a = swap(back_a, "gx", 1)
    x_b = pair_b(back_b, "gx", "gy")
    loose = [xor for xor in range(2, ny) if ny != 4 or xor != 3]
    back_a, back_b, near, sums, *back = call(
        lambda *refs: add_x(ny, *refs),
        [
            (CORNERS + rows, 128),
            (CORNERS + (rows if ny == 4 else 0), 128),
            fine.shape,
            (rows, 128),
        ]
        + [(rows, 128)] * len(loose),
        [fine, picks, core, x_a, x_b],
        [pltpu.VMEM((NC * CORE, 128), f32), pltpu.VMEM((total * NC, 128), f32)],
    )
    y_a = swap(rim_a, "gy", 1)
    y_b = pair_b(rim_b, "gy", "gx")
    small_a = swap(back_a, "gy", 1)
    small_b = ring_b(back_b, "gy")
    others = [swap(value, "gy", xor) for xor, value in zip(loose, back)]
    grad_delta, grad_alpha = call(
        add_y,
        [fine.shape, control.shape],
        [control_near, near, sums, y_a, y_b, small_a, small_b, *others],
    )
    return grad_delta.reshape(delta.shape), grad_alpha.reshape(alpha.shape)


def solution(mesh):
    return jax.shard_map(
        on_device,
        mesh=mesh,
        in_specs=(
            P(None, "gx", "gy", None),
            P("gx", "gy", None, None),
            P("gx", "gy", None),
            P(None, "gx", "gy", None),
            P("gx", "gy"),
            P(("gx", "gy"), None, None),
            P("gx", "gy", None),
            P("gx", "gy", None),
            P("gx", "gy", None),
            P("gx", "gy", None),
            P("gx", "gy", None, None, None),
            P("gx", "gy", None),
        ),
        out_specs=(P(None, "gx", "gy", None), P("gx", "gy", None, None)),
        check_vma=False,
    )
```

```python
import jax
import jax.numpy as jnp
from jax import lax
from jax.experimental import pallas as pl
from jax.experimental.pallas import tpu as pltpu
from jax.sharding import PartitionSpec as P

STEPS = 3
RIM = 3
INNER = RIM - 1
NC = 4
CX = 16
CY = 16
BLOCKS = CX + 8
PITCH = CY + 8
FIRST = 4
FIELD = BLOCKS * PITCH
CORE = CX * PITCH
OWN_BEAMS = 8
BEAM_BITS = 3

profile_weight = 0.125
f32 = jnp.float32
bf16 = jnp.bfloat16

VMEM = pl.BlockSpec(memory_space=pltpu.VMEM)
HBM = pl.BlockSpec(memory_space=pltpu.HBM)


def call(
    body, outs, ins, scratch=(), in_specs=None, out_specs=None, flops=1000000, limit=40 * 2**20
):
    shapes = [
        out if isinstance(out, jax.ShapeDtypeStruct) else jax.ShapeDtypeStruct(out, f32)
        for out in outs
    ]
    size = sum(4 * value.size for value in ins)
    return pl.pallas_call(
        body,
        out_shape=shapes,
        in_specs=in_specs or [VMEM] * len(ins),
        out_specs=out_specs or [VMEM] * len(shapes),
        scratch_shapes=list(scratch),
        compiler_params=pltpu.CompilerParams(vmem_limit_bytes=limit),
        cost_estimate=pl.CostEstimate(flops=flops, bytes_accessed=size, transcendentals=0),
    )(*ins)


def swap(block, axis, xor):
    return lax.ppermute(block, axis, [(i, i ^ xor) for i in range(lax.axis_size(axis))])


def pair_b(block, axis, other):
    count, across = lax.axis_size(axis), lax.axis_size(other)

    def place(i, j):
        return i * across + j if axis == "gx" else j * count + i

    pairs = []
    for j in range(across):
        for i in range(count):
            if i in (0, count - 1):
                pairs.append((place(i, j), place(i, j ^ 1)))
            else:
                pairs.append((place(i, j), place(i + 1 if i % 2 else i - 1, j)))
    return lax.ppermute(block, ("gx", "gy"), pairs)


def ring_b(block, axis):
    count = lax.axis_size(axis)
    pairs = [(i, (i + 1 if i % 2 else i - 1) % count) for i in range(count)]
    return lax.ppermute(block, axis, pairs)


def place_on(axis):
    me = lax.axis_index(axis)
    return lax.rem(me, 2) == 0, me > 0, me < lax.axis_size(axis) - 1


def split(value):
    top = value.astype(bf16)
    return top, (value - top.astype(f32)).astype(bf16)


def two_part_dot(left, value):
    top, low = split(value)
    return jnp.dot(left, top, preferred_element_type=f32) + jnp.dot(
        left, low, preferred_element_type=f32
    )


def layers(reach):
    found, at = [], 0
    for away in range(1, reach + 1):
        found.append((away, at, reach - away))
        at += CY + 2 * (reach - away)
    return found, at


WIDE, WIDE_ROWS = layers(RIM)
SLIM, SLIM_ROWS = layers(INNER)
X_COEF = NC * WIDE_ROWS
CORNERS = NC * 2 * sum(extra for _, _, extra in WIDE)
X_HALO = X_COEF + 3 * SLIM_ROWS

Y_COEF = NC * RIM * CX
Y_TILE = Y_COEF + 3 * INNER * CX
Y_HALO = Y_TILE + CX


def pack_y(
    delta,
    eddy,
    courant,
    alpha,
    tile_map,
    gate_beam,
    gate_index,
    gate_column,
    gate_live,
    precision,
    beam_rows,
    out_a,
    out_b,
    fine,
    coefs,
    profiles,
    near_tiles,
    meta,
    beams,
    tiles,
    gates,
    values,
    sems,
):
    even, _, _ = place_on("gy")
    moves = [
        pltpu.make_async_copy(source, target, sems.at[i])
        for i, (source, target) in enumerate(
            [
                (delta, fine),
                (eddy, coefs.at[0]),
                (courant.at[0], coefs.at[1]),
                (courant.at[1], coefs.at[2]),
                (tile_map, tiles),
                (alpha, profiles),
                (gate_beam, gates.at[0]),
                (gate_index, gates.at[1]),
                (gate_column, gates.at[2]),
                (gate_live, gates.at[3]),
                (precision, values),
                (beam_rows, beams),
            ]
        )
    ]
    for move in moves:
        move.start()
    for move in moves[1:]:
        move.wait()

    def put(at, field, away):
        north = field[pl.ds(CY - away, CX, stride=CY)]
        south = field[pl.ds(away - 1, CX, stride=CY)]
        out_a[at : at + CX] = jnp.where(even, north, south)
        out_b[at : at + CX] = jnp.where(even, south, north)

    for f in range(3):
        for away in range(1, INNER + 1):
            put(Y_COEF + (f * INNER + away - 1) * CX, coefs.at[f], away)
    near_tiles[...] = jnp.full((CX, 128), -1.0, f32)
    near_tiles[:, 0:CY] = tiles[...].astype(f32)
    for out in (out_a, out_b):
        out[Y_TILE : Y_TILE + CX] = near_tiles[...]
    out_a[Y_HALO:] = profiles[...]
    held = BEAM_BITS
    beam = gates[0]
    owner = jnp.bitwise_xor(beam >> held, lax.axis_index("gx"))
    meta[...] = jnp.zeros(meta.shape, f32)
    meta[0:1] = gates[2].astype(f32)
    meta[1:2] = ((owner << held) | (beam & ((1 << held) - 1))).astype(f32)
    meta[2:3] = gates[1].astype(f32)
    meta[3:4] = gates[3].astype(f32) * values[...]
    moves[0].wait()
    for c in range(NC):
        for away in range(1, RIM + 1):
            put((c * RIM + away - 1) * CX, fine.at[c], away)


def y_sides(got_a, got_b, rows, fill=0.0):
    even, low, high = place_on("gy")
    first, second = got_a[rows], got_b[rows]
    north, south = jnp.where(even, first, second), jnp.where(even, second, first)
    return jnp.where(high, north, fill), jnp.where(low, south, fill)


def x_sides(got_a, got_b, rows):
    even, low, high = place_on("gx")
    first, second = got_a[rows], got_b[rows]
    west, east = jnp.where(even, second, first), jnp.where(even, first, second)
    return jnp.where(low, west, 0.0), jnp.where(high, east, 0.0)


def gather_known(alpha, got_a, others, known):
    owned = alpha.shape[0]
    known[0:owned] = alpha[...]
    known[owned : 2 * owned] = got_a[Y_HALO:]
    for s, other in enumerate(others):
        known[(2 + s) * owned : (3 + s) * owned] = other[...]


def tile_numbers(near_tiles, got_a, got_b, tiles):
    spot = lax.broadcasted_iota(jnp.int32, (CX, 128), 1)
    north, south = y_sides(got_a, got_b, pl.ds(Y_TILE, CX), -1.0)
    near = jnp.where(
        (spot >= CY) & (spot < CY + RIM),
        pltpu.roll(north, CY, 1),
        jnp.where((spot >= PITCH - RIM) & (spot < PITCH), pltpu.roll(south, PITCH - CY, 1), -1.0),
    )
    tiles[...] = jnp.full(tiles.shape, -1.0, f32)
    tiles[0:CX] = jnp.where(spot < CY, near_tiles[...], near)
    return jnp.transpose(tiles[...])[0:PITCH]


def tile_ids(ny, owned):
    me = lax.axis_index("gy")
    lane = lax.broadcasted_iota(jnp.int32, (1, ny * owned), 1)
    ids = lane
    for s in range(ny):
        here = (lane >= s * owned) & (lane < (s + 1) * owned)
        ids = jnp.where(here, jnp.bitwise_xor(me, s) * owned + lane - s * owned, ids)
    return ids.astype(f32)


def by_variable(ref, count):
    return jnp.concatenate([ref[pl.ds(c, count, stride=NC)] for c in range(NC)], axis=1)


def pack_x(ny, delta, coefs, alpha, near_tiles, _, y_a, y_b, *rest):
    others = rest[: ny - 2]
    out_a, out_b, field, picks, known, tiles = rest[ny - 2 :]
    even, _, _ = place_on("gx")
    owned = alpha.shape[0] // NC
    gather_known(alpha, y_a, others, known)
    turned = tile_numbers(near_tiles, y_a, y_b, tiles)
    ids = tile_ids(ny, owned)
    columns = [x for x in range(RIM)] + [CX - RIM + x for x in range(RIM)]
    for i, x in enumerate(columns):
        picks[i * PITCH : (i + 1) * PITCH] = (turned[:, x : x + 1] == ids).astype(f32)
    fine = two_part_dot(picks[...].astype(bf16), by_variable(known, ny * owned))

    def fill(own, y_base, reach, c):
        for i, x in enumerate(columns):
            at = i * PITCH
            field[at + CY : at + PITCH] = jnp.zeros((PITCH - CY, 128), f32)
            field[at : at + CY] = own[x * CY : (x + 1) * CY]
        for away in range(1, reach + 1):
            for first, base in ((0, 0), (CX - RIM, RIM * PITCH)):
                rows = pl.ds(y_base + (away - 1) * CX + first, RIM)
                north, south = y_sides(y_a, y_b, rows)
                field[pl.ds(base + CY - 1 + away, RIM, stride=PITCH)] = north
                field[pl.ds(base + PITCH - away, RIM, stride=PITCH)] = south
        if c is not None:
            field[...] += profile_weight * fine[:, c * 128 : (c + 1) * 128]

    def put(at, found):
        for away, start, extra in found:
            east, west = (2 * RIM - away) * PITCH, (away - 1) * PITCH
            here = at + start
            for source, target, size in (
                (PITCH - extra, 0, extra),
                (0, extra, CY + extra),
            ):
                if size:
                    first = field[east + source : east + source + size]
                    second = field[west + source : west + source + size]
                    rows = slice(here + target, here + target + size)
                    out_a[rows] = jnp.where(even, first, second)
                    out_b[rows] = jnp.where(even, second, first)

    for c in range(NC):
        fill(delta.at[c], c * RIM * CX, RIM, c)
        put(c * WIDE_ROWS, WIDE)
    for f in range(3):
        fill(coefs.at[f], Y_COEF + f * INNER * CX, INNER, None)
        put(X_COEF + f * SLIM_ROWS, SLIM)


def one_hots(meta, weights, wide, slot_pick, slot_push, beam_pick, columns, edge_pick):
    slots = meta.shape[1]
    for c in range(NC):
        wide[:, c * 128 : (c + 1) * 128] = weights[pl.ds(c, slots, stride=NC)]
    per_beam = beam_pick.shape[1]
    turned = jnp.transpose(meta[...])
    columns[...] = turned
    slot_lane = lax.broadcasted_iota(jnp.int32, (slots, CX * CY), 1).astype(f32)
    slot_pick[...] = (slot_lane == turned[:, 0:1]).astype(f32).astype(bf16)
    edge_lane = lax.broadcasted_iota(jnp.int32, (slots, 128), 1)
    half = RIM * CY
    place = jnp.where(edge_lane < half, edge_lane, edge_lane + CX * CY - 2 * half)
    place = jnp.where(edge_lane < 2 * half, place, -1).astype(f32)
    near_edge = (place == turned[:, 0:1]).astype(f32).astype(bf16)
    edge_pick[:, 0:128] = near_edge
    edge_pick[:, 128:256] = near_edge
    column_row = lax.broadcasted_iota(jnp.int32, (CX * CY, slots), 0).astype(f32)
    slot_push[...] = (column_row == meta[0:1]).astype(f32).astype(bf16)
    beam_lane = lax.broadcasted_iota(jnp.int32, (slots, per_beam), 1).astype(f32)
    beam_pick[...] = (beam_lane == turned[:, 1:2]).astype(f32).astype(bf16)


def prepare(ny, delta, coefs, alpha, near_tiles, columns, slot_pick, wide, y_a, y_b, *rest):
    others = rest[: ny - 2]
    core, coef, picks, state_1, state_2, tally, state_3, known, tiles = rest[ny - 2 :]
    owned = alpha.shape[0] // NC

    def fill(ref, base, own, y_base, reach):
        for x in range(CX):
            at = base + x * PITCH
            ref[at : at + CY] = own[x * CY : (x + 1) * CY]
            ref[at + CY : at + PITCH] = jnp.zeros((PITCH - CY, 128), f32)
        for away in range(1, reach + 1):
            north, south = y_sides(y_a, y_b, pl.ds(y_base + (away - 1) * CX, CX))
            ref[pl.ds(base + CY - 1 + away, CX, stride=PITCH)] = north
            ref[pl.ds(base + PITCH - away, CX, stride=PITCH)] = south

    for c in range(NC):
        fill(core, c * CORE, delta.at[c], c * RIM * CX, RIM)
    for f in range(3):
        fill(coef, f * CORE, coefs.at[f], Y_COEF + f * INNER * CX, INNER)

    def combine(b, carry):
        at = pl.multiple_of(b * PITCH, 8)
        combined = combine_coefs(*[coef[pl.ds(f * CORE + at, PITCH)] for f in range(3)])
        for f, value in enumerate(combined):
            coef[pl.ds(f * CORE + at, PITCH)] = value
        return carry

    lax.fori_loop(0, CX, combine, 0)

    gather_known(alpha, y_a, others, known)
    turned = tile_numbers(near_tiles, y_a, y_b, tiles)
    ids = tile_ids(ny, owned)
    for x in range(CX):
        picks[x * PITCH : (x + 1) * PITCH] = (turned[:, x : x + 1] == ids).astype(f32)
    fine = two_part_dot(picks[...].astype(bf16), by_variable(known, ny * owned))
    for c in range(NC):
        core[c * CORE : (c + 1) * CORE] += profile_weight * fine[:, c * 128 : (c + 1) * 128]

    slots = columns.shape[0]
    states = [core, state_1, state_2, state_3]
    for step in range(STEPS):
        source, target = states[step], states[step + 1]

        def body(x, carry, source=source, target=target):
            at = pl.multiple_of(x * PITCH, 8)
            k = [coef[pl.ds(f * CORE + at, PITCH)] for f in range(5)]
            for c in range(NC):
                base = c * CORE + at
                target[pl.ds(base, PITCH)] = forward_column(source, base, k)
            return carry

        lax.fori_loop(step + 1, CX - 1 - step, body, 0, unroll=True)
        own = []
        for c in range(NC):
            pieces = [jnp.zeros(((step + 1) * CY, 128), f32)]
            for x in range(step + 1, CX - 1 - step):
                at = c * CORE + x * PITCH
                pieces.append(target[at : at + CY])
            own.append(jnp.concatenate(pieces + pieces[:1], axis=0))
        seen = two_part_dot(slot_pick[...], jnp.concatenate(own, axis=1)) * wide[...]
        total = seen[:, 0:128]
        for c in range(1, NC):
            total = total + seen[:, c * 128 : (c + 1) * 128]
        tally[step * slots : (step + 1) * slots] = total


def forward_column(source, base, k):
    here = source[pl.ds(base, PITCH)]
    return (
        k[0] * here
        + k[1] * source[pl.ds(base + PITCH, PITCH)]
        + k[2] * source[pl.ds(base - PITCH, PITCH)]
        + k[3] * pltpu.roll(here, PITCH - 1, 0)
        + k[4] * pltpu.roll(here, 1, 0)
    )


def backward_column(source, base, coef, at):
    here = source[pl.ds(base, PITCH)]
    return (
        coef[pl.ds(at, PITCH)] * here
        + coef[pl.ds(FIELD + at - PITCH, PITCH)] * source[pl.ds(base - PITCH, PITCH)]
        + coef[pl.ds(2 * FIELD + at + PITCH, PITCH)] * source[pl.ds(base + PITCH, PITCH)]
        + pltpu.roll(coef[pl.ds(3 * FIELD + at, PITCH)] * here, 1, 0)
        + pltpu.roll(coef[pl.ds(4 * FIELD + at, PITCH)] * here, PITCH - 1, 0)
    )


def combine_coefs(viscous, along_x, along_y):
    half_x, half_y = 0.5 * along_x, 0.5 * along_y
    return (
        1.0 - 4.0 * viscous,
        viscous - half_x,
        viscous + half_x,
        viscous - half_y,
        viscous + half_y,
    )


def clear(ref, base, blocks):
    for b in blocks:
        at = base + b * PITCH
        ref[at : at + PITCH] = jnp.zeros((PITCH, 128), f32)


def edges(
    core,
    core_coef,
    near_1,
    near_2,
    tally,
    wide,
    edge_pick,
    x_a,
    x_b,
    coef,
    totals,
    state_0,
    state_1,
    state_2,
    state_3,
    raw,
):
    slots = wide.shape[0]

    def fill(ref, base, x_base, found):
        for away, start, extra in found:
            for source, target, size in (
                (0, PITCH - extra, extra),
                (extra, 0, CY + extra),
            ):
                if size:
                    at = x_base + start + source
                    west, east = x_sides(x_a, x_b, pl.ds(at, size))
                    at = base + (FIRST - away) * PITCH + target
                    ref[at : at + size] = west
                    at = base + (FIRST + CX - 1 + away) * PITCH + target
                    ref[at : at + size] = east

    def copy(source, target, x, count):
        for c in range(NC):
            first = c * CORE + x * PITCH
            at = c * FIELD + (FIRST + x) * PITCH
            target[at : at + count * PITCH] = source[first : first + count * PITCH]

    rim = [FIRST - 3, FIRST - 2, FIRST - 1, FIRST + CX, FIRST + CX + 1, FIRST + CX + 2]
    for x, (source, target) in enumerate(((core, state_0), (near_1, state_1), (near_2, state_2))):
        copy(source, target, x, 2)
        copy(source, target, CX - 2 - x, 2)
    for c in range(NC):
        clear(state_0, c * FIELD, rim)
        fill(state_0, c * FIELD, c * WIDE_ROWS, WIDE)
    for f in range(3):
        clear(raw, f * FIELD, rim[1:5])
        fill(raw, f * FIELD, X_COEF + f * SLIM_ROWS, SLIM)
    for f in range(5):
        for x in (0, CX - RIM):
            first, at = f * CORE + x * PITCH, f * FIELD + (FIRST + x) * PITCH
            coef[at : at + RIM * PITCH] = core_coef[first : first + RIM * PITCH]
        clear(coef, f * FIELD, [0, 1, BLOCKS - 2, BLOCKS - 1])
    for b in rim[1:5]:
        rows = [slice(f * FIELD + b * PITCH, f * FIELD + (b + 1) * PITCH) for f in range(5)]
        for f, value in enumerate(combine_coefs(*[raw[rows[f]] for f in range(3)])):
            coef[rows[f]] = value

    outer = [*range(RIM), *range(CX - RIM, CX)]
    half = RIM * CY
    states = [state_0, state_1, state_2, state_3]
    for step in range(STEPS):
        source, target = states[step], states[step + 1]
        for x in range(step - 2, step + 1):
            for b in (FIRST + x, FIRST + CX - 1 - x):
                at = b * PITCH
                k = [coef[f * FIELD + at : f * FIELD + at + PITCH] for f in range(5)]
                for c in range(NC):
                    base = c * FIELD + at
                    target[base : base + PITCH] = forward_column(source, base, k)
        zero = jnp.zeros((CY, 128), f32)
        parts = []
        for c in range(NC):
            pieces = []
            for x in outer:
                at = c * FIELD + (FIRST + x) * PITCH
                known = x <= step or x >= CX - 1 - step
                pieces.append(target[at : at + CY] if known else zero)
            value = jnp.concatenate(pieces + [jnp.zeros((128 - 2 * half, 128), f32)], axis=0)
            parts.append(jnp.concatenate(split(value), axis=0))
        seen = jnp.dot(
            edge_pick[...], jnp.concatenate(parts, axis=1), preferred_element_type=f32
        )
        seen = seen * wide[...]
        rows = slice(step * slots, (step + 1) * slots)
        total = tally[rows]
        for c in range(NC):
            total = total + seen[:, c * 128 : (c + 1) * 128]
        totals[rows] = total


def push_edges(coef, totals, wide, slot_push, beam_pick, columns, *rest):
    beams = rest[:-9]
    out_a, out_b, back_2, back_1, tops, lows, state_0, state_3, forcing = rest[-9:]
    even, _, _ = place_on("gx")
    slots = columns.shape[0]
    gate_lane = lax.broadcasted_iota(jnp.int32, (slots, 128), 1).astype(f32)
    gate_here = gate_lane == columns[:, 2:3]
    scaled = columns[:, 3:4]
    outer = [*range(RIM), *range(CX - RIM, CX)]
    half = RIM * CY
    push = jnp.concatenate([slot_push[0:half], slot_push[CX * CY - half :]], axis=0)
    for step in range(STEPS):
        table = []
        for part in beams:
            for at in range(0, part.shape[0], STEPS * OWN_BEAMS):
                first = at + step * OWN_BEAMS
                table.append(part[first : first + OWN_BEAMS])
        table = two_part_dot(beam_pick[...], jnp.concatenate(table, axis=0))
        rows = slice(step * slots, (step + 1) * slots)
        total = totals[rows] - jnp.where(gate_here, table, 0.0)
        misfit = scaled * jnp.sum(total, axis=1, keepdims=True)
        top, low = split(misfit * wide[...])
        tops[rows] = top
        lows[rows] = low
        forcing[step * 2 * half : (step + 1) * 2 * half] = jnp.dot(
            push, top, preferred_element_type=f32
        ) + jnp.dot(push, low, preferred_element_type=f32)

    def forced(step, i, c):
        at = step * 2 * half + i * CY
        return forcing[at : at + CY, c * 128 : (c + 1) * 128]

    for c in range(NC):
        clear(state_0, c * FIELD, [2, 3, BLOCKS - 4, BLOCKS - 3])
        clear(back_2, c * FIELD, [1, 2, BLOCKS - 3, BLOCKS - 2])
        clear(back_1, c * FIELD, [0, 1, BLOCKS - 2, BLOCKS - 1])
        for i, x in enumerate(outer):
            at = c * FIELD + (FIRST + x) * PITCH
            state_0[at : at + CY] = forced(STEPS - 1, i, c)
            state_0[at + CY : at + PITCH] = jnp.zeros((PITCH - CY, 128), f32)
    fields = [state_0, back_2, back_1, state_3]
    for step in range(STEPS):
        source, target = fields[step], fields[step + 1]
        for x in range(-1 - step, 2 - step):
            for b in (FIRST + x, FIRST + CX - 1 - x):
                for c in range(NC):
                    base = c * FIELD + b * PITCH
                    target[base : base + PITCH] = backward_column(source, base, coef, b * PITCH)
        if step < STEPS - 1:
            for i, x in enumerate(outer):
                if x < 2 - step or x > CX - 3 + step:
                    for c in range(NC):
                        at = c * FIELD + (FIRST + x) * PITCH
                        target[at : at + CY] += forced(STEPS - 2 - step, i, c)
    for c in range(NC):
        for away, start, extra in WIDE:
            for source, target, size in (
                (PITCH - extra, 0, extra),
                (0, extra, CY + extra),
            ):
                if size:
                    at = c * FIELD + (FIRST - away) * PITCH + source
                    west = state_3[at : at + size]
                    at = c * FIELD + (FIRST + CX - 1 + away) * PITCH + source
                    east = state_3[at : at + size]
                    at = c * WIDE_ROWS + start + target
                    out_a[at : at + size] = jnp.where(even, east, west)
                    out_b[at : at + size] = jnp.where(even, west, east)


def interior(
    core_coef,
    edge_coef,
    back_2,
    back_1,
    tops,
    lows,
    slot_push,
    picks,
    out,
    out_a,
    out_b,
    out_picks,
    *scratch,
):
    coef, forced, field_2, field_1, forcing = scratch
    out_picks[...] = jnp.transpose(picks[...]).astype(bf16)
    for f in range(5):
        at = f * FIELD + FIRST * PITCH
        coef[at : at + CORE] = core_coef[f * CORE : (f + 1) * CORE]
        for b in (FIRST - 1, FIRST + CX):
            at = f * FIELD + b * PITCH
            coef[at : at + PITCH] = edge_coef[at : at + PITCH]
    for step in range(STEPS):
        rows = slice(step * CX * CY, (step + 1) * CX * CY)
        forcing[rows] = jnp.dot(
            slot_push[...], tops[rows], preferred_element_type=f32
        ) + jnp.dot(slot_push[...], lows[rows], preferred_element_type=f32)

    def add_forcing(ref, step, columns):
        for c in range(NC):
            for x in columns:
                at = c * FIELD + (FIRST + x) * PITCH
                first = step * CX * CY + x * CY
                value = forcing[first : first + CY, c * 128 : (c + 1) * 128]
                if step == STEPS - 1:
                    ref[at : at + CY] = value
                    ref[at + CY : at + PITCH] = jnp.zeros((PITCH - CY, 128), f32)
                else:
                    ref[at : at + CY] += value

    def sweep(source, target, low, high):
        def body(x, carry):
            at = pl.multiple_of((x + FIRST) * PITCH, 8)
            for c in range(NC):
                value = backward_column(source, c * FIELD + at, coef, at)
                if target is out:
                    target[pl.ds(pl.multiple_of(c * CORE + x * PITCH, 8), PITCH)] = value
                else:
                    target[pl.ds(c * FIELD + at, PITCH)] = value
            return carry

        lax.fori_loop(low, high, body, 0, unroll=True)

    def copy(source, target, columns):
        for c in range(NC):
            for x in columns:
                at = c * FIELD + (FIRST + x) * PITCH
                target[at : at + PITCH] = source[at : at + PITCH]

    add_forcing(forced, STEPS - 1, range(CX))
    sweep(forced, field_2, 2, CX - 2)
    add_forcing(field_2, STEPS - 2, range(2, CX - 2))
    copy(back_2, field_2, (0, 1, CX - 2, CX - 1))
    sweep(field_2, field_1, 1, CX - 1)
    add_forcing(field_1, STEPS - 3, range(1, CX - 1))
    copy(back_1, field_1, (-1, 0, CX - 1, CX))
    sweep(field_1, out, 0, CX)
    even, _, _ = place_on("gy")
    for c in range(NC):
        for away in range(1, RIM + 1):
            north = out[pl.ds(c * CORE + CY - 1 + away, CX, stride=PITCH)]
            south = out[pl.ds(c * CORE + PITCH - away, CX, stride=PITCH)]
            at = (c * RIM + away - 1) * CX
            out_a[at : at + CX] = jnp.where(even, north, south)
            out_b[at : at + CX] = jnp.where(even, south, north)


def add_x(ny, delta, picks, core, x_a, x_b, *rest):
    out_a, out_b, out_near, out_sums = rest[:4]
    out_others = rest[4:-2]
    merged = ny == 4
    field, sums = rest[-2:]
    even, _, _ = place_on("gy")
    total = picks.shape[0]
    rows = total * NC // ny
    field[...] = core[...]
    for c in range(NC):
        for away, start, extra in WIDE:
            for source, target, size in (
                (0, PITCH - extra, extra),
                (extra, 0, CY + extra),
            ):
                if size:
                    at = c * WIDE_ROWS + start + source
                    west, east = x_sides(x_a, x_b, pl.ds(at, size))
                    at = c * CORE + (away - 1) * PITCH + target
                    field[at : at + size] += west
                    at = c * CORE + (CX - away) * PITCH + target
                    field[at : at + size] += east
    at = 0
    for c in range(NC):
        for away, start, extra in WIDE:
            if extra:
                first = c * WIDE_ROWS + start
                south = x_sides(x_a, x_b, pl.ds(first, extra))
                north = x_sides(x_a, x_b, pl.ds(first + extra + CY, extra))
                for side in range(2):
                    out_a[at : at + extra] = jnp.where(even, north[side], south[side])
                    out_b[at : at + extra] = jnp.where(even, south[side], north[side])
                    at += extra
    for c in range(NC):
        for x in range(CX):
            at = c * CORE + x * PITCH
            here = slice(x * CY, (x + 1) * CY)
            out_near[c, here] = delta[c, here] + field[at : at + CY]
    adjoint = jnp.concatenate([field[c * CORE : (c + 1) * CORE] for c in range(NC)], axis=1)
    tile_sums = two_part_dot(picks[...], adjoint)
    for c in range(NC):
        sums[pl.ds(c, total, stride=NC)] = tile_sums[:, c * 128 : (c + 1) * 128]
    out_sums[...] = sums[0:rows]
    out_a[CORNERS:] = sums[rows : 2 * rows]
    if merged:
        out_b[CORNERS:] = sums[3 * rows : 4 * rows]
    for s, other in enumerate(out_others):
        other[...] = sums[(2 + s) * rows : (3 + s) * rows]


def add_y(alpha, near, sums, y_a, y_b, small_a, small_b, *rest):
    others = rest[:-4]
    result, out_alpha, out_delta, sems = rest[-4:]
    moves = []
    at = 0
    for c in range(NC):
        out_delta[c] = near[c]
        for away, start, extra in WIDE:
            north, south = y_sides(y_a, y_b, pl.ds((c * RIM + away - 1) * CX, CX))
            high = pl.ds(CY - away, CX, stride=CY)
            low = pl.ds(away - 1, CX, stride=CY)
            out_delta[c, high] = out_delta[c, high] + north
            out_delta[c, low] = out_delta[c, low] + south
            if extra:
                for x in (away - 1, CX - away):
                    north, south = y_sides(small_a, small_b, pl.ds(at, extra))
                    out_delta[c, (x + 1) * CY - extra : (x + 1) * CY] += north
                    out_delta[c, x * CY : x * CY + extra] += south
                    at += extra
        move = pltpu.make_async_copy(out_delta.at[c], result.at[c], sems.at[c])
        move.start()
        moves.append(move)
    total = sums[...] + small_a[CORNERS:]
    if small_b.shape[0] > CORNERS:
        total = total + small_b[CORNERS:]
    for other in others:
        total = total + other[...]
    out_alpha[...] = alpha[...] + profile_weight * total
    for move in moves:
        move.wait()


def on_device(
    delta,
    alpha,
    eddy,
    courant,
    tile_map,
    obs_rows,
    gate_beam,
    gate_index,
    gate_column,
    gate_live,
    obs_weight,
    obs_precision,
):
    nx = lax.axis_size("gx")
    ny = lax.axis_size("gy")
    owned = alpha.shape[1]
    slots = gate_column.shape[2]
    fine = delta.reshape(NC, CX * CY, 128)
    eddy = eddy.reshape(CX * CY, 128)
    courant = courant.reshape(2, CX * CY, 128)
    control = alpha.reshape(owned * NC, 128)
    weights = obs_weight.reshape(slots * NC, 128)
    gates = [
        value.reshape(1, slots)
        for value in (gate_beam, gate_index, gate_column, gate_live, obs_precision)
    ]
    own_beams = jnp.transpose(obs_rows, (1, 0, 2)).reshape(STEPS * OWN_BEAMS, 128)
    beam_count = nx * OWN_BEAMS
    rows = owned * NC
    total = ny * owned

    y_a, y_b, fine, coefs, control_near, near_tiles, meta, near_beams = call(
        pack_y,
        [
            (Y_HALO + rows, 128),
            (Y_HALO, 128),
            fine.shape,
            (3, CX * CY, 128),
            control.shape,
            (CX, 128),
            (8, slots),
            own_beams.shape,
        ],
        [
            pltpu.with_memory_space_constraint(value, pltpu.HBM)
            for value in (fine, eddy, courant, control, tile_map, *gates, own_beams)
        ],
        [
            pltpu.VMEM(tile_map.shape, jnp.int32),
            pltpu.VMEM((4, 1, slots), jnp.int32),
            pltpu.VMEM((1, slots), f32),
            pltpu.SemaphoreType.DMA((12,)),
        ],
        in_specs=[HBM] * 11,
    )
    y_a = swap(y_a, "gy", 1)
    y_b = pair_b(y_b, "gy", "gx")
    others = [swap(control, "gy", xor) for xor in range(2, ny)]
    beams = jnp.concatenate([near_beams, swap(own_beams, "gx", 1)])
    beams = [beams] + [swap(beams, "gx", xor) for xor in range(2, nx, 2)]

    wide, slot_pick, slot_push, beam_pick, columns, edge_pick = call(
        one_hots,
        [
            (slots, NC * 128),
            jax.ShapeDtypeStruct((slots, CX * CY), bf16),
            jax.ShapeDtypeStruct((CX * CY, slots), bf16),
            jax.ShapeDtypeStruct((slots, beam_count), bf16),
            (slots, 8),
            jax.ShapeDtypeStruct((slots, 256), bf16),
        ],
        [meta, weights],
    )
    x_a, x_b = call(
        lambda *refs: pack_x(ny, *refs),
        [(X_HALO, 128), (X_HALO, 128)],
        [fine, coefs, control_near, near_tiles, columns, y_a, y_b, *others],
        [
            pltpu.VMEM((2 * RIM * PITCH, 128), f32),
            pltpu.VMEM((2 * RIM * PITCH, total), f32),
            pltpu.VMEM((total * NC, 128), f32),
            pltpu.VMEM((128, 128), f32),
        ],
    )
    x_a = swap(x_a, "gx", 1)
    x_b = pair_b(x_b, "gx", "gy")

    big = (NC * FIELD, 128)
    core, coef, picks, state_1, state_2, tally = call(
        lambda *refs: prepare(ny, *refs),
        [
            (NC * CORE, 128),
            (5 * CORE, 128),
            (CORE, total),
            (NC * CORE, 128),
            (NC * CORE, 128),
            (STEPS * slots, 128),
        ],
        [fine, coefs, control_near, near_tiles, columns, slot_pick, wide, y_a, y_b, *others],
        [
            pltpu.VMEM((NC * CORE, 128), f32),
            pltpu.VMEM((total * NC, 128), f32),
            pltpu.VMEM((128, 128), f32),
        ],
        flops=3000000,
    )
    edge_coef, totals = call(
        edges,
        [(5 * FIELD, 128), (STEPS * slots, 128)],
        [core, coef, state_1, state_2, tally, wide, edge_pick, x_a, x_b],
        [pltpu.VMEM(big, f32)] * 4 + [pltpu.VMEM((3 * FIELD, 128), f32)],
        flops=10000000,
    )
    back_a, back_b, back_2, back_1, tops, lows = call(
        push_edges,
        [
            (X_COEF, 128),
            (X_COEF, 128),
            big,
            big,
            jax.ShapeDtypeStruct((STEPS * slots, NC * 128), bf16),
            jax.ShapeDtypeStruct((STEPS * slots, NC * 128), bf16),
        ],
        [edge_coef, totals, wide, slot_push, beam_pick, columns, *beams],
        [
            pltpu.VMEM(big, f32),
            pltpu.VMEM(big, f32),
            pltpu.VMEM((STEPS * 2 * RIM * CY, NC * 128), f32),
        ],
        flops=10000000,
    )
    core, rim_a, rim_b, picks = call(
        interior,
        [
            (NC * CORE, 128),
            (Y_COEF, 128),
            (Y_COEF, 128),
            jax.ShapeDtypeStruct((total, CORE), bf16),
        ],
        [coef, edge_coef, back_2, back_1, tops, lows, slot_push, picks],
        [pltpu.VMEM((5 * FIELD, 128), f32)]
        + [pltpu.VMEM(big, f32)] * 3
        + [pltpu.VMEM((STEPS * CX * CY, NC * 128), f32)],
        flops=10000000,
    )
    x_a = swap(back_a, "gx", 1)
    x_b = pair_b(back_b, "gx", "gy")
    loose = [xor for xor in range(2, ny) if ny != 4 or xor != 3]
    back_a, back_b, near, sums, *back = call(
        lambda *refs: add_x(ny, *refs),
        [
            (CORNERS + rows, 128),
            (CORNERS + (rows if ny == 4 else 0), 128),
            fine.shape,
            (rows, 128),
        ]
        + [(rows, 128)] * len(loose),
        [fine, picks, core, x_a, x_b],
        [pltpu.VMEM((NC * CORE, 128), f32), pltpu.VMEM((total * NC, 128), f32)],
    )
    y_a = swap(rim_a, "gy", 1)
    y_b = pair_b(rim_b, "gy", "gx")
    small_a = swap(back_a, "gy", 1)
    small_b = ring_b(back_b, "gy")
    others = [swap(value, "gy", xor) for xor, value in zip(loose, back)]
    grad_delta, grad_alpha = call(
        add_y,
        [fine.shape, control.shape],
        [control_near, near, sums, y_a, y_b, small_a, small_b, *others],
        [pltpu.VMEM(fine.shape, f32), pltpu.SemaphoreType.DMA((NC,))],
        out_specs=[HBM, VMEM],
    )
    return grad_delta.reshape(delta.shape), grad_alpha.reshape(alpha.shape)


def solution(mesh):
    return jax.shard_map(
        on_device,
        mesh=mesh,
        in_specs=(
            P(None, "gx", "gy", None),
            P("gx", "gy", None, None),
            P("gx", "gy", None),
            P(None, "gx", "gy", None),
            P("gx", "gy"),
            P(("gx", "gy"), None, None),
            P("gx", "gy", None),
            P("gx", "gy", None),
            P("gx", "gy", None),
            P("gx", "gy", None),
            P("gx", "gy", None, None, None),
            P("gx", "gy", None),
        ),
        out_specs=(P(None, "gx", "gy", None), P("gx", "gy", None, None)),
        check_vma=False,
    )
```

```python
import jax
import jax.numpy as jnp
from jax import lax
from jax.experimental import pallas as pl
from jax.experimental.pallas import tpu as pltpu
from jax.sharding import PartitionSpec as P

STEPS = 3
RIM = 3
INNER = RIM - 1
NC = 4
CX = 16
CY = 16
BLOCKS = CX + 8
PITCH = CY + 8
FIRST = 4
FIELD = BLOCKS * PITCH
CORE = CX * PITCH
OWN_BEAMS = 8
BEAM_BITS = 3

profile_weight = 0.125
f32 = jnp.float32
bf16 = jnp.bfloat16

VMEM = pl.BlockSpec(memory_space=pltpu.VMEM)
HBM = pl.BlockSpec(memory_space=pltpu.HBM)


def call(body, outs, ins, scratch=(), in_specs=None, flops=1000000, limit=40 * 2**20):
    shapes = [
        out if isinstance(out, jax.ShapeDtypeStruct) else jax.ShapeDtypeStruct(out, f32)
        for out in outs
    ]
    size = sum(4 * value.size for value in ins)
    return pl.pallas_call(
        body,
        out_shape=shapes,
        in_specs=in_specs or [VMEM] * len(ins),
        out_specs=[VMEM] * len(shapes),
        scratch_shapes=list(scratch),
        compiler_params=pltpu.CompilerParams(vmem_limit_bytes=limit),
        cost_estimate=pl.CostEstimate(flops=flops, bytes_accessed=size, transcendentals=0),
    )(*ins)


def swap(block, axis, xor):
    return lax.ppermute(block, axis, [(i, i ^ xor) for i in range(lax.axis_size(axis))])


def pair_b(block, axis, other):
    count, across = lax.axis_size(axis), lax.axis_size(other)

    def place(i, j):
        return i * across + j if axis == "gx" else j * count + i

    pairs = []
    for j in range(across):
        for i in range(count):
            if i in (0, count - 1):
                pairs.append((place(i, j), place(i, j ^ 1)))
            else:
                pairs.append((place(i, j), place(i + 1 if i % 2 else i - 1, j)))
    return lax.ppermute(block, ("gx", "gy"), pairs)


def ring_b(block, axis):
    count = lax.axis_size(axis)
    pairs = [(i, (i + 1 if i % 2 else i - 1) % count) for i in range(count)]
    return lax.ppermute(block, axis, pairs)


def place_on(axis):
    me = lax.axis_index(axis)
    return lax.rem(me, 2) == 0, me > 0, me < lax.axis_size(axis) - 1


def split(value):
    top = value.astype(bf16)
    return top, (value - top.astype(f32)).astype(bf16)


def two_part_dot(left, value):
    top, low = split(value)
    return jnp.dot(left, top, preferred_element_type=f32) + jnp.dot(
        left, low, preferred_element_type=f32
    )


def layers(reach):
    found, at = [], 0
    for away in range(1, reach + 1):
        found.append((away, at, reach - away))
        at += CY + 2 * (reach - away)
    return found, at


WIDE, WIDE_ROWS = layers(RIM)
SLIM, SLIM_ROWS = layers(INNER)
X_COEF = NC * WIDE_ROWS
CORNERS = NC * 2 * sum(extra for _, _, extra in WIDE)
X_HALO = X_COEF + 3 * SLIM_ROWS

Y_COEF = NC * RIM * CX
Y_TILE = Y_COEF + 3 * INNER * CX
Y_HALO = Y_TILE + CX


def pack_y(
    delta,
    eddy,
    courant,
    alpha,
    tile_map,
    gate_beam,
    gate_index,
    gate_column,
    gate_live,
    precision,
    beam_rows,
    out_a,
    out_b,
    fine,
    coefs,
    profiles,
    near_tiles,
    meta,
    beams,
    tiles,
    gates,
    values,
    sems,
):
    even, _, _ = place_on("gy")
    moves = [
        pltpu.make_async_copy(source, target, sems.at[i])
        for i, (source, target) in enumerate(
            [
                (delta, fine),
                (eddy, coefs.at[0]),
                (courant.at[0], coefs.at[1]),
                (courant.at[1], coefs.at[2]),
                (tile_map, tiles),
                (alpha, profiles),
                (gate_beam, gates.at[0]),
                (gate_index, gates.at[1]),
                (gate_column, gates.at[2]),
                (gate_live, gates.at[3]),
                (precision, values),
                (beam_rows, beams),
            ]
        )
    ]
    for move in moves:
        move.start()
    for move in moves[1:]:
        move.wait()

    def put(at, field, away):
        north = field[pl.ds(CY - away, CX, stride=CY)]
        south = field[pl.ds(away - 1, CX, stride=CY)]
        out_a[at : at + CX] = jnp.where(even, north, south)
        out_b[at : at + CX] = jnp.where(even, south, north)

    for f in range(3):
        for away in range(1, INNER + 1):
            put(Y_COEF + (f * INNER + away - 1) * CX, coefs.at[f], away)
    near_tiles[...] = jnp.full((CX, 128), -1.0, f32)
    near_tiles[:, 0:CY] = tiles[...].astype(f32)
    for out in (out_a, out_b):
        out[Y_TILE : Y_TILE + CX] = near_tiles[...]
    out_a[Y_HALO:] = profiles[...]
    held = BEAM_BITS
    beam = gates[0]
    owner = jnp.bitwise_xor(beam >> held, lax.axis_index("gx"))
    meta[...] = jnp.zeros(meta.shape, f32)
    meta[0:1] = gates[2].astype(f32)
    meta[1:2] = ((owner << held) | (beam & ((1 << held) - 1))).astype(f32)
    meta[2:3] = gates[1].astype(f32)
    meta[3:4] = gates[3].astype(f32) * values[...]
    moves[0].wait()
    for c in range(NC):
        for away in range(1, RIM + 1):
            put((c * RIM + away - 1) * CX, fine.at[c], away)


def y_sides(got_a, got_b, rows, fill=0.0):
    even, low, high = place_on("gy")
    first, second = got_a[rows], got_b[rows]
    north, south = jnp.where(even, first, second), jnp.where(even, second, first)
    return jnp.where(high, north, fill), jnp.where(low, south, fill)


def x_sides(got_a, got_b, rows):
    even, low, high = place_on("gx")
    first, second = got_a[rows], got_b[rows]
    west, east = jnp.where(even, second, first), jnp.where(even, first, second)
    return jnp.where(low, west, 0.0), jnp.where(high, east, 0.0)


def gather_known(alpha, got_a, others, known):
    owned = alpha.shape[0]
    known[0:owned] = alpha[...]
    known[owned : 2 * owned] = got_a[Y_HALO:]
    for s, other in enumerate(others):
        known[(2 + s) * owned : (3 + s) * owned] = other[...]


def tile_numbers(near_tiles, got_a, got_b, tiles):
    spot = lax.broadcasted_iota(jnp.int32, (CX, 128), 1)
    north, south = y_sides(got_a, got_b, pl.ds(Y_TILE, CX), -1.0)
    near = jnp.where(
        (spot >= CY) & (spot < CY + RIM),
        pltpu.roll(north, CY, 1),
        jnp.where((spot >= PITCH - RIM) & (spot < PITCH), pltpu.roll(south, PITCH - CY, 1), -1.0),
    )
    tiles[...] = jnp.full(tiles.shape, -1.0, f32)
    tiles[0:CX] = jnp.where(spot < CY, near_tiles[...], near)
    return jnp.transpose(tiles[...])[0:PITCH]


def tile_ids(ny, owned):
    me = lax.axis_index("gy")
    lane = lax.broadcasted_iota(jnp.int32, (1, ny * owned), 1)
    ids = lane
    for s in range(ny):
        here = (lane >= s * owned) & (lane < (s + 1) * owned)
        ids = jnp.where(here, jnp.bitwise_xor(me, s) * owned + lane - s * owned, ids)
    return ids.astype(f32)


def by_variable(ref, count):
    return jnp.concatenate([ref[pl.ds(c, count, stride=NC)] for c in range(NC)], axis=1)


def pack_x(ny, delta, coefs, alpha, near_tiles, _, y_a, y_b, *rest):
    others = rest[: ny - 2]
    out_a, out_b, field, picks, known, tiles = rest[ny - 2 :]
    even, _, _ = place_on("gx")
    owned = alpha.shape[0] // NC
    gather_known(alpha, y_a, others, known)
    turned = tile_numbers(near_tiles, y_a, y_b, tiles)
    ids = tile_ids(ny, owned)
    columns = [x for x in range(RIM)] + [CX - RIM + x for x in range(RIM)]
    for i, x in enumerate(columns):
        picks[i * PITCH : (i + 1) * PITCH] = (turned[:, x : x + 1] == ids).astype(f32)
    fine = two_part_dot(picks[...].astype(bf16), by_variable(known, ny * owned))

    def fill(own, y_base, reach, c):
        for i, x in enumerate(columns):
            at = i * PITCH
            field[at + CY : at + PITCH] = jnp.zeros((PITCH - CY, 128), f32)
            field[at : at + CY] = own[x * CY : (x + 1) * CY]
        for away in range(1, reach + 1):
            for first, base in ((0, 0), (CX - RIM, RIM * PITCH)):
                rows = pl.ds(y_base + (away - 1) * CX + first, RIM)
                north, south = y_sides(y_a, y_b, rows)
                field[pl.ds(base + CY - 1 + away, RIM, stride=PITCH)] = north
                field[pl.ds(base + PITCH - away, RIM, stride=PITCH)] = south
        if c is not None:
            field[...] += profile_weight * fine[:, c * 128 : (c + 1) * 128]

    def put(at, found):
        for away, start, extra in found:
            east, west = (2 * RIM - away) * PITCH, (away - 1) * PITCH
            here = at + start
            for source, target, size in (
                (PITCH - extra, 0, extra),
                (0, extra, CY + extra),
            ):
                if size:
                    first = field[east + source : east + source + size]
                    second = field[west + source : west + source + size]
                    rows = slice(here + target, here + target + size)
                    out_a[rows] = jnp.where(even, first, second)
                    out_b[rows] = jnp.where(even, second, first)

    for c in range(NC):
        fill(delta.at[c], c * RIM * CX, RIM, c)
        put(c * WIDE_ROWS, WIDE)
    for f in range(3):
        fill(coefs.at[f], Y_COEF + f * INNER * CX, INNER, None)
        put(X_COEF + f * SLIM_ROWS, SLIM)


def one_hots(meta, weights, wide, slot_pick, slot_push, beam_pick, columns, edge_pick):
    slots = meta.shape[1]
    for c in range(NC):
        wide[:, c * 128 : (c + 1) * 128] = weights[pl.ds(c, slots, stride=NC)]
    per_beam = beam_pick.shape[1]
    turned = jnp.transpose(meta[...])
    columns[...] = turned
    slot_lane = lax.broadcasted_iota(jnp.int32, (slots, CX * CY), 1).astype(f32)
    slot_pick[...] = (slot_lane == turned[:, 0:1]).astype(f32).astype(bf16)
    edge_lane = lax.broadcasted_iota(jnp.int32, (slots, 128), 1)
    half = RIM * CY
    place = jnp.where(edge_lane < half, edge_lane, edge_lane + CX * CY - 2 * half)
    place = jnp.where(edge_lane < 2 * half, place, -1).astype(f32)
    near_edge = (place == turned[:, 0:1]).astype(f32).astype(bf16)
    edge_pick[:, 0:128] = near_edge
    edge_pick[:, 128:256] = near_edge
    column_row = lax.broadcasted_iota(jnp.int32, (CX * CY, slots), 0).astype(f32)
    slot_push[...] = (column_row == meta[0:1]).astype(f32).astype(bf16)
    beam_lane = lax.broadcasted_iota(jnp.int32, (slots, per_beam), 1).astype(f32)
    beam_pick[...] = (beam_lane == turned[:, 1:2]).astype(f32).astype(bf16)


def prepare(ny, delta, coefs, alpha, near_tiles, columns, slot_pick, wide, y_a, y_b, *rest):
    others = rest[: ny - 2]
    core, coef, picks, state_1, state_2, tally, state_3, known, tiles = rest[ny - 2 :]
    owned = alpha.shape[0] // NC

    def fill(ref, base, own, y_base, reach):
        for x in range(CX):
            at = base + x * PITCH
            ref[at : at + CY] = own[x * CY : (x + 1) * CY]
            ref[at + CY : at + PITCH] = jnp.zeros((PITCH - CY, 128), f32)
        for away in range(1, reach + 1):
            north, south = y_sides(y_a, y_b, pl.ds(y_base + (away - 1) * CX, CX))
            ref[pl.ds(base + CY - 1 + away, CX, stride=PITCH)] = north
            ref[pl.ds(base + PITCH - away, CX, stride=PITCH)] = south

    for c in range(NC):
        fill(core, c * CORE, delta.at[c], c * RIM * CX, RIM)
    for f in range(3):
        fill(coef, f * CORE, coefs.at[f], Y_COEF + f * INNER * CX, INNER)

    def combine(b, carry):
        at = pl.multiple_of(b * PITCH, 8)
        combined = combine_coefs(*[coef[pl.ds(f * CORE + at, PITCH)] for f in range(3)])
        for f, value in enumerate(combined):
            coef[pl.ds(f * CORE + at, PITCH)] = value
        return carry

    lax.fori_loop(0, CX, combine, 0, unroll=True)

    gather_known(alpha, y_a, others, known)
    turned = tile_numbers(near_tiles, y_a, y_b, tiles)
    ids = tile_ids(ny, owned)
    for x in range(CX):
        picks[x * PITCH : (x + 1) * PITCH] = (turned[:, x : x + 1] == ids).astype(f32)
    fine = two_part_dot(picks[...].astype(bf16), by_variable(known, ny * owned))
    for c in range(NC):
        core[c * CORE : (c + 1) * CORE] += profile_weight * fine[:, c * 128 : (c + 1) * 128]

    slots = columns.shape[0]
    states = [core, state_1, state_2, state_3]
    for step in range(STEPS):
        source, target = states[step], states[step + 1]

        def body(x, carry, source=source, target=target):
            at = pl.multiple_of(x * PITCH, 8)
            k = [coef[pl.ds(f * CORE + at, PITCH)] for f in range(5)]
            for c in range(NC):
                base = c * CORE + at
                target[pl.ds(base, PITCH)] = forward_column(source, base, k)
            return carry

        lax.fori_loop(step + 1, CX - 1 - step, body, 0, unroll=True)
        own = []
        for c in range(NC):
            pieces = [jnp.zeros(((step + 1) * CY, 128), f32)]
            for x in range(step + 1, CX - 1 - step):
                at = c * CORE + x * PITCH
                pieces.append(target[at : at + CY])
            own.append(jnp.concatenate(pieces + pieces[:1], axis=0))
        seen = two_part_dot(slot_pick[...], jnp.concatenate(own, axis=1)) * wide[...]
        total = seen[:, 0:128]
        for c in range(1, NC):
            total = total + seen[:, c * 128 : (c + 1) * 128]
        tally[step * slots : (step + 1) * slots] = total


def forward_column(source, base, k):
    here = source[pl.ds(base, PITCH)]
    return (
        k[0] * here
        + k[1] * source[pl.ds(base + PITCH, PITCH)]
        + k[2] * source[pl.ds(base - PITCH, PITCH)]
        + k[3] * pltpu.roll(here, PITCH - 1, 0)
        + k[4] * pltpu.roll(here, 1, 0)
    )


def backward_column(source, base, coef, at):
    here = source[pl.ds(base, PITCH)]
    return (
        coef[pl.ds(at, PITCH)] * here
        + coef[pl.ds(FIELD + at - PITCH, PITCH)] * source[pl.ds(base - PITCH, PITCH)]
        + coef[pl.ds(2 * FIELD + at + PITCH, PITCH)] * source[pl.ds(base + PITCH, PITCH)]
        + pltpu.roll(coef[pl.ds(3 * FIELD + at, PITCH)] * here, 1, 0)
        + pltpu.roll(coef[pl.ds(4 * FIELD + at, PITCH)] * here, PITCH - 1, 0)
    )


def combine_coefs(viscous, along_x, along_y):
    half_x, half_y = 0.5 * along_x, 0.5 * along_y
    return (
        1.0 - 4.0 * viscous,
        viscous - half_x,
        viscous + half_x,
        viscous - half_y,
        viscous + half_y,
    )


def clear(ref, base, blocks):
    for b in blocks:
        at = base + b * PITCH
        ref[at : at + PITCH] = jnp.zeros((PITCH, 128), f32)


def edges(
    core,
    core_coef,
    near_1,
    near_2,
    tally,
    wide,
    edge_pick,
    x_a,
    x_b,
    coef,
    totals,
    state_0,
    state_1,
    state_2,
    state_3,
    raw,
):
    slots = wide.shape[0]

    def fill(ref, base, x_base, found):
        for away, start, extra in found:
            for source, target, size in (
                (0, PITCH - extra, extra),
                (extra, 0, CY + extra),
            ):
                if size:
                    at = x_base + start + source
                    west, east = x_sides(x_a, x_b, pl.ds(at, size))
                    at = base + (FIRST - away) * PITCH + target
                    ref[at : at + size] = west
                    at = base + (FIRST + CX - 1 + away) * PITCH + target
                    ref[at : at + size] = east

    def copy(source, target, x, count):
        for c in range(NC):
            first = c * CORE + x * PITCH
            at = c * FIELD + (FIRST + x) * PITCH
            target[at : at + count * PITCH] = source[first : first + count * PITCH]

    rim = [FIRST - 3, FIRST - 2, FIRST - 1, FIRST + CX, FIRST + CX + 1, FIRST + CX + 2]
    for x, (source, target) in enumerate(((core, state_0), (near_1, state_1), (near_2, state_2))):
        copy(source, target, x, 2)
        copy(source, target, CX - 2 - x, 2)
    for c in range(NC):
        clear(state_0, c * FIELD, rim)
        fill(state_0, c * FIELD, c * WIDE_ROWS, WIDE)
    for f in range(3):
        clear(raw, f * FIELD, rim[1:5])
        fill(raw, f * FIELD, X_COEF + f * SLIM_ROWS, SLIM)
    for f in range(5):
        for x in (0, CX - RIM):
            first, at = f * CORE + x * PITCH, f * FIELD + (FIRST + x) * PITCH
            coef[at : at + RIM * PITCH] = core_coef[first : first + RIM * PITCH]
        clear(coef, f * FIELD, [0, 1, BLOCKS - 2, BLOCKS - 1])
    for b in rim[1:5]:
        rows = [slice(f * FIELD + b * PITCH, f * FIELD + (b + 1) * PITCH) for f in range(5)]
        for f, value in enumerate(combine_coefs(*[raw[rows[f]] for f in range(3)])):
            coef[rows[f]] = value

    outer = [*range(RIM), *range(CX - RIM, CX)]
    half = RIM * CY
    states = [state_0, state_1, state_2, state_3]
    for step in range(STEPS):
        source, target = states[step], states[step + 1]
        for x in range(step - 2, step + 1):
            for b in (FIRST + x, FIRST + CX - 1 - x):
                at = b * PITCH
                k = [coef[f * FIELD + at : f * FIELD + at + PITCH] for f in range(5)]
                for c in range(NC):
                    base = c * FIELD + at
                    target[base : base + PITCH] = forward_column(source, base, k)
        zero = jnp.zeros((CY, 128), f32)
        parts = []
        for c in range(NC):
            pieces = []
            for x in outer:
                at = c * FIELD + (FIRST + x) * PITCH
                known = x <= step or x >= CX - 1 - step
                pieces.append(target[at : at + CY] if known else zero)
            value = jnp.concatenate(pieces + [jnp.zeros((128 - 2 * half, 128), f32)], axis=0)
            parts.append(jnp.concatenate(split(value), axis=0))
        seen = jnp.dot(
            edge_pick[...], jnp.concatenate(parts, axis=1), preferred_element_type=f32
        )
        seen = seen * wide[...]
        rows = slice(step * slots, (step + 1) * slots)
        total = tally[rows]
        for c in range(NC):
            total = total + seen[:, c * 128 : (c + 1) * 128]
        totals[rows] = total


def push_edges(coef, totals, wide, slot_push, beam_pick, columns, *rest):
    beams = rest[:-9]
    out_a, out_b, back_2, back_1, tops, lows, state_0, state_3, forcing = rest[-9:]
    even, _, _ = place_on("gx")
    slots = columns.shape[0]
    gate_lane = lax.broadcasted_iota(jnp.int32, (slots, 128), 1).astype(f32)
    gate_here = gate_lane == columns[:, 2:3]
    scaled = columns[:, 3:4]
    outer = [*range(RIM), *range(CX - RIM, CX)]
    half = RIM * CY
    push = jnp.concatenate([slot_push[0:half], slot_push[CX * CY - half :]], axis=0)
    for step in range(STEPS):
        table = []
        for part in beams:
            for at in range(0, part.shape[0], STEPS * OWN_BEAMS):
                first = at + step * OWN_BEAMS
                table.append(part[first : first + OWN_BEAMS])
        table = two_part_dot(beam_pick[...], jnp.concatenate(table, axis=0))
        rows = slice(step * slots, (step + 1) * slots)
        total = totals[rows] - jnp.where(gate_here, table, 0.0)
        misfit = scaled * jnp.sum(total, axis=1, keepdims=True)
        top, low = split(misfit * wide[...])
        tops[rows] = top
        lows[rows] = low
        forcing[step * 2 * half : (step + 1) * 2 * half] = jnp.dot(
            push, top, preferred_element_type=f32
        ) + jnp.dot(push, low, preferred_element_type=f32)

    def forced(step, i, c):
        at = step * 2 * half + i * CY
        return forcing[at : at + CY, c * 128 : (c + 1) * 128]

    for c in range(NC):
        clear(state_0, c * FIELD, [2, 3, BLOCKS - 4, BLOCKS - 3])
        clear(back_2, c * FIELD, [1, 2, BLOCKS - 3, BLOCKS - 2])
        clear(back_1, c * FIELD, [0, 1, BLOCKS - 2, BLOCKS - 1])
        for i, x in enumerate(outer):
            at = c * FIELD + (FIRST + x) * PITCH
            state_0[at : at + CY] = forced(STEPS - 1, i, c)
            state_0[at + CY : at + PITCH] = jnp.zeros((PITCH - CY, 128), f32)
    fields = [state_0, back_2, back_1, state_3]
    for step in range(STEPS):
        source, target = fields[step], fields[step + 1]
        for x in range(-1 - step, 2 - step):
            for b in (FIRST + x, FIRST + CX - 1 - x):
                for c in range(NC):
                    base = c * FIELD + b * PITCH
                    target[base : base + PITCH] = backward_column(source, base, coef, b * PITCH)
        if step < STEPS - 1:
            for i, x in enumerate(outer):
                if x < 2 - step or x > CX - 3 + step:
                    for c in range(NC):
                        at = c * FIELD + (FIRST + x) * PITCH
                        target[at : at + CY] += forced(STEPS - 2 - step, i, c)
    for c in range(NC):
        for away, start, extra in WIDE:
            for source, target, size in (
                (PITCH - extra, 0, extra),
                (0, extra, CY + extra),
            ):
                if size:
                    at = c * FIELD + (FIRST - away) * PITCH + source
                    west = state_3[at : at + size]
                    at = c * FIELD + (FIRST + CX - 1 + away) * PITCH + source
                    east = state_3[at : at + size]
                    at = c * WIDE_ROWS + start + target
                    out_a[at : at + size] = jnp.where(even, east, west)
                    out_b[at : at + size] = jnp.where(even, west, east)


def interior(
    core_coef,
    edge_coef,
    back_2,
    back_1,
    tops,
    lows,
    slot_push,
    picks,
    out,
    out_a,
    out_b,
    out_picks,
    *scratch,
):
    coef, forced, field_2, field_1, forcing = scratch
    out_picks[...] = jnp.transpose(picks[...]).astype(bf16)
    for f in range(5):
        at = f * FIELD + FIRST * PITCH
        coef[at : at + CORE] = core_coef[f * CORE : (f + 1) * CORE]
        for b in (FIRST - 1, FIRST + CX):
            at = f * FIELD + b * PITCH
            coef[at : at + PITCH] = edge_coef[at : at + PITCH]
    for step in range(STEPS):
        rows = slice(step * CX * CY, (step + 1) * CX * CY)
        forcing[rows] = jnp.dot(
            slot_push[...], tops[rows], preferred_element_type=f32
        ) + jnp.dot(slot_push[...], lows[rows], preferred_element_type=f32)

    def add_forcing(ref, step, columns):
        for c in range(NC):
            for x in columns:
                at = c * FIELD + (FIRST + x) * PITCH
                first = step * CX * CY + x * CY
                value = forcing[first : first + CY, c * 128 : (c + 1) * 128]
                if step == STEPS - 1:
                    ref[at : at + CY] = value
                    ref[at + CY : at + PITCH] = jnp.zeros((PITCH - CY, 128), f32)
                else:
                    ref[at : at + CY] += value

    def sweep(source, target, low, high):
        def body(x, carry):
            at = pl.multiple_of((x + FIRST) * PITCH, 8)
            for c in range(NC):
                value = backward_column(source, c * FIELD + at, coef, at)
                if target is out:
                    target[pl.ds(pl.multiple_of(c * CORE + x * PITCH, 8), PITCH)] = value
                else:
                    target[pl.ds(c * FIELD + at, PITCH)] = value
            return carry

        lax.fori_loop(low, high, body, 0, unroll=True)

    def copy(source, target, columns):
        for c in range(NC):
            for x in columns:
                at = c * FIELD + (FIRST + x) * PITCH
                target[at : at + PITCH] = source[at : at + PITCH]

    add_forcing(forced, STEPS - 1, range(CX))
    sweep(forced, field_2, 2, CX - 2)
    add_forcing(field_2, STEPS - 2, range(2, CX - 2))
    copy(back_2, field_2, (0, 1, CX - 2, CX - 1))
    sweep(field_2, field_1, 1, CX - 1)
    add_forcing(field_1, STEPS - 3, range(1, CX - 1))
    copy(back_1, field_1, (-1, 0, CX - 1, CX))
    sweep(field_1, out, 0, CX)
    even, _, _ = place_on("gy")
    for c in range(NC):
        for away in range(1, RIM + 1):
            north = out[pl.ds(c * CORE + CY - 1 + away, CX, stride=PITCH)]
            south = out[pl.ds(c * CORE + PITCH - away, CX, stride=PITCH)]
            at = (c * RIM + away - 1) * CX
            out_a[at : at + CX] = jnp.where(even, north, south)
            out_b[at : at + CX] = jnp.where(even, south, north)


def add_x(ny, delta, picks, core, x_a, x_b, *rest):
    out_a, out_b, out_near, out_sums = rest[:4]
    out_others = rest[4:-2]
    merged = ny == 4
    field, sums = rest[-2:]
    even, _, _ = place_on("gy")
    total = picks.shape[0]
    rows = total * NC // ny
    field[...] = core[...]
    for c in range(NC):
        for away, start, extra in WIDE:
            for source, target, size in (
                (0, PITCH - extra, extra),
                (extra, 0, CY + extra),
            ):
                if size:
                    at = c * WIDE_ROWS + start + source
                    west, east = x_sides(x_a, x_b, pl.ds(at, size))
                    at = c * CORE + (away - 1) * PITCH + target
                    field[at : at + size] += west
                    at = c * CORE + (CX - away) * PITCH + target
                    field[at : at + size] += east
    at = 0
    for c in range(NC):
        for away, start, extra in WIDE:
            if extra:
                first = c * WIDE_ROWS + start
                south = x_sides(x_a, x_b, pl.ds(first, extra))
                north = x_sides(x_a, x_b, pl.ds(first + extra + CY, extra))
                for side in range(2):
                    out_a[at : at + extra] = jnp.where(even, north[side], south[side])
                    out_b[at : at + extra] = jnp.where(even, south[side], north[side])
                    at += extra
    for c in range(NC):
        for x in range(CX):
            at = c * CORE + x * PITCH
            here = slice(x * CY, (x + 1) * CY)
            out_near[c, here] = delta[c, here] + field[at : at + CY]
    adjoint = jnp.concatenate([field[c * CORE : (c + 1) * CORE] for c in range(NC)], axis=1)
    tile_sums = two_part_dot(picks[...], adjoint)
    for c in range(NC):
        sums[pl.ds(c, total, stride=NC)] = tile_sums[:, c * 128 : (c + 1) * 128]
    out_sums[...] = sums[0:rows]
    out_a[CORNERS:] = sums[rows : 2 * rows]
    if merged:
        out_b[CORNERS:] = sums[3 * rows : 4 * rows]
    for s, other in enumerate(out_others):
        other[...] = sums[(2 + s) * rows : (3 + s) * rows]


def add_y(alpha, near, sums, y_a, y_b, small_a, small_b, *rest):
    others = rest[:-2]
    out_delta, out_alpha = rest[-2:]
    out_delta[...] = near[...]
    at = 0
    for c in range(NC):
        for away, start, extra in WIDE:
            north, south = y_sides(y_a, y_b, pl.ds((c * RIM + away - 1) * CX, CX))
            high = pl.ds(CY - away, CX, stride=CY)
            low = pl.ds(away - 1, CX, stride=CY)
            out_delta[c, high] = out_delta[c, high] + north
            out_delta[c, low] = out_delta[c, low] + south
            if extra:
                for x in (away - 1, CX - away):
                    north, south = y_sides(small_a, small_b, pl.ds(at, extra))
                    out_delta[c, (x + 1) * CY - extra : (x + 1) * CY] += north
                    out_delta[c, x * CY : x * CY + extra] += south
                    at += extra
    total = sums[...] + small_a[CORNERS:]
    if small_b.shape[0] > CORNERS:
        total = total + small_b[CORNERS:]
    for other in others:
        total = total + other[...]
    out_alpha[...] = alpha[...] + profile_weight * total


def on_device(
    delta,
    alpha,
    eddy,
    courant,
    tile_map,
    obs_rows,
    gate_beam,
    gate_index,
    gate_column,
    gate_live,
    obs_weight,
    obs_precision,
):
    nx = lax.axis_size("gx")
    ny = lax.axis_size("gy")
    owned = alpha.shape[1]
    slots = gate_column.shape[2]
    fine = delta.reshape(NC, CX * CY, 128)
    eddy = eddy.reshape(CX * CY, 128)
    courant = courant.reshape(2, CX * CY, 128)
    control = alpha.reshape(owned * NC, 128)
    weights = obs_weight.reshape(slots * NC, 128)
    gates = [
        value.reshape(1, slots)
        for value in (gate_beam, gate_index, gate_column, gate_live, obs_precision)
    ]
    own_beams = jnp.transpose(obs_rows, (1, 0, 2)).reshape(STEPS * OWN_BEAMS, 128)
    beam_count = nx * OWN_BEAMS
    rows = owned * NC
    total = ny * owned

    y_a, y_b, fine, coefs, control_near, near_tiles, meta, near_beams = call(
        pack_y,
        [
            (Y_HALO + rows, 128),
            (Y_HALO, 128),
            fine.shape,
            (3, CX * CY, 128),
            control.shape,
            (CX, 128),
            (8, slots),
            own_beams.shape,
        ],
        [
            pltpu.with_memory_space_constraint(value, pltpu.HBM)
            for value in (fine, eddy, courant, control, tile_map, *gates, own_beams)
        ],
        [
            pltpu.VMEM(tile_map.shape, jnp.int32),
            pltpu.VMEM((4, 1, slots), jnp.int32),
            pltpu.VMEM((1, slots), f32),
            pltpu.SemaphoreType.DMA((12,)),
        ],
        in_specs=[HBM] * 11,
    )
    y_a = swap(y_a, "gy", 1)
    y_b = pair_b(y_b, "gy", "gx")
    others = [swap(control, "gy", xor) for xor in range(2, ny)]
    beams = jnp.concatenate([near_beams, swap(own_beams, "gx", 1)])
    beams = [beams] + [swap(beams, "gx", xor) for xor in range(2, nx, 2)]

    wide, slot_pick, slot_push, beam_pick, columns, edge_pick = call(
        one_hots,
        [
            (slots, NC * 128),
            jax.ShapeDtypeStruct((slots, CX * CY), bf16),
            jax.ShapeDtypeStruct((CX * CY, slots), bf16),
            jax.ShapeDtypeStruct((slots, beam_count), bf16),
            (slots, 8),
            jax.ShapeDtypeStruct((slots, 256), bf16),
        ],
        [meta, weights],
    )
    x_a, x_b = call(
        lambda *refs: pack_x(ny, *refs),
        [(X_HALO, 128), (X_HALO, 128)],
        [fine, coefs, control_near, near_tiles, columns, y_a, y_b, *others],
        [
            pltpu.VMEM((2 * RIM * PITCH, 128), f32),
            pltpu.VMEM((2 * RIM * PITCH, total), f32),
            pltpu.VMEM((total * NC, 128), f32),
            pltpu.VMEM((128, 128), f32),
        ],
    )
    x_a = swap(x_a, "gx", 1)
    x_b = pair_b(x_b, "gx", "gy")

    big = (NC * FIELD, 128)
    core, coef, picks, state_1, state_2, tally = call(
        lambda *refs: prepare(ny, *refs),
        [
            (NC * CORE, 128),
            (5 * CORE, 128),
            (CORE, total),
            (NC * CORE, 128),
            (NC * CORE, 128),
            (STEPS * slots, 128),
        ],
        [fine, coefs, control_near, near_tiles, columns, slot_pick, wide, y_a, y_b, *others],
        [
            pltpu.VMEM((NC * CORE, 128), f32),
            pltpu.VMEM((total * NC, 128), f32),
            pltpu.VMEM((128, 128), f32),
        ],
        flops=3000000,
    )
    edge_coef, totals = call(
        edges,
        [(5 * FIELD, 128), (STEPS * slots, 128)],
        [core, coef, state_1, state_2, tally, wide, edge_pick, x_a, x_b],
        [pltpu.VMEM(big, f32)] * 4 + [pltpu.VMEM((3 * FIELD, 128), f32)],
        flops=10000000,
    )
    back_a, back_b, back_2, back_1, tops, lows = call(
        push_edges,
        [
            (X_COEF, 128),
            (X_COEF, 128),
            big,
            big,
            jax.ShapeDtypeStruct((STEPS * slots, NC * 128), bf16),
            jax.ShapeDtypeStruct((STEPS * slots, NC * 128), bf16),
        ],
        [edge_coef, totals, wide, slot_push, beam_pick, columns, *beams],
        [
            pltpu.VMEM(big, f32),
            pltpu.VMEM(big, f32),
            pltpu.VMEM((STEPS * 2 * RIM * CY, NC * 128), f32),
        ],
        flops=10000000,
    )
    core, rim_a, rim_b, picks = call(
        interior,
        [
            (NC * CORE, 128),
            (Y_COEF, 128),
            (Y_COEF, 128),
            jax.ShapeDtypeStruct((total, CORE), bf16),
        ],
        [coef, edge_coef, back_2, back_1, tops, lows, slot_push, picks],
        [pltpu.VMEM((5 * FIELD, 128), f32)]
        + [pltpu.VMEM(big, f32)] * 3
        + [pltpu.VMEM((STEPS * CX * CY, NC * 128), f32)],
        flops=10000000,
    )
    x_a = swap(back_a, "gx", 1)
    x_b = pair_b(back_b, "gx", "gy")
    loose = [xor for xor in range(2, ny) if ny != 4 or xor != 3]
    back_a, back_b, near, sums, *back = call(
        lambda *refs: add_x(ny, *refs),
        [
            (CORNERS + rows, 128),
            (CORNERS + (rows if ny == 4 else 0), 128),
            fine.shape,
            (rows, 128),
        ]
        + [(rows, 128)] * len(loose),
        [fine, picks, core, x_a, x_b],
        [pltpu.VMEM((NC * CORE, 128), f32), pltpu.VMEM((total * NC, 128), f32)],
    )
    y_a = swap(rim_a, "gy", 1)
    y_b = pair_b(rim_b, "gy", "gx")
    small_a = swap(back_a, "gy", 1)
    small_b = ring_b(back_b, "gy")
    others = [swap(value, "gy", xor) for xor, value in zip(loose, back)]
    grad_delta, grad_alpha = call(
        add_y,
        [fine.shape, control.shape],
        [control_near, near, sums, y_a, y_b, small_a, small_b, *others],
    )
    return grad_delta.reshape(delta.shape), grad_alpha.reshape(alpha.shape)


def solution(mesh):
    return jax.shard_map(
        on_device,
        mesh=mesh,
        in_specs=(
            P(None, "gx", "gy", None),
            P("gx", "gy", None, None),
            P("gx", "gy", None),
            P(None, "gx", "gy", None),
            P("gx", "gy"),
            P(("gx", "gy"), None, None),
            P("gx", "gy", None),
            P("gx", "gy", None),
            P("gx", "gy", None),
            P("gx", "gy", None),
            P("gx", "gy", None, None, None),
            P("gx", "gy", None),
        ),
        out_specs=(P(None, "gx", "gy", None), P("gx", "gy", None, None)),
        check_vma=False,
    )
```

```python
import jax
import jax.numpy as jnp
from jax import lax
from jax.experimental import pallas as pl
from jax.experimental.pallas import tpu as pltpu
from jax.sharding import PartitionSpec as P

STEPS = 3
RIM = 3
INNER = RIM - 1
NC = 4
CX = 16
CY = 16
BLOCKS = CX + 8
PITCH = CY + 8
FIRST = 4
FIELD = BLOCKS * PITCH
CORE = CX * PITCH
OWN_BEAMS = 8
BEAM_BITS = 3

profile_weight = 0.125
f32 = jnp.float32
bf16 = jnp.bfloat16

VMEM = pl.BlockSpec(memory_space=pltpu.VMEM)
HBM = pl.BlockSpec(memory_space=pltpu.HBM)


def call(body, outs, ins, scratch=(), in_specs=None, flops=1000000, limit=40 * 2**20):
    shapes = [
        out if isinstance(out, jax.ShapeDtypeStruct) else jax.ShapeDtypeStruct(out, f32)
        for out in outs
    ]
    size = sum(4 * value.size for value in ins)
    return pl.pallas_call(
        body,
        out_shape=shapes,
        in_specs=in_specs or [VMEM] * len(ins),
        out_specs=[VMEM] * len(shapes),
        scratch_shapes=list(scratch),
        compiler_params=pltpu.CompilerParams(vmem_limit_bytes=limit),
        cost_estimate=pl.CostEstimate(flops=flops, bytes_accessed=size, transcendentals=0),
    )(*ins)


def swap(block, axis, xor):
    return lax.ppermute(block, axis, [(i, i ^ xor) for i in range(lax.axis_size(axis))])


def pair_b(block, axis, other):
    count, across = lax.axis_size(axis), lax.axis_size(other)

    def place(i, j):
        return i * across + j if axis == "gx" else j * count + i

    pairs = []
    for j in range(across):
        for i in range(count):
            if i in (0, count - 1):
                pairs.append((place(i, j), place(i, j ^ 1)))
            else:
                pairs.append((place(i, j), place(i + 1 if i % 2 else i - 1, j)))
    return lax.ppermute(block, ("gx", "gy"), pairs)


def ring_b(block, axis):
    count = lax.axis_size(axis)
    pairs = [(i, (i + 1 if i % 2 else i - 1) % count) for i in range(count)]
    return lax.ppermute(block, axis, pairs)


def place_on(axis):
    me = lax.axis_index(axis)
    return lax.rem(me, 2) == 0, me > 0, me < lax.axis_size(axis) - 1


def split(value):
    top = value.astype(bf16)
    return top, (value - top.astype(f32)).astype(bf16)


def two_part_dot(left, value):
    top, low = split(value)
    return jnp.dot(left, top, preferred_element_type=f32) + jnp.dot(
        left, low, preferred_element_type=f32
    )


def layers(reach):
    found, at = [], 0
    for away in range(1, reach + 1):
        found.append((away, at, reach - away))
        at += CY + 2 * (reach - away)
    return found, at


WIDE, WIDE_ROWS = layers(RIM)
SLIM, SLIM_ROWS = layers(INNER)
X_COEF = NC * WIDE_ROWS
CORNERS = NC * 2 * sum(extra for _, _, extra in WIDE)
X_HALO = X_COEF + 3 * SLIM_ROWS

Y_COEF = NC * RIM * CX
Y_TILE = Y_COEF + 3 * INNER * CX
Y_HALO = Y_TILE + CX


def pack_y(
    delta,
    eddy,
    courant,
    alpha,
    tile_map,
    gate_beam,
    gate_index,
    gate_column,
    gate_live,
    precision,
    beam_rows,
    out_a,
    out_b,
    fine,
    coefs,
    profiles,
    near_tiles,
    meta,
    beams,
    tiles,
    gates,
    values,
    sems,
):
    even, _, _ = place_on("gy")
    moves = [
        pltpu.make_async_copy(source, target, sems.at[i])
        for i, (source, target) in enumerate(
            [
                (delta, fine),
                (eddy, coefs.at[0]),
                (courant.at[0], coefs.at[1]),
                (courant.at[1], coefs.at[2]),
                (tile_map, tiles),
                (alpha, profiles),
                (gate_beam, gates.at[0]),
                (gate_index, gates.at[1]),
                (gate_column, gates.at[2]),
                (gate_live, gates.at[3]),
                (precision, values),
                (beam_rows, beams),
            ]
        )
    ]
    for move in moves:
        move.start()
    for move in moves[1:]:
        move.wait()

    def put(at, field, away):
        north = field[pl.ds(CY - away, CX, stride=CY)]
        south = field[pl.ds(away - 1, CX, stride=CY)]
        out_a[at : at + CX] = jnp.where(even, north, south)
        out_b[at : at + CX] = jnp.where(even, south, north)

    for f in range(3):
        for away in range(1, INNER + 1):
            put(Y_COEF + (f * INNER + away - 1) * CX, coefs.at[f], away)
    near_tiles[...] = jnp.full((CX, 128), -1.0, f32)
    near_tiles[:, 0:CY] = tiles[...].astype(f32)
    for out in (out_a, out_b):
        out[Y_TILE : Y_TILE + CX] = near_tiles[...]
    out_a[Y_HALO:] = profiles[...]
    held = BEAM_BITS
    beam = gates[0]
    owner = jnp.bitwise_xor(beam >> held, lax.axis_index("gx"))
    meta[...] = jnp.zeros(meta.shape, f32)
    meta[0:1] = gates[2].astype(f32)
    half = lax.axis_size("gx") // 2
    owner = (((half - (owner >> 1)) & (half - 1)) << 1) | (owner & 1)
    meta[1:2] = ((owner << held) | (beam & ((1 << held) - 1))).astype(f32)
    meta[2:3] = gates[1].astype(f32)
    meta[3:4] = gates[3].astype(f32) * values[...]
    moves[0].wait()
    for c in range(NC):
        for away in range(1, RIM + 1):
            put((c * RIM + away - 1) * CX, fine.at[c], away)


def y_sides(got_a, got_b, rows, fill=0.0):
    even, low, high = place_on("gy")
    first, second = got_a[rows], got_b[rows]
    north, south = jnp.where(even, first, second), jnp.where(even, second, first)
    return jnp.where(high, north, fill), jnp.where(low, south, fill)


def x_sides(got_a, got_b, rows):
    even, low, high = place_on("gx")
    first, second = got_a[rows], got_b[rows]
    west, east = jnp.where(even, second, first), jnp.where(even, first, second)
    return jnp.where(low, west, 0.0), jnp.where(high, east, 0.0)


def gather_known(alpha, got_a, others, known):
    owned = alpha.shape[0]
    known[0:owned] = alpha[...]
    known[owned : 2 * owned] = got_a[Y_HALO:]
    for s, other in enumerate(others):
        known[(2 + s) * owned : (3 + s) * owned] = other[...]


def tile_numbers(near_tiles, got_a, got_b, tiles):
    spot = lax.broadcasted_iota(jnp.int32, (CX, 128), 1)
    north, south = y_sides(got_a, got_b, pl.ds(Y_TILE, CX), -1.0)
    near = jnp.where(
        (spot >= CY) & (spot < CY + RIM),
        pltpu.roll(north, CY, 1),
        jnp.where((spot >= PITCH - RIM) & (spot < PITCH), pltpu.roll(south, PITCH - CY, 1), -1.0),
    )
    tiles[...] = jnp.full(tiles.shape, -1.0, f32)
    tiles[0:CX] = jnp.where(spot < CY, near_tiles[...], near)
    return jnp.transpose(tiles[...])[0:PITCH]


def tile_ids(ny, owned):
    me = lax.axis_index("gy")
    lane = lax.broadcasted_iota(jnp.int32, (1, ny * owned), 1)
    ids = lane
    for s in range(ny):
        here = (lane >= s * owned) & (lane < (s + 1) * owned)
        ids = jnp.where(here, jnp.bitwise_xor(me, s) * owned + lane - s * owned, ids)
    return ids.astype(f32)


def by_variable(ref, count):
    return jnp.concatenate([ref[pl.ds(c, count, stride=NC)] for c in range(NC)], axis=1)


def pack_x(ny, delta, coefs, alpha, near_tiles, _, y_a, y_b, *rest):
    others = rest[: ny - 2]
    out_a, out_b, field, picks, known, tiles = rest[ny - 2 :]
    even, _, _ = place_on("gx")
    owned = alpha.shape[0] // NC
    gather_known(alpha, y_a, others, known)
    turned = tile_numbers(near_tiles, y_a, y_b, tiles)
    ids = tile_ids(ny, owned)
    columns = [x for x in range(RIM)] + [CX - RIM + x for x in range(RIM)]
    for i, x in enumerate(columns):
        picks[i * PITCH : (i + 1) * PITCH] = (turned[:, x : x + 1] == ids).astype(f32)
    fine = two_part_dot(picks[...].astype(bf16), by_variable(known, ny * owned))

    def fill(own, y_base, reach, c):
        for i, x in enumerate(columns):
            at = i * PITCH
            field[at + CY : at + PITCH] = jnp.zeros((PITCH - CY, 128), f32)
            field[at : at + CY] = own[x * CY : (x + 1) * CY]
        for away in range(1, reach + 1):
            for first, base in ((0, 0), (CX - RIM, RIM * PITCH)):
                rows = pl.ds(y_base + (away - 1) * CX + first, RIM)
                north, south = y_sides(y_a, y_b, rows)
                field[pl.ds(base + CY - 1 + away, RIM, stride=PITCH)] = north
                field[pl.ds(base + PITCH - away, RIM, stride=PITCH)] = south
        if c is not None:
            field[...] += profile_weight * fine[:, c * 128 : (c + 1) * 128]

    def put(at, found):
        for away, start, extra in found:
            east, west = (2 * RIM - away) * PITCH, (away - 1) * PITCH
            here = at + start
            for source, target, size in (
                (PITCH - extra, 0, extra),
                (0, extra, CY + extra),
            ):
                if size:
                    first = field[east + source : east + source + size]
                    second = field[west + source : west + source + size]
                    rows = slice(here + target, here + target + size)
                    out_a[rows] = jnp.where(even, first, second)
                    out_b[rows] = jnp.where(even, second, first)

    for c in range(NC):
        fill(delta.at[c], c * RIM * CX, RIM, c)
        put(c * WIDE_ROWS, WIDE)
    for f in range(3):
        fill(coefs.at[f], Y_COEF + f * INNER * CX, INNER, None)
        put(X_COEF + f * SLIM_ROWS, SLIM)


def one_hots(meta, weights, wide, slot_pick, slot_push, beam_pick, columns, edge_pick):
    slots = meta.shape[1]
    for c in range(NC):
        wide[:, c * 128 : (c + 1) * 128] = weights[pl.ds(c, slots, stride=NC)]
    per_beam = beam_pick.shape[1]
    turned = jnp.transpose(meta[...])
    columns[...] = turned
    slot_lane = lax.broadcasted_iota(jnp.int32, (slots, CX * CY), 1).astype(f32)
    slot_pick[...] = (slot_lane == turned[:, 0:1]).astype(f32).astype(bf16)
    edge_lane = lax.broadcasted_iota(jnp.int32, (slots, 128), 1)
    half = RIM * CY
    place = jnp.where(edge_lane < half, edge_lane, edge_lane + CX * CY - 2 * half)
    place = jnp.where(edge_lane < 2 * half, place, -1).astype(f32)
    near_edge = (place == turned[:, 0:1]).astype(f32).astype(bf16)
    edge_pick[:, 0:128] = near_edge
    edge_pick[:, 128:256] = near_edge
    column_row = lax.broadcasted_iota(jnp.int32, (CX * CY, slots), 0).astype(f32)
    slot_push[...] = (column_row == meta[0:1]).astype(f32).astype(bf16)
    beam_lane = lax.broadcasted_iota(jnp.int32, (slots, per_beam), 1).astype(f32)
    beam_pick[...] = (beam_lane == turned[:, 1:2]).astype(f32).astype(bf16)


def prepare(ny, delta, coefs, alpha, near_tiles, columns, slot_pick, wide, y_a, y_b, *rest):
    others = rest[: ny - 2]
    core, coef, picks, state_1, state_2, tally, state_3, known, tiles = rest[ny - 2 :]
    owned = alpha.shape[0] // NC

    def fill(ref, base, own, y_base, reach):
        for x in range(CX):
            at = base + x * PITCH
            ref[at : at + CY] = own[x * CY : (x + 1) * CY]
            ref[at + CY : at + PITCH] = jnp.zeros((PITCH - CY, 128), f32)
        for away in range(1, reach + 1):
            north, south = y_sides(y_a, y_b, pl.ds(y_base + (away - 1) * CX, CX))
            ref[pl.ds(base + CY - 1 + away, CX, stride=PITCH)] = north
            ref[pl.ds(base + PITCH - away, CX, stride=PITCH)] = south

    for c in range(NC):
        fill(core, c * CORE, delta.at[c], c * RIM * CX, RIM)
    for f in range(3):
        fill(coef, f * CORE, coefs.at[f], Y_COEF + f * INNER * CX, INNER)

    def combine(b, carry):
        at = pl.multiple_of(b * PITCH, 8)
        combined = combine_coefs(*[coef[pl.ds(f * CORE + at, PITCH)] for f in range(3)])
        for f, value in enumerate(combined):
            coef[pl.ds(f * CORE + at, PITCH)] = value
        return carry

    lax.fori_loop(0, CX, combine, 0, unroll=True)

    gather_known(alpha, y_a, others, known)
    turned = tile_numbers(near_tiles, y_a, y_b, tiles)
    ids = tile_ids(ny, owned)
    for x in range(CX):
        picks[x * PITCH : (x + 1) * PITCH] = (turned[:, x : x + 1] == ids).astype(f32)
    fine = two_part_dot(picks[...].astype(bf16), by_variable(known, ny * owned))
    for c in range(NC):
        core[c * CORE : (c + 1) * CORE] += profile_weight * fine[:, c * 128 : (c + 1) * 128]

    slots = columns.shape[0]
    states = [core, state_1, state_2, state_3]
    for step in range(STEPS):
        source, target = states[step], states[step + 1]

        def body(x, carry, source=source, target=target):
            at = pl.multiple_of(x * PITCH, 8)
            k = [coef[pl.ds(f * CORE + at, PITCH)] for f in range(5)]
            for c in range(NC):
                base = c * CORE + at
                target[pl.ds(base, PITCH)] = forward_column(source, base, k)
            return carry

        lax.fori_loop(step + 1, CX - 1 - step, body, 0, unroll=True)
        own = []
        for c in range(NC):
            pieces = [jnp.zeros(((step + 1) * CY, 128), f32)]
            for x in range(step + 1, CX - 1 - step):
                at = c * CORE + x * PITCH
                pieces.append(target[at : at + CY])
            own.append(jnp.concatenate(pieces + pieces[:1], axis=0))
        seen = two_part_dot(slot_pick[...], jnp.concatenate(own, axis=1)) * wide[...]
        total = seen[:, 0:128]
        for c in range(1, NC):
            total = total + seen[:, c * 128 : (c + 1) * 128]
        tally[step * slots : (step + 1) * slots] = total


def forward_column(source, base, k):
    here = source[pl.ds(base, PITCH)]
    return (
        k[0] * here
        + k[1] * source[pl.ds(base + PITCH, PITCH)]
        + k[2] * source[pl.ds(base - PITCH, PITCH)]
        + k[3] * pltpu.roll(here, PITCH - 1, 0)
        + k[4] * pltpu.roll(here, 1, 0)
    )


def backward_column(source, base, coef, at):
    here = source[pl.ds(base, PITCH)]
    return (
        coef[pl.ds(at, PITCH)] * here
        + coef[pl.ds(FIELD + at - PITCH, PITCH)] * source[pl.ds(base - PITCH, PITCH)]
        + coef[pl.ds(2 * FIELD + at + PITCH, PITCH)] * source[pl.ds(base + PITCH, PITCH)]
        + pltpu.roll(coef[pl.ds(3 * FIELD + at, PITCH)] * here, 1, 0)
        + pltpu.roll(coef[pl.ds(4 * FIELD + at, PITCH)] * here, PITCH - 1, 0)
    )


def combine_coefs(viscous, along_x, along_y):
    half_x, half_y = 0.5 * along_x, 0.5 * along_y
    return (
        1.0 - 4.0 * viscous,
        viscous - half_x,
        viscous + half_x,
        viscous - half_y,
        viscous + half_y,
    )


def clear(ref, base, blocks):
    for b in blocks:
        at = base + b * PITCH
        ref[at : at + PITCH] = jnp.zeros((PITCH, 128), f32)


def edges(
    core,
    core_coef,
    near_1,
    near_2,
    tally,
    wide,
    edge_pick,
    x_a,
    x_b,
    coef,
    totals,
    state_0,
    state_1,
    state_2,
    state_3,
    raw,
):
    slots = wide.shape[0]

    def fill(ref, base, x_base, found):
        for away, start, extra in found:
            for source, target, size in (
                (0, PITCH - extra, extra),
                (extra, 0, CY + extra),
            ):
                if size:
                    at = x_base + start + source
                    west, east = x_sides(x_a, x_b, pl.ds(at, size))
                    at = base + (FIRST - away) * PITCH + target
                    ref[at : at + size] = west
                    at = base + (FIRST + CX - 1 + away) * PITCH + target
                    ref[at : at + size] = east

    def copy(source, target, x, count):
        for c in range(NC):
            first = c * CORE + x * PITCH
            at = c * FIELD + (FIRST + x) * PITCH
            target[at : at + count * PITCH] = source[first : first + count * PITCH]

    rim = [FIRST - 3, FIRST - 2, FIRST - 1, FIRST + CX, FIRST + CX + 1, FIRST + CX + 2]
    for x, (source, target) in enumerate(((core, state_0), (near_1, state_1), (near_2, state_2))):
        copy(source, target, x, 2)
        copy(source, target, CX - 2 - x, 2)
    for c in range(NC):
        clear(state_0, c * FIELD, rim)
        fill(state_0, c * FIELD, c * WIDE_ROWS, WIDE)
    for f in range(3):
        clear(raw, f * FIELD, rim[1:5])
        fill(raw, f * FIELD, X_COEF + f * SLIM_ROWS, SLIM)
    for f in range(5):
        for x in (0, CX - RIM):
            first, at = f * CORE + x * PITCH, f * FIELD + (FIRST + x) * PITCH
            coef[at : at + RIM * PITCH] = core_coef[first : first + RIM * PITCH]
        clear(coef, f * FIELD, [0, 1, BLOCKS - 2, BLOCKS - 1])
    for b in rim[1:5]:
        rows = [slice(f * FIELD + b * PITCH, f * FIELD + (b + 1) * PITCH) for f in range(5)]
        for f, value in enumerate(combine_coefs(*[raw[rows[f]] for f in range(3)])):
            coef[rows[f]] = value

    outer = [*range(RIM), *range(CX - RIM, CX)]
    half = RIM * CY
    states = [state_0, state_1, state_2, state_3]
    for step in range(STEPS):
        source, target = states[step], states[step + 1]
        for x in range(step - 2, step + 1):
            for b in (FIRST + x, FIRST + CX - 1 - x):
                at = b * PITCH
                k = [coef[f * FIELD + at : f * FIELD + at + PITCH] for f in range(5)]
                for c in range(NC):
                    base = c * FIELD + at
                    target[base : base + PITCH] = forward_column(source, base, k)
        zero = jnp.zeros((CY, 128), f32)
        parts = []
        for c in range(NC):
            pieces = []
            for x in outer:
                at = c * FIELD + (FIRST + x) * PITCH
                known = x <= step or x >= CX - 1 - step
                pieces.append(target[at : at + CY] if known else zero)
            value = jnp.concatenate(pieces + [jnp.zeros((128 - 2 * half, 128), f32)], axis=0)
            parts.append(jnp.concatenate(split(value), axis=0))
        seen = jnp.dot(
            edge_pick[...], jnp.concatenate(parts, axis=1), preferred_element_type=f32
        )
        seen = seen * wide[...]
        rows = slice(step * slots, (step + 1) * slots)
        total = tally[rows]
        for c in range(NC):
            total = total + seen[:, c * 128 : (c + 1) * 128]
        totals[rows] = total


def push_edges(coef, totals, wide, slot_push, beam_pick, columns, *rest):
    beams = rest[:-9]
    out_a, out_b, back_2, back_1, tops, lows, state_0, state_3, forcing = rest[-9:]
    even, _, _ = place_on("gx")
    slots = columns.shape[0]
    gate_lane = lax.broadcasted_iota(jnp.int32, (slots, 128), 1).astype(f32)
    gate_here = gate_lane == columns[:, 2:3]
    scaled = columns[:, 3:4]
    outer = [*range(RIM), *range(CX - RIM, CX)]
    half = RIM * CY
    push = jnp.concatenate([slot_push[0:half], slot_push[CX * CY - half :]], axis=0)
    for step in range(STEPS):
        table = []
        for part in beams:
            for at in range(0, part.shape[0], STEPS * OWN_BEAMS):
                first = at + step * OWN_BEAMS
                table.append(part[first : first + OWN_BEAMS])
        table = two_part_dot(beam_pick[...], jnp.concatenate(table, axis=0))
        rows = slice(step * slots, (step + 1) * slots)
        total = totals[rows] - jnp.where(gate_here, table, 0.0)
        misfit = scaled * jnp.sum(total, axis=1, keepdims=True)
        top, low = split(misfit * wide[...])
        tops[rows] = top
        lows[rows] = low
        forcing[step * 2 * half : (step + 1) * 2 * half] = jnp.dot(
            push, top, preferred_element_type=f32
        ) + jnp.dot(push, low, preferred_element_type=f32)

    def forced(step, i, c):
        at = step * 2 * half + i * CY
        return forcing[at : at + CY, c * 128 : (c + 1) * 128]

    for c in range(NC):
        clear(state_0, c * FIELD, [2, 3, BLOCKS - 4, BLOCKS - 3])
        clear(back_2, c * FIELD, [1, 2, BLOCKS - 3, BLOCKS - 2])
        clear(back_1, c * FIELD, [0, 1, BLOCKS - 2, BLOCKS - 1])
        for i, x in enumerate(outer):
            at = c * FIELD + (FIRST + x) * PITCH
            state_0[at : at + CY] = forced(STEPS - 1, i, c)
            state_0[at + CY : at + PITCH] = jnp.zeros((PITCH - CY, 128), f32)
    fields = [state_0, back_2, back_1, state_3]
    for step in range(STEPS):
        source, target = fields[step], fields[step + 1]
        for x in range(-1 - step, 2 - step):
            for b in (FIRST + x, FIRST + CX - 1 - x):
                for c in range(NC):
                    base = c * FIELD + b * PITCH
                    target[base : base + PITCH] = backward_column(source, base, coef, b * PITCH)
        if step < STEPS - 1:
            for i, x in enumerate(outer):
                if x < 2 - step or x > CX - 3 + step:
                    for c in range(NC):
                        at = c * FIELD + (FIRST + x) * PITCH
                        target[at : at + CY] += forced(STEPS - 2 - step, i, c)
    for c in range(NC):
        for away, start, extra in WIDE:
            for source, target, size in (
                (PITCH - extra, 0, extra),
                (0, extra, CY + extra),
            ):
                if size:
                    at = c * FIELD + (FIRST - away) * PITCH + source
                    west = state_3[at : at + size]
                    at = c * FIELD + (FIRST + CX - 1 + away) * PITCH + source
                    east = state_3[at : at + size]
                    at = c * WIDE_ROWS + start + target
                    out_a[at : at + size] = jnp.where(even, east, west)
                    out_b[at : at + size] = jnp.where(even, west, east)


def interior(
    core_coef,
    edge_coef,
    back_2,
    back_1,
    tops,
    lows,
    slot_push,
    picks,
    out,
    out_a,
    out_b,
    out_picks,
    *scratch,
):
    coef, forced, field_2, field_1, forcing = scratch
    out_picks[...] = jnp.transpose(picks[...]).astype(bf16)
    for f in range(5):
        at = f * FIELD + FIRST * PITCH
        coef[at : at + CORE] = core_coef[f * CORE : (f + 1) * CORE]
        for b in (FIRST - 1, FIRST + CX):
            at = f * FIELD + b * PITCH
            coef[at : at + PITCH] = edge_coef[at : at + PITCH]
    for step in range(STEPS):
        rows = slice(step * CX * CY, (step + 1) * CX * CY)
        forcing[rows] = jnp.dot(
            slot_push[...], tops[rows], preferred_element_type=f32
        ) + jnp.dot(slot_push[...], lows[rows], preferred_element_type=f32)

    def add_forcing(ref, step, columns):
        for c in range(NC):
            for x in columns:
                at = c * FIELD + (FIRST + x) * PITCH
                first = step * CX * CY + x * CY
                value = forcing[first : first + CY, c * 128 : (c + 1) * 128]
                if step == STEPS - 1:
                    ref[at : at + CY] = value
                    ref[at + CY : at + PITCH] = jnp.zeros((PITCH - CY, 128), f32)
                else:
                    ref[at : at + CY] += value

    def sweep(source, target, low, high):
        def body(x, carry):
            at = pl.multiple_of((x + FIRST) * PITCH, 8)
            for c in range(NC):
                value = backward_column(source, c * FIELD + at, coef, at)
                if target is out:
                    target[pl.ds(pl.multiple_of(c * CORE + x * PITCH, 8), PITCH)] = value
                else:
                    target[pl.ds(c * FIELD + at, PITCH)] = value
            return carry

        lax.fori_loop(low, high, body, 0, unroll=True)

    def copy(source, target, columns):
        for c in range(NC):
            for x in columns:
                at = c * FIELD + (FIRST + x) * PITCH
                target[at : at + PITCH] = source[at : at + PITCH]

    add_forcing(forced, STEPS - 1, range(CX))
    sweep(forced, field_2, 2, CX - 2)
    add_forcing(field_2, STEPS - 2, range(2, CX - 2))
    copy(back_2, field_2, (0, 1, CX - 2, CX - 1))
    sweep(field_2, field_1, 1, CX - 1)
    add_forcing(field_1, STEPS - 3, range(1, CX - 1))
    copy(back_1, field_1, (-1, 0, CX - 1, CX))
    sweep(field_1, out, 0, CX)
    even, _, _ = place_on("gy")
    for c in range(NC):
        for away in range(1, RIM + 1):
            north = out[pl.ds(c * CORE + CY - 1 + away, CX, stride=PITCH)]
            south = out[pl.ds(c * CORE + PITCH - away, CX, stride=PITCH)]
            at = (c * RIM + away - 1) * CX
            out_a[at : at + CX] = jnp.where(even, north, south)
            out_b[at : at + CX] = jnp.where(even, south, north)


def add_x(ny, delta, picks, core, x_a, x_b, *rest):
    out_a, out_b, out_near, out_sums = rest[:4]
    out_others = rest[4:-2]
    merged = ny == 4
    field, sums = rest[-2:]
    even, _, _ = place_on("gy")
    total = picks.shape[0]
    rows = total * NC // ny
    field[...] = core[...]
    for c in range(NC):
        for away, start, extra in WIDE:
            for source, target, size in (
                (0, PITCH - extra, extra),
                (extra, 0, CY + extra),
            ):
                if size:
                    at = c * WIDE_ROWS + start + source
                    west, east = x_sides(x_a, x_b, pl.ds(at, size))
                    at = c * CORE + (away - 1) * PITCH + target
                    field[at : at + size] += west
                    at = c * CORE + (CX - away) * PITCH + target
                    field[at : at + size] += east
    at = 0
    for c in range(NC):
        for away, start, extra in WIDE:
            if extra:
                first = c * WIDE_ROWS + start
                south = x_sides(x_a, x_b, pl.ds(first, extra))
                north = x_sides(x_a, x_b, pl.ds(first + extra + CY, extra))
                for side in range(2):
                    out_a[at : at + extra] = jnp.where(even, north[side], south[side])
                    out_b[at : at + extra] = jnp.where(even, south[side], north[side])
                    at += extra
    for c in range(NC):
        for x in range(CX):
            at = c * CORE + x * PITCH
            here = slice(x * CY, (x + 1) * CY)
            out_near[c, here] = delta[c, here] + field[at : at + CY]
    adjoint = jnp.concatenate([field[c * CORE : (c + 1) * CORE] for c in range(NC)], axis=1)
    tile_sums = two_part_dot(picks[...], adjoint)
    for c in range(NC):
        sums[pl.ds(c, total, stride=NC)] = tile_sums[:, c * 128 : (c + 1) * 128]
    out_sums[...] = sums[0:rows]
    out_a[CORNERS:] = sums[rows : 2 * rows]
    if merged:
        out_b[CORNERS:] = sums[3 * rows : 4 * rows]
    for s, other in enumerate(out_others):
        other[...] = sums[(2 + s) * rows : (3 + s) * rows]


def add_y(alpha, near, sums, y_a, y_b, small_a, small_b, *rest):
    others = rest[:-2]
    out_delta, out_alpha = rest[-2:]
    out_delta[...] = near[...]
    at = 0
    for c in range(NC):
        for away, start, extra in WIDE:
            north, south = y_sides(y_a, y_b, pl.ds((c * RIM + away - 1) * CX, CX))
            high = pl.ds(CY - away, CX, stride=CY)
            low = pl.ds(away - 1, CX, stride=CY)
            out_delta[c, high] = out_delta[c, high] + north
            out_delta[c, low] = out_delta[c, low] + south
            if extra:
                for x in (away - 1, CX - away):
                    north, south = y_sides(small_a, small_b, pl.ds(at, extra))
                    out_delta[c, (x + 1) * CY - extra : (x + 1) * CY] += north
                    out_delta[c, x * CY : x * CY + extra] += south
                    at += extra
    total = sums[...] + small_a[CORNERS:]
    if small_b.shape[0] > CORNERS:
        total = total + small_b[CORNERS:]
    for other in others:
        total = total + other[...]
    out_alpha[...] = alpha[...] + profile_weight * total


def on_device(
    delta,
    alpha,
    eddy,
    courant,
    tile_map,
    obs_rows,
    gate_beam,
    gate_index,
    gate_column,
    gate_live,
    obs_weight,
    obs_precision,
):
    nx = lax.axis_size("gx")
    ny = lax.axis_size("gy")
    owned = alpha.shape[1]
    slots = gate_column.shape[2]
    fine = delta.reshape(NC, CX * CY, 128)
    eddy = eddy.reshape(CX * CY, 128)
    courant = courant.reshape(2, CX * CY, 128)
    control = alpha.reshape(owned * NC, 128)
    weights = obs_weight.reshape(slots * NC, 128)
    gates = [
        value.reshape(1, slots)
        for value in (gate_beam, gate_index, gate_column, gate_live, obs_precision)
    ]
    own_beams = jnp.transpose(obs_rows, (1, 0, 2)).reshape(STEPS * OWN_BEAMS, 128)
    beam_count = nx * OWN_BEAMS
    rows = owned * NC
    total = ny * owned

    y_a, y_b, fine, coefs, control_near, near_tiles, meta, near_beams = call(
        pack_y,
        [
            (Y_HALO + rows, 128),
            (Y_HALO, 128),
            fine.shape,
            (3, CX * CY, 128),
            control.shape,
            (CX, 128),
            (8, slots),
            own_beams.shape,
        ],
        [
            pltpu.with_memory_space_constraint(value, pltpu.HBM)
            for value in (fine, eddy, courant, control, tile_map, *gates, own_beams)
        ],
        [
            pltpu.VMEM(tile_map.shape, jnp.int32),
            pltpu.VMEM((4, 1, slots), jnp.int32),
            pltpu.VMEM((1, slots), f32),
            pltpu.SemaphoreType.DMA((12,)),
        ],
        in_specs=[HBM] * 11,
    )
    y_a = swap(y_a, "gy", 1)
    y_b = pair_b(y_b, "gy", "gx")
    others = [swap(control, "gy", xor) for xor in range(2, ny)]
    beams = jnp.concatenate([near_beams, swap(own_beams, "gx", 1)])
    beams = [beams] + [swap(beams, "gx", xor) for xor in range(nx - 2, 0, -2)]

    wide, slot_pick, slot_push, beam_pick, columns, edge_pick = call(
        one_hots,
        [
            (slots, NC * 128),
            jax.ShapeDtypeStruct((slots, CX * CY), bf16),
            jax.ShapeDtypeStruct((CX * CY, slots), bf16),
            jax.ShapeDtypeStruct((slots, beam_count), bf16),
            (slots, 8),
            jax.ShapeDtypeStruct((slots, 256), bf16),
        ],
        [meta, weights],
    )
    x_a, x_b = call(
        lambda *refs: pack_x(ny, *refs),
        [(X_HALO, 128), (X_HALO, 128)],
        [fine, coefs, control_near, near_tiles, columns, y_a, y_b, *others],
        [
            pltpu.VMEM((2 * RIM * PITCH, 128), f32),
            pltpu.VMEM((2 * RIM * PITCH, total), f32),
            pltpu.VMEM((total * NC, 128), f32),
            pltpu.VMEM((128, 128), f32),
        ],
    )
    x_a = swap(x_a, "gx", 1)
    x_b = pair_b(x_b, "gx", "gy")

    big = (NC * FIELD, 128)
    core, coef, picks, state_1, state_2, tally = call(
        lambda *refs: prepare(ny, *refs),
        [
            (NC * CORE, 128),
            (5 * CORE, 128),
            (CORE, total),
            (NC * CORE, 128),
            (NC * CORE, 128),
            (STEPS * slots, 128),
        ],
        [fine, coefs, control_near, near_tiles, columns, slot_pick, wide, y_a, y_b, *others],
        [
            pltpu.VMEM((NC * CORE, 128), f32),
            pltpu.VMEM((total * NC, 128), f32),
            pltpu.VMEM((128, 128), f32),
        ],
        flops=3000000,
    )
    edge_coef, totals = call(
        edges,
        [(5 * FIELD, 128), (STEPS * slots, 128)],
        [core, coef, state_1, state_2, tally, wide, edge_pick, x_a, x_b],
        [pltpu.VMEM(big, f32)] * 4 + [pltpu.VMEM((3 * FIELD, 128), f32)],
        flops=10000000,
    )
    back_a, back_b, back_2, back_1, tops, lows = call(
        push_edges,
        [
            (X_COEF, 128),
            (X_COEF, 128),
            big,
            big,
            jax.ShapeDtypeStruct((STEPS * slots, NC * 128), bf16),
            jax.ShapeDtypeStruct((STEPS * slots, NC * 128), bf16),
        ],
        [edge_coef, totals, wide, slot_push, beam_pick, columns, *beams],
        [
            pltpu.VMEM(big, f32),
            pltpu.VMEM(big, f32),
            pltpu.VMEM((STEPS * 2 * RIM * CY, NC * 128), f32),
        ],
        flops=10000000,
    )
    core, rim_a, rim_b, picks = call(
        interior,
        [
            (NC * CORE, 128),
            (Y_COEF, 128),
            (Y_COEF, 128),
            jax.ShapeDtypeStruct((total, CORE), bf16),
        ],
        [coef, edge_coef, back_2, back_1, tops, lows, slot_push, picks],
        [pltpu.VMEM((5 * FIELD, 128), f32)]
        + [pltpu.VMEM(big, f32)] * 3
        + [pltpu.VMEM((STEPS * CX * CY, NC * 128), f32)],
        flops=10000000,
    )
    x_a = swap(back_a, "gx", 1)
    x_b = pair_b(back_b, "gx", "gy")
    loose = [xor for xor in range(2, ny) if ny != 4 or xor != 3]
    back_a, back_b, near, sums, *back = call(
        lambda *refs: add_x(ny, *refs),
        [
            (CORNERS + rows, 128),
            (CORNERS + (rows if ny == 4 else 0), 128),
            fine.shape,
            (rows, 128),
        ]
        + [(rows, 128)] * len(loose),
        [fine, picks, core, x_a, x_b],
        [pltpu.VMEM((NC * CORE, 128), f32), pltpu.VMEM((total * NC, 128), f32)],
    )
    y_a = swap(rim_a, "gy", 1)
    y_b = pair_b(rim_b, "gy", "gx")
    small_a = swap(back_a, "gy", 1)
    small_b = ring_b(back_b, "gy")
    others = [swap(value, "gy", xor) for xor, value in zip(loose, back)]
    grad_delta, grad_alpha = call(
        add_y,
        [fine.shape, control.shape],
        [control_near, near, sums, y_a, y_b, small_a, small_b, *others],
    )
    return grad_delta.reshape(delta.shape), grad_alpha.reshape(alpha.shape)


def solution(mesh):
    return jax.shard_map(
        on_device,
        mesh=mesh,
        in_specs=(
            P(None, "gx", "gy", None),
            P("gx", "gy", None, None),
            P("gx", "gy", None),
            P(None, "gx", "gy", None),
            P("gx", "gy"),
            P(("gx", "gy"), None, None),
            P("gx", "gy", None),
            P("gx", "gy", None),
            P("gx", "gy", None),
            P("gx", "gy", None),
            P("gx", "gy", None, None, None),
            P("gx", "gy", None),
        ),
        out_specs=(P(None, "gx", "gy", None), P("gx", "gy", None, None)),
        check_vma=False,
    )
```
